32 devices in a mesh: dp: 8 (over z, x), seq: 4 (over y, core).
Axes of the slice: x: 2, y: 2, z: 4, core: 2. Of those that a mesh axis runs over, the one named last changes fastest.
Arguments:
- tokens_in: bfloat16 [16, 1024, 768], P('dp', 'seq'), may hold values from -6 to 6
- w_in: bfloat16 [768, 2304], P('dp', 'seq'), may hold values from -0.21875 to 0.21875
- w_out: bfloat16 [768, 768], P('dp', 'seq'), may hold values from -0.21875 to 0.21875
- w_up: bfloat16 [768, 3072], P('dp', 'seq'), may hold values from -0.21875 to 0.21875
- w_down: bfloat16 [3072, 768], P('dp', 'seq'), may hold values from -0.109375 to 0.109375
- norm_gains: bfloat16 [2, 768], P(None, 'seq'), may hold values from 0.5 to 1.5
- kernel: bfloat16 [1024, 768], P('dp', 'seq'), may hold values from -0.375 to 0.375
- taps: int32 [768], P('seq'), may hold values from 256 to 1024, as said below
- cotangent: bfloat16 [16, 1024, 768], P('dp', 'seq'), may hold values from -6 to 6
Outputs:
- output: bfloat16 [16, 1024, 768], P('dp', 'seq')
- grad_in: bfloat16 [16, 1024, 768], P('dp', 'seq')
- grad_w_in: float32 [768, 2304], P('dp', 'seq')
- grad_w_out: float32 [768, 768], P('dp', 'seq')
- grad_w_up: float32 [768, 3072], P('dp', 'seq')
- grad_w_down: float32 [3072, 768], P('dp', 'seq')
- grad_gains: float32 [2, 768], P(None, 'seq')
- grad_kernel: float32 [1024, 768], P('dp', 'seq')
The draws below stay inside these ranges and needn't reach their ends.
Inputs may be any that keep to these rules, and one draw needn't show every extreme that they name: taps[d] is the number of live taps of channel d; kernel entries at taps taps[d] and later are padding and never act. Some channel has all 1024 taps live and some has a quarter of 1024.
All inputs are finite; a program needn't handle non-finite values.
Results may differ from the reference program's by a relative error of at most 0.018.
Values may be sent and summed in bfloat16 or wider, within the bound.
A program may use at most 192 MiB of HBM per device.

```python
from functools import partial
import jax
import jax.numpy as jnp
from jax import lax

D = 768
FF = 3072
LENGTH = 1024
SEQUENCES = 16


def draw_taps(key, part):
    key = jax.random.fold_in(key, 7)
    key_count, key_long, key_short = jax.random.split(key, 3)
    counts = jax.random.randint(key_count, (D,), LENGTH // 4, LENGTH + 1)
    longest = jax.random.randint(key_long, (), 0, D)
    shortest = (longest + 1 + jax.random.randint(key_short, (), 0, D - 1)) % D
    channel = jnp.arange(D, dtype=jnp.int32)
    counts = jnp.where(channel == longest, LENGTH, counts)
    counts = jnp.where(channel == shortest, LENGTH // 4, counts)
    return counts.astype(jnp.int32)


def block_levels(key, shape, shards, low, top_value):
    loudness, own = 1.0, jax.random.fold_in(key, 6)
    for axis_at, shards_of in shards:
        steps = jnp.exp(jax.random.uniform(jax.random.fold_in(own, axis_at), (shards_of,), jnp.float32, low / len(shards), top_value / len(shards)))
        loudness = loudness * jnp.repeat(steps, shape[axis_at] // shards_of).reshape([-1 if axis == axis_at else 1 for axis in range(len(shape))])
    return loudness


def gaussian(own_key, dims, scale, most, cuts=(), kind=jnp.bfloat16):
    array = scale * jax.random.normal(own_key, dims, jnp.float32)
    if cuts:
        array = array * block_levels(own_key, dims, cuts, -0.22, 0.18)
    return jnp.clip(array, -most, most).astype(kind)


def setup_inputs(seed: int = 0) -> dict:
    splits = jax.random.split(jax.random.key(seed), 10)
    tokens_in = gaussian(splits[0], (SEQUENCES, LENGTH, D), 1.0, 6.0, ((0, 8), (1, 4)))
    w_in = gaussian(splits[1], (D, 3 * D), D ** -0.5, 0.21875, ((0, 8), (1, 4)))
    w_out = gaussian(splits[2], (D, D), D ** -0.5, 0.21875, ((0, 8), (1, 4)))
    w_up = gaussian(splits[3], (D, FF), D ** -0.5, 0.21875, ((0, 8), (1, 4)))
    w_down = gaussian(splits[4], (FF, D), FF ** -0.5, 0.109375, ((0, 8), (1, 4)))
    norm_gains = jnp.clip(1.0 + 0.1 * jax.random.normal(splits[5], (2, D), jnp.float32), 0.5, 1.5).astype(jnp.bfloat16)
    kernel = gaussian(splits[6], (LENGTH, D), (LENGTH // 4) ** -0.5, 0.375, ((0, 8), (1, 4)))
    taps = draw_taps(jax.random.fold_in(splits[9], 71), 0)
    cotangent = gaussian(splits[8], (SEQUENCES, LENGTH, D), 1.0, 6.0, ((0, 8), (1, 4)))
    return dict(tokens_in=tokens_in, w_in=w_in, w_out=w_out, w_up=w_up, w_down=w_down, norm_gains=norm_gains, kernel=kernel, taps=taps, cotangent=cotangent)


EPSILON = 1e-05
SHRINK_SCALE = 0.003

@jax.custom_vjp
def low(v):
    return lax.optimization_barrier(v.astype(jnp.bfloat16)).astype(jnp.float32)

@jax.custom_vjp
def low_back(v):
    return v

def low_keep(v):
    return (low(v), None)

def low_pass(kept, grad):
    return (grad,)

def back_keep(v):
    return (v, None)

def back_low(kept, grad):
    return (low(grad),)
low.defvjp(low_keep, low_pass)
low_back.defvjp(back_keep, back_low)

def highest(left, right):
    return jnp.dot(left, right, precision=lax.Precision.HIGHEST)

def norm_rows(values, gain):
    center = values - lax.optimization_barrier(jnp.mean(values, axis=-1, keepdims=True))
    spread = lax.optimization_barrier(jnp.mean(center * center, axis=-1, keepdims=True))
    return center * lax.rsqrt(spread + EPSILON) * gain

def shape_filter(kernel, taps):
    length = kernel.shape[0]
    position = jnp.arange(length, dtype=jnp.int32)[:, None]
    live_mask = (position < taps[None, :]).astype(kernel.dtype)
    masked = kernel * live_mask
    shrunk = masked - SHRINK_SCALE * jnp.tanh(masked / SHRINK_SCALE)
    padded = jnp.pad(shrunk, ((1, 1), (0, 0)))
    pooled = (padded[:-2] + padded[1:-1] + padded[2:]) / 3.0
    return pooled * live_mask

def causal_conv(filt, signal):
    length = signal.shape[0]
    total = 2 * length
    spec_signal = jnp.fft.rfft(signal, n=total, axis=0)
    spec_filter = jnp.fft.rfft(filt, n=total, axis=0)
    return jnp.fft.irfft(spec_signal * spec_filter, n=total, axis=0)[:length]

def block(tokens, w_in, w_out, w_up, w_down, gains, kernel, taps):
    width = tokens.shape[1]
    normed = low(norm_rows(tokens, gains[0]))
    proj = low_back(highest(normed, w_in))
    values = proj[:, :width]
    gate_one = proj[:, width:2 * width]
    gate_two = proj[:, 2 * width:]
    mixed = low(low_back(gate_one * values))
    conv = low(low_back(causal_conv(shape_filter(kernel, taps), mixed)))
    gated = low(gate_two * conv)
    resid = tokens + low_back(highest(gated, w_out))
    normed_two = low(norm_rows(resid, gains[1]))
    hidden_pre = low_back(highest(normed_two, w_up))
    active = low(jax.nn.gelu(hidden_pre, approximate=True))
    return resid + highest(active, w_down)

def reference(tokens_in, w_in, w_out, w_up, w_down, norm_gains, kernel, taps, cotangent):
    params = (w_in.astype(jnp.float32), w_out.astype(jnp.float32), w_up.astype(jnp.float32), w_down.astype(jnp.float32), norm_gains.astype(jnp.float32), kernel.astype(jnp.float32))
    layer = partial(block, taps=taps)

    def one_sequence(totals, pair):
        sequence, grad_seq = pair
        result, pullback = jax.vjp(layer, sequence.astype(jnp.float32), *params)
        grads = pullback(grad_seq.astype(jnp.float32))
        totals = tuple((total + grad for total, grad in zip(totals, grads[1:])))
        return (totals, (result.astype(jnp.bfloat16), grads[0].astype(jnp.bfloat16)))
    start = tuple((jnp.zeros_like(param) for param in params))
    totals, (results, grad_tokens) = lax.scan(one_sequence, start, (tokens_in, cotangent))
    return (results, grad_tokens, totals[0], totals[1], totals[2], totals[3], totals[4], totals[5])
```

```python
from functools import partial
import math

import jax
from jax.experimental import pallas as pl
from jax.experimental.pallas import tpu as pltpu
import ml_dtypes
import numpy as np
import jax.numpy as jnp
from jax import lax
from jax.sharding import PartitionSpec as P

EPSILON = 1e-05
SHRINK_SCALE = 0.003
HIGHEST = lax.Precision.HIGHEST


def norm_rows(values, gain):
    center = values - jnp.mean(values, axis=-1, keepdims=True)
    spread = jnp.mean(center * center, axis=-1, keepdims=True)
    return center * lax.rsqrt(spread + EPSILON) * gain


def shape_filter(kernel, taps):
    length = kernel.shape[0]
    position = jnp.arange(length, dtype=jnp.int32)[:, None]
    live_mask = (position < taps[None, :]).astype(kernel.dtype)
    masked = kernel * live_mask
    shrunk = masked - SHRINK_SCALE * jnp.tanh(masked / SHRINK_SCALE)
    padded = jnp.pad(shrunk, ((1, 1), (0, 0)))
    pooled = (padded[:-2] + padded[1:-1] + padded[2:]) / 3.0
    return pooled * live_mask


def gelu_tanh(values):
    return jax.nn.gelu(values, approximate=True)


def contract_rows(left, right):
    return lax.dot_general(
        left, right, (((0,), (0,)), ((), ())), preferred_element_type=jnp.float32
    )


def times_transposed(left, weight):
    return lax.dot_general(
        left, weight, (((1,), (1,)), ((), ())), preferred_element_type=jnp.float32
    )


def phase_table(count_rows, count_cols, period):
    row_index = lax.broadcasted_iota(jnp.int32, (count_rows, count_cols), 0)
    col_index = lax.broadcasted_iota(jnp.int32, (count_rows, count_cols), 1)
    angles = 2.0 * math.pi / period * (row_index * col_index % period).astype(jnp.float32)
    return (jnp.cos(angles), jnp.sin(angles))


def dft_factors(length):
    total = 2 * length
    first = max(2, total // 128)
    return (total, first, total // first)


def mix_last(field, table):
    return jnp.einsum("bckn,nm->bckm", field, table, precision=HIGHEST)


def forward_dft(field):
    batch, length, chans = field.shape
    total, first, second = dft_factors(length)
    half = first // 2
    blocks = field.reshape(batch, half, second, chans)
    cos_one, sin_one = phase_table(half, first, first)
    part_re = jnp.einsum("hk,bhnc->bckn", cos_one, blocks, precision=HIGHEST)
    part_im = -jnp.einsum("hk,bhnc->bckn", sin_one, blocks, precision=HIGHEST)
    cos_two, sin_two = phase_table(first, second, total)
    turn_re = part_re * cos_two + part_im * sin_two
    turn_im = part_im * cos_two - part_re * sin_two
    cos_three, sin_three = phase_table(second, second, second)
    spec_re = mix_last(turn_re, cos_three) + mix_last(turn_im, sin_three)
    spec_im = mix_last(turn_im, cos_three) - mix_last(turn_re, sin_three)
    return (spec_re, spec_im)


def inverse_dft(spec_re, spec_im):
    batch, chans, first, second = spec_re.shape
    total = first * second
    half = first // 2
    cos_three, sin_three = phase_table(second, second, second)
    back_re = mix_last(spec_re, cos_three) - mix_last(spec_im, sin_three)
    back_im = mix_last(spec_re, sin_three) + mix_last(spec_im, cos_three)
    cos_two, sin_two = phase_table(first, second, total)
    turn_re = back_re * cos_two - back_im * sin_two
    turn_im = back_re * sin_two + back_im * cos_two
    cos_one, sin_one = phase_table(half, first, first)
    blocks = jnp.einsum("hk,bckn->bhnc", cos_one, turn_re, precision=HIGHEST)
    blocks = blocks - jnp.einsum("hk,bckn->bhnc", sin_one, turn_im, precision=HIGHEST)
    return blocks.reshape(batch, half * second, chans) / total


def to_channels(field):
    return lax.all_to_all(field, "seq", split_axis=2, concat_axis=1, tiled=True)


def to_tokens(field):
    return lax.all_to_all(field, "seq", split_axis=1, concat_axis=2, tiled=True)


def general_body(tokens_in, w_in, w_out, w_up, w_down, norm_gains, kernel, taps, cotangent):
    w_in_rows, w_out_rows, w_up_rows, w_down_rows, gains = (
        lax.all_gather(w_in, "seq", axis=1, tiled=True),
        lax.all_gather(w_out, "seq", axis=1, tiled=True),
        lax.all_gather(w_up, "seq", axis=1, tiled=True),
        lax.all_gather(w_down, "seq", axis=1, tiled=True),
        lax.all_gather(norm_gains, "seq", axis=1, tiled=True),
    )
    full_in, full_out, full_up, full_down, kernel_cols = (
        lax.all_gather(w_in_rows, "dp", axis=0, tiled=True),
        lax.all_gather(w_out_rows, "dp", axis=0, tiled=True),
        lax.all_gather(w_up_rows, "dp", axis=0, tiled=True),
        lax.all_gather(w_down_rows, "dp", axis=0, tiled=True),
        lax.all_gather(kernel, "dp", axis=0, tiled=True),
    )
    num_seqs, local_len, width = tokens_in.shape
    total_rows = num_seqs * local_len
    inputs = tokens_in.reshape(total_rows, width).astype(jnp.float32)
    gains_wide = gains.astype(jnp.float32)
    normed, norm_back_one = jax.vjp(norm_rows, inputs, gains_wide[0])
    normed_low = normed.astype(jnp.bfloat16)
    proj = jnp.dot(normed_low, full_in, preferred_element_type=jnp.float32)
    values = proj[:, :width]
    gate_one = proj[:, width : 2 * width]
    gate_two = proj[:, 2 * width :]
    mixed_low = (gate_one * values).astype(jnp.bfloat16).reshape(num_seqs, local_len, width)
    by_channel = to_channels(mixed_low)
    filt, filter_back = jax.vjp(partial(shape_filter, taps=taps), kernel_cols.astype(jnp.float32))
    filt_re, filt_im = forward_dft(filt[None])
    sig_re, sig_im = forward_dft(by_channel.astype(jnp.float32))
    conv = inverse_dft(sig_re * filt_re - sig_im * filt_im, sig_re * filt_im + sig_im * filt_re)
    conv_tok = to_tokens(conv.astype(jnp.bfloat16)).reshape(total_rows, width).astype(jnp.float32)
    gated = (gate_two * conv_tok).astype(jnp.bfloat16)
    resid = inputs + jnp.dot(gated, full_out, preferred_element_type=jnp.float32)
    normed_two, norm_back_two = jax.vjp(norm_rows, resid, gains_wide[1])
    normed_two_low = normed_two.astype(jnp.bfloat16)
    hidden_pre = jnp.dot(normed_two_low, full_up, preferred_element_type=jnp.float32)
    active, gelu_back = jax.vjp(gelu_tanh, hidden_pre)
    active_low = active.astype(jnp.bfloat16)
    result = (resid + jnp.dot(active_low, full_down, preferred_element_type=jnp.float32)).astype(
        jnp.bfloat16
    )
    grad_rows = cotangent.reshape(total_rows, width)
    grad_down = contract_rows(active_low, grad_rows)
    grad_active = times_transposed(grad_rows, full_down)
    grad_pre = gelu_back(grad_active)[0].astype(jnp.bfloat16)
    grad_up = contract_rows(normed_two_low, grad_pre)
    grad_normed_two = times_transposed(grad_pre, full_up)
    grad_resid_part, grad_gain_two = norm_back_two(grad_normed_two)
    grad_resid = grad_rows.astype(jnp.float32) + grad_resid_part
    resid_low = grad_resid.astype(jnp.bfloat16)
    grad_outw = contract_rows(gated, resid_low)
    grad_gated = times_transposed(resid_low, full_out)
    grad_gate_two = grad_gated * conv_tok
    grad_conv = (grad_gated * gate_two).astype(jnp.bfloat16).reshape(num_seqs, local_len, width)
    grad_channel = to_channels(grad_conv).astype(jnp.float32)
    back_re, back_im = forward_dft(grad_channel)
    grad_signal = inverse_dft(
        back_re * filt_re + back_im * filt_im, back_im * filt_re - back_re * filt_im
    )
    cross_re = jnp.sum(back_re * sig_re + back_im * sig_im, axis=0, keepdims=True)
    cross_im = jnp.sum(back_im * sig_re - back_re * sig_im, axis=0, keepdims=True)
    grad_filt = inverse_dft(cross_re, cross_im)[0]
    grad_kern = filter_back(grad_filt)[0]
    grad_mixed = (
        to_tokens(grad_signal.astype(jnp.bfloat16)).reshape(total_rows, width).astype(jnp.float32)
    )
    grad_proj = jnp.concatenate([grad_mixed * gate_one, grad_mixed * values, grad_gate_two], axis=1)
    grad_proj = grad_proj.astype(jnp.bfloat16)
    grad_inw = contract_rows(normed_low, grad_proj)
    grad_normed = times_transposed(grad_proj, full_in)
    grad_input_part, grad_gain_one = norm_back_one(grad_normed)
    grad_inputs = (
        (grad_resid + grad_input_part).astype(jnp.bfloat16).reshape(num_seqs, local_len, width)
    )
    grad_gain_pair = jnp.stack([grad_gain_one, grad_gain_two])
    in_part, outw_part, up_part, down_part, kern_done = (
        lax.psum_scatter(
            grad_inw.astype(jnp.bfloat16), "dp", scatter_dimension=0, tiled=True
        ).astype(jnp.float32),
        lax.psum_scatter(
            grad_outw.astype(jnp.bfloat16), "dp", scatter_dimension=0, tiled=True
        ).astype(jnp.float32),
        lax.psum_scatter(
            grad_up.astype(jnp.bfloat16), "dp", scatter_dimension=0, tiled=True
        ).astype(jnp.float32),
        lax.psum_scatter(
            grad_down.astype(jnp.bfloat16), "dp", scatter_dimension=0, tiled=True
        ).astype(jnp.float32),
        lax.psum_scatter(
            grad_kern.astype(jnp.bfloat16), "dp", scatter_dimension=0, tiled=True
        ).astype(jnp.float32),
    )
    in_done, outw_done, up_done, down_done, gain_part = (
        lax.psum_scatter(
            in_part.astype(jnp.bfloat16), "seq", scatter_dimension=1, tiled=True
        ).astype(jnp.float32),
        lax.psum_scatter(
            outw_part.astype(jnp.bfloat16), "seq", scatter_dimension=1, tiled=True
        ).astype(jnp.float32),
        lax.psum_scatter(
            up_part.astype(jnp.bfloat16), "seq", scatter_dimension=1, tiled=True
        ).astype(jnp.float32),
        lax.psum_scatter(
            down_part.astype(jnp.bfloat16), "seq", scatter_dimension=1, tiled=True
        ).astype(jnp.float32),
        lax.psum_scatter(
            grad_gain_pair.astype(jnp.bfloat16), "seq", scatter_dimension=1, tiled=True
        ).astype(jnp.float32),
    )
    gain_done = lax.psum(gain_part, "dp")
    return (
        result.reshape(num_seqs, local_len, width),
        grad_inputs,
        in_done,
        outw_done,
        up_done,
        down_done,
        gain_done,
        kern_done,
    )


MESH = pl.DeviceIdType.MESH
BF = jnp.bfloat16
F32 = jnp.float32


def place():
    dp, sq = lax.axis_index("dp"), lax.axis_index("seq")
    return dp // 2, dp % 2, sq // 2, sq % 2


class Wire:
    def __init__(self, send, recv):
        self.send, self.recv, self.made = send, recv, []

    def start(self, src, dst, peer):
        k = len(self.made)
        copy = pltpu.make_async_remote_copy(
            src_ref=src, dst_ref=dst, send_sem=self.send.at[k], recv_sem=self.recv.at[k],
            device_id=peer, device_id_type=MESH,
        )
        copy.start()
        self.made.append(copy)
        return copy

    def drain(self):
        for copy in self.made:
            copy.wait_send()


class Local:
    def __init__(self, sems):
        self.sems, self.made, self.open = sems, 0, []

    def start(self, src, dst):
        copy = pltpu.make_async_copy(src, dst, self.sems.at[self.made])
        self.made += 1
        copy.start()
        self.open.append(copy)
        return copy

    def wait(self, copy):
        copy.wait()
        self.open.remove(copy)

    def drain(self):
        for copy in list(self.open):
            self.wait(copy)


def arrived(copies):
    for copy in copies:
        copy.wait_recv()


class Spots:
    def __init__(self, num_z):
        z, x, y, c = place()
        self.num_z = num_z
        self.z, self.x, self.y, self.c = z, x, y, c
        self.across_z = [self.at((z + k) % num_z, x, y, c) for k in range(1, num_z)]
        self.core = self.at(z, x, y, 1 - c)
        self.first = self.at(z, jnp.where(c == 0, 1 - x, x), jnp.where(c == 0, y, 1 - y), c)
        self.second = self.at(z, jnp.where(c == 0, x, 1 - x), jnp.where(c == 0, 1 - y, y), c)
        self.x_side = self.at(z, 1 - x, y, c)
        self.group = [((y + i) % 2, (c + j) % 2) for i, j in ((0, 1), (1, 0), (1, 1))]
        self.mates = [self.at(z, x, yy, cc) for yy, cc in self.group]

    def at(self, z, x, y, c):
        return (z * 2 + x, y * 2 + c)

    def meet(self):
        barrier = pltpu.get_barrier_semaphore()
        peers = self.across_z + [self.x_side] + self.mates
        for peer in peers:
            pl.semaphore_signal(barrier, inc=1, device_id=peer, device_id_type=MESH)
        pl.semaphore_wait(barrier, len(peers))


class Gather:
    def __init__(self, wire, spots, full):
        self.wire, self.s, self.full = wire, spots, full
        self.last = []

    def over_z(self):
        s = self.s
        mine = self.full.at[s.y, s.z, s.x, s.c]
        self.last = [self.wire.start(mine, mine, peer) for peer in s.across_z]

    def over_first(self):
        arrived(self.last)
        s = self.s
        mine = self.full.at[s.y, :, s.x, s.c]
        self.last = [self.wire.start(mine, mine, s.first)]

    def over_second(self):
        arrived(self.last)
        s = self.s
        self.last = []
        for i in range(2):
            mine = self.full.at[jnp.where(s.c == 0, s.y, i), :, jnp.where(s.c == 0, i, s.x), s.c]
            self.last.append(self.wire.start(mine, mine, s.second))

    def over_core(self):
        arrived(self.last)
        s = self.s
        self.last = []
        for i in range(2):
            mine = self.full.at[i, :, :, s.c]
            self.last.append(self.wire.start(mine, mine, s.core))

    def done(self):
        arrived(self.last)


def norm_parts(values):
    center = values - jnp.mean(values, axis=-1, keepdims=True)
    spread = jnp.mean(center * center, axis=-1, keepdims=True)
    scale = lax.rsqrt(spread + EPSILON)
    return center * scale, scale


def dot(left, right):
    return jnp.dot(left, right, preferred_element_type=F32)


def make_filter(kern, taps):
    length = kern.shape[0]
    position = lax.broadcasted_iota(jnp.int32, kern.shape, 0)
    live = position.astype(F32) < taps
    masked = jnp.where(live, kern, 0.0)
    shrunk = masked - SHRINK_SCALE * jnp.tanh(masked / SHRINK_SCALE)
    before = jnp.where(position == 0, 0.0, pltpu.roll(shrunk, 1, 0))
    after = jnp.where(position == length - 1, 0.0, pltpu.roll(shrunk, length - 1, 0))
    return jnp.where(live, (before + shrunk + after) / 3.0, 0.0)


def spectrum_product(re_a, im_a, re_b, im_b):
    return re_a * re_b - im_a * im_b, re_a * im_b + im_a * re_b


GELU_K = math.sqrt(2.0 / math.pi)


def gelu_both(v):
    square = v * v
    t = jnp.tanh(GELU_K * v * (1.0 + 0.044715 * square))
    half = 0.5 * (1.0 + t)
    slope = half + 0.5 * v * (1.0 - t * t) * (GELU_K * (1.0 + 3 * 0.044715 * square))
    return v * half, slope


def forward_kernel(
    num_z,
    tok, w_in, w_out, w_up, w_down, kern, small, fwd_hbm, inv_hbm,
    out_o, win_o, wout_o, wup_o, wdown_o, kern_o, small_o, proj_o, normed_o, sig_o, spec_o, filt_o, conv_o,
    gated_o, resid_o, normed_two_o, act_o, slope_o,
    win_v, wout_v, wup_v, wdown_v, kern_v, small_v,
    pre_in, pre_out, pre_up, pre_down, pre_kern,
    fwd_v, inv_v, proj_v, normed_v, mixed_v, sig_v, spec_v, filt_v, filt_low, turned_v, conv_ch, conv_v,
    gated_v, resid_v, normed_two_v, act_v, slope_v, out_v,
    send, recv, local,
):
    s = Spots(num_z)
    z, x, y, c = s.z, s.x, s.y, s.c
    wire, inner = Wire(send, recv), Local(local)
    load_fwd = inner.start(fwd_hbm, fwd_v)
    load_inv = inner.start(inv_hbm, inv_v)
    s.meet()

    pairs = [(w_in, pre_in, win_v), (kern, pre_kern, kern_v), (w_out, pre_out, wout_v),
             (w_up, pre_up, wup_v), (w_down, pre_down, wdown_v)]
    traded = []
    for src, pre, _ in pairs:
        half = src.shape[0] // 2
        traded.append(wire.start(src.at[pl.ds((1 - c) * half, half)], pre.at[c], s.core))
    me = y * 2 + c
    small_v[me] = small[...]
    smalls = [wire.start(small, small_v.at[me], peer) for peer in s.mates]
    for src, pre, _ in pairs:
        half = src.shape[0] // 2
        pre[c] = src[pl.ds(c * half, half)]

    def join(i):
        traded[i].wait_recv()
        _, pre, full = pairs[i]
        both = jnp.concatenate([pre[0], pre[1]], axis=-1)
        if full is kern_v:
            full[z, x, c] = both
        else:
            full[y, z, x, c] = both

    g_in, g_out, g_up, g_down = (Gather(wire, s, v) for v in (win_v, wout_v, wup_v, wdown_v))
    join(0)
    g_in.over_z()
    join(1)
    own = kern_v.at[z, x, c]
    kern_z = [wire.start(own, own, peer) for peer in s.across_z]
    join(2)
    join(3)
    join(4)

    arrived(smalls)
    gains = jnp.concatenate([small_v[k] for k in range(4)], axis=-1)
    rows, width = tok.shape
    group = width // 2
    normed, _ = norm_parts(tok[...].astype(F32))
    normed_v[...] = (normed * gains[0:1]).astype(BF)

    g_in.over_first()
    g_out.over_z()
    g_up.over_z()
    arrived(kern_z)
    own = kern_v.at[:, x, c]
    kern_x = [wire.start(own, own, s.x_side)]
    g_in.over_second()
    arrived(kern_x)
    own = kern_v.at[:, :, c]
    kern_c = [wire.start(own, own, s.core)]
    g_out.over_first()

    arrived(kern_c)
    taps = jnp.concatenate([small_v[2 * y], small_v[2 * y + 1]], axis=-1)[2:3]
    length = turned_v.shape[0] // 2
    tile = 128
    for j in range(group // tile):
        cols = slice(j * tile, (j + 1) * tile)
        filt = make_filter(kern_v[:, :, :, :, cols].reshape(length, tile).astype(F32), taps[:, cols])
        filt_low[:, cols] = filt.astype(BF)
    inner.wait(load_fwd)
    step = 256

    def spectrum(source, target):
        def one(i, _):
            at = pl.ds(pl.multiple_of(i * step, step), step)
            target[at] = dot(fwd_v[at], source[...]).astype(target.dtype)
            return 0
        lax.fori_loop(0, 2 * length // step, one, 0)

    spectrum(filt_low, filt_v)
    g_in.over_core()
    g_down.over_z()
    g_up.over_first()
    g_out.over_second()
    g_in.done()

    def project(j):
        weight = win_v[j // 3, :, :, :, :, (j % 3) * group : (j % 3 + 1) * group].reshape(width, group)
        return dot(normed_v[...], weight)

    for h in range(2):
        value, gate = project(h), project(2 + h)
        proj_v[h] = value.astype(BF)
        proj_v[2 + h] = gate.astype(BF)
        mixed_v[h] = (value * gate).astype(BF)
    span = rows // 2
    chunk = pl.ds(pl.multiple_of((2 * y + c) * span, span), span)
    to_channels = [
        wire.start(mixed_v.at[yy, pl.ds(pl.multiple_of(cc * span, span), span)], sig_v.at[chunk], peer)
        for (yy, cc), peer in zip(s.group, s.mates)
    ]
    sig_v[chunk] = mixed_v[y, pl.ds(pl.multiple_of(c * span, span), span)]
    for h in range(2):
        proj_v[4 + h] = project(4 + h).astype(BF)
    g_out.over_core()
    g_up.over_second()
    g_down.over_first()
    inner.wait(load_inv)
    arrived(to_channels)

    def convolve(i, _):
        real = pl.ds(pl.multiple_of(i * step, step), step)
        imag = pl.ds(pl.multiple_of(length + i * step, step), step)
        re_s, im_s = dot(fwd_v[real], sig_v[...]), dot(fwd_v[imag], sig_v[...])
        spec_v[real] = re_s.astype(BF)
        spec_v[imag] = im_s.astype(BF)
        re, im = spectrum_product(re_s, im_s, filt_v[real].astype(F32), filt_v[imag].astype(F32))
        turned_v[real] = re.astype(BF)
        turned_v[imag] = im.astype(BF)
        return 0
    lax.fori_loop(0, length // step, convolve, 0)

    def back(i, _):
        at = pl.ds(pl.multiple_of(i * step, step), step)
        conv_ch[at] = (dot(inv_v[at], turned_v[...]) * (1.0 / length)).astype(BF)
        return 0
    lax.fori_loop(0, length // step, back, 0)

    home = pl.ds(pl.multiple_of(c * span, span), span)
    to_tokens = [
        wire.start(conv_ch.at[pl.ds(pl.multiple_of((2 * yy + cc) * span, span), span)], conv_v.at[y, home], peer)
        for (yy, cc), peer in zip(s.group, s.mates)
    ]
    conv_v[y, home] = conv_ch[chunk]
    g_up.over_core()
    g_down.over_second()
    for src, dst in ((win_v, win_o), (kern_v, kern_o), (small_v, small_o), (proj_v, proj_o),
                     (normed_v, normed_o), (sig_v, sig_o), (spec_v, spec_o), (filt_v, filt_o)):
        inner.start(src, dst)
    g_out.done()
    arrived(to_tokens)

    for h in range(2):
        gated_v[:, h * group : (h + 1) * group] = (
            proj_v[4 + h].astype(F32) * conv_v[h].astype(F32)
        ).astype(BF)
    for h in range(2):
        cols = slice(h * group, (h + 1) * group)
        resid_v[:, cols] = tok[:, cols].astype(F32) + dot(gated_v[...], wout_v[h].reshape(width, group))
    normed_two, _ = norm_parts(resid_v[...])
    normed_two_v[...] = (normed_two * gains[1:2]).astype(BF)
    for src, dst in ((wout_v, wout_o), (conv_v, conv_o), (gated_v, gated_o), (resid_v, resid_o),
                     (normed_two_v, normed_two_o)):
        inner.start(src, dst)
    g_down.over_core()
    g_up.done()

    hidden = act_v.shape[1]
    wide = 256
    per = hidden // 2 // wide

    def feed(j, _):
        cols = pl.ds(pl.multiple_of((j % per) * wide, wide), wide)
        weight = wup_v[j // per, :, :, :, :, cols].reshape(width, wide)
        act, slope = gelu_both(dot(normed_two_v[...], weight))
        at = pl.ds(pl.multiple_of(j * wide, wide), wide)
        act_v[:, at] = act.astype(BF)
        slope_v[:, at] = slope.astype(BF)
        return 0
    lax.fori_loop(0, 2 * per, feed, 0)
    inner.start(wup_v, wup_o)
    inner.start(act_v, act_o)
    inner.start(slope_v, slope_o)
    g_down.done()
    inner.start(wdown_v, wdown_o)
    for h in range(2):
        cols = slice(h * group, (h + 1) * group)
        out_v[:, cols] = (resid_v[:, cols] + dot(act_v[...], wdown_v[h].reshape(hidden, group))).astype(BF)
    inner.start(out_v, out_o)
    wire.drain()
    inner.drain()


def transform_table(length):
    k = np.arange(length)[:, None]
    t = np.arange(length)[None, :]
    angle = np.pi / (2 * length) * (((2 * k + 1) * t) % (4 * length))
    return np.concatenate([np.cos(angle), np.sin(angle)]).astype(np.float32).astype(ml_dtypes.bfloat16)


def forward(num_z, length, tokens, w_in, w_out, w_up, w_down, kernel, small, fwd_table, inv_table):
    rows, width = tokens.shape
    group = width // 2
    hidden = w_down.shape[0] * num_z * 2
    sds = jax.ShapeDtypeStruct

    def full(block):
        return (2, num_z, 2, 2, block.shape[0] // 2, block.shape[1] * 2)

    weights = [full(b) for b in (w_in, w_out, w_up, w_down)]
    kern_full = (num_z, 2, 2, kernel.shape[0] // 2, kernel.shape[1] * 2)
    small_full = (4,) + small.shape
    acts = dict(
        proj=((6, rows, group), BF), normed=((rows, width), BF), sig=((length, group), BF),
        spec=((2 * length, group), BF), filt=((2 * length, group), BF), conv=((2, rows, group), BF),
        gated=((rows, width), BF), resid=((rows, width), F32), normed_two=((rows, width), BF),
        act=((rows, hidden), BF), slope=((rows, hidden), BF),
    )
    outs = [sds((rows, width), BF)] + [sds(w, BF) for w in weights]
    outs += [sds(kern_full, BF), sds(small_full, F32)] + [sds(*acts[k]) for k in acts]
    vm = lambda k: pltpu.VMEM(*acts[k])
    scratch = [pltpu.VMEM(w, BF) for w in weights] + [pltpu.VMEM(kern_full, BF), pltpu.VMEM(small_full, F32)]
    scratch += [pltpu.VMEM((2, b.shape[0] // 2, b.shape[1]), BF) for b in (w_in, w_out, w_up, w_down, kernel)]
    scratch += [pltpu.VMEM(fwd_table.shape, BF), pltpu.VMEM(inv_table.shape, BF), vm("proj"), vm("normed"),
                pltpu.VMEM((2, rows, group), BF), vm("sig"), vm("spec"), vm("filt"),
                pltpu.VMEM((length, group), BF), pltpu.VMEM((2 * length, group), BF), pltpu.VMEM((length, group), BF),
                vm("conv"), vm("gated"), vm("resid"), vm("normed_two"), vm("act"), vm("slope"),
                pltpu.VMEM((rows, width), BF)]
    copies = 80
    scratch += [pltpu.SemaphoreType.DMA((copies,)), pltpu.SemaphoreType.DMA((copies,)), pltpu.SemaphoreType.DMA((40,))]
    vmem, hbm = pl.BlockSpec(memory_space=pltpu.VMEM), pl.BlockSpec(memory_space=pl.ANY)
    return pl.pallas_call(
        partial(forward_kernel, num_z),
        out_shape=outs,
        in_specs=[vmem] * 7 + [hbm] * 2,
        out_specs=[hbm] * len(outs),
        scratch_shapes=scratch,
        compiler_params=pltpu.CompilerParams(collective_id=0, has_side_effects=True, vmem_limit_bytes=60 * 2**20),
        cost_estimate=pl.CostEstimate(flops=12 * 10**9, bytes_accessed=50 * 10**6, transcendentals=2 * 10**6),
    )(tokens, w_in, w_out, w_up, w_down, kernel, small, fwd_table, inv_table)


def fits(num_dp, num_seq, tokens, w_in, w_out, w_up, w_down, kernel):
    if num_seq != 4 or num_dp % 2 or kernel.shape[0] * num_dp > 1024:
        return False
    blocks = (w_in, w_out, w_up, w_down, kernel)
    return all(b.shape[0] % 32 == 0 and b.shape[1] * 2 % 128 == 0 for b in blocks) and tokens.shape[0] == 2


def unfold(full):
    flat = full.reshape(2, -1, full.shape[-1])
    return jnp.concatenate([flat[0], flat[1]], axis=1)


def body(num_dp, num_seq, tokens_in, w_in, w_out, w_up, w_down, norm_gains, kernel, taps, cotangent):
    if not fits(num_dp, num_seq, tokens_in, w_in, w_out, w_up, w_down, kernel):
        return general_body(tokens_in, w_in, w_out, w_up, w_down, norm_gains, kernel, taps, cotangent)
    num_seqs, local_len, width = tokens_in.shape
    total_rows = num_seqs * local_len
    length = kernel.shape[0] * num_dp
    table = transform_table(length)
    small = jnp.concatenate(
        [norm_gains.astype(F32), taps.astype(F32)[None], jnp.zeros((5, taps.shape[0]), F32)]
    )
    tokens = tokens_in.reshape(total_rows, width)
    (out, win_f, wout_f, wup_f, wdown_f, kern_f, small_f, proj, normed, sig, spec, filt_s, conv, gated, resid,
     normed_two, act, slope) = forward(
        num_dp // 2, length, tokens, w_in, w_out, w_up, w_down, kernel, small,
        jnp.asarray(table), jnp.asarray(np.ascontiguousarray(table.T)))
    full_in, full_out, full_up, full_down = unfold(win_f), unfold(wout_f), unfold(wup_f), unfold(wdown_f)
    gains_wide = jnp.concatenate([small_f[k] for k in range(4)], axis=-1)[:2]
    chan = lax.axis_index("seq") // 2
    core = lax.axis_index("seq") % 2
    group = width // 2
    proj = proj.astype(F32)
    values, gate_one, gate_two = [jnp.concatenate([proj[2 * k], proj[2 * k + 1]], axis=1) for k in range(3)]
    conv_tok = jnp.concatenate([conv[0], conv[1]], axis=1).astype(F32)
    inputs = tokens.astype(F32)
    _, norm_back_one = jax.vjp(norm_rows, inputs, gains_wide[0])
    _, norm_back_two = jax.vjp(norm_rows, resid, gains_wide[1])
    grad_rows = cotangent.reshape(total_rows, width)
    grad_down = contract_rows(act, grad_rows)
    grad_active = times_transposed(grad_rows, full_down)
    grad_pre = (slope.astype(F32) * grad_active).astype(BF)
    grad_up = contract_rows(normed_two, grad_pre)
    grad_normed_two = times_transposed(grad_pre, full_up)
    grad_resid_part, grad_gain_two = norm_back_two(grad_normed_two)
    grad_resid = grad_rows.astype(jnp.float32) + grad_resid_part
    resid_low = grad_resid.astype(jnp.bfloat16)
    grad_outw = contract_rows(gated, resid_low)
    grad_gated = times_transposed(resid_low, full_out)
    grad_gate_two = grad_gated * conv_tok
    grad_conv = (grad_gated * gate_two).astype(jnp.bfloat16).reshape(2, local_len, 2, group)
    sent = grad_conv.transpose(2, 0, 1, 3).reshape(4, local_len, group)
    grad_ch = lax.all_to_all(sent, "seq", split_axis=0, concat_axis=0, tiled=True).reshape(length, group)
    tab = jnp.asarray(table)
    back = dot(tab, grad_ch)
    be, bf = back[:length], back[length:]
    hc, hd = filt_s[:length].astype(F32), filt_s[length:].astype(F32)
    sa, sb = spec[:length].astype(F32), spec[length:].astype(F32)
    inv = lambda re, im: contract_rows(tab, jnp.concatenate([re, im]).astype(BF)) / length
    grad_signal = inv(hc * be + hd * bf, hc * bf - hd * be).astype(BF)
    grad_filt = inv(sa * be + sb * bf, sa * bf - sb * be)
    home = lax.all_to_all(grad_signal.reshape(4, local_len, group), "seq", split_axis=0, concat_axis=0, tiled=True)
    grad_mixed = home.reshape(2, 2, local_len, group).transpose(1, 2, 0, 3).reshape(total_rows, width).astype(F32)
    kern_cols = kern_f.reshape(length, group).astype(F32)
    taps_f = jnp.concatenate([small_f[2 * chan], small_f[2 * chan + 1]], axis=-1)[2]
    _, filter_back = jax.vjp(partial(shape_filter, taps=taps_f.astype(jnp.int32)), kern_cols)
    grad_kern = filter_back(grad_filt)[0]
    swap = [(2 * i + j, 2 * i + 1 - j) for i in range(2) for j in range(2)]
    part = group // 2
    mine = lax.dynamic_slice_in_dim(grad_kern, core * part, part, 1)
    other = lax.dynamic_slice_in_dim(grad_kern, (1 - core) * part, part, 1)
    mine = mine + lax.ppermute(other.astype(BF), "seq", swap).astype(F32)
    grad_proj = jnp.concatenate([grad_mixed * gate_one, grad_mixed * values, grad_gate_two], axis=1)
    grad_proj = grad_proj.astype(jnp.bfloat16)
    grad_inw = contract_rows(normed, grad_proj)
    grad_normed = times_transposed(grad_proj, full_in)
    grad_input_part, grad_gain_one = norm_back_one(grad_normed)
    grad_inputs = (
        (grad_resid + grad_input_part).astype(jnp.bfloat16).reshape(num_seqs, local_len, width)
    )
    grad_gain_pair = jnp.stack([grad_gain_one, grad_gain_two])

    def scatter_dp(v):
        return lax.psum_scatter(v.astype(BF), "dp", scatter_dimension=0, tiled=True).astype(F32)

    def scatter_seq(v):
        return lax.psum_scatter(v.astype(BF), "seq", scatter_dimension=1, tiled=True).astype(F32)

    weights = [scatter_seq(scatter_dp(v)) for v in (grad_inw, grad_outw, grad_up, grad_down)]
    kern_done = scatter_dp(mine)
    gain_done = lax.psum(scatter_seq(grad_gain_pair), "dp")
    return (out.reshape(num_seqs, local_len, width), grad_inputs, *weights, gain_done, kern_done)


def solution(mesh):
    return jax.shard_map(
        partial(body, mesh.shape["dp"], mesh.shape["seq"]),
        mesh=mesh,
        in_specs=(
            P("dp", "seq", None),
            P("dp", "seq"),
            P("dp", "seq"),
            P("dp", "seq"),
            P("dp", "seq"),
            P(None, "seq"),
            P("dp", "seq"),
            P("seq"),
            P("dp", "seq", None),
        ),
        out_specs=(
            P("dp", "seq", None),
            P("dp", "seq", None),
            P("dp", "seq"),
            P("dp", "seq"),
            P("dp", "seq"),
            P("dp", "seq"),
            P(None, "seq"),
            P("dp", "seq"),
        ),
        check_vma=False,
    )
```

```python
from functools import partial
import math

import jax
from jax.experimental import pallas as pl
from jax.experimental.pallas import tpu as pltpu
import ml_dtypes
import numpy as np
import jax.numpy as jnp
from jax import lax
from jax.sharding import PartitionSpec as P

EPSILON = 1e-05
SHRINK_SCALE = 0.003
HIGHEST = lax.Precision.HIGHEST


def norm_rows(values, gain):
    center = values - jnp.mean(values, axis=-1, keepdims=True)
    spread = jnp.mean(center * center, axis=-1, keepdims=True)
    return center * lax.rsqrt(spread + EPSILON) * gain


def shape_filter(kernel, taps):
    length = kernel.shape[0]
    position = jnp.arange(length, dtype=jnp.int32)[:, None]
    live_mask = (position < taps[None, :]).astype(kernel.dtype)
    masked = kernel * live_mask
    shrunk = masked - SHRINK_SCALE * jnp.tanh(masked / SHRINK_SCALE)
    padded = jnp.pad(shrunk, ((1, 1), (0, 0)))
    pooled = (padded[:-2] + padded[1:-1] + padded[2:]) / 3.0
    return pooled * live_mask


def gelu_tanh(values):
    return jax.nn.gelu(values, approximate=True)


def contract_rows(left, right):
    return lax.dot_general(
        left, right, (((0,), (0,)), ((), ())), preferred_element_type=jnp.float32
    )


def times_transposed(left, weight):
    return lax.dot_general(
        left, weight, (((1,), (1,)), ((), ())), preferred_element_type=jnp.float32
    )


def phase_table(count_rows, count_cols, period):
    row_index = lax.broadcasted_iota(jnp.int32, (count_rows, count_cols), 0)
    col_index = lax.broadcasted_iota(jnp.int32, (count_rows, count_cols), 1)
    angles = 2.0 * math.pi / period * (row_index * col_index % period).astype(jnp.float32)
    return (jnp.cos(angles), jnp.sin(angles))


def dft_factors(length):
    total = 2 * length
    first = max(2, total // 128)
    return (total, first, total // first)


def mix_last(field, table):
    return jnp.einsum("bckn,nm->bckm", field, table, precision=HIGHEST)


def forward_dft(field):
    batch, length, chans = field.shape
    total, first, second = dft_factors(length)
    half = first // 2
    blocks = field.reshape(batch, half, second, chans)
    cos_one, sin_one = phase_table(half, first, first)
    part_re = jnp.einsum("hk,bhnc->bckn", cos_one, blocks, precision=HIGHEST)
    part_im = -jnp.einsum("hk,bhnc->bckn", sin_one, blocks, precision=HIGHEST)
    cos_two, sin_two = phase_table(first, second, total)
    turn_re = part_re * cos_two + part_im * sin_two
    turn_im = part_im * cos_two - part_re * sin_two
    cos_three, sin_three = phase_table(second, second, second)
    spec_re = mix_last(turn_re, cos_three) + mix_last(turn_im, sin_three)
    spec_im = mix_last(turn_im, cos_three) - mix_last(turn_re, sin_three)
    return (spec_re, spec_im)


def inverse_dft(spec_re, spec_im):
    batch, chans, first, second = spec_re.shape
    total = first * second
    half = first // 2
    cos_three, sin_three = phase_table(second, second, second)
    back_re = mix_last(spec_re, cos_three) - mix_last(spec_im, sin_three)
    back_im = mix_last(spec_re, sin_three) + mix_last(spec_im, cos_three)
    cos_two, sin_two = phase_table(first, second, total)
    turn_re = back_re * cos_two - back_im * sin_two
    turn_im = back_re * sin_two + back_im * cos_two
    cos_one, sin_one = phase_table(half, first, first)
    blocks = jnp.einsum("hk,bckn->bhnc", cos_one, turn_re, precision=HIGHEST)
    blocks = blocks - jnp.einsum("hk,bckn->bhnc", sin_one, turn_im, precision=HIGHEST)
    return blocks.reshape(batch, half * second, chans) / total


def to_channels(field):
    return lax.all_to_all(field, "seq", split_axis=2, concat_axis=1, tiled=True)


def to_tokens(field):
    return lax.all_to_all(field, "seq", split_axis=1, concat_axis=2, tiled=True)


def general_body(tokens_in, w_in, w_out, w_up, w_down, norm_gains, kernel, taps, cotangent):
    w_in_rows, w_out_rows, w_up_rows, w_down_rows, gains = (
        lax.all_gather(w_in, "seq", axis=1, tiled=True),
        lax.all_gather(w_out, "seq", axis=1, tiled=True),
        lax.all_gather(w_up, "seq", axis=1, tiled=True),
        lax.all_gather(w_down, "seq", axis=1, tiled=True),
        lax.all_gather(norm_gains, "seq", axis=1, tiled=True),
    )
    full_in, full_out, full_up, full_down, kernel_cols = (
        lax.all_gather(w_in_rows, "dp", axis=0, tiled=True),
        lax.all_gather(w_out_rows, "dp", axis=0, tiled=True),
        lax.all_gather(w_up_rows, "dp", axis=0, tiled=True),
        lax.all_gather(w_down_rows, "dp", axis=0, tiled=True),
        lax.all_gather(kernel, "dp", axis=0, tiled=True),
    )
    num_seqs, local_len, width = tokens_in.shape
    total_rows = num_seqs * local_len
    inputs = tokens_in.reshape(total_rows, width).astype(jnp.float32)
    gains_wide = gains.astype(jnp.float32)
    normed, norm_back_one = jax.vjp(norm_rows, inputs, gains_wide[0])
    normed_low = normed.astype(jnp.bfloat16)
    proj = jnp.dot(normed_low, full_in, preferred_element_type=jnp.float32)
    values = proj[:, :width]
    gate_one = proj[:, width : 2 * width]
    gate_two = proj[:, 2 * width :]
    mixed_low = (gate_one * values).astype(jnp.bfloat16).reshape(num_seqs, local_len, width)
    by_channel = to_channels(mixed_low)
    filt, filter_back = jax.vjp(partial(shape_filter, taps=taps), kernel_cols.astype(jnp.float32))
    filt_re, filt_im = forward_dft(filt[None])
    sig_re, sig_im = forward_dft(by_channel.astype(jnp.float32))
    conv = inverse_dft(sig_re * filt_re - sig_im * filt_im, sig_re * filt_im + sig_im * filt_re)
    conv_tok = to_tokens(conv.astype(jnp.bfloat16)).reshape(total_rows, width).astype(jnp.float32)
    gated = (gate_two * conv_tok).astype(jnp.bfloat16)
    resid = inputs + jnp.dot(gated, full_out, preferred_element_type=jnp.float32)
    normed_two, norm_back_two = jax.vjp(norm_rows, resid, gains_wide[1])
    normed_two_low = normed_two.astype(jnp.bfloat16)
    hidden_pre = jnp.dot(normed_two_low, full_up, preferred_element_type=jnp.float32)
    active, gelu_back = jax.vjp(gelu_tanh, hidden_pre)
    active_low = active.astype(jnp.bfloat16)
    result = (resid + jnp.dot(active_low, full_down, preferred_element_type=jnp.float32)).astype(
        jnp.bfloat16
    )
    grad_rows = cotangent.reshape(total_rows, width)
    grad_down = contract_rows(active_low, grad_rows)
    grad_active = times_transposed(grad_rows, full_down)
    grad_pre = gelu_back(grad_active)[0].astype(jnp.bfloat16)
    grad_up = contract_rows(normed_two_low, grad_pre)
    grad_normed_two = times_transposed(grad_pre, full_up)
    grad_resid_part, grad_gain_two = norm_back_two(grad_normed_two)
    grad_resid = grad_rows.astype(jnp.float32) + grad_resid_part
    resid_low = grad_resid.astype(jnp.bfloat16)
    grad_outw = contract_rows(gated, resid_low)
    grad_gated = times_transposed(resid_low, full_out)
    grad_gate_two = grad_gated * conv_tok
    grad_conv = (grad_gated * gate_two).astype(jnp.bfloat16).reshape(num_seqs, local_len, width)
    grad_channel = to_channels(grad_conv).astype(jnp.float32)
    back_re, back_im = forward_dft(grad_channel)
    grad_signal = inverse_dft(
        back_re * filt_re + back_im * filt_im, back_im * filt_re - back_re * filt_im
    )
    cross_re = jnp.sum(back_re * sig_re + back_im * sig_im, axis=0, keepdims=True)
    cross_im = jnp.sum(back_im * sig_re - back_re * sig_im, axis=0, keepdims=True)
    grad_filt = inverse_dft(cross_re, cross_im)[0]
    grad_kern = filter_back(grad_filt)[0]
    grad_mixed = (
        to_tokens(grad_signal.astype(jnp.bfloat16)).reshape(total_rows, width).astype(jnp.float32)
    )
    grad_proj = jnp.concatenate([grad_mixed * gate_one, grad_mixed * values, grad_gate_two], axis=1)
    grad_proj = grad_proj.astype(jnp.bfloat16)
    grad_inw = contract_rows(normed_low, grad_proj)
    grad_normed = times_transposed(grad_proj, full_in)
    grad_input_part, grad_gain_one = norm_back_one(grad_normed)
    grad_inputs = (
        (grad_resid + grad_input_part).astype(jnp.bfloat16).reshape(num_seqs, local_len, width)
    )
    grad_gain_pair = jnp.stack([grad_gain_one, grad_gain_two])
    in_part, outw_part, up_part, down_part, kern_done = (
        lax.psum_scatter(
            grad_inw.astype(jnp.bfloat16), "dp", scatter_dimension=0, tiled=True
        ).astype(jnp.float32),
        lax.psum_scatter(
            grad_outw.astype(jnp.bfloat16), "dp", scatter_dimension=0, tiled=True
        ).astype(jnp.float32),
        lax.psum_scatter(
            grad_up.astype(jnp.bfloat16), "dp", scatter_dimension=0, tiled=True
        ).astype(jnp.float32),
        lax.psum_scatter(
            grad_down.astype(jnp.bfloat16), "dp", scatter_dimension=0, tiled=True
        ).astype(jnp.float32),
        lax.psum_scatter(
            grad_kern.astype(jnp.bfloat16), "dp", scatter_dimension=0, tiled=True
        ).astype(jnp.float32),
    )
    in_done, outw_done, up_done, down_done, gain_part = (
        lax.psum_scatter(
            in_part.astype(jnp.bfloat16), "seq", scatter_dimension=1, tiled=True
        ).astype(jnp.float32),
        lax.psum_scatter(
            outw_part.astype(jnp.bfloat16), "seq", scatter_dimension=1, tiled=True
        ).astype(jnp.float32),
        lax.psum_scatter(
            up_part.astype(jnp.bfloat16), "seq", scatter_dimension=1, tiled=True
        ).astype(jnp.float32),
        lax.psum_scatter(
            down_part.astype(jnp.bfloat16), "seq", scatter_dimension=1, tiled=True
        ).astype(jnp.float32),
        lax.psum_scatter(
            grad_gain_pair.astype(jnp.bfloat16), "seq", scatter_dimension=1, tiled=True
        ).astype(jnp.float32),
    )
    gain_done = lax.psum(gain_part, "dp")
    return (
        result.reshape(num_seqs, local_len, width),
        grad_inputs,
        in_done,
        outw_done,
        up_done,
        down_done,
        gain_done,
        kern_done,
    )


MESH = pl.DeviceIdType.MESH
BF = jnp.bfloat16
F32 = jnp.float32


def place():
    dp, sq = lax.axis_index("dp"), lax.axis_index("seq")
    return dp // 2, dp % 2, sq // 2, sq % 2


class Wire:
    def __init__(self, send, recv):
        self.send, self.recv, self.made = send, recv, []

    def start(self, src, dst, peer):
        k = len(self.made)
        copy = pltpu.make_async_remote_copy(
            src_ref=src, dst_ref=dst, send_sem=self.send.at[k], recv_sem=self.recv.at[k],
            device_id=peer, device_id_type=MESH,
        )
        copy.start()
        self.made.append(copy)
        return copy

    def drain(self):
        for copy in self.made:
            copy.wait_send()


class Local:
    def __init__(self, sems):
        self.sems, self.made, self.open = sems, 0, []

    def start(self, src, dst):
        copy = pltpu.make_async_copy(src, dst, self.sems.at[self.made])
        self.made += 1
        copy.start()
        self.open.append(copy)
        return copy

    def wait(self, copy):
        copy.wait()
        self.open = [other for other in self.open if other is not copy]

    def drain(self):
        for copy in list(self.open):
            self.wait(copy)


def arrived(copies):
    for copy in copies:
        copy.wait_recv()


class Spots:
    def __init__(self, num_z):
        z, x, y, c = place()
        self.num_z = num_z
        self.z, self.x, self.y, self.c = z, x, y, c
        self.across_z = [self.at((z + k) % num_z, x, y, c) for k in range(1, num_z)]
        self.core = self.at(z, x, y, 1 - c)
        self.first = self.at(z, jnp.where(c == 0, 1 - x, x), jnp.where(c == 0, y, 1 - y), c)
        self.second = self.at(z, jnp.where(c == 0, x, 1 - x), jnp.where(c == 0, 1 - y, y), c)
        self.x_side = self.at(z, 1 - x, y, c)
        self.group = [((y + i) % 2, (c + j) % 2) for i, j in ((0, 1), (1, 0), (1, 1))]
        self.mates = [self.at(z, x, yy, cc) for yy, cc in self.group]

    def at(self, z, x, y, c):
        return (z * 2 + x, y * 2 + c)

    def meet(self):
        barrier = pltpu.get_barrier_semaphore()
        peers = self.across_z + [self.x_side] + self.mates
        for peer in peers:
            pl.semaphore_signal(barrier, inc=1, device_id=peer, device_id_type=MESH)
        pl.semaphore_wait(barrier, len(peers))


class Gather:
    def __init__(self, wire, spots, full):
        self.wire, self.s, self.full = wire, spots, full
        self.last = []

    def over_z(self):
        s = self.s
        mine = self.full.at[s.y, s.z, s.x, s.c]
        self.last = [self.wire.start(mine, mine, peer) for peer in s.across_z]

    def over_first(self):
        arrived(self.last)
        s = self.s
        mine = self.full.at[s.y, :, s.x, s.c]
        self.last = [self.wire.start(mine, mine, s.first)]

    def over_second(self):
        arrived(self.last)
        s = self.s
        self.last = []
        for i in range(2):
            mine = self.full.at[jnp.where(s.c == 0, s.y, i), :, jnp.where(s.c == 0, i, s.x), s.c]
            self.last.append(self.wire.start(mine, mine, s.second))

    def over_core(self):
        arrived(self.last)
        s = self.s
        self.last = []
        for i in range(2):
            mine = self.full.at[i, :, :, s.c]
            self.last.append(self.wire.start(mine, mine, s.core))

    def done(self):
        arrived(self.last)


def norm_parts(values):
    center = values - jnp.mean(values, axis=-1, keepdims=True)
    spread = jnp.mean(center * center, axis=-1, keepdims=True)
    scale = lax.rsqrt(spread + EPSILON)
    return center * scale, scale


def dot(left, right):
    return jnp.dot(left, right, preferred_element_type=F32)


def dot_rows(left, right):
    return lax.dot_general(left, right, (((0,), (0,)), ((), ())), preferred_element_type=F32)


def dot_cols(left, right):
    return lax.dot_general(left, right, (((1,), (1,)), ((), ())), preferred_element_type=F32)


def make_filter(kern, taps):
    length = kern.shape[0]
    position = lax.broadcasted_iota(jnp.int32, kern.shape, 0)
    live = position.astype(F32) < taps
    masked = jnp.where(live, kern, 0.0)
    shrunk = masked - SHRINK_SCALE * jnp.tanh(masked / SHRINK_SCALE)
    before = jnp.where(position == 0, 0.0, pltpu.roll(shrunk, 1, 0))
    after = jnp.where(position == length - 1, 0.0, pltpu.roll(shrunk, length - 1, 0))
    return jnp.where(live, (before + shrunk + after) / 3.0, 0.0)


def spectrum_product(re_a, im_a, re_b, im_b):
    return re_a * re_b - im_a * im_b, re_a * im_b + im_a * re_b


GELU_K = math.sqrt(2.0 / math.pi)


def gelu_both(v):
    square = v * v
    t = jnp.tanh(GELU_K * v * (1.0 + 0.044715 * square))
    half = 0.5 * (1.0 + t)
    slope = half + 0.5 * v * (1.0 - t * t) * (GELU_K * (1.0 + 3 * 0.044715 * square))
    return v * half, slope


def forward_kernel(
    num_z,
    tok, cot, w_in, w_out, w_up, w_down, kern, small, twist, table_hbm,
    out_o, win_o, wout_o, wup_o, gdown_o, kern_o, small_o, proj_o, normed_o, sig_o, spec_o, filt_o, conv_o,
    gated_o, resid_o, normed_two_o, gpre_o,
    win_v, wout_v, wup_v, wdown_v, kern_v, small_v,
    pre_in, pre_out, pre_up, pre_down, pre_kern,
    table_v, proj_v, normed_v, mixed_v, sig_v, spec_v, filt_v, filt_low, turned_v, conv_ch, conv_v,
    gated_v, resid_v, normed_two_v, act_v, slope_v, gdown_v, out_v,
    send, recv, local,
):
    s = Spots(num_z)
    z, x, y, c = s.z, s.x, s.y, s.c
    wire, inner = Wire(send, recv), Local(local)
    load_table = inner.start(table_hbm, table_v)
    s.meet()

    pairs = [(w_in, pre_in, win_v), (kern, pre_kern, kern_v), (w_out, pre_out, wout_v),
             (w_up, pre_up, wup_v), (w_down, pre_down, wdown_v)]
    traded = []
    for src, pre, _ in pairs:
        half = src.shape[0] // 2
        traded.append(wire.start(src.at[pl.ds((1 - c) * half, half)], pre.at[c], s.core))
    me = y * 2 + c
    small_v[me] = small[...]
    smalls = [wire.start(small, small_v.at[me], peer) for peer in s.mates]
    for src, pre, _ in pairs:
        half = src.shape[0] // 2
        pre[c] = src[pl.ds(c * half, half)]

    def join(i):
        traded[i].wait_recv()
        _, pre, full = pairs[i]
        both = jnp.concatenate([pre[0], pre[1]], axis=-1)
        if full is kern_v:
            full[z, x, c] = both
        else:
            full[y, z, x, c] = both

    g_in, g_out, g_up, g_down = (Gather(wire, s, v) for v in (win_v, wout_v, wup_v, wdown_v))
    join(0)
    g_in.over_z()
    join(1)
    own = kern_v.at[z, x, c]
    kern_z = [wire.start(own, own, peer) for peer in s.across_z]
    join(2)
    join(3)
    join(4)

    arrived(smalls)
    gains = jnp.concatenate([small_v[k] for k in range(4)], axis=-1)
    rows, width = tok.shape
    group = width // 2
    normed, _ = norm_parts(tok[...].astype(F32))
    normed_v[...] = (normed * gains[0:1]).astype(BF)

    g_in.over_first()
    g_out.over_z()
    g_up.over_z()
    arrived(kern_z)
    own = kern_v.at[:, x, c]
    kern_x = [wire.start(own, own, s.x_side)]
    g_in.over_second()
    arrived(kern_x)
    own = kern_v.at[:, :, c]
    kern_c = [wire.start(own, own, s.core)]
    g_out.over_first()

    arrived(kern_c)
    taps = jnp.concatenate([small_v[2 * y], small_v[2 * y + 1]], axis=-1)[2:3]
    length = turned_v.shape[0] // 2
    tile = 128
    for j in range(group // tile):
        cols = slice(j * tile, (j + 1) * tile)
        filt = make_filter(kern_v[:, :, :, :, cols].reshape(length, tile).astype(F32), taps[:, cols])
        filt_low[:, cols] = filt.astype(BF)
    inner.wait(load_table)
    step = 256

    def spectrum(i, _):
        real = pl.ds(pl.multiple_of(i * step, step), step)
        imag = pl.ds(pl.multiple_of(length + i * step, step), step)
        re, im = dot(table_v[real], filt_low[...]), dot(table_v[imag], filt_low[...])
        cosine, sine = twist[real, 0:1], twist[real, 1:2]
        filt_v[real] = (re * cosine + im * sine).astype(BF)
        filt_v[imag] = (im * cosine - re * sine).astype(BF)
        return 0
    lax.fori_loop(0, length // step, spectrum, 0)
    g_in.over_core()
    g_down.over_z()
    g_up.over_first()
    g_out.over_second()
    g_in.done()

    def project(j):
        weight = win_v[j // 3, :, :, :, :, (j % 3) * group : (j % 3 + 1) * group].reshape(width, group)
        return dot(normed_v[...], weight)

    for h in range(2):
        value, gate = project(h), project(2 + h)
        proj_v[h] = value.astype(BF)
        proj_v[2 + h] = gate.astype(BF)
        mixed_v[h] = (value * gate).astype(BF)
    span = rows // 2
    chunk = pl.ds(pl.multiple_of((2 * y + c) * span, span), span)
    to_channels = [
        wire.start(mixed_v.at[yy, pl.ds(pl.multiple_of(cc * span, span), span)], sig_v.at[chunk], peer)
        for (yy, cc), peer in zip(s.group, s.mates)
    ]
    sig_v[chunk] = mixed_v[y, pl.ds(pl.multiple_of(c * span, span), span)]
    for h in range(2):
        proj_v[4 + h] = project(4 + h).astype(BF)
    g_out.over_core()
    g_up.over_second()
    g_down.over_first()
    arrived(to_channels)

    def convolve(i, _):
        real = pl.ds(pl.multiple_of(i * step, step), step)
        imag = pl.ds(pl.multiple_of(length + i * step, step), step)
        re_s, im_s = dot(table_v[real], sig_v[...]), dot(table_v[imag], sig_v[...])
        spec_v[real] = re_s.astype(BF)
        spec_v[imag] = im_s.astype(BF)
        re, im = spectrum_product(re_s, im_s, filt_v[real].astype(F32), filt_v[imag].astype(F32))
        turned_v[real] = re.astype(BF)
        turned_v[imag] = im.astype(BF)
        return 0
    lax.fori_loop(0, length // step, convolve, 0)

    def back(i, _):
        at = pl.ds(pl.multiple_of(i * step, step), step)
        imag = pl.ds(pl.multiple_of(length + i * step, step), step)
        both = dot(table_v[at], turned_v[0:length]) + dot(table_v[imag], turned_v[length:])
        conv_ch[at] = (both * (1.0 / length)).astype(BF)
        return 0
    lax.fori_loop(0, length // step, back, 0)

    home = pl.ds(pl.multiple_of(c * span, span), span)
    to_tokens = [
        wire.start(conv_ch.at[pl.ds(pl.multiple_of((2 * yy + cc) * span, span), span)], conv_v.at[y, home], peer)
        for (yy, cc), peer in zip(s.group, s.mates)
    ]
    conv_v[y, home] = conv_ch[chunk]
    g_up.over_core()
    g_down.over_second()
    for src, dst in ((win_v, win_o), (kern_v, kern_o), (small_v, small_o), (proj_v, proj_o),
                     (normed_v, normed_o), (sig_v, sig_o), (spec_v, spec_o), (filt_v, filt_o)):
        inner.start(src, dst)
    g_out.done()
    arrived(to_tokens)

    for h in range(2):
        gated_v[:, h * group : (h + 1) * group] = (
            proj_v[4 + h].astype(F32) * conv_v[h].astype(F32)
        ).astype(BF)
    for h in range(2):
        cols = slice(h * group, (h + 1) * group)
        resid_v[:, cols] = tok[:, cols].astype(F32) + dot(gated_v[...], wout_v[h].reshape(width, group))
    normed_two, _ = norm_parts(resid_v[...])
    normed_two_v[...] = (normed_two * gains[1:2]).astype(BF)
    for src, dst in ((wout_v, wout_o), (conv_v, conv_o), (gated_v, gated_o), (resid_v, resid_o),
                     (normed_two_v, normed_two_o)):
        inner.start(src, dst)
    g_down.over_core()
    g_up.done()

    hidden = act_v.shape[1]
    wide = 256
    per = hidden // 2 // wide

    def feed(j, _):
        cols = pl.ds(pl.multiple_of((j % per) * wide, wide), wide)
        weight = wup_v[j // per, :, :, :, :, cols].reshape(width, wide)
        act, slope = gelu_both(dot(normed_two_v[...], weight))
        at = pl.ds(pl.multiple_of(j * wide, wide), wide)
        act_v[:, at] = act.astype(BF)
        slope_v[:, at] = slope.astype(BF)
        return 0
    lax.fori_loop(0, 2 * per, feed, 0)
    inner.start(wup_v, wup_o)

    deep = hidden // (2 * num_z)

    def down_grad(i, _):
        grad = dot_rows(act_v[:, pl.ds(pl.multiple_of(i * deep, deep), deep)], cot[...]).astype(BF)
        for h in range(2):
            gdown_v[h, i // 2, i % 2] = grad[:, h * group : (h + 1) * group].reshape(2, deep // 2, group)
        return 0
    lax.fori_loop(0, 2 * num_z, down_grad, 0)
    inner.start(gdown_v, gdown_o)
    g_down.done()
    for h in range(2):
        cols = slice(h * group, (h + 1) * group)
        out_v[:, cols] = (resid_v[:, cols] + dot(act_v[...], wdown_v[h].reshape(hidden, group))).astype(BF)
    inner.start(out_v, out_o)

    def pre_grad(i, _):
        at = pl.ds(pl.multiple_of(i * deep, deep), deep)
        grad = sum(
            dot_cols(cot[:, h * group : (h + 1) * group], wdown_v[h, i // 2, i % 2].reshape(deep, group))
            for h in range(2)
        )
        slope_v[:, at] = (slope_v[:, at].astype(F32) * grad).astype(BF)
        return 0
    lax.fori_loop(0, 2 * num_z, pre_grad, 0)
    inner.start(slope_v, gpre_o)
    wire.drain()
    inner.drain()


def transform_table(length):
    k = 2 * np.arange(length)[:, None] + 1
    angle = np.pi / (4 * length) * ((k * k.T) % (8 * length))
    return np.concatenate([np.cos(angle), np.sin(angle)]).astype(np.float32).astype(ml_dtypes.bfloat16)


def twist_table(length):
    angle = np.pi / (4 * length) * (2 * np.arange(length) + 1)
    return np.stack([np.cos(angle), np.sin(angle)], axis=1).astype(np.float32)


def forward(num_z, length, tokens, cot, w_in, w_out, w_up, w_down, kernel, small, twist, table):
    rows, width = tokens.shape
    group = width // 2
    hidden = w_down.shape[0] * num_z * 2
    sds = jax.ShapeDtypeStruct

    def full(block):
        return (2, num_z, 2, 2, block.shape[0] // 2, block.shape[1] * 2)

    weights = [full(b) for b in (w_in, w_out, w_up, w_down)]
    kern_full = (num_z, 2, 2, kernel.shape[0] // 2, kernel.shape[1] * 2)
    small_full = (4,) + small.shape
    acts = dict(
        proj=((6, rows, group), BF), normed=((rows, width), BF), sig=((length, group), BF),
        spec=((2 * length, group), BF), filt=((2 * length, group), BF), conv=((2, rows, group), BF),
        gated=((rows, width), BF), resid=((rows, width), F32), normed_two=((rows, width), BF),
        grad_pre=((rows, hidden), BF),
    )
    outs = [sds((rows, width), BF)] + [sds(w, BF) for w in weights]
    outs += [sds(kern_full, BF), sds(small_full, F32)] + [sds(*acts[k]) for k in acts]
    vm = lambda k: pltpu.VMEM(*acts[k])
    scratch = [pltpu.VMEM(w, BF) for w in weights] + [pltpu.VMEM(kern_full, BF), pltpu.VMEM(small_full, F32)]
    scratch += [pltpu.VMEM((2, b.shape[0] // 2, b.shape[1]), BF) for b in (w_in, w_out, w_up, w_down, kernel)]
    scratch += [pltpu.VMEM(table.shape, BF), vm("proj"), vm("normed"),
                pltpu.VMEM((2, rows, group), BF), vm("sig"), vm("spec"), vm("filt"),
                pltpu.VMEM((length, group), BF), pltpu.VMEM((2 * length, group), BF), pltpu.VMEM((length, group), BF),
                vm("conv"), vm("gated"), vm("resid"), vm("normed_two"), vm("grad_pre"), vm("grad_pre"),
                pltpu.VMEM(weights[3], BF), pltpu.VMEM((rows, width), BF)]
    copies = 80
    scratch += [pltpu.SemaphoreType.DMA((copies,)), pltpu.SemaphoreType.DMA((copies,)), pltpu.SemaphoreType.DMA((40,))]
    vmem, hbm = pl.BlockSpec(memory_space=pltpu.VMEM), pl.BlockSpec(memory_space=pl.ANY)
    return pl.pallas_call(
        partial(forward_kernel, num_z),
        out_shape=outs,
        in_specs=[vmem] * 9 + [hbm],
        out_specs=[hbm] * len(outs),
        scratch_shapes=scratch,
        compiler_params=pltpu.CompilerParams(collective_id=0, has_side_effects=True, vmem_limit_bytes=60 * 2**20),
        cost_estimate=pl.CostEstimate(flops=17 * 10**9, bytes_accessed=50 * 10**6, transcendentals=2 * 10**6),
    )(tokens, cot, w_in, w_out, w_up, w_down, kernel, small, twist, table)


class Scatter:
    def __init__(self, wire, spots, total, from_core, from_second, from_first, from_z, ends, away=None):
        self.wire, self.s, self.total = wire, spots, total
        self.from_core, self.from_second, self.from_first = from_core, from_second, from_first
        self.from_z, self.ends, self.away = from_z, ends, away
        self.last = []

    def mine(self, yy, zz, xx):
        if self.away is None:
            return self.total.at[yy, zz, xx, self.s.c]
        return self.total.at[yy, zz, xx]

    def send_core(self):
        s = self.s
        source = self.total if self.away is None else self.away
        self.last = [
            self.wire.start(source.at[i, :, :, 1 - s.c], self.from_core.at[i], s.core) for i in range(2)
        ]

    def add(self, into, term):
        into[...] = (into[...].astype(F32) + term.astype(F32)).astype(BF)

    def add_core(self):
        arrived(self.last)
        num_z = self.s.num_z

        def one(i, _):
            yy, zz, xx = i // (2 * num_z), (i // 2) % num_z, i % 2
            self.add(self.mine(yy, zz, xx), self.from_core[yy, zz, xx])
            return 0
        lax.fori_loop(0, 4 * num_z, one, 0)

    def send_second(self):
        s = self.s
        self.last = []
        for i in range(2):
            yy, xx = jnp.where(s.c == 0, 1 - s.y, i), jnp.where(s.c == 0, i, 1 - s.x)
            self.last.append(self.wire.start(self.mine(yy, slice(None), xx), self.from_second.at[i], s.second))

    def add_second(self):
        arrived(self.last)
        s = self.s

        def one(k, _):
            i, zz = k // s.num_z, k % s.num_z
            yy, xx = jnp.where(s.c == 0, s.y, i), jnp.where(s.c == 0, i, s.x)
            self.add(self.mine(yy, zz, xx), self.from_second[i, zz])
            return 0
        lax.fori_loop(0, 2 * s.num_z, one, 0)

    def send_first(self):
        s = self.s
        yy, xx = jnp.where(s.c == 0, s.y, 1 - s.y), jnp.where(s.c == 0, 1 - s.x, s.x)
        self.last = [self.wire.start(self.mine(yy, slice(None), xx), self.from_first, s.first)]

    def add_first(self):
        arrived(self.last)
        s = self.s

        def one(zz, _):
            self.add(self.mine(s.y, zz, s.x), self.from_first[zz])
            return 0
        lax.fori_loop(0, s.num_z, one, 0)

    def send_z(self):
        s = self.s
        self.last = [
            self.wire.start(self.mine(s.y, (s.z + k) % s.num_z, s.x), self.from_z.at[k - 1], peer)
            for k, peer in zip(range(1, s.num_z), s.across_z)
        ]

    def add_z(self):
        arrived(self.last)
        s = self.s
        total = self.mine(s.y, s.z, s.x)[...].astype(F32)
        for k in range(s.num_z - 1):
            total = total + self.from_z[k].astype(F32)
        part = total.shape[-1] // 2
        for core in range(2):
            self.ends[core] = total[:, core * part : (core + 1) * part]
        self.last = [self.wire.start(self.ends.at[1 - s.c], self.ends.at[2], s.core)]

    def finish(self, out):
        arrived(self.last)
        half = self.ends.shape[1]
        c = self.s.c
        out[pl.ds(pl.multiple_of(c * half, 16), half)] = self.ends[c]
        out[pl.ds(pl.multiple_of((1 - c) * half, 16), half)] = self.ends[2]


class ScatterTaps(Scatter):
    def send_core(self):
        s = self.s
        self.last = [self.wire.start(self.total.at[:, :, 1 - s.c], self.from_core, s.core)]

    def add_core(self):
        arrived(self.last)

        def one(i, _):
            zz, xx = i // 2, i % 2
            self.add(self.total.at[zz, xx, self.s.c], self.from_core[zz, xx])
            return 0
        lax.fori_loop(0, 2 * self.s.num_z, one, 0)

    def send_first(self):
        s = self.s
        self.last = [self.wire.start(self.total.at[:, 1 - s.x, s.c], self.from_first, s.x_side)]

    def mine(self, yy, zz, xx):
        return self.total.at[zz, xx, self.s.c]


def norm_back(normal, scale, grad, gain):
    p = grad * gain
    flat = jnp.mean(p, axis=-1, keepdims=True)
    along = jnp.mean(p * normal, axis=-1, keepdims=True)
    return (p - flat - normal * along) * scale, jnp.sum(grad * normal, axis=0, keepdims=True)


def backward_kernel(
    num_z, length,
    tok, cot, twist, small_v, table_h, win_h, wout_h, wup_h, gdown_h, kern_h, proj_h, normed_h, sig_h, spec_h,
    filt_h, conv_h, gated_h, resid_h, normed_two_h, gpre_h,
    grad_in_o, gin_o, gout_o, gup_o, gdn_o, gains_o, gkern_o,
    table_v, win_v, wout_v, wup_v, kern_v, proj_v, spec_v, filt_v, conv_v,
    gated_v, resid_v, normed_two_v, gpre_v,
    gup_v, gdn_v, gkern_v,
    core_in, core_out, core_up, core_dn, core_kern,
    two_in, two_out, two_up, two_dn,
    one_in, one_out, one_up, one_dn, one_kern,
    z_in, z_out, z_up, z_dn, z_kern,
    ends_in, ends_out, ends_up, ends_dn, ends_kern,
    low_v, gconv_v, gch_v, gmix_v, gain_v, gain_got,
    send, recv, local,
):
    s = Spots(num_z)
    z, x, y, c = s.z, s.x, s.y, s.c
    wire, inner = Wire(send, recv), Local(local)
    rows, width = tok.shape
    group = width // 2
    hidden = gpre_v.shape[1]
    own_dn = [inner.start(gdown_h.at[i, :, :, c], gdn_v.at[i]) for i in range(2)]
    loads = {}
    for name, src, dst in (
        ("normed_two", normed_two_h, normed_two_v), ("gpre", gpre_h, gpre_v), ("wup", wup_h, wup_v),
        ("resid", resid_h, resid_v), ("wout", wout_h, wout_v), ("proj", proj_h, proj_v), ("conv", conv_h, conv_v),
        ("gated", gated_h, gated_v), ("table", table_h, table_v), ("spec", spec_h, spec_v), ("filt", filt_h, filt_v),
        ("kern", kern_h, kern_v), ("win", win_h, win_v),
    ):
        loads[name] = inner.start(src, dst)

    def need(*names):
        for name in names:
            inner.wait(loads[name])

    s.meet()
    gin_v, gout_v = wup_v.at[:, :, :, :, :, 0 : 3 * group], wup_v.at[:, :, :, :, :, 3 * group : 4 * group]
    down = Scatter(wire, s, gdn_v, core_dn, two_dn, one_dn, z_dn, ends_dn, away=gdown_h)
    up = Scatter(wire, s, gup_v, core_up, two_up, one_up, z_up, ends_up)
    out = Scatter(wire, s, gout_v, core_out, two_out, one_out, z_out, ends_out)
    into = Scatter(wire, s, gin_v, core_in, two_in, one_in, z_in, ends_in)
    taps_grad = ScatterTaps(wire, s, gkern_v, core_kern, None, one_kern, z_kern, ends_kern)
    down.send_core()

    gains = jnp.concatenate([small_v[k] for k in range(4)], axis=-1)

    need("normed_two", "gpre")
    wide = 256
    per = hidden // 2 // wide

    def up_grad(j, _):
        at = pl.ds(pl.multiple_of(j * wide, wide), wide)
        grad = dot_rows(normed_two_v[...], gpre_v[:, at]).astype(BF)
        cols = pl.ds(pl.multiple_of((j % per) * wide, wide), wide)
        gup_v[j // per, :, :, :, :, cols] = grad.reshape(num_z, 2, 2, width // (4 * num_z), wide)
        return 0
    lax.fori_loop(0, 2 * per, up_grad, 0)
    normed_v = normed_two_v
    loads["normed"] = inner.start(normed_h, normed_v)
    up.send_core()
    for copy in own_dn:
        inner.wait(copy)
    down.add_core()
    down.send_second()

    need("wup", "resid")
    half = hidden // 2
    grad = sum(
        dot_cols(gpre_v[:, h * half : (h + 1) * half], wup_v[h].reshape(width, half)) for h in range(2)
    )
    normal, scale = norm_parts(resid_v[...])
    part, gain_two = norm_back(normal, scale, grad, gains[1:2])
    resid_v[...] = cot[...].astype(F32) + part
    low_v[...] = resid_v[...].astype(BF)

    need("wout", "proj", "conv")
    span = rows // 2
    for h in range(2):
        grad = sum(
            dot_cols(
                low_v[:, k * group : (k + 1) * group],
                wout_v[k].reshape(width, group)[h * group : (h + 1) * group],
            )
            for k in range(2)
        )
        gconv_v[h] = (grad * proj_v[4 + h].astype(F32)).astype(BF)
        gpre_v[:, (4 + h) * group : (5 + h) * group] = (grad * conv_v[h].astype(F32)).astype(BF)
    chunk = pl.ds(pl.multiple_of((2 * y + c) * span, span), span)
    to_channels = [
        wire.start(gconv_v.at[yy, pl.ds(pl.multiple_of(cc * span, span), span)], gch_v.at[chunk], peer)
        for (yy, cc), peer in zip(s.group, s.mates)
    ]
    gch_v[chunk] = gconv_v[y, pl.ds(pl.multiple_of(c * span, span), span)]
    up.add_core()
    up.send_second()

    need("gated")
    for h in range(2):
        grad = dot_rows(gated_v[...], low_v[:, h * group : (h + 1) * group]).astype(BF)
        gout_v[h] = grad.reshape(num_z, 2, 2, width // (4 * num_z), group)
    out.send_core()
    down.add_second()
    down.send_first()

    need("table", "spec", "filt")
    arrived(to_channels)
    step = 256

    def turn(i, _):
        real = pl.ds(pl.multiple_of(i * step, step), step)
        imag = pl.ds(pl.multiple_of(length + i * step, step), step)
        re, im = dot(table_v[real], gch_v[...]), dot(table_v[imag], gch_v[...])
        re_f, im_f = filt_v[real].astype(F32), filt_v[imag].astype(F32)
        filt_v[real] = (re_f * re + im_f * im).astype(BF)
        filt_v[imag] = (re_f * im - im_f * re).astype(BF)
        re_s, im_s = spec_v[real].astype(F32), spec_v[imag].astype(F32)
        re_k, im_k = re_s * re + im_s * im, re_s * im - im_s * re
        cosine, sine = twist[real, 0:1], twist[real, 1:2]
        spec_v[real] = (re_k * cosine - im_k * sine).astype(BF)
        spec_v[imag] = (im_k * cosine + re_k * sine).astype(BF)
        return 0
    lax.fori_loop(0, length // step, turn, 0)

    def back(i, _):
        at = pl.ds(pl.multiple_of(i * step, step), step)
        imag = pl.ds(pl.multiple_of(length + i * step, step), step)
        both = dot(table_v[at], filt_v[0:length]) + dot(table_v[imag], filt_v[length:])
        gch_v[at] = (both * (1.0 / length)).astype(BF)
        return 0
    lax.fori_loop(0, length // step, back, 0)
    home = pl.ds(pl.multiple_of(c * span, span), span)
    to_tokens = [
        wire.start(gch_v.at[pl.ds(pl.multiple_of((2 * yy + cc) * span, span), span)], gmix_v.at[y, home], peer)
        for (yy, cc), peer in zip(s.group, s.mates)
    ]
    gmix_v[y, home] = gch_v[chunk]
    out.add_core()
    out.send_second()

    need("kern")
    taps = jnp.concatenate([small_v[2 * y], small_v[2 * y + 1]], axis=-1)[2:3]
    tile = 128
    for j in range(group // tile):
        cols = slice(j * tile, (j + 1) * tile)
        both = dot(table_v[0:length], spec_v[0:length, cols]) + dot(table_v[length:], spec_v[length:, cols])
        grad = kernel_back(kern_v[:, :, :, :, cols].reshape(length, tile).astype(F32), taps[:, cols],
                           both * (1.0 / length))
        gkern_v[:, :, :, :, cols] = grad.astype(BF).reshape(num_z, 2, 2, length // (4 * num_z), tile)
    taps_grad.send_core()
    down.add_first()
    down.send_z()
    up.add_second()
    up.send_first()

    need("normed", "win")
    arrived(to_tokens)
    for h in range(2):
        grad = gmix_v[h].astype(F32)
        gpre_v[:, h * group : (h + 1) * group] = (grad * proj_v[2 + h].astype(F32)).astype(BF)
        gpre_v[:, (2 + h) * group : (3 + h) * group] = (grad * proj_v[h].astype(F32)).astype(BF)
    for j in range(6):
        grad = dot_rows(normed_v[...], gpre_v[:, j * group : (j + 1) * group]).astype(BF)
        gin_v[j // 3, :, :, :, :, (j % 3) * group : (j % 3 + 1) * group] = grad.reshape(
            num_z, 2, 2, width // (4 * num_z), group)
    into.send_core()
    out.add_second()
    out.send_first()
    taps_grad.add_core()
    taps_grad.send_first()
    into.add_core()
    into.send_second()

    wide_in = 3 * group
    grad = sum(
        dot_cols(gpre_v[:, h * wide_in : (h + 1) * wide_in], win_v[h].reshape(width, wide_in)) for h in range(2)
    )
    normal, scale = norm_parts(tok[...].astype(F32))
    part, gain_one = norm_back(normal, scale, grad, gains[0:1])
    low_v[...] = (resid_v[...] + part).astype(BF)
    inner.start(low_v, grad_in_o)

    gain_v[0] = jnp.concatenate([gain_one, gain_two, jnp.zeros((6, width), F32)], axis=0)
    got = [wire.start(gain_v.at[0], gain_got.at[k], peer) for k, peer in enumerate(s.mates)]
    up.add_first()
    up.send_z()
    arrived(got)
    gain_v[1] = gain_v[0] + gain_got[0] + gain_got[1] + gain_got[2]
    got = [wire.start(gain_v.at[1], gain_got.at[3], s.x_side)]
    out.add_first()
    out.send_z()
    taps_grad.add_first()
    taps_grad.send_z()
    arrived(got)
    gain_v[2] = gain_v[1] + gain_got[3]
    got = [wire.start(gain_v.at[2], gain_got.at[3 + k], peer) for k, peer in zip(range(1, num_z), s.across_z)]
    into.add_second()
    into.send_first()
    down.add_z()
    up.add_z()
    out.add_z()
    taps_grad.add_z()
    arrived(got)
    total = gain_v[2]
    for k in range(1, num_z):
        total = total + gain_got[3 + k]
    part = width // 4
    mine = total[:, 0:part]
    for k in range(1, 4):
        mine = jnp.where(2 * y + c == k, total[:, k * part : (k + 1) * part], mine)
    gains_o[...] = mine
    into.add_first()
    into.send_z()
    down.finish(gdn_o)
    up.finish(gup_o)
    out.finish(gout_o)
    taps_grad.finish(gkern_o)
    into.add_z()
    into.finish(gin_o)
    wire.drain()
    inner.drain()


def kernel_back(kern, taps, grad):
    length = kern.shape[0]
    position = lax.broadcasted_iota(jnp.int32, kern.shape, 0)
    live = position.astype(F32) < taps
    slope = jnp.tanh(jnp.where(live, kern, 0.0) / SHRINK_SCALE)
    pooled = jnp.where(live, grad, 0.0)
    before = jnp.where(position == 0, 0.0, pltpu.roll(pooled, 1, 0))
    after = jnp.where(position == length - 1, 0.0, pltpu.roll(pooled, length - 1, 0))
    return jnp.where(live, (before + pooled + after) / 3.0 * slope * slope, 0.0)


def backward(num_z, length, tokens, cot, twist, small_f, table, full):
    rows, width = tokens.shape
    group = width // 2
    sds = jax.ShapeDtypeStruct
    win, wout, wup, gdown, kern, proj, normed, sig, spec, filt, conv, gated, resid, normed_two, gpre = full
    weights = (win, wout, wup, gdown)
    vmem, hbm = pl.BlockSpec(memory_space=pltpu.VMEM), pl.BlockSpec(memory_space=pl.ANY)

    def vm(shape, dtype=BF):
        return pltpu.VMEM(tuple(shape), dtype)

    like = lambda a: vm(a.shape, a.dtype)
    blocks = [(2 * w.shape[-2], w.shape[-1] // 2) for w in (win, wout, wup, gdown, kern)]
    outs = [sds((rows, width), BF)] + [sds(b, F32) for b in blocks[:4]]
    outs += [sds((8, width // 4), F32), sds(blocks[4], F32)]
    scratch = [like(a) for a in (table, win, wout, wup, kern, proj, spec, filt, conv, gated, resid,
                                 normed_two, gpre)]
    scratch += [like(wup), vm(gdown.shape[:3] + gdown.shape[4:]), like(kern)]
    scratch += [vm(w.shape[:3] + w.shape[4:]) for w in weights] + [vm(kern.shape[:2] + kern.shape[3:])]
    scratch += [vm((2, num_z) + w.shape[4:]) for w in weights]
    scratch += [vm((num_z,) + w.shape[-2:]) for w in weights + (kern,)]
    scratch += [vm((num_z - 1,) + w.shape[-2:]) for w in weights + (kern,)]
    scratch += [vm((3, w.shape[-2], w.shape[-1] // 2), F32) for w in weights + (kern,)]
    scratch += [vm((rows, width)), vm((2, rows, group)), vm((length, group)),
                vm((2, rows, group)), vm((3, 8, width), F32), vm((3 + num_z, 8, width), F32)]
    scratch += [pltpu.SemaphoreType.DMA((80,)), pltpu.SemaphoreType.DMA((80,)), pltpu.SemaphoreType.DMA((40,))]
    return pl.pallas_call(
        partial(backward_kernel, num_z, length),
        out_shape=outs,
        in_specs=[vmem] * 4 + [hbm] * 16,
        out_specs=[hbm] + [vmem] * 6,
        scratch_shapes=scratch,
        compiler_params=pltpu.CompilerParams(collective_id=1, has_side_effects=True, vmem_limit_bytes=63 * 2**20),
        cost_estimate=pl.CostEstimate(flops=17 * 10**9, bytes_accessed=50 * 10**6, transcendentals=2 * 10**6),
    )(tokens, cot, twist, small_f, table, *full)


def fits(num_dp, num_seq, tokens, w_in, w_out, w_up, w_down, kernel):
    if num_seq != 4 or num_dp % 2 or kernel.shape[0] * num_dp > 1024:
        return False
    blocks = (w_in, w_out, w_up, w_down, kernel)
    return all(b.shape[0] % 32 == 0 and b.shape[1] * 2 % 128 == 0 for b in blocks) and tokens.shape[0] == 2


def body(num_dp, num_seq, tokens_in, w_in, w_out, w_up, w_down, norm_gains, kernel, taps, cotangent):
    if not fits(num_dp, num_seq, tokens_in, w_in, w_out, w_up, w_down, kernel):
        return general_body(tokens_in, w_in, w_out, w_up, w_down, norm_gains, kernel, taps, cotangent)
    width = tokens_in.shape[-1]
    length = kernel.shape[0] * num_dp
    num_z = num_dp // 2
    table, twist = jnp.asarray(transform_table(length)), jnp.asarray(twist_table(length))
    small = jnp.concatenate(
        [norm_gains.astype(F32), taps.astype(F32)[None], jnp.zeros((5, taps.shape[0]), F32)]
    )
    tokens, cot = tokens_in.reshape(-1, width), cotangent.reshape(-1, width)
    out, win, wout, wup, gdown, kern, small_f, *saved = forward(
        num_z, length, tokens, cot, w_in, w_out, w_up, w_down, kernel, small, twist, table)
    grad_in, gin, gout, gup, gdn, gains, gkern = backward(
        num_z, length, tokens, cot, twist, small_f, table, [win, wout, wup, gdown, kern, *saved])
    return (out.reshape(tokens_in.shape), grad_in.reshape(tokens_in.shape), gin, gout, gup, gdn, gains[:2], gkern)


def solution(mesh):
    return jax.shard_map(
        partial(body, mesh.shape["dp"], mesh.shape["seq"]),
        mesh=mesh,
        in_specs=(
            P("dp", "seq", None),
            P("dp", "seq"),
            P("dp", "seq"),
            P("dp", "seq"),
            P("dp", "seq"),
            P(None, "seq"),
            P("dp", "seq"),
            P("seq"),
            P("dp", "seq", None),
        ),
        out_specs=(
            P("dp", "seq", None),
            P("dp", "seq", None),
            P("dp", "seq"),
            P("dp", "seq"),
            P("dp", "seq"),
            P("dp", "seq"),
            P(None, "seq"),
            P("dp", "seq"),
        ),
        check_vma=False,
    )
```

```python
from functools import partial
import math

import jax
from jax.experimental import pallas as pl
from jax.experimental.pallas import tpu as pltpu
import ml_dtypes
import numpy as np
import jax.numpy as jnp
from jax import lax
from jax.sharding import PartitionSpec as P

EPSILON = 1e-05
SHRINK_SCALE = 0.003
HIGHEST = lax.Precision.HIGHEST


def norm_rows(values, gain):
    center = values - jnp.mean(values, axis=-1, keepdims=True)
    spread = jnp.mean(center * center, axis=-1, keepdims=True)
    return center * lax.rsqrt(spread + EPSILON) * gain


def shape_filter(kernel, taps):
    length = kernel.shape[0]
    position = jnp.arange(length, dtype=jnp.int32)[:, None]
    live_mask = (position < taps[None, :]).astype(kernel.dtype)
    masked = kernel * live_mask
    shrunk = masked - SHRINK_SCALE * jnp.tanh(masked / SHRINK_SCALE)
    padded = jnp.pad(shrunk, ((1, 1), (0, 0)))
    pooled = (padded[:-2] + padded[1:-1] + padded[2:]) / 3.0
    return pooled * live_mask


def gelu_tanh(values):
    return jax.nn.gelu(values, approximate=True)


def contract_rows(left, right):
    return lax.dot_general(
        left, right, (((0,), (0,)), ((), ())), preferred_element_type=jnp.float32
    )


def times_transposed(left, weight):
    return lax.dot_general(
        left, weight, (((1,), (1,)), ((), ())), preferred_element_type=jnp.float32
    )


def phase_table(count_rows, count_cols, period):
    row_index = lax.broadcasted_iota(jnp.int32, (count_rows, count_cols), 0)
    col_index = lax.broadcasted_iota(jnp.int32, (count_rows, count_cols), 1)
    angles = 2.0 * math.pi / period * (row_index * col_index % period).astype(jnp.float32)
    return (jnp.cos(angles), jnp.sin(angles))


def dft_factors(length):
    total = 2 * length
    first = max(2, total // 128)
    return (total, first, total // first)


def mix_last(field, table):
    return jnp.einsum("bckn,nm->bckm", field, table, precision=HIGHEST)


def forward_dft(field):
    batch, length, chans = field.shape
    total, first, second = dft_factors(length)
    half = first // 2
    blocks = field.reshape(batch, half, second, chans)
    cos_one, sin_one = phase_table(half, first, first)
    part_re = jnp.einsum("hk,bhnc->bckn", cos_one, blocks, precision=HIGHEST)
    part_im = -jnp.einsum("hk,bhnc->bckn", sin_one, blocks, precision=HIGHEST)
    cos_two, sin_two = phase_table(first, second, total)
    turn_re = part_re * cos_two + part_im * sin_two
    turn_im = part_im * cos_two - part_re * sin_two
    cos_three, sin_three = phase_table(second, second, second)
    spec_re = mix_last(turn_re, cos_three) + mix_last(turn_im, sin_three)
    spec_im = mix_last(turn_im, cos_three) - mix_last(turn_re, sin_three)
    return (spec_re, spec_im)


def inverse_dft(spec_re, spec_im):
    batch, chans, first, second = spec_re.shape
    total = first * second
    half = first // 2
    cos_three, sin_three = phase_table(second, second, second)
    back_re = mix_last(spec_re, cos_three) - mix_last(spec_im, sin_three)
    back_im = mix_last(spec_re, sin_three) + mix_last(spec_im, cos_three)
    cos_two, sin_two = phase_table(first, second, total)
    turn_re = back_re * cos_two - back_im * sin_two
    turn_im = back_re * sin_two + back_im * cos_two
    cos_one, sin_one = phase_table(half, first, first)
    blocks = jnp.einsum("hk,bckn->bhnc", cos_one, turn_re, precision=HIGHEST)
    blocks = blocks - jnp.einsum("hk,bckn->bhnc", sin_one, turn_im, precision=HIGHEST)
    return blocks.reshape(batch, half * second, chans) / total


def to_channels(field):
    return lax.all_to_all(field, "seq", split_axis=2, concat_axis=1, tiled=True)


def to_tokens(field):
    return lax.all_to_all(field, "seq", split_axis=1, concat_axis=2, tiled=True)


def general_body(tokens_in, w_in, w_out, w_up, w_down, norm_gains, kernel, taps, cotangent):
    w_in_rows, w_out_rows, w_up_rows, w_down_rows, gains = (
        lax.all_gather(w_in, "seq", axis=1, tiled=True),
        lax.all_gather(w_out, "seq", axis=1, tiled=True),
        lax.all_gather(w_up, "seq", axis=1, tiled=True),
        lax.all_gather(w_down, "seq", axis=1, tiled=True),
        lax.all_gather(norm_gains, "seq", axis=1, tiled=True),
    )
    full_in, full_out, full_up, full_down, kernel_cols = (
        lax.all_gather(w_in_rows, "dp", axis=0, tiled=True),
        lax.all_gather(w_out_rows, "dp", axis=0, tiled=True),
        lax.all_gather(w_up_rows, "dp", axis=0, tiled=True),
        lax.all_gather(w_down_rows, "dp", axis=0, tiled=True),
        lax.all_gather(kernel, "dp", axis=0, tiled=True),
    )
    num_seqs, local_len, width = tokens_in.shape
    total_rows = num_seqs * local_len
    inputs = tokens_in.reshape(total_rows, width).astype(jnp.float32)
    gains_wide = gains.astype(jnp.float32)
    normed, norm_back_one = jax.vjp(norm_rows, inputs, gains_wide[0])
    normed_low = normed.astype(jnp.bfloat16)
    proj = jnp.dot(normed_low, full_in, preferred_element_type=jnp.float32)
    values = proj[:, :width]
    gate_one = proj[:, width : 2 * width]
    gate_two = proj[:, 2 * width :]
    mixed_low = (gate_one * values).astype(jnp.bfloat16).reshape(num_seqs, local_len, width)
    by_channel = to_channels(mixed_low)
    filt, filter_back = jax.vjp(partial(shape_filter, taps=taps), kernel_cols.astype(jnp.float32))
    filt_re, filt_im = forward_dft(filt[None])
    sig_re, sig_im = forward_dft(by_channel.astype(jnp.float32))
    conv = inverse_dft(sig_re * filt_re - sig_im * filt_im, sig_re * filt_im + sig_im * filt_re)
    conv_tok = to_tokens(conv.astype(jnp.bfloat16)).reshape(total_rows, width).astype(jnp.float32)
    gated = (gate_two * conv_tok).astype(jnp.bfloat16)
    resid = inputs + jnp.dot(gated, full_out, preferred_element_type=jnp.float32)
    normed_two, norm_back_two = jax.vjp(norm_rows, resid, gains_wide[1])
    normed_two_low = normed_two.astype(jnp.bfloat16)
    hidden_pre = jnp.dot(normed_two_low, full_up, preferred_element_type=jnp.float32)
    active, gelu_back = jax.vjp(gelu_tanh, hidden_pre)
    active_low = active.astype(jnp.bfloat16)
    result = (resid + jnp.dot(active_low, full_down, preferred_element_type=jnp.float32)).astype(
        jnp.bfloat16
    )
    grad_rows = cotangent.reshape(total_rows, width)
    grad_down = contract_rows(active_low, grad_rows)
    grad_active = times_transposed(grad_rows, full_down)
    grad_pre = gelu_back(grad_active)[0].astype(jnp.bfloat16)
    grad_up = contract_rows(normed_two_low, grad_pre)
    grad_normed_two = times_transposed(grad_pre, full_up)
    grad_resid_part, grad_gain_two = norm_back_two(grad_normed_two)
    grad_resid = grad_rows.astype(jnp.float32) + grad_resid_part
    resid_low = grad_resid.astype(jnp.bfloat16)
    grad_outw = contract_rows(gated, resid_low)
    grad_gated = times_transposed(resid_low, full_out)
    grad_gate_two = grad_gated * conv_tok
    grad_conv = (grad_gated * gate_two).astype(jnp.bfloat16).reshape(num_seqs, local_len, width)
    grad_channel = to_channels(grad_conv).astype(jnp.float32)
    back_re, back_im = forward_dft(grad_channel)
    grad_signal = inverse_dft(
        back_re * filt_re + back_im * filt_im, back_im * filt_re - back_re * filt_im
    )
    cross_re = jnp.sum(back_re * sig_re + back_im * sig_im, axis=0, keepdims=True)
    cross_im = jnp.sum(back_im * sig_re - back_re * sig_im, axis=0, keepdims=True)
    grad_filt = inverse_dft(cross_re, cross_im)[0]
    grad_kern = filter_back(grad_filt)[0]
    grad_mixed = (
        to_tokens(grad_signal.astype(jnp.bfloat16)).reshape(total_rows, width).astype(jnp.float32)
    )
    grad_proj = jnp.concatenate([grad_mixed * gate_one, grad_mixed * values, grad_gate_two], axis=1)
    grad_proj = grad_proj.astype(jnp.bfloat16)
    grad_inw = contract_rows(normed_low, grad_proj)
    grad_normed = times_transposed(grad_proj, full_in)
    grad_input_part, grad_gain_one = norm_back_one(grad_normed)
    grad_inputs = (
        (grad_resid + grad_input_part).astype(jnp.bfloat16).reshape(num_seqs, local_len, width)
    )
    grad_gain_pair = jnp.stack([grad_gain_one, grad_gain_two])
    in_part, outw_part, up_part, down_part, kern_done = (
        lax.psum_scatter(
            grad_inw.astype(jnp.bfloat16), "dp", scatter_dimension=0, tiled=True
        ).astype(jnp.float32),
        lax.psum_scatter(
            grad_outw.astype(jnp.bfloat16), "dp", scatter_dimension=0, tiled=True
        ).astype(jnp.float32),
        lax.psum_scatter(
            grad_up.astype(jnp.bfloat16), "dp", scatter_dimension=0, tiled=True
        ).astype(jnp.float32),
        lax.psum_scatter(
            grad_down.astype(jnp.bfloat16), "dp", scatter_dimension=0, tiled=True
        ).astype(jnp.float32),
        lax.psum_scatter(
            grad_kern.astype(jnp.bfloat16), "dp", scatter_dimension=0, tiled=True
        ).astype(jnp.float32),
    )
    in_done, outw_done, up_done, down_done, gain_part = (
        lax.psum_scatter(
            in_part.astype(jnp.bfloat16), "seq", scatter_dimension=1, tiled=True
        ).astype(jnp.float32),
        lax.psum_scatter(
            outw_part.astype(jnp.bfloat16), "seq", scatter_dimension=1, tiled=True
        ).astype(jnp.float32),
        lax.psum_scatter(
            up_part.astype(jnp.bfloat16), "seq", scatter_dimension=1, tiled=True
        ).astype(jnp.float32),
        lax.psum_scatter(
            down_part.astype(jnp.bfloat16), "seq", scatter_dimension=1, tiled=True
        ).astype(jnp.float32),
        lax.psum_scatter(
            grad_gain_pair.astype(jnp.bfloat16), "seq", scatter_dimension=1, tiled=True
        ).astype(jnp.float32),
    )
    gain_done = lax.psum(gain_part, "dp")
    return (
        result.reshape(num_seqs, local_len, width),
        grad_inputs,
        in_done,
        outw_done,
        up_done,
        down_done,
        gain_done,
        kern_done,
    )


MESH = pl.DeviceIdType.MESH
BF = jnp.bfloat16
F32 = jnp.float32


class Remote:
    def __init__(self, wire, slot, src, dst, peer):
        self.wire, self.slot, self.src, self.dst, self.peer = wire, slot, src, dst, peer

    def named(self):
        return pltpu.make_async_remote_copy(
            src_ref=self.src(), dst_ref=self.dst(), send_sem=self.wire.send.at[self.slot],
            recv_sem=self.wire.recv.at[self.slot], device_id=self.peer, device_id_type=MESH,
        )

    def wait_recv(self):
        self.named().wait_recv()


class Wire:
    def __init__(self, send, recv, spots):
        self.send, self.recv, self.s, self.made = send, recv, spots, []

    def start(self, src, dst, peer, core=None):
        src, dst = (end if callable(end) else partial(lambda ref: ref, end) for end in (src, dst))
        copy = Remote(self, len(self.made), src, dst, peer)
        copy.named().start()
        self.made.append((core, copy))
        return copy

    def drain(self):
        for which in (None, 0, 1):
            @self.s.on(which)
            def _():
                for core, copy in self.made:
                    if core == which:
                        copy.named().wait_send()


class Local:
    def __init__(self, sems):
        self.sems, self.made, self.open = sems, 0, []

    def start(self, src, dst):
        copy = pltpu.make_async_copy(src, dst, self.sems.at[self.made])
        self.made += 1
        copy.start()
        self.open.append(copy)
        return copy

    def wait(self, copy):
        copy.wait()
        self.open = [other for other in self.open if other is not copy]

    def drain(self):
        for copy in list(self.open):
            self.wait(copy)


def arrived(copies):
    for copy in copies:
        copy.wait_recv()


class Spots:
    def __init__(self, num_z):
        dp, sq = lax.axis_index("dp"), lax.axis_index("seq")
        z, x, y, c = dp // 2, dp % 2, sq // 2, sq % 2
        self.num_z = num_z
        self.z, self.x, self.y, self.c = z, x, y, c
        self.own = dict(x=x, y=y, z=z)
        self.size = dict(x=2, y=2, z=num_z)
        self.core = self.at(z, x, y, 1 - c)
        self.others = dict(x=[1 - x], y=[1 - y], z=[(z + k) % num_z for k in range(1, num_z)])
        self.along = dict(
            x=[self.at(z, 1 - x, y, c)], y=[self.at(z, x, 1 - y, c)],
            z=[self.at(other, x, y, c) for other in self.others["z"]],
        )
        self.group = [((y + i) % 2, (c + j) % 2) for i, j in ((1, 0), (1, 1), (0, 1))]
        self.mates = [self.at(z, x, yy, cc) for yy, cc in self.group]

    def at(self, z, x, y, c):
        return (z * 2 + x, y * 2 + c)

    def on(self, core):
        return (lambda body: body()) if core is None else pl.when(self.c == core)

    def meet(self):
        barrier = pltpu.get_barrier_semaphore()
        peers = self.along["z"] + self.along["x"] + self.mates
        for peer in peers:
            pl.semaphore_signal(barrier, inc=1, device_id=peer, device_id_type=MESH)
        pl.semaphore_wait(barrier, len(peers))


def both_cores(orders):
    return [(None, orders[0])] if len(orders) == 1 else list(enumerate(orders))


def block_index(s, axes, wide, core, at=None):
    place = {**s.own, **(at or {})}
    index = tuple(slice(None) if axis in wide else place[axis] for axis in axes)
    return index if core is None else index + (core,)


class Gather:
    def __init__(self, wire, spots, full, axes, *orders, part=None):
        self.wire, self.s, self.full, self.axes, self.part = wire, spots, full, axes, part
        self.orders, self.last = both_cores(orders), {}

    def view(self, have):
        index = block_index(self.s, self.axes, have, self.s.c)
        return self.full.at[index if self.part is None else index + (self.part,)]

    def settle(self):
        for core, copies in self.last.items():
            self.s.on(core)(partial(arrived, copies))
        self.last = {}

    def step(self, n):
        s = self.s
        if n == len(self.orders[0][1]):
            self.settle()
            view = partial(self.view, self.axes)
            self.last[None] = [self.wire.start(view, view, s.core)]
            return
        before, self.last = self.last, {}
        for core, order in self.orders:
            @s.on(core)
            def _():
                arrived(before.get(core, []))
                view = partial(self.view, order[:n])
                self.last[core] = [self.wire.start(view, view, peer, core) for peer in s.along[order[n]]]

    def done(self):
        self.settle()


class Scatter:
    def __init__(self, wire, spots, total, axes, orders, from_core, got, result, away=None):
        self.wire, self.s, self.total, self.axes = wire, spots, total, axes
        self.orders = [(core, order[::-1]) for core, order in both_cores(orders)]
        self.from_core, self.got, self.result, self.away = from_core, got, result, away
        self.last = {}

    def mine(self, wide, at=None):
        return self.total.at[block_index(self.s, self.axes, wide, None if self.away is not None else self.s.c, at)]

    def send_core(self):
        s = self.s
        source = self.total if self.away is None else self.away
        rest = (slice(None),) * (len(self.axes) - 1) + (1 - s.c,)
        self.last = [
            self.wire.start(source.at[(i,) + rest], self.from_core.at[i], s.core)
            for i in range(self.from_core.shape[0])
        ]

    def add_core(self):
        arrived(self.last)
        self.last = {}
        s = self.s
        count = math.prod(s.size[axis] for axis in self.axes)

        def one(i, _):
            at, left = {}, i
            for axis in reversed(self.axes):
                at[axis], left = left % s.size[axis], left // s.size[axis]
            into = self.mine("", at)
            term = self.from_core[tuple(at[axis] for axis in self.axes)]
            into[...] = (into[...].astype(F32) + term.astype(F32)).astype(BF)
            return 0
        lax.fori_loop(0, count, one, 0)

    def stages(self, order, n):
        s = self.s
        begin = 0
        for k in range(n + 1):
            wide = sorted(order[k + 1 :])
            count = math.prod(s.size[axis] for axis in wide)
            if k < n:
                begin += count * (s.size[order[k]] - 1)
        return order[n], wide, count, begin

    def slots(self, start, count):
        return self.got.at[start] if count is None else self.got.at[start : start + count]

    def send(self, n):
        s = self.s
        for core, order in self.orders:
            axis, wide, count, begin = self.stages(order, n)

            @s.on(core)
            def _():
                self.last[core] = []
                for j, (other, peer) in enumerate(zip(s.others[axis], s.along[axis])):
                    outer = s.size[wide[0]] if len(wide) == 2 else 1
                    inner = count // outer
                    for i in range(outer):
                        at = {axis: other}
                        if len(wide) == 2:
                            at[wide[0]] = i
                        start = begin + j * count + i * inner
                        src = partial(self.mine, wide[-1:], at)
                        dst = partial(self.slots, start, inner if wide else None)
                        self.last[core].append(self.wire.start(src, dst, peer, core))

    def add(self, n):
        s = self.s
        for core, order in self.orders:
            axis, wide, count, begin = self.stages(order, n)
            peers = len(s.others[axis])

            @s.on(core)
            def _():
                arrived(self.last[core])
                if n == len(order) - 1:
                    total = self.mine("")[...].astype(F32)
                    for j in range(peers):
                        total = total + self.got[begin + j].astype(F32)
                    self.result[...] = total
                    return

                def one(i, _):
                    at, left = {}, i
                    for a in reversed(wide):
                        at[a], left = left % s.size[a], left // s.size[a]
                    into = self.mine("", at)
                    total = into[...].astype(F32)
                    for j in range(peers):
                        total = total + self.got[begin + j * count + i].astype(F32)
                    into[...] = total.astype(BF)
                    return 0
                lax.fori_loop(0, count, one, 0)

    def trade(self, ends):
        part = ends.shape[-1]
        for core in range(2):
            ends[core] = self.result[:, core * part : (core + 1) * part]
        self.last = [self.wire.start(ends.at[1 - self.s.c], ends.at[2], self.s.core)]
        self.ends = ends

    def finish(self, out, turned=False):
        arrived(self.last)
        c, own, other = self.s.c, self.ends[self.s.c], self.ends[2]
        both = jnp.concatenate([jnp.where(c == 0, own, other), jnp.where(c == 0, other, own)], axis=0)
        out[...] = both.T if turned else both


def norm_parts(values):
    center = values - jnp.mean(values, axis=-1, keepdims=True)
    spread = jnp.mean(center * center, axis=-1, keepdims=True)
    scale = lax.rsqrt(spread + EPSILON)
    return center * scale, scale


def norm_back(normal, scale, grad, gain):
    p = grad * gain
    flat = jnp.mean(p, axis=-1, keepdims=True)
    along = jnp.mean(p * normal, axis=-1, keepdims=True)
    return (p - flat - normal * along) * scale, jnp.sum(grad * normal, axis=0, keepdims=True)


def dot(left, right):
    return jnp.dot(left, right, preferred_element_type=F32)


def dot_rows(left, right):
    return lax.dot_general(left, right, (((0,), (0,)), ((), ())), preferred_element_type=F32)


def dot_cols(left, right):
    return lax.dot_general(left, right, (((1,), (1,)), ((), ())), preferred_element_type=F32)


def live_taps(kern, taps):
    position = lax.broadcasted_iota(jnp.int32, kern.shape, 0)
    return position, position.astype(F32) < taps


def pool(values, position):
    length = values.shape[0]
    before = jnp.where(position == 0, 0.0, pltpu.roll(values, 1, 0))
    after = jnp.where(position == length - 1, 0.0, pltpu.roll(values, length - 1, 0))
    return (before + values + after) / 3.0


def make_filter(kern, taps):
    position, live = live_taps(kern, taps)
    masked = jnp.where(live, kern, 0.0)
    shrunk = masked - SHRINK_SCALE * jnp.tanh(masked / SHRINK_SCALE)
    return jnp.where(live, pool(shrunk, position), 0.0)


def kernel_back(kern, taps, grad):
    position, live = live_taps(kern, taps)
    slope = jnp.tanh(jnp.where(live, kern, 0.0) / SHRINK_SCALE)
    return jnp.where(live, pool(jnp.where(live, grad, 0.0), position) * slope * slope, 0.0)


GELU_K = math.sqrt(2.0 / math.pi)


def gelu_both(v):
    square = v * v
    t = jnp.tanh(GELU_K * v * (1.0 + 0.044715 * square))
    half = 0.5 * (1.0 + t)
    slope = half + 0.5 * v * (1.0 - t * t) * (GELU_K * (1.0 + 3 * 0.044715 * square))
    return v * half, slope


def spans(start, size, step=16):
    return pl.ds(pl.multiple_of(start, step), size)


def transform_table(length):
    k = 2 * np.arange(length)[:, None] + 1
    angle = np.pi / (4 * length) * ((k * k.T) % (8 * length))
    return np.concatenate([np.cos(angle), np.sin(angle)]).astype(np.float32).astype(ml_dtypes.bfloat16)


def twist_table(length):
    angle = np.pi / (4 * length) * (2 * np.arange(length) + 1)
    return np.stack([np.cos(angle), np.sin(angle)], axis=1).astype(np.float32)


ORDER_OUT = ("zxy", "zyx")
ORDER_UP = ("zxy", "zyx")
ORDER_DOWN = ("zyx", "yzx")
STEP = 256


def forward_kernel(
    num_z, length,
    tok, cot, w_in, w_out, w_up, w_down_t, kern_t, gains_in, taps_in, twist, table_hbm,
    out_o, win_o, wout_o, wup_o, gdown_o, kern_o, small_o, proj_o, normed_o, spec_o, filt_o, conv_o,
    gated_o, resid_o, normed_two_o, gpre_o,
    win_v, wout_v, wup_v, wdown_v, kern_v, small_v,
    pre_in, pre_out, pre_up, pre_down, pre_kern, w_down, kern,
    table_v, proj_v, normed_own, normed_v, sig_v, spec_v, filt_v, filt_low, turned_v, conv_v, gated_ch,
    gated_v, resid_v, normed_two_v, act_v, slope_v, gdown_v, out_v,
    send, recv, local,
):
    s = Spots(num_z)
    z, x, y, c = s.z, s.x, s.y, s.c
    wire, inner = Wire(send, recv, s), Local(local)
    load_table = inner.start(table_hbm, table_v)
    rows, width = tok.shape
    group, span = width // 2, rows // 2
    hidden = act_v.shape[1]
    me = 2 * y + c
    w_down[...] = w_down_t[...].T
    kern[...] = kern_t[...].T
    small_v[me, 0:2] = gains_in[...].astype(F32)
    small_v[me, 2:3] = taps_in[...].astype(F32)
    s.meet()

    half = w_in.shape[0] // 2
    trade_in = [
        wire.start(w_in.at[spans(cc * half, half)], pre_in.at[me], peer) for (yy, cc), peer in zip(s.group, s.mates)
    ]
    smalls = [wire.start(small_v.at[me], small_v.at[me], peer) for peer in s.mates]
    pairs = [(kern, pre_kern), (w_out, pre_out), (w_up, pre_up), (w_down, pre_down)]
    traded = []
    for src, pre in pairs:
        half = src.shape[0] // 2
        traded.append(wire.start(src.at[spans((1 - c) * half, half)], pre.at[c], s.core))
    half = w_in.shape[0] // 2
    pre_in[me] = w_in[spans(c * half, half)]
    for src, pre in pairs:
        half = src.shape[0] // 2
        pre[c] = src[spans(c * half, half)]

    g_in = [Gather(wire, s, win_v, "zx", "zx", part=k) for k in range(3)]
    g_kern = Gather(wire, s, kern_v, "zx", "zx")
    g_out = Gather(wire, s, wout_v, "yzx", *ORDER_OUT)
    g_up = Gather(wire, s, wup_v, "yzx", *ORDER_UP)
    g_down = Gather(wire, s, wdown_v, "yzx", *ORDER_DOWN)

    def join(i, full):
        traded[i].wait_recv()
        pre = pairs[i][1]
        full[block_index(s, "zx" if i == 0 else "yzx", "", c)] = jnp.concatenate([pre[0], pre[1]], axis=-1)

    arrived(trade_in)
    whole = jnp.concatenate([pre_in[k] for k in range(4)], axis=-1)
    for k in range(3):
        left, right = (whole[:, (2 * k + h) * group : (2 * k + h + 1) * group] for h in range(2))
        win_v[z, x, c, k] = jnp.where(y == 0, left, right)
        g_in[k].step(0)

    arrived(smalls)
    gains = jnp.concatenate([small_v[k] for k in range(4)], axis=-1)
    normed, _ = norm_parts(tok[...].astype(F32))
    normed_own[...] = (normed * gains[0:1]).astype(BF)
    chunk = spans(me * span, span)
    to_group = [
        wire.start(normed_own.at[spans(cc * span, span)], normed_v.at[chunk], peer)
        for (yy, cc), peer in zip(s.group, s.mates)
    ]
    normed_v[chunk] = normed_own[spans(c * span, span)]
    join(0, kern_v)
    g_kern.step(0)
    join(1, wout_v)
    join(2, wup_v)
    join(3, wdown_v)

    g_in[0].step(1)
    g_in[1].step(1)
    g_out.step(0)
    g_in[2].step(1)
    g_up.step(0)
    g_kern.step(1)
    g_in[0].step(2)
    g_in[1].step(2)
    g_down.step(0)
    g_in[2].step(2)
    g_kern.step(2)
    g_out.step(1)

    g_kern.done()
    taps = jnp.concatenate([small_v[2 * y], small_v[2 * y + 1]], axis=-1)[2:3]
    tile = 128
    for j in range(group // tile):
        cols = slice(j * tile, (j + 1) * tile)
        filt = make_filter(kern_v[:, :, :, :, cols].reshape(length, tile).astype(F32), taps[:, cols])
        filt_low[:, cols] = filt.astype(BF)
    inner.wait(load_table)

    def spectrum(i, _):
        real, imag = spans(i * STEP, STEP, STEP), spans(length + i * STEP, STEP, STEP)
        re, im = dot(table_v[real], filt_low[...]), dot(table_v[imag], filt_low[...])
        cosine, sine = twist[real, 0:1], twist[real, 1:2]
        filt_v[real] = (re * cosine + im * sine).astype(BF)
        filt_v[imag] = (im * cosine - re * sine).astype(BF)
        return 0
    lax.fori_loop(0, length // STEP, spectrum, 0)

    g_up.step(1)
    g_out.step(2)
    arrived(to_group)
    g_in[0].done()
    g_in[1].done()

    def project(k, at):
        return dot(normed_v[at], win_v[:, :, :, k].reshape(width, group))

    tall = length // 2
    for i in range(2):
        at = slice(i * tall, (i + 1) * tall)
        value, gate = project(0, at), project(1, at)
        proj_v[0, at] = value.astype(BF)
        proj_v[1, at] = gate.astype(BF)
        sig_v[at] = (value * gate).astype(BF)
    g_up.step(2)
    g_down.step(1)
    g_in[2].done()
    for i in range(2):
        at = slice(i * tall, (i + 1) * tall)
        proj_v[2, at] = project(2, at).astype(BF)

    def convolve(i, _):
        real, imag = spans(i * STEP, STEP, STEP), spans(length + i * STEP, STEP, STEP)
        re_s, im_s = dot(table_v[real], sig_v[...]), dot(table_v[imag], sig_v[...])
        spec_v[real] = re_s.astype(BF)
        spec_v[imag] = im_s.astype(BF)
        re_f, im_f = filt_v[real].astype(F32), filt_v[imag].astype(F32)
        turned_v[real] = (re_s * re_f - im_s * im_f).astype(BF)
        turned_v[imag] = (re_s * im_f + im_s * re_f).astype(BF)
        return 0
    lax.fori_loop(0, length // STEP, convolve, 0)

    def back(i, _):
        at, imag = spans(i * STEP, STEP, STEP), spans(length + i * STEP, STEP, STEP)
        both = dot(table_v[at], turned_v[0:length]) + dot(table_v[imag], turned_v[length:])
        conv = (both * (1.0 / length)).astype(BF)
        conv_v[at] = conv
        gated_ch[at] = (proj_v[2, at].astype(F32) * conv.astype(F32)).astype(BF)
        return 0
    lax.fori_loop(0, length // STEP, back, 0)

    home = spans(c * span, span)
    to_tokens = [
        wire.start(gated_ch.at[spans((2 * yy + cc) * span, span)], gated_v.at[y, home], peer)
        for (yy, cc), peer in zip(s.group, s.mates)
    ]
    gated_v[y, home] = gated_ch[chunk]
    g_out.step(3)
    g_down.step(2)
    g_up.step(3)
    for src, dst in ((win_v, win_o), (kern_v, kern_o), (small_v, small_o), (proj_v, proj_o),
                     (normed_v, normed_o), (spec_v, spec_o), (filt_v, filt_o), (conv_v, conv_o)):
        inner.start(src, dst)
    g_out.done()
    arrived(to_tokens)

    for k in range(2):
        cols = slice(k * group, (k + 1) * group)
        mixed = sum(
            dot(gated_v[h], wout_v[k, h * num_z // 2 : (h + 1) * num_z // 2].reshape(group, group)) for h in range(2)
        )
        resid_v[:, cols] = tok[:, cols].astype(F32) + mixed
    normed_two, _ = norm_parts(resid_v[...])
    normed_two_v[...] = (normed_two * gains[1:2]).astype(BF)
    for src, dst in ((wout_v, wout_o), (gated_v, gated_o), (resid_v, resid_o), (normed_two_v, normed_two_o)):
        inner.start(src, dst)
    g_up.done()

    wide = 256
    per = hidden // 2 // wide

    def feed(j, _):
        weight = wup_v[j // per, :, :, :, :, spans((j % per) * wide, wide, wide)].reshape(width, wide)
        act, slope = gelu_both(dot(normed_two_v[...], weight))
        at = spans(j * wide, wide, wide)
        act_v[:, at] = act.astype(BF)
        slope_v[:, at] = slope.astype(BF)
        return 0
    lax.fori_loop(0, 2 * per, feed, 0)
    inner.start(wup_v, wup_o)
    g_down.step(3)

    deep = hidden // (2 * num_z)

    def down_grad(i, _):
        grad = dot_rows(act_v[:, spans(i * deep, deep, deep)], cot[...]).astype(BF)
        for h in range(2):
            gdown_v[h, i // 2, i % 2] = grad[:, h * group : (h + 1) * group].reshape(2, deep // 2, group)
        return 0
    lax.fori_loop(0, 2 * num_z, down_grad, 0)
    inner.start(gdown_v, gdown_o)
    g_down.done()

    def pre_grad(i, _):
        at = spans(i * deep, deep, deep)
        grad = sum(
            dot_cols(cot[:, h * group : (h + 1) * group], wdown_v[h, i // 2, i % 2].reshape(deep, group))
            for h in range(2)
        )
        slope_v[:, at] = (slope_v[:, at].astype(F32) * grad).astype(BF)
        return 0
    lax.fori_loop(0, 2 * num_z, pre_grad, 0)
    inner.start(slope_v, gpre_o)
    for h in range(2):
        cols = slice(h * group, (h + 1) * group)
        out_v[:, cols] = (resid_v[:, cols] + dot(act_v[...], wdown_v[h].reshape(hidden, group))).astype(BF)
    inner.start(out_v, out_o)
    wire.drain()
    inner.drain()


def vm(shape, dtype=BF):
    return pltpu.VMEM(tuple(shape), dtype)


VMEM_SPEC, HBM_SPEC = pl.BlockSpec(memory_space=pltpu.VMEM), pl.BlockSpec(memory_space=pl.ANY)


def forward(num_z, length, tokens, cot, w_in, w_out, w_up, w_down_t, kernel_t, gains, taps, twist, table):
    rows, width = tokens.shape
    group = width // 2
    part = w_down_t.shape[1]
    hidden = part * num_z * 2
    sds = jax.ShapeDtypeStruct
    axes = (2, num_z, 2, 2)
    win = axes[1:] + (3, w_in.shape[0] // 2, group)
    wout, wup, wdown = axes + (w_out.shape[0] // 2, group), axes + (w_up.shape[0] // 2, hidden // 2), axes + (part // 2, group)
    kern = axes[1:] + (kernel_t.shape[1] // 2, group)
    small = (4, 8, width // 4)
    acts = dict(
        proj=((3, length, group), BF), normed=((length, width), BF), spec=((2 * length, group), BF),
        filt=((2 * length, group), BF), conv=((length, group), BF), gated=((2, rows, group), BF),
        resid=((rows, width), F32), normed_two=((rows, width), BF), gpre=((rows, hidden), BF),
    )
    outs = [sds((rows, width), BF)] + [sds(w, BF) for w in (win, wout, wup, wdown, kern)] + [sds(small, F32)]
    outs += [sds(*acts[k]) for k in acts]
    act = lambda k: vm(*acts[k])
    scratch = [vm(w) for w in (win, wout, wup, wdown, kern)] + [vm(small, F32)]
    scratch += [vm((4, w_in.shape[0] // 2, w_in.shape[1])), vm((2, w_out.shape[0] // 2, w_out.shape[1])),
                vm((2, w_up.shape[0] // 2, w_up.shape[1])), vm((2, part // 2, w_down_t.shape[0])),
                vm((2, kernel_t.shape[1] // 2, kernel_t.shape[0])), vm(w_down_t.shape[::-1]), vm(kernel_t.shape[::-1])]
    scratch += [vm(table.shape), act("proj"), vm((rows, width)), act("normed"), vm((length, group)), act("spec"),
                act("filt"), vm((length, group)), vm((2 * length, group)), act("conv"), vm((length, group)),
                act("gated"), act("resid"), act("normed_two"), act("gpre"), act("gpre"), vm(wdown), vm((rows, width))]
    scratch += [pltpu.SemaphoreType.DMA((160,)), pltpu.SemaphoreType.DMA((160,)), pltpu.SemaphoreType.DMA((40,))]
    return pl.pallas_call(
        partial(forward_kernel, num_z, length),
        out_shape=outs,
        in_specs=[VMEM_SPEC] * 10 + [HBM_SPEC],
        out_specs=[HBM_SPEC] * len(outs),
        scratch_shapes=scratch,
        compiler_params=pltpu.CompilerParams(collective_id=0, has_side_effects=True, vmem_limit_bytes=61 * 2**20),
        cost_estimate=pl.CostEstimate(flops=17 * 10**9, bytes_accessed=50 * 10**6, transcendentals=2 * 10**6),
    )(tokens, cot, w_in, w_out, w_up, w_down_t, kernel_t, gains, taps, twist, table)


def backward_kernel(
    num_z, length,
    tok, cot, twist, small_v, table_h, win_h, wout_h, wup_h, gdown_h, kern_h, proj_h, normed_h, spec_h,
    filt_h, conv_h, gated_h, resid_h, normed_two_h, gpre_h,
    grad_in_o, gin_o, gout_o, gup_o, gdn_o, gains_o, gkern_o,
    table_v, win_v, wout_v, wup_v, kern_v, proj_v, normed_v, spec_v, filt_v, conv_v,
    gated_v, resid_v, normed_two_v, gpre_v,
    gup_v, gdn_v, gkern_v,
    core_in, core_out, core_up, core_dn, core_kern,
    got_in, got_out, got_up, got_dn, got_kern,
    sum_in, sum_out, sum_up, sum_dn, sum_kern,
    ends_out, ends_up, ends_dn, ends_kern, swap_core, swap_y,
    low_v, ggate_v, gch_v, gnorm_got, gain_v, gain_got,
    send, recv, local,
):
    s = Spots(num_z)
    z, x, y, c = s.z, s.x, s.y, s.c
    wire, inner = Wire(send, recv, s), Local(local)
    rows, width = tok.shape
    group, span = width // 2, rows // 2
    hidden = gpre_v.shape[1]
    me = 2 * y + c
    own_dn = [inner.start(gdown_h.at[i, :, :, c], gdn_v.at[i]) for i in range(2)]
    loads = {}
    for name, src, dst in (
        ("gpre", gpre_h, gpre_v), ("wup", wup_h, wup_v), ("normed_two", normed_two_h, normed_two_v),
        ("resid", resid_h, resid_v), ("wout", wout_h, wout_v), ("proj", proj_h, proj_v), ("conv", conv_h, conv_v),
        ("gated", gated_h, gated_v), ("table", table_h, table_v), ("spec", spec_h, spec_v), ("filt", filt_h, filt_v),
        ("kern", kern_h, kern_v), ("normed", normed_h, normed_v), ("win", win_h, win_v),
    ):
        loads[name] = inner.start(src, dst)

    def need(*names):
        for name in names:
            inner.wait(loads[name])

    s.meet()
    block = width // (4 * num_z)
    gout_v = wup_v.at[:, :, :, :, :, 0:group]
    gin_v = win_v
    down = Scatter(wire, s, gdn_v, "yzx", ORDER_DOWN, core_dn, got_dn, sum_dn, away=gdown_h)
    up = Scatter(wire, s, gup_v, "yzx", ORDER_UP, core_up, got_up, sum_up)
    out = Scatter(wire, s, gout_v, "yzx", ORDER_OUT, core_out, got_out, sum_out)
    into = Scatter(wire, s, gin_v, "zx", ("zx",), core_in, got_in, sum_in)
    taps_grad = Scatter(wire, s, gkern_v, "zx", ("zx",), core_kern, got_kern, sum_kern)
    down.send_core()
    gains = jnp.concatenate([small_v[k] for k in range(4)], axis=-1)

    need("gpre", "wup", "resid")
    half = hidden // 2
    grad = sum(
        dot_cols(gpre_v[:, h * half : (h + 1) * half], wup_v[h].reshape(width, half)) for h in range(2)
    )
    normal, scale = norm_parts(resid_v[...])
    part, gain_two = norm_back(normal, scale, grad, gains[1:2])
    resid_v[...] = cot[...].astype(F32) + part
    low_v[...] = resid_v[...].astype(BF)

    for copy in own_dn:
        inner.wait(copy)
    down.add_core()
    down.send(0)

    need("wout")
    for h in range(2):
        grad = sum(
            dot_cols(
                low_v[:, k * group : (k + 1) * group],
                wout_v[k, h * num_z // 2 : (h + 1) * num_z // 2].reshape(group, group),
            )
            for k in range(2)
        )
        ggate_v[h] = grad.astype(BF)
    chunk, home = spans(me * span, span), spans(c * span, span)
    to_channels = [
        wire.start(ggate_v.at[yy, spans(cc * span, span)], gch_v.at[chunk], peer)
        for (yy, cc), peer in zip(s.group, s.mates)
    ]
    gch_v[chunk] = ggate_v[y, home]

    need("normed_two")
    wide = 256
    per = hidden // 2 // wide

    def up_grad(j, _):
        grad = dot_rows(normed_two_v[...], gpre_v[:, spans(j * wide, wide, wide)]).astype(BF)
        cols = spans((j % per) * wide, wide, wide)
        gup_v[j // per, :, :, :, :, cols] = grad.reshape(num_z, 2, 2, block, wide)
        return 0
    lax.fori_loop(0, 2 * per, up_grad, 0)
    up.send_core()
    down.add(0)
    down.send(1)

    need("gated")
    for h in range(2):
        for k in range(2):
            grad = dot_rows(gated_v[h], low_v[:, k * group : (k + 1) * group]).astype(BF)
            gout_v[k, h * num_z // 2 : (h + 1) * num_z // 2] = grad.reshape(num_z // 2, 2, 2, block, group)
    out.send_core()
    up.add_core()
    up.send(0)

    need("proj", "conv", "table", "spec", "filt")
    arrived(to_channels)

    def gate(i, _):
        at = spans(i * STEP, STEP, STEP)
        grad = gch_v[at].astype(F32)
        gch_v[at] = (grad * proj_v[2, at].astype(F32)).astype(BF)
        proj_v[2, at] = (grad * conv_v[at].astype(F32)).astype(BF)
        return 0
    lax.fori_loop(0, length // STEP, gate, 0)

    def turn(i, _):
        real, imag = spans(i * STEP, STEP, STEP), spans(length + i * STEP, STEP, STEP)
        re, im = dot(table_v[real], gch_v[...]), dot(table_v[imag], gch_v[...])
        re_f, im_f = filt_v[real].astype(F32), filt_v[imag].astype(F32)
        filt_v[real] = (re_f * re + im_f * im).astype(BF)
        filt_v[imag] = (re_f * im - im_f * re).astype(BF)
        re_s, im_s = spec_v[real].astype(F32), spec_v[imag].astype(F32)
        re_k, im_k = re_s * re + im_s * im, re_s * im - im_s * re
        cosine, sine = twist[real, 0:1], twist[real, 1:2]
        spec_v[real] = (re_k * cosine - im_k * sine).astype(BF)
        spec_v[imag] = (im_k * cosine + re_k * sine).astype(BF)
        return 0
    lax.fori_loop(0, length // STEP, turn, 0)
    down.add(1)
    down.send(2)
    out.add_core()
    out.send(0)

    def back(i, _):
        at, imag = spans(i * STEP, STEP, STEP), spans(length + i * STEP, STEP, STEP)
        both = dot(table_v[at], filt_v[0:length]) + dot(table_v[imag], filt_v[length:])
        grad = (both * (1.0 / length)).astype(BF).astype(F32)
        value, first = proj_v[0, at].astype(F32), proj_v[1, at].astype(F32)
        proj_v[0, at] = (grad * first).astype(BF)
        proj_v[1, at] = (grad * value).astype(BF)
        return 0
    lax.fori_loop(0, length // STEP, back, 0)

    need("normed", "win")

    def normed_grad(j):
        grad = sum(
            dot_cols(proj_v[k, spans(j * span, span)], win_v[:, :, :, k].reshape(width, group)) for k in range(3)
        )
        return grad.astype(BF)

    to_owner = []
    for i, ((yy, cc), peer) in enumerate(zip(s.group, s.mates)):
        place = gpre_v.at[0:span, i * width : (i + 1) * width]
        place[...] = normed_grad(2 * yy + cc)
        to_owner.append(wire.start(place, gnorm_got.at[i], peer))
    mine = gpre_v.at[0:span, 3 * width : 4 * width]
    mine[...] = normed_grad(me)

    up.add(0)
    up.send(1)
    for k in range(3):
        grad = dot_rows(normed_v[...], proj_v[k]).astype(BF)
        gin_v[:, :, :, k] = grad.reshape(num_z, 2, 2, block, group)
    into.send_core()
    out.add(0)
    out.send(1)
    into.add_core()
    into.send(0)

    need("kern")
    taps = jnp.concatenate([small_v[2 * y], small_v[2 * y + 1]], axis=-1)[2:3]
    tile = 128
    for j in range(group // tile):
        cols = slice(j * tile, (j + 1) * tile)
        both = dot(table_v[0:length], spec_v[0:length, cols]) + dot(table_v[length:], spec_v[length:, cols])
        grad = kernel_back(kern_v[:, :, :, :, cols].reshape(length, tile).astype(F32), taps[:, cols],
                           both * (1.0 / length))
        gkern_v[:, :, :, :, cols] = grad.astype(BF).reshape(num_z, 2, 2, length // (4 * num_z), tile)
    taps_grad.send_core()
    up.add(1)
    up.send(2)
    into.add(0)
    into.send(1)
    taps_grad.add_core()
    taps_grad.send(0)
    out.add(1)
    out.send(2)
    down.add(2)
    down.trade(ends_dn)

    arrived(to_owner)
    across, diagonal, beside = (gnorm_got[i].astype(F32) for i in range(3))
    here = mine[...].astype(F32) + across
    there = beside + diagonal
    first_rows, second_rows = jnp.where(c == 0, here, there), jnp.where(c == 0, there, here)
    grad = jnp.concatenate([first_rows, second_rows], axis=0)
    normal, scale = norm_parts(tok[...].astype(F32))
    part, gain_one = norm_back(normal, scale, grad, gains[0:1])
    low_v[...] = (resid_v[...] + part).astype(BF)
    inner.start(low_v, grad_in_o)

    gain_v[0] = jnp.concatenate([gain_one, gain_two, jnp.zeros((6, width), F32)], axis=0)
    got = [wire.start(gain_v.at[0], gain_got.at[k], peer) for k, peer in enumerate(s.mates)]
    taps_grad.add(0)
    taps_grad.send(1)
    arrived(got)
    gain_v[1] = gain_v[0] + gain_got[0] + gain_got[1] + gain_got[2]
    got = [wire.start(gain_v.at[1], gain_got.at[3], s.along["x"][0])]
    up.add(2)
    up.trade(ends_up)
    out.add(2)
    out.trade(ends_out)
    arrived(got)
    gain_v[2] = gain_v[1] + gain_got[3]
    got = [wire.start(gain_v.at[2], gain_got.at[3 + k], peer) for k, peer in zip(range(1, num_z), s.along["z"])]

    into.add(1)
    first, second, third = sum_in[y], sum_in[y + 1], sum_in[(y + 2) % 3]
    swap_core[0, 0], swap_core[0, 1] = first.astype(BF), second.astype(BF)
    swap_y[0] = third.astype(BF)
    swaps = [wire.start(swap_y.at[0], swap_y.at[1], s.mates[0]), wire.start(swap_y.at[0], swap_y.at[2], s.mates[1]),
             wire.start(swap_core.at[0], swap_core.at[1], s.core)]
    taps_grad.add(1)
    taps_grad.trade(ends_kern)
    down.finish(gdn_o, turned=True)
    up.finish(gup_o)
    out.finish(gout_o)
    arrived(got)
    total = gain_v[2]
    for k in range(1, num_z):
        total = total + gain_got[3 + k]
    part = width // 4
    mine = total[:, 0:part]
    for k in range(1, 4):
        mine = jnp.where(me == k, total[:, k * part : (k + 1) * part], mine)
    gains_o[...] = mine[0:2]
    taps_grad.finish(gkern_o, turned=True)
    arrived(swaps)
    cut = group // 2
    for row, near, far in ((c, swap_core.at[0], swap_y.at[1]), (1 - c, swap_core.at[1], swap_y.at[2])):
        far = far[...].astype(F32)
        left = jnp.concatenate([near[0].astype(F32), far[:, 0:cut]], axis=-1)
        right = jnp.concatenate([far[:, cut:], near[1].astype(F32)], axis=-1)
        gin_o[spans(row * block, block)] = jnp.where(c == 0, left, right)
    wire.drain()
    inner.drain()


def backward(num_z, length, tokens, cot, twist, small_f, table, full):
    rows, width = tokens.shape
    group = width // 2
    sds = jax.ShapeDtypeStruct
    win, wout, wup, gdown, kern, proj, normed, spec, filt, conv, gated, resid, normed_two, gpre = full
    like = lambda a: vm(a.shape, a.dtype)
    weights = (win, wout, wup, gdown, kern)
    blocks = [a.shape[-2:] for a in weights]
    blocks[0] = win.shape[-3:]
    counts = [7, 15, 15, 15, 7]
    outs = [sds((rows, width), BF), sds((2 * win.shape[-2], width * 3 // 4), F32)]
    outs += [sds((2 * w.shape[-2], w.shape[-1] // 2), F32) for w in (wout, wup)]
    outs += [sds((gdown.shape[-1] // 2, 2 * gdown.shape[-2]), F32), sds((2, width // 4), F32)]
    outs += [sds((kern.shape[-1] // 2, 2 * kern.shape[-2]), F32)]
    scratch = [like(a) for a in (table, win, wout, wup, kern, proj, normed, spec, filt, conv, gated, resid,
                                 normed_two, gpre)]
    scratch += [like(wup), vm(gdown.shape[:3] + gdown.shape[4:]), like(kern)]
    scratch += [vm(win.shape[:2] + win.shape[3:])] + [vm(w.shape[:3] + w.shape[4:]) for w in (wout, wup, gdown)]
    scratch += [vm(kern.shape[:2] + kern.shape[3:])]
    scratch += [vm((n,) + b) for n, b in zip(counts, blocks)] + [vm(b, F32) for b in blocks]
    scratch += [vm((3, b[0], b[1] // 2), F32) for b in blocks[1:]]
    scratch += [vm((2, 2) + blocks[0][1:]), vm((3,) + blocks[0][1:])]
    scratch += [vm((rows, width)), vm((2, rows, group)), vm((length, group)), vm((3, rows // 2, width)),
                vm((3, 8, width), F32), vm((3 + num_z, 8, width), F32)]
    scratch += [pltpu.SemaphoreType.DMA((160,)), pltpu.SemaphoreType.DMA((160,)), pltpu.SemaphoreType.DMA((40,))]
    return pl.pallas_call(
        partial(backward_kernel, num_z, length),
        out_shape=outs,
        in_specs=[VMEM_SPEC] * 4 + [HBM_SPEC] * 15,
        out_specs=[HBM_SPEC] + [VMEM_SPEC] * 6,
        scratch_shapes=scratch,
        compiler_params=pltpu.CompilerParams(collective_id=1, has_side_effects=True, vmem_limit_bytes=63 * 2**20),
        cost_estimate=pl.CostEstimate(flops=17 * 10**9, bytes_accessed=50 * 10**6, transcendentals=2 * 10**6),
    )(tokens, cot, twist, small_f, table, *full)


def publish(*arrays):
    def copy_all(*refs):
        for src, dst in zip(refs[: len(arrays)], refs[len(arrays) :]):
            dst[...] = src[...]

    return pl.pallas_call(
        copy_all,
        out_shape=[jax.ShapeDtypeStruct(a.shape, a.dtype) for a in arrays],
        in_specs=[VMEM_SPEC] * len(arrays),
        out_specs=[VMEM_SPEC] * len(arrays),
    )(*arrays)


def fits(num_dp, num_seq, tokens, w_in, w_out, w_up, w_down, kernel):
    if num_seq != 4 or num_dp % 4 or kernel.shape[0] * num_dp > 1024 or kernel.shape[0] * num_dp % 512:
        return False
    blocks = (w_in, w_out, w_up, w_down, kernel)
    return all(b.shape[0] % 32 == 0 and b.shape[1] * 2 % 128 == 0 for b in blocks) and tokens.shape[0] == 2


def body(num_dp, num_seq, tokens_in, w_in, w_out, w_up, w_down, norm_gains, kernel, taps, cotangent):
    if not fits(num_dp, num_seq, tokens_in, w_in, w_out, w_up, w_down, kernel):
        return general_body(tokens_in, w_in, w_out, w_up, w_down, norm_gains, kernel, taps, cotangent)
    width = tokens_in.shape[-1]
    length = kernel.shape[0] * num_dp
    num_z = num_dp // 2
    table, twist = jnp.asarray(transform_table(length)), jnp.asarray(twist_table(length))
    tokens, cot = tokens_in.reshape(-1, width), cotangent.reshape(-1, width)
    out, win, wout, wup, gdown, kern, small, *saved = forward(
        num_z, length, tokens, cot, w_in, w_out, w_up, w_down.T, kernel.T, norm_gains, taps[None], twist, table)
    results = backward(num_z, length, tokens, cot, twist, small, table, [win, wout, wup, gdown, kern, *saved])
    out, grad_in, gin, gout, gup, gdn, gains, gkern = publish(out, *results)
    return (out.reshape(tokens_in.shape), grad_in.reshape(tokens_in.shape), gin, gout, gup, gdn.T, gains, gkern.T)


def solution(mesh):
    return jax.shard_map(
        partial(body, mesh.shape["dp"], mesh.shape["seq"]),
        mesh=mesh,
        in_specs=(
            P("dp", "seq", None),
            P("dp", "seq"),
            P("dp", "seq"),
            P("dp", "seq"),
            P("dp", "seq"),
            P(None, "seq"),
            P("dp", "seq"),
            P("seq"),
            P("dp", "seq", None),
        ),
        out_specs=(
            P("dp", "seq", None),
            P("dp", "seq", None),
            P("dp", "seq"),
            P("dp", "seq"),
            P("dp", "seq"),
            P("dp", "seq"),
            P(None, "seq"),
            P("dp", "seq"),
        ),
        check_vma=False,
    )
```

```python
from functools import partial
import math

import jax
from jax.experimental import pallas as pl
from jax.experimental.pallas import tpu as pltpu
import ml_dtypes
import numpy as np
import jax.numpy as jnp
from jax import lax
from jax.sharding import PartitionSpec as P

EPSILON = 1e-05
SHRINK_SCALE = 0.003
HIGHEST = lax.Precision.HIGHEST


def norm_rows(values, gain):
    center = values - jnp.mean(values, axis=-1, keepdims=True)
    spread = jnp.mean(center * center, axis=-1, keepdims=True)
    return center * lax.rsqrt(spread + EPSILON) * gain


def shape_filter(kernel, taps):
    length = kernel.shape[0]
    position = jnp.arange(length, dtype=jnp.int32)[:, None]
    live_mask = (position < taps[None, :]).astype(kernel.dtype)
    masked = kernel * live_mask
    shrunk = masked - SHRINK_SCALE * jnp.tanh(masked / SHRINK_SCALE)
    padded = jnp.pad(shrunk, ((1, 1), (0, 0)))
    pooled = (padded[:-2] + padded[1:-1] + padded[2:]) / 3.0
    return pooled * live_mask


def gelu_tanh(values):
    return jax.nn.gelu(values, approximate=True)


def contract_rows(left, right):
    return lax.dot_general(
        left, right, (((0,), (0,)), ((), ())), preferred_element_type=jnp.float32
    )


def times_transposed(left, weight):
    return lax.dot_general(
        left, weight, (((1,), (1,)), ((), ())), preferred_element_type=jnp.float32
    )


def phase_table(count_rows, count_cols, period):
    row_index = lax.broadcasted_iota(jnp.int32, (count_rows, count_cols), 0)
    col_index = lax.broadcasted_iota(jnp.int32, (count_rows, count_cols), 1)
    angles = 2.0 * math.pi / period * (row_index * col_index % period).astype(jnp.float32)
    return (jnp.cos(angles), jnp.sin(angles))


def dft_factors(length):
    total = 2 * length
    first = max(2, total // 128)
    return (total, first, total // first)


def mix_last(field, table):
    return jnp.einsum("bckn,nm->bckm", field, table, precision=HIGHEST)


def forward_dft(field):
    batch, length, chans = field.shape
    total, first, second = dft_factors(length)
    half = first // 2
    blocks = field.reshape(batch, half, second, chans)
    cos_one, sin_one = phase_table(half, first, first)
    part_re = jnp.einsum("hk,bhnc->bckn", cos_one, blocks, precision=HIGHEST)
    part_im = -jnp.einsum("hk,bhnc->bckn", sin_one, blocks, precision=HIGHEST)
    cos_two, sin_two = phase_table(first, second, total)
    turn_re = part_re * cos_two + part_im * sin_two
    turn_im = part_im * cos_two - part_re * sin_two
    cos_three, sin_three = phase_table(second, second, second)
    spec_re = mix_last(turn_re, cos_three) + mix_last(turn_im, sin_three)
    spec_im = mix_last(turn_im, cos_three) - mix_last(turn_re, sin_three)
    return (spec_re, spec_im)


def inverse_dft(spec_re, spec_im):
    batch, chans, first, second = spec_re.shape
    total = first * second
    half = first // 2
    cos_three, sin_three = phase_table(second, second, second)
    back_re = mix_last(spec_re, cos_three) - mix_last(spec_im, sin_three)
    back_im = mix_last(spec_re, sin_three) + mix_last(spec_im, cos_three)
    cos_two, sin_two = phase_table(first, second, total)
    turn_re = back_re * cos_two - back_im * sin_two
    turn_im = back_re * sin_two + back_im * cos_two
    cos_one, sin_one = phase_table(half, first, first)
    blocks = jnp.einsum("hk,bckn->bhnc", cos_one, turn_re, precision=HIGHEST)
    blocks = blocks - jnp.einsum("hk,bckn->bhnc", sin_one, turn_im, precision=HIGHEST)
    return blocks.reshape(batch, half * second, chans) / total


def to_channels(field):
    return lax.all_to_all(field, "seq", split_axis=2, concat_axis=1, tiled=True)


def to_tokens(field):
    return lax.all_to_all(field, "seq", split_axis=1, concat_axis=2, tiled=True)


def general_body(tokens_in, w_in, w_out, w_up, w_down, norm_gains, kernel, taps, cotangent):
    w_in_rows, w_out_rows, w_up_rows, w_down_rows, gains = (
        lax.all_gather(w_in, "seq", axis=1, tiled=True),
        lax.all_gather(w_out, "seq", axis=1, tiled=True),
        lax.all_gather(w_up, "seq", axis=1, tiled=True),
        lax.all_gather(w_down, "seq", axis=1, tiled=True),
        lax.all_gather(norm_gains, "seq", axis=1, tiled=True),
    )
    full_in, full_out, full_up, full_down, kernel_cols = (
        lax.all_gather(w_in_rows, "dp", axis=0, tiled=True),
        lax.all_gather(w_out_rows, "dp", axis=0, tiled=True),
        lax.all_gather(w_up_rows, "dp", axis=0, tiled=True),
        lax.all_gather(w_down_rows, "dp", axis=0, tiled=True),
        lax.all_gather(kernel, "dp", axis=0, tiled=True),
    )
    num_seqs, local_len, width = tokens_in.shape
    total_rows = num_seqs * local_len
    inputs = tokens_in.reshape(total_rows, width).astype(jnp.float32)
    gains_wide = gains.astype(jnp.float32)
    normed, norm_back_one = jax.vjp(norm_rows, inputs, gains_wide[0])
    normed_low = normed.astype(jnp.bfloat16)
    proj = jnp.dot(normed_low, full_in, preferred_element_type=jnp.float32)
    values = proj[:, :width]
    gate_one = proj[:, width : 2 * width]
    gate_two = proj[:, 2 * width :]
    mixed_low = (gate_one * values).astype(jnp.bfloat16).reshape(num_seqs, local_len, width)
    by_channel = to_channels(mixed_low)
    filt, filter_back = jax.vjp(partial(shape_filter, taps=taps), kernel_cols.astype(jnp.float32))
    filt_re, filt_im = forward_dft(filt[None])
    sig_re, sig_im = forward_dft(by_channel.astype(jnp.float32))
    conv = inverse_dft(sig_re * filt_re - sig_im * filt_im, sig_re * filt_im + sig_im * filt_re)
    conv_tok = to_tokens(conv.astype(jnp.bfloat16)).reshape(total_rows, width).astype(jnp.float32)
    gated = (gate_two * conv_tok).astype(jnp.bfloat16)
    resid = inputs + jnp.dot(gated, full_out, preferred_element_type=jnp.float32)
    normed_two, norm_back_two = jax.vjp(norm_rows, resid, gains_wide[1])
    normed_two_low = normed_two.astype(jnp.bfloat16)
    hidden_pre = jnp.dot(normed_two_low, full_up, preferred_element_type=jnp.float32)
    active, gelu_back = jax.vjp(gelu_tanh, hidden_pre)
    active_low = active.astype(jnp.bfloat16)
    result = (resid + jnp.dot(active_low, full_down, preferred_element_type=jnp.float32)).astype(
        jnp.bfloat16
    )
    grad_rows = cotangent.reshape(total_rows, width)
    grad_down = contract_rows(active_low, grad_rows)
    grad_active = times_transposed(grad_rows, full_down)
    grad_pre = gelu_back(grad_active)[0].astype(jnp.bfloat16)
    grad_up = contract_rows(normed_two_low, grad_pre)
    grad_normed_two = times_transposed(grad_pre, full_up)
    grad_resid_part, grad_gain_two = norm_back_two(grad_normed_two)
    grad_resid = grad_rows.astype(jnp.float32) + grad_resid_part
    resid_low = grad_resid.astype(jnp.bfloat16)
    grad_outw = contract_rows(gated, resid_low)
    grad_gated = times_transposed(resid_low, full_out)
    grad_gate_two = grad_gated * conv_tok
    grad_conv = (grad_gated * gate_two).astype(jnp.bfloat16).reshape(num_seqs, local_len, width)
    grad_channel = to_channels(grad_conv).astype(jnp.float32)
    back_re, back_im = forward_dft(grad_channel)
    grad_signal = inverse_dft(
        back_re * filt_re + back_im * filt_im, back_im * filt_re - back_re * filt_im
    )
    cross_re = jnp.sum(back_re * sig_re + back_im * sig_im, axis=0, keepdims=True)
    cross_im = jnp.sum(back_im * sig_re - back_re * sig_im, axis=0, keepdims=True)
    grad_filt = inverse_dft(cross_re, cross_im)[0]
    grad_kern = filter_back(grad_filt)[0]
    grad_mixed = (
        to_tokens(grad_signal.astype(jnp.bfloat16)).reshape(total_rows, width).astype(jnp.float32)
    )
    grad_proj = jnp.concatenate([grad_mixed * gate_one, grad_mixed * values, grad_gate_two], axis=1)
    grad_proj = grad_proj.astype(jnp.bfloat16)
    grad_inw = contract_rows(normed_low, grad_proj)
    grad_normed = times_transposed(grad_proj, full_in)
    grad_input_part, grad_gain_one = norm_back_one(grad_normed)
    grad_inputs = (
        (grad_resid + grad_input_part).astype(jnp.bfloat16).reshape(num_seqs, local_len, width)
    )
    grad_gain_pair = jnp.stack([grad_gain_one, grad_gain_two])
    in_part, outw_part, up_part, down_part, kern_done = (
        lax.psum_scatter(
            grad_inw.astype(jnp.bfloat16), "dp", scatter_dimension=0, tiled=True
        ).astype(jnp.float32),
        lax.psum_scatter(
            grad_outw.astype(jnp.bfloat16), "dp", scatter_dimension=0, tiled=True
        ).astype(jnp.float32),
        lax.psum_scatter(
            grad_up.astype(jnp.bfloat16), "dp", scatter_dimension=0, tiled=True
        ).astype(jnp.float32),
        lax.psum_scatter(
            grad_down.astype(jnp.bfloat16), "dp", scatter_dimension=0, tiled=True
        ).astype(jnp.float32),
        lax.psum_scatter(
            grad_kern.astype(jnp.bfloat16), "dp", scatter_dimension=0, tiled=True
        ).astype(jnp.float32),
    )
    in_done, outw_done, up_done, down_done, gain_part = (
        lax.psum_scatter(
            in_part.astype(jnp.bfloat16), "seq", scatter_dimension=1, tiled=True
        ).astype(jnp.float32),
        lax.psum_scatter(
            outw_part.astype(jnp.bfloat16), "seq", scatter_dimension=1, tiled=True
        ).astype(jnp.float32),
        lax.psum_scatter(
            up_part.astype(jnp.bfloat16), "seq", scatter_dimension=1, tiled=True
        ).astype(jnp.float32),
        lax.psum_scatter(
            down_part.astype(jnp.bfloat16), "seq", scatter_dimension=1, tiled=True
        ).astype(jnp.float32),
        lax.psum_scatter(
            grad_gain_pair.astype(jnp.bfloat16), "seq", scatter_dimension=1, tiled=True
        ).astype(jnp.float32),
    )
    gain_done = lax.psum(gain_part, "dp")
    return (
        result.reshape(num_seqs, local_len, width),
        grad_inputs,
        in_done,
        outw_done,
        up_done,
        down_done,
        gain_done,
        kern_done,
    )


MESH = pl.DeviceIdType.MESH
BF = jnp.bfloat16
F32 = jnp.float32


class Remote:
    def __init__(self, wire, slot, src, dst, peer):
        self.wire, self.slot, self.src, self.dst, self.peer = wire, slot, src, dst, peer

    def named(self):
        return pltpu.make_async_remote_copy(
            src_ref=self.src(), dst_ref=self.dst(), send_sem=self.wire.send.at[self.slot],
            recv_sem=self.wire.recv.at[self.slot], device_id=self.peer, device_id_type=MESH,
        )

    def wait_recv(self):
        self.named().wait_recv()


class Wire:
    def __init__(self, send, recv, spots):
        self.send, self.recv, self.s, self.made = send, recv, spots, []

    def start(self, src, dst, peer, core=None):
        src, dst = (end if callable(end) else partial(lambda ref: ref, end) for end in (src, dst))
        copy = Remote(self, len(self.made), src, dst, peer)
        copy.named().start()
        self.made.append((core, copy))
        return copy

    def drain(self):
        for which in (None, 0, 1):
            @self.s.on(which)
            def _():
                for core, copy in self.made:
                    if core == which:
                        copy.named().wait_send()


class Local:
    def __init__(self, sems):
        self.sems, self.made, self.open = sems, 0, []

    def start(self, src, dst):
        copy = pltpu.make_async_copy(src, dst, self.sems.at[self.made])
        self.made += 1
        copy.start()
        self.open.append(copy)
        return copy

    def wait(self, copy):
        copy.wait()
        self.open = [other for other in self.open if other is not copy]

    def drain(self):
        for copy in list(self.open):
            self.wait(copy)


def arrived(copies):
    for copy in copies:
        copy.wait_recv()


class Spots:
    def __init__(self, num_z):
        dp, sq = lax.axis_index("dp"), lax.axis_index("seq")
        z, x, y, c = dp // 2, dp % 2, sq // 2, sq % 2
        self.num_z = num_z
        self.z, self.x, self.y, self.c = z, x, y, c
        self.own = dict(x=x, y=y, z=z)
        self.size = dict(x=2, y=2, z=num_z)
        self.core = self.at(z, x, y, 1 - c)
        self.others = dict(x=[1 - x], y=[1 - y], z=[(z + k) % num_z for k in range(1, num_z)])
        self.along = dict(
            x=[self.at(z, 1 - x, y, c)], y=[self.at(z, x, 1 - y, c)],
            z=[self.at(other, x, y, c) for other in self.others["z"]],
        )
        self.group = [((y + i) % 2, (c + j) % 2) for i, j in ((1, 0), (1, 1), (0, 1))]
        self.mates = [self.at(z, x, yy, cc) for yy, cc in self.group]

    def at(self, z, x, y, c):
        return (z * 2 + x, y * 2 + c)

    def on(self, core):
        return (lambda body: body()) if core is None else pl.when(self.c == core)

    def meet(self):
        barrier = pltpu.get_barrier_semaphore()
        peers = self.along["z"] + self.along["x"] + self.mates
        for peer in peers:
            pl.semaphore_signal(barrier, inc=1, device_id=peer, device_id_type=MESH)
        pl.semaphore_wait(barrier, len(peers))


def both_cores(orders):
    return [(None, orders[0])] if len(orders) == 1 else list(enumerate(orders))


def block_index(s, axes, wide, core, at=None):
    place = {**s.own, **(at or {})}
    index = tuple(slice(None) if axis in wide else place[axis] for axis in axes)
    return index if core is None else index + (core,)


class Gather:
    def __init__(self, wire, spots, full, axes, *orders, part=()):
        self.wire, self.s, self.full, self.axes, self.part = wire, spots, full, axes, part
        self.orders, self.last = both_cores(orders), {}

    def view(self, have):
        return self.full.at[block_index(self.s, self.axes, have, self.s.c) + self.part]

    def settle(self):
        for core, copies in self.last.items():
            self.s.on(core)(partial(arrived, copies))
        self.last = {}

    def step(self, n):
        s = self.s
        if n == len(self.orders[0][1]):
            self.settle()
            view = partial(self.view, self.axes)
            self.last[None] = [self.wire.start(view, view, s.core)]
            return
        before, self.last = self.last, {}
        for core, order in self.orders:
            @s.on(core)
            def _():
                arrived(before.get(core, []))
                view = partial(self.view, order[:n])
                self.last[core] = [self.wire.start(view, view, peer, core) for peer in s.along[order[n]]]

    def done(self):
        self.settle()


class Rounds:
    LAG = 2

    def __init__(self, gathers):
        self.gathers, self.now = gathers, 0

    def run(self, count=1):
        for _ in range(count):
            for step in reversed(range(4)):
                k = self.now - step * self.LAG
                if 0 <= k < len(self.gathers) and step <= len(self.gathers[k].orders[0][1]):
                    self.gathers[k].step(step)
            self.now += 1


class Scatter:
    def __init__(self, wire, spots, total, axes, orders, from_core, got, result, away=None, part=()):
        self.wire, self.s, self.total, self.axes, self.part = wire, spots, total, axes, part
        self.orders = [(core, order[::-1]) for core, order in both_cores(orders)]
        self.from_core, self.got, self.result, self.away = from_core, got, result, away
        self.last = {}

    def mine(self, wide, at=None):
        core = None if self.away is not None else self.s.c
        return self.total.at[block_index(self.s, self.axes, wide, core, at) + self.part]

    def send_core(self):
        s = self.s
        source = self.total if self.away is None else self.away
        whole = (slice(None),) * (len(self.axes) - 1)
        self.last = [
            self.wire.start(source.at[(i,) + whole + (1 - s.c,) + self.part],
                            self.from_core.at[(i,) + whole + self.part], s.core)
            for i in range(self.from_core.shape[0])
        ]

    def add_core(self):
        arrived(self.last)
        self.last = {}
        s = self.s
        count = math.prod(s.size[axis] for axis in self.axes)

        def one(i, _):
            at, left = {}, i
            for axis in reversed(self.axes):
                at[axis], left = left % s.size[axis], left // s.size[axis]
            into = self.mine("", at)
            term = self.from_core[tuple(at[axis] for axis in self.axes) + self.part]
            into[...] = (into[...].astype(F32) + term.astype(F32)).astype(BF)
            return 0
        lax.fori_loop(0, count, one, 0)

    def stages(self, order, n):
        s = self.s
        begin = 0
        for k in range(n + 1):
            wide = sorted(order[k + 1 :])
            count = math.prod(s.size[axis] for axis in wide)
            if k < n:
                begin += count * (s.size[order[k]] - 1)
        return order[n], wide, count, begin

    def slots(self, start, count):
        return self.got.at[(start if count is None else slice(start, start + count),) + self.part]

    def send(self, n):
        s = self.s
        for core, order in self.orders:
            axis, wide, count, begin = self.stages(order, n)

            @s.on(core)
            def _():
                self.last[core] = []
                for j, (other, peer) in enumerate(zip(s.others[axis], s.along[axis])):
                    outer = s.size[wide[0]] if len(wide) == 2 else 1
                    inner = count // outer
                    for i in range(outer):
                        at = {axis: other}
                        if len(wide) == 2:
                            at[wide[0]] = i
                        start = begin + j * count + i * inner
                        src = partial(self.mine, wide[-1:], at)
                        dst = partial(self.slots, start, inner if wide else None)
                        self.last[core].append(self.wire.start(src, dst, peer, core))

    def add(self, n):
        s = self.s
        for core, order in self.orders:
            axis, wide, count, begin = self.stages(order, n)
            peers = len(s.others[axis])

            @s.on(core)
            def _():
                arrived(self.last[core])
                if n == len(order) - 1:
                    total = self.mine("")[...].astype(F32)
                    for j in range(peers):
                        total = total + self.got[(begin + j,) + self.part].astype(F32)
                    self.result[self.part or ...] = total
                    return

                def one(i, _):
                    at, left = {}, i
                    for a in reversed(wide):
                        at[a], left = left % s.size[a], left // s.size[a]
                    into = self.mine("", at)
                    total = into[...].astype(F32)
                    for j in range(peers):
                        total = total + self.got[(begin + j * count + i,) + self.part].astype(F32)
                    into[...] = total.astype(BF)
                    return 0
                lax.fori_loop(0, count, one, 0)


    def go(self, n):
        if n == 0:
            self.add_core()
        else:
            self.add(n - 1)
        if n < len(self.orders[0][1]):
            self.send(n)


class Trade:
    def __init__(self, wire, spots, result, ends):
        self.s, self.ends = spots, ends
        width = ends.shape[-1]
        for core in range(2):
            ends[core] = result[:, core * width : (core + 1) * width]
        self.copy = wire.start(ends.at[1 - spots.c], ends.at[2], spots.core)

    def finish(self, out, turned=False):
        self.copy.wait_recv()
        c, own, other = self.s.c, self.ends[self.s.c], self.ends[2]
        both = jnp.concatenate([jnp.where(c == 0, own, other), jnp.where(c == 0, other, own)], axis=0)
        out[...] = both.T if turned else both


def row_parts(rows):
    size = rows // PARTS
    return [(slice(i * size, (i + 1) * size),) for i in range(PARTS)]


def norm_parts(values):
    center = values - jnp.mean(values, axis=-1, keepdims=True)
    spread = jnp.mean(center * center, axis=-1, keepdims=True)
    scale = lax.rsqrt(spread + EPSILON)
    return center * scale, scale


def norm_back(normal, scale, grad, gain):
    p = grad * gain
    flat = jnp.mean(p, axis=-1, keepdims=True)
    along = jnp.mean(p * normal, axis=-1, keepdims=True)
    return (p - flat - normal * along) * scale, jnp.sum(grad * normal, axis=0, keepdims=True)


def dot(left, right):
    return jnp.dot(left, right, preferred_element_type=F32)


def dot_rows(left, right):
    return lax.dot_general(left, right, (((0,), (0,)), ((), ())), preferred_element_type=F32)


def dot_cols(left, right):
    return lax.dot_general(left, right, (((1,), (1,)), ((), ())), preferred_element_type=F32)


def live_taps(kern, taps):
    position = lax.broadcasted_iota(jnp.int32, kern.shape, 0)
    return position, position.astype(F32) < taps


def pool(values, position):
    length = values.shape[0]
    before = jnp.where(position == 0, 0.0, pltpu.roll(values, 1, 0))
    after = jnp.where(position == length - 1, 0.0, pltpu.roll(values, length - 1, 0))
    return (before + values + after) / 3.0


def make_filter(kern, taps):
    position, live = live_taps(kern, taps)
    masked = jnp.where(live, kern, 0.0)
    shrunk = masked - SHRINK_SCALE * jnp.tanh(masked / SHRINK_SCALE)
    return jnp.where(live, pool(shrunk, position), 0.0)


def kernel_back(kern, taps, grad):
    position, live = live_taps(kern, taps)
    slope = jnp.tanh(jnp.where(live, kern, 0.0) / SHRINK_SCALE)
    return jnp.where(live, pool(jnp.where(live, grad, 0.0), position) * slope * slope, 0.0)


GELU_K = math.sqrt(2.0 / math.pi)


def gelu_both(v):
    square = v * v
    t = jnp.tanh(GELU_K * v * (1.0 + 0.044715 * square))
    half = 0.5 * (1.0 + t)
    slope = half + 0.5 * v * (1.0 - t * t) * (GELU_K * (1.0 + 3 * 0.044715 * square))
    return v * half, slope


def spans(start, size, step=16):
    return pl.ds(pl.multiple_of(start, step), size)


def transform_table(length):
    k = 2 * np.arange(length)[:, None] + 1
    angle = np.pi / (4 * length) * ((k * k.T) % (8 * length))
    return np.concatenate([np.cos(angle), np.sin(angle)]).astype(np.float32).astype(ml_dtypes.bfloat16)


def twist_table(length):
    angle = np.pi / (4 * length) * (2 * np.arange(length) + 1)
    return np.stack([np.cos(angle), np.sin(angle)], axis=1).astype(np.float32)


ORDER_OUT = ("zxy", "zyx")
ORDER_UP = ("zxy", "zyx")
ORDER_DOWN = ("zxy", "yzx")
PARTS = 3
STEP = 256


def forward_kernel(
    num_z, length,
    tok, cot, w_in, w_out, w_up, w_down_t, kern_t, gains_in, taps_in, twist, table_hbm,
    out_o, win_o, wout_o, wup_o, gdown_o, kern_o, small_o, proj_o, normed_o, spec_o, filt_o, conv_o,
    gated_o, resid_o, normed_two_o, gpre_o,
    win_v, wout_v, wup_v, wdown_v, kern_v, small_v,
    pre_in, pre_out, pre_up, pre_down, pre_kern, w_down, kern,
    table_v, proj_v, normed_own, normed_v, sig_v, spec_v, filt_v, filt_low, turned_v, conv_v, gated_ch,
    gated_v, resid_v, normed_two_v, act_v, slope_v, gdown_v, out_v,
    send, recv, local,
):
    s = Spots(num_z)
    z, x, y, c = s.z, s.x, s.y, s.c
    wire, inner = Wire(send, recv, s), Local(local)
    load_table = inner.start(table_hbm, table_v)
    rows, width = tok.shape
    group, span = width // 2, rows // 2
    hidden = act_v.shape[1]
    me = 2 * y + c
    w_down[...] = w_down_t[...].T
    kern[...] = kern_t[...].T
    small_v[me, 0:2] = gains_in[...].astype(F32)
    small_v[me, 2:3] = taps_in[...].astype(F32)
    s.meet()

    half = w_in.shape[0] // 2
    trade_in = [
        wire.start(w_in.at[spans(cc * half, half)], pre_in.at[me], peer) for (yy, cc), peer in zip(s.group, s.mates)
    ]
    smalls = [wire.start(small_v.at[me], small_v.at[me], peer) for peer in s.mates]
    pairs = [(kern, pre_kern), (w_out, pre_out), (w_up, pre_up), (w_down, pre_down)]
    traded = []
    for src, pre in pairs:
        half = src.shape[0] // 2
        traded.append(wire.start(src.at[spans((1 - c) * half, half)], pre.at[c], s.core))
    half = w_in.shape[0] // 2
    pre_in[me] = w_in[spans(c * half, half)]
    for src, pre in pairs:
        half = src.shape[0] // 2
        pre[c] = src[spans(c * half, half)]

    g_in = [Gather(wire, s, win_v, "zx", "zx", part=(k,)) for k in range(3)]
    g_kern = Gather(wire, s, kern_v, "zx", "zx")
    g_out = Gather(wire, s, wout_v, "yzx", *ORDER_OUT)
    g_up = [Gather(wire, s, wup_v, "yzx", *ORDER_UP, part=part) for part in row_parts(wup_v.shape[-2])]
    g_down = [Gather(wire, s, wdown_v, "yzx", *ORDER_DOWN, part=part) for part in row_parts(wdown_v.shape[-2])]

    rounds = Rounds([*g_in, g_kern, g_out, *g_up, *g_down])

    def join(i, full):
        traded[i].wait_recv()
        pre = pairs[i][1]
        full[block_index(s, "zx" if i == 0 else "yzx", "", c)] = jnp.concatenate([pre[0], pre[1]], axis=-1)

    arrived(trade_in)
    whole = jnp.concatenate([pre_in[k] for k in range(4)], axis=-1)
    for k in range(3):
        left, right = (whole[:, (2 * k + h) * group : (2 * k + h + 1) * group] for h in range(2))
        win_v[z, x, c, k] = jnp.where(y == 0, left, right)
        if k < 2:
            rounds.run()

    arrived(smalls)
    gains = jnp.concatenate([small_v[k] for k in range(4)], axis=-1)
    normed, _ = norm_parts(tok[...].astype(F32))
    normed_own[...] = (normed * gains[0:1]).astype(BF)
    chunk = spans(me * span, span)
    to_group = [
        wire.start(normed_own.at[spans(cc * span, span)], normed_v.at[chunk], peer)
        for (yy, cc), peer in zip(s.group, s.mates)
    ]
    normed_v[chunk] = normed_own[spans(c * span, span)]
    join(0, kern_v)
    join(1, wout_v)
    join(2, wup_v)
    join(3, wdown_v)
    rounds.run(5)


    arrived(to_group)
    g_in[0].done()
    g_in[1].done()

    def project(k, at):
        return dot(normed_v[at], win_v[:, :, :, k].reshape(width, group))

    tall = length // 2
    for i in range(2):
        at = slice(i * tall, (i + 1) * tall)
        value, gate = project(0, at), project(1, at)
        proj_v[0, at] = value.astype(BF)
        proj_v[1, at] = gate.astype(BF)
        sig_v[at] = (value * gate).astype(BF)
    g_in[2].done()
    rounds.run()
    for i in range(2):
        at = slice(i * tall, (i + 1) * tall)
        proj_v[2, at] = project(2, at).astype(BF)
    rounds.run()

    g_kern.done()
    taps = jnp.concatenate([small_v[2 * y], small_v[2 * y + 1]], axis=-1)[2:3]
    tile = 128
    for j in range(group // tile):
        cols = slice(j * tile, (j + 1) * tile)
        filt = make_filter(kern_v[:, :, :, :, cols].reshape(length, tile).astype(F32), taps[:, cols])
        filt_low[:, cols] = filt.astype(BF)
    inner.wait(load_table)

    def spectrum(i, _):
        real, imag = spans(i * STEP, STEP, STEP), spans(length + i * STEP, STEP, STEP)
        re, im = dot(table_v[real], filt_low[...]), dot(table_v[imag], filt_low[...])
        cosine, sine = twist[real, 0:1], twist[real, 1:2]
        filt_v[real] = (re * cosine + im * sine).astype(BF)
        filt_v[imag] = (im * cosine - re * sine).astype(BF)
        return 0
    lax.fori_loop(0, length // STEP, spectrum, 0)


    rounds.run()

    def convolve(i, _):
        real, imag = spans(i * STEP, STEP, STEP), spans(length + i * STEP, STEP, STEP)
        re_s, im_s = dot(table_v[real], sig_v[...]), dot(table_v[imag], sig_v[...])
        spec_v[real] = re_s.astype(BF)
        spec_v[imag] = im_s.astype(BF)
        re_f, im_f = filt_v[real].astype(F32), filt_v[imag].astype(F32)
        turned_v[real] = (re_s * re_f - im_s * im_f).astype(BF)
        turned_v[imag] = (re_s * im_f + im_s * re_f).astype(BF)
        return 0
    lax.fori_loop(0, length // STEP, convolve, 0)

    rounds.run()

    def back(i, _):
        at, imag = spans(i * STEP, STEP, STEP), spans(length + i * STEP, STEP, STEP)
        both = dot(table_v[at], turned_v[0:length]) + dot(table_v[imag], turned_v[length:])
        conv = (both * (1.0 / length)).astype(BF)
        conv_v[at] = conv
        gated_ch[at] = (proj_v[2, at].astype(F32) * conv.astype(F32)).astype(BF)
        return 0
    lax.fori_loop(0, length // STEP, back, 0)

    home = spans(c * span, span)
    to_tokens = [
        wire.start(gated_ch.at[spans((2 * yy + cc) * span, span)], gated_v.at[y, home], peer)
        for (yy, cc), peer in zip(s.group, s.mates)
    ]
    gated_v[y, home] = gated_ch[chunk]
    for src, dst in ((win_v, win_o), (kern_v, kern_o), (small_v, small_o), (proj_v, proj_o),
                     (normed_v, normed_o), (spec_v, spec_o), (filt_v, filt_o), (conv_v, conv_o)):
        inner.start(src, dst)
    rounds.run()
    g_out.done()
    rounds.run()
    arrived(to_tokens)

    for k in range(2):
        cols = slice(k * group, (k + 1) * group)
        mixed = sum(
            dot(gated_v[h], wout_v[k, h * num_z // 2 : (h + 1) * num_z // 2].reshape(group, group)) for h in range(2)
        )
        resid_v[:, cols] = tok[:, cols].astype(F32) + mixed
    normed_two, _ = norm_parts(resid_v[...])
    normed_two_v[...] = (normed_two * gains[1:2]).astype(BF)
    for src, dst in ((wout_v, wout_o), (gated_v, gated_o), (resid_v, resid_o), (normed_two_v, normed_two_o)):
        inner.start(src, dst)
    rounds.run(2)
    for g in g_up:
        g.done()

    wide = 256
    per = hidden // 2 // wide

    def feed(j, _):
        weight = wup_v[j // per, :, :, :, :, spans((j % per) * wide, wide, wide)].reshape(width, wide)
        act, slope = gelu_both(dot(normed_two_v[...], weight))
        at = spans(j * wide, wide, wide)
        act_v[:, at] = act.astype(BF)
        slope_v[:, at] = slope.astype(BF)
        return 0
    lax.fori_loop(0, per, feed, 0)
    rounds.run()
    lax.fori_loop(per, 2 * per, feed, 0)
    inner.start(wup_v, wup_o)

    rounds.run()

    deep = hidden // (2 * num_z)

    def down_grad(i, _):
        grad = dot_rows(act_v[:, spans(i * deep, deep, deep)], cot[...]).astype(BF)
        for h in range(2):
            gdown_v[h, i // 2, i % 2] = grad[:, h * group : (h + 1) * group].reshape(2, deep // 2, group)
        return 0
    lax.fori_loop(0, 2 * num_z, down_grad, 0)
    inner.start(gdown_v, gdown_o)
    rounds.run()
    for g in g_down:
        g.done()

    def pre_grad(i, _):
        at = spans(i * deep, deep, deep)
        grad = sum(
            dot_cols(cot[:, h * group : (h + 1) * group], wdown_v[h, i // 2, i % 2].reshape(deep, group))
            for h in range(2)
        )
        slope_v[:, at] = (slope_v[:, at].astype(F32) * grad).astype(BF)
        return 0
    lax.fori_loop(0, 2 * num_z, pre_grad, 0)
    inner.start(slope_v, gpre_o)
    for h in range(2):
        cols = slice(h * group, (h + 1) * group)
        out_v[:, cols] = (resid_v[:, cols] + dot(act_v[...], wdown_v[h].reshape(hidden, group))).astype(BF)
    inner.start(out_v, out_o)
    wire.drain()
    inner.drain()


def vm(shape, dtype=BF):
    return pltpu.VMEM(tuple(shape), dtype)


VMEM_SPEC, HBM_SPEC = pl.BlockSpec(memory_space=pltpu.VMEM), pl.BlockSpec(memory_space=pl.ANY)


def forward(num_z, length, tokens, cot, w_in, w_out, w_up, w_down_t, kernel_t, gains, taps, twist, table):
    rows, width = tokens.shape
    group = width // 2
    part = w_down_t.shape[1]
    hidden = part * num_z * 2
    sds = jax.ShapeDtypeStruct
    axes = (2, num_z, 2, 2)
    win = axes[1:] + (3, w_in.shape[0] // 2, group)
    wout, wup, wdown = axes + (w_out.shape[0] // 2, group), axes + (w_up.shape[0] // 2, hidden // 2), axes + (part // 2, group)
    kern = axes[1:] + (kernel_t.shape[1] // 2, group)
    small = (4, 8, width // 4)
    acts = dict(
        proj=((3, length, group), BF), normed=((length, width), BF), spec=((2 * length, group), BF),
        filt=((2 * length, group), BF), conv=((length, group), BF), gated=((2, rows, group), BF),
        resid=((rows, width), F32), normed_two=((rows, width), BF), gpre=((rows, hidden), BF),
    )
    outs = [sds((rows, width), BF)] + [sds(w, BF) for w in (win, wout, wup, wdown, kern)] + [sds(small, F32)]
    outs += [sds(*acts[k]) for k in acts]
    act = lambda k: vm(*acts[k])
    scratch = [vm(w) for w in (win, wout, wup, wdown, kern)] + [vm(small, F32)]
    scratch += [vm((4, w_in.shape[0] // 2, w_in.shape[1])), vm((2, w_out.shape[0] // 2, w_out.shape[1])),
                vm((2, w_up.shape[0] // 2, w_up.shape[1])), vm((2, part // 2, w_down_t.shape[0])),
                vm((2, kernel_t.shape[1] // 2, kernel_t.shape[0])), vm(w_down_t.shape[::-1]), vm(kernel_t.shape[::-1])]
    scratch += [vm(table.shape), act("proj"), vm((rows, width)), act("normed"), vm((length, group)), act("spec"),
                act("filt"), vm((length, group)), vm((2 * length, group)), act("conv"), vm((length, group)),
                act("gated"), act("resid"), act("normed_two"), act("gpre"), act("gpre"), vm(wdown), vm((rows, width))]
    scratch += [pltpu.SemaphoreType.DMA((160,)), pltpu.SemaphoreType.DMA((160,)), pltpu.SemaphoreType.DMA((40,))]
    return pl.pallas_call(
        partial(forward_kernel, num_z, length),
        out_shape=outs,
        in_specs=[VMEM_SPEC] * 10 + [HBM_SPEC],
        out_specs=[HBM_SPEC] * len(outs),
        scratch_shapes=scratch,
        compiler_params=pltpu.CompilerParams(collective_id=0, has_side_effects=True, vmem_limit_bytes=61 * 2**20),
        cost_estimate=pl.CostEstimate(flops=17 * 10**9, bytes_accessed=50 * 10**6, transcendentals=2 * 10**6),
    )(tokens, cot, w_in, w_out, w_up, w_down_t, kernel_t, gains, taps, twist, table)


def backward_kernel(
    num_z, length,
    tok, cot, twist, small_v, table_h, win_h, wout_h, wup_h, gdown_h, kern_h, proj_h, normed_h, spec_h,
    filt_h, conv_h, gated_h, resid_h, normed_two_h, gpre_h,
    grad_in_o, gin_o, gout_o, gup_o, gdn_o, gains_o, gkern_o,
    table_v, win_v, wout_v, wup_v, kern_v, proj_v, normed_v, spec_v, filt_v, conv_v,
    gated_v, resid_v, normed_two_v, gpre_v,
    gup_v, gdn_v, gkern_v,
    core_in, core_out, core_up, core_dn, core_kern,
    got_in, got_out, got_up, got_dn, got_kern,
    sum_in, sum_out, sum_up, sum_dn, sum_kern,
    ends_out, ends_up, ends_dn, ends_kern, swap_core, swap_y,
    low_v, ggate_v, gch_v, gnorm_got, gain_v, gain_got,
    send, recv, local,
):
    s = Spots(num_z)
    z, x, y, c = s.z, s.x, s.y, s.c
    wire, inner = Wire(send, recv, s), Local(local)
    rows, width = tok.shape
    group, span = width // 2, rows // 2
    hidden = gpre_v.shape[1]
    me = 2 * y + c
    own_dn = [inner.start(gdown_h.at[i, :, :, c], gdn_v.at[i]) for i in range(2)]
    loads = {}
    for name, src, dst in (
        ("gpre", gpre_h, gpre_v), ("wup", wup_h, wup_v), ("normed_two", normed_two_h, normed_two_v),
        ("resid", resid_h, resid_v), ("wout", wout_h, wout_v), ("proj", proj_h, proj_v), ("conv", conv_h, conv_v),
        ("gated", gated_h, gated_v), ("table", table_h, table_v), ("spec", spec_h, spec_v), ("filt", filt_h, filt_v),
        ("kern", kern_h, kern_v), ("normed", normed_h, normed_v), ("win", win_h, win_v),
    ):
        loads[name] = inner.start(src, dst)

    def need(*names):
        for name in names:
            inner.wait(loads[name])

    s.meet()
    block = width // (4 * num_z)
    gout_v = wup_v.at[:, :, :, :, :, 0:group]
    gin_v = win_v
    down = [Scatter(wire, s, gdn_v, "yzx", ORDER_DOWN, core_dn, got_dn, sum_dn, away=gdown_h, part=part)
            for part in row_parts(gdn_v.shape[-2])]
    up = [Scatter(wire, s, gup_v, "yzx", ORDER_UP, core_up, got_up, sum_up, part=part)
          for part in row_parts(gup_v.shape[-2])]
    out = Scatter(wire, s, gout_v, "yzx", ORDER_OUT, core_out, got_out, sum_out)
    into = [Scatter(wire, s, gin_v, "zx", ("zx",), core_in, got_in, sum_in, part=(k,)) for k in range(3)]
    taps_grad = Scatter(wire, s, gkern_v, "zx", ("zx",), core_kern, got_kern, sum_kern)
    for k in range(3):
        down[k].send_core()
    gains = jnp.concatenate([small_v[k] for k in range(4)], axis=-1)

    need("gpre", "wup", "resid")
    half = hidden // 2
    grad = sum(
        dot_cols(gpre_v[:, h * half : (h + 1) * half], wup_v[h].reshape(width, half)) for h in range(2)
    )
    normal, scale = norm_parts(resid_v[...])
    part, gain_two = norm_back(normal, scale, grad, gains[1:2])
    resid_v[...] = cot[...].astype(F32) + part
    low_v[...] = resid_v[...].astype(BF)

    for copy in own_dn:
        inner.wait(copy)
    down[0].go(0)
    down[1].go(0)

    need("wout")
    for h in range(2):
        grad = sum(
            dot_cols(
                low_v[:, k * group : (k + 1) * group],
                wout_v[k, h * num_z // 2 : (h + 1) * num_z // 2].reshape(group, group),
            )
            for k in range(2)
        )
        ggate_v[h] = grad.astype(BF)
    chunk, home = spans(me * span, span), spans(c * span, span)
    to_channels = [
        wire.start(ggate_v.at[yy, spans(cc * span, span)], gch_v.at[chunk], peer)
        for (yy, cc), peer in zip(s.group, s.mates)
    ]
    gch_v[chunk] = ggate_v[y, home]

    down[2].go(0)

    need("normed_two")
    wide = 256
    per = hidden // 2 // wide

    def up_grad(j, _):
        grad = dot_rows(normed_two_v[...], gpre_v[:, spans(j * wide, wide, wide)]).astype(BF)
        cols = spans((j % per) * wide, wide, wide)
        gup_v[j // per, :, :, :, :, cols] = grad.reshape(num_z, 2, 2, block, wide)
        return 0
    lax.fori_loop(0, 2 * per, up_grad, 0)
    for k in range(3):
        up[k].send_core()
    down[0].go(1)
    down[1].go(1)
    up[0].go(0)

    need("gated")
    for h in range(2):
        for k in range(2):
            grad = dot_rows(gated_v[h], low_v[:, k * group : (k + 1) * group]).astype(BF)
            gout_v[k, h * num_z // 2 : (h + 1) * num_z // 2] = grad.reshape(num_z // 2, 2, 2, block, group)
    out.send_core()
    down[2].go(1)
    down[0].go(2)
    up[1].go(0)

    need("proj", "conv", "table", "spec", "filt")
    arrived(to_channels)

    def gate(i, _):
        at = spans(i * STEP, STEP, STEP)
        grad = gch_v[at].astype(F32)
        gch_v[at] = (grad * proj_v[2, at].astype(F32)).astype(BF)
        proj_v[2, at] = (grad * conv_v[at].astype(F32)).astype(BF)
        return 0
    lax.fori_loop(0, length // STEP, gate, 0)

    def turn(i, _):
        real, imag = spans(i * STEP, STEP, STEP), spans(length + i * STEP, STEP, STEP)
        re, im = dot(table_v[real], gch_v[...]), dot(table_v[imag], gch_v[...])
        re_f, im_f = filt_v[real].astype(F32), filt_v[imag].astype(F32)
        filt_v[real] = (re_f * re + im_f * im).astype(BF)
        filt_v[imag] = (re_f * im - im_f * re).astype(BF)
        re_s, im_s = spec_v[real].astype(F32), spec_v[imag].astype(F32)
        re_k, im_k = re_s * re + im_s * im, re_s * im - im_s * re
        cosine, sine = twist[real, 0:1], twist[real, 1:2]
        spec_v[real] = (re_k * cosine - im_k * sine).astype(BF)
        spec_v[imag] = (im_k * cosine + re_k * sine).astype(BF)
        return 0
    lax.fori_loop(0, length // STEP, turn, 0)
    down[1].go(2)
    up[2].go(0)
    up[0].go(1)
    out.go(0)

    def back(i, _):
        at, imag = spans(i * STEP, STEP, STEP), spans(length + i * STEP, STEP, STEP)
        both = dot(table_v[at], filt_v[0:length]) + dot(table_v[imag], filt_v[length:])
        grad = (both * (1.0 / length)).astype(BF).astype(F32)
        value, first = proj_v[0, at].astype(F32), proj_v[1, at].astype(F32)
        proj_v[0, at] = (grad * first).astype(BF)
        proj_v[1, at] = (grad * value).astype(BF)
        return 0
    lax.fori_loop(0, length // STEP, back, 0)

    need("normed", "win")

    def normed_grad(j):
        grad = sum(
            dot_cols(proj_v[k, spans(j * span, span)], win_v[:, :, :, k].reshape(width, group)) for k in range(3)
        )
        return grad.astype(BF)

    to_owner = []
    for i, ((yy, cc), peer) in enumerate(zip(s.group, s.mates)):
        place = gpre_v.at[0:span, i * width : (i + 1) * width]
        place[...] = normed_grad(2 * yy + cc)
        to_owner.append(wire.start(place, gnorm_got.at[i], peer))
    mine = gpre_v.at[0:span, 3 * width : 4 * width]
    mine[...] = normed_grad(me)

    down[2].go(2)
    up[1].go(1)
    for k in range(3):
        grad = dot_rows(normed_v[...], proj_v[k]).astype(BF)
        gin_v[:, :, :, k] = grad.reshape(num_z, 2, 2, block, group)
        into[k].send_core()
    up[0].go(2)
    for k in range(3):
        into[k].go(0)
    up[2].go(1)
    out.go(1)

    need("kern")
    taps = jnp.concatenate([small_v[2 * y], small_v[2 * y + 1]], axis=-1)[2:3]
    tile = 128
    for j in range(group // tile):
        cols = slice(j * tile, (j + 1) * tile)
        both = dot(table_v[0:length], spec_v[0:length, cols]) + dot(table_v[length:], spec_v[length:, cols])
        grad = kernel_back(kern_v[:, :, :, :, cols].reshape(length, tile).astype(F32), taps[:, cols],
                           both * (1.0 / length))
        gkern_v[:, :, :, :, cols] = grad.astype(BF).reshape(num_z, 2, 2, length // (4 * num_z), tile)
    taps_grad.send_core()
    up[1].go(2)
    for k in range(3):
        into[k].go(1)
    taps_grad.go(0)
    up[2].go(2)
    out.go(2)
    for k in range(3):
        down[k].go(3)
    trade_dn = Trade(wire, s, sum_dn, ends_dn)
    taps_grad.go(1)

    arrived(to_owner)
    across, diagonal, beside = (gnorm_got[i].astype(F32) for i in range(3))
    here = mine[...].astype(F32) + across
    there = beside + diagonal
    first_rows, second_rows = jnp.where(c == 0, here, there), jnp.where(c == 0, there, here)
    grad = jnp.concatenate([first_rows, second_rows], axis=0)
    normal, scale = norm_parts(tok[...].astype(F32))
    part, gain_one = norm_back(normal, scale, grad, gains[0:1])
    low_v[...] = (resid_v[...] + part).astype(BF)
    inner.start(low_v, grad_in_o)

    gain_v[0] = jnp.concatenate([gain_one, gain_two, jnp.zeros((6, width), F32)], axis=0)
    got = [wire.start(gain_v.at[0], gain_got.at[k], peer) for k, peer in enumerate(s.mates)]
    arrived(got)
    gain_v[1] = gain_v[0] + gain_got[0] + gain_got[1] + gain_got[2]
    got = [wire.start(gain_v.at[1], gain_got.at[3], s.along["x"][0])]
    for k in range(3):
        up[k].go(3)
    trade_up = Trade(wire, s, sum_up, ends_up)
    out.go(3)
    trade_out = Trade(wire, s, sum_out, ends_out)
    arrived(got)
    gain_v[2] = gain_v[1] + gain_got[3]
    got = [wire.start(gain_v.at[2], gain_got.at[3 + k], peer) for k, peer in zip(range(1, num_z), s.along["z"])]

    for k in range(3):
        into[k].go(2)
    first, second, third = sum_in[y], sum_in[y + 1], sum_in[(y + 2) % 3]
    swap_core[0, 0], swap_core[0, 1] = first.astype(BF), second.astype(BF)
    swap_y[0] = third.astype(BF)
    swaps = [wire.start(swap_y.at[0], swap_y.at[1], s.mates[0]), wire.start(swap_y.at[0], swap_y.at[2], s.mates[1]),
             wire.start(swap_core.at[0], swap_core.at[1], s.core)]
    taps_grad.go(2)
    trade_kern = Trade(wire, s, sum_kern, ends_kern)
    trade_dn.finish(gdn_o, turned=True)
    trade_up.finish(gup_o)
    trade_out.finish(gout_o)
    arrived(got)
    total = gain_v[2]
    for k in range(1, num_z):
        total = total + gain_got[3 + k]
    part = width // 4
    mine = total[:, 0:part]
    for k in range(1, 4):
        mine = jnp.where(me == k, total[:, k * part : (k + 1) * part], mine)
    gains_o[...] = mine[0:2]
    trade_kern.finish(gkern_o, turned=True)
    arrived(swaps)
    cut = group // 2
    for row, near, far in ((c, swap_core.at[0], swap_y.at[1]), (1 - c, swap_core.at[1], swap_y.at[2])):
        far = far[...].astype(F32)
        left = jnp.concatenate([near[0].astype(F32), far[:, 0:cut]], axis=-1)
        right = jnp.concatenate([far[:, cut:], near[1].astype(F32)], axis=-1)
        gin_o[spans(row * block, block)] = jnp.where(c == 0, left, right)
    wire.drain()
    inner.drain()


def backward(num_z, length, tokens, cot, twist, small_f, table, full):
    rows, width = tokens.shape
    group = width // 2
    sds = jax.ShapeDtypeStruct
    win, wout, wup, gdown, kern, proj, normed, spec, filt, conv, gated, resid, normed_two, gpre = full
    like = lambda a: vm(a.shape, a.dtype)
    weights = (win, wout, wup, gdown, kern)
    blocks = [a.shape[-2:] for a in weights]
    blocks[0] = win.shape[-3:]
    counts = [7, 15, 15, 15, 7]
    outs = [sds((rows, width), BF), sds((2 * win.shape[-2], width * 3 // 4), F32)]
    outs += [sds((2 * w.shape[-2], w.shape[-1] // 2), F32) for w in (wout, wup)]
    outs += [sds((gdown.shape[-1] // 2, 2 * gdown.shape[-2]), F32), sds((2, width // 4), F32)]
    outs += [sds((kern.shape[-1] // 2, 2 * kern.shape[-2]), F32)]
    scratch = [like(a) for a in (table, win, wout, wup, kern, proj, normed, spec, filt, conv, gated, resid,
                                 normed_two, gpre)]
    scratch += [like(wup), vm(gdown.shape[:3] + gdown.shape[4:]), like(kern)]
    scratch += [vm(win.shape[:2] + win.shape[3:])] + [vm(w.shape[:3] + w.shape[4:]) for w in (wout, wup, gdown)]
    scratch += [vm(kern.shape[:2] + kern.shape[3:])]
    scratch += [vm((n,) + b) for n, b in zip(counts, blocks)] + [vm(b, F32) for b in blocks]
    scratch += [vm((3, b[0], b[1] // 2), F32) for b in blocks[1:]]
    scratch += [vm((2, 2) + blocks[0][1:]), vm((3,) + blocks[0][1:])]
    scratch += [vm((rows, width)), vm((2, rows, group)), vm((length, group)), vm((3, rows // 2, width)),
                vm((3, 8, width), F32), vm((3 + num_z, 8, width), F32)]
    scratch += [pltpu.SemaphoreType.DMA((160,)), pltpu.SemaphoreType.DMA((160,)), pltpu.SemaphoreType.DMA((40,))]
    return pl.pallas_call(
        partial(backward_kernel, num_z, length),
        out_shape=outs,
        in_specs=[VMEM_SPEC] * 4 + [HBM_SPEC] * 15,
        out_specs=[HBM_SPEC] + [VMEM_SPEC] * 6,
        scratch_shapes=scratch,
        compiler_params=pltpu.CompilerParams(collective_id=1, has_side_effects=True, vmem_limit_bytes=63 * 2**20),
        cost_estimate=pl.CostEstimate(flops=17 * 10**9, bytes_accessed=50 * 10**6, transcendentals=2 * 10**6),
    )(tokens, cot, twist, small_f, table, *full)


def publish(*arrays):
    def copy_all(*refs):
        for src, dst in zip(refs[: len(arrays)], refs[len(arrays) :]):
            dst[...] = src[...]

    return pl.pallas_call(
        copy_all,
        out_shape=[jax.ShapeDtypeStruct(a.shape, a.dtype) for a in arrays],
        in_specs=[VMEM_SPEC] * len(arrays),
        out_specs=[VMEM_SPEC] * len(arrays),
    )(*arrays)


def fits(num_dp, num_seq, tokens, w_in, w_out, w_up, w_down, kernel):
    if num_seq != 4 or num_dp % 4 or kernel.shape[0] * num_dp > 1024 or kernel.shape[0] * num_dp % 512:
        return False
    blocks = (w_in, w_out, w_up, w_down, kernel)
    return all(b.shape[0] % 32 == 0 and b.shape[1] * 2 % 128 == 0 for b in blocks) and tokens.shape[0] == 2


def body(num_dp, num_seq, tokens_in, w_in, w_out, w_up, w_down, norm_gains, kernel, taps, cotangent):
    if not fits(num_dp, num_seq, tokens_in, w_in, w_out, w_up, w_down, kernel):
        return general_body(tokens_in, w_in, w_out, w_up, w_down, norm_gains, kernel, taps, cotangent)
    width = tokens_in.shape[-1]
    length = kernel.shape[0] * num_dp
    num_z = num_dp // 2
    table, twist = jnp.asarray(transform_table(length)), jnp.asarray(twist_table(length))
    tokens, cot = tokens_in.reshape(-1, width), cotangent.reshape(-1, width)
    out, win, wout, wup, gdown, kern, small, *saved = forward(
        num_z, length, tokens, cot, w_in, w_out, w_up, w_down.T, kernel.T, norm_gains, taps[None], twist, table)
    results = backward(num_z, length, tokens, cot, twist, small, table, [win, wout, wup, gdown, kern, *saved])
    out, grad_in, gin, gout, gup, gdn, gains, gkern = publish(out, *results)
    return (out.reshape(tokens_in.shape), grad_in.reshape(tokens_in.shape), gin, gout, gup, gdn.T, gains, gkern.T)


def solution(mesh):
    return jax.shard_map(
        partial(body, mesh.shape["dp"], mesh.shape["seq"]),
        mesh=mesh,
        in_specs=(
            P("dp", "seq", None),
            P("dp", "seq"),
            P("dp", "seq"),
            P("dp", "seq"),
            P("dp", "seq"),
            P(None, "seq"),
            P("dp", "seq"),
            P("seq"),
            P("dp", "seq", None),
        ),
        out_specs=(
            P("dp", "seq", None),
            P("dp", "seq", None),
            P("dp", "seq"),
            P("dp", "seq"),
            P("dp", "seq"),
            P("dp", "seq"),
            P(None, "seq"),
            P("dp", "seq"),
        ),
        check_vma=False,
    )
```

```python
from functools import partial
import math

import jax
from jax.experimental import pallas as pl
from jax.experimental.pallas import tpu as pltpu
import ml_dtypes
import numpy as np
import jax.numpy as jnp
from jax import lax
from jax.sharding import PartitionSpec as P

EPSILON = 1e-05
SHRINK_SCALE = 0.003
HIGHEST = lax.Precision.HIGHEST


def norm_rows(values, gain):
    center = values - jnp.mean(values, axis=-1, keepdims=True)
    spread = jnp.mean(center * center, axis=-1, keepdims=True)
    return center * lax.rsqrt(spread + EPSILON) * gain


def shape_filter(kernel, taps):
    length = kernel.shape[0]
    position = jnp.arange(length, dtype=jnp.int32)[:, None]
    live_mask = (position < taps[None, :]).astype(kernel.dtype)
    masked = kernel * live_mask
    shrunk = masked - SHRINK_SCALE * jnp.tanh(masked / SHRINK_SCALE)
    padded = jnp.pad(shrunk, ((1, 1), (0, 0)))
    pooled = (padded[:-2] + padded[1:-1] + padded[2:]) / 3.0
    return pooled * live_mask


def gelu_tanh(values):
    return jax.nn.gelu(values, approximate=True)


def contract_rows(left, right):
    return lax.dot_general(
        left, right, (((0,), (0,)), ((), ())), preferred_element_type=jnp.float32
    )


def times_transposed(left, weight):
    return lax.dot_general(
        left, weight, (((1,), (1,)), ((), ())), preferred_element_type=jnp.float32
    )


def phase_table(count_rows, count_cols, period):
    row_index = lax.broadcasted_iota(jnp.int32, (count_rows, count_cols), 0)
    col_index = lax.broadcasted_iota(jnp.int32, (count_rows, count_cols), 1)
    angles = 2.0 * math.pi / period * (row_index * col_index % period).astype(jnp.float32)
    return (jnp.cos(angles), jnp.sin(angles))


def dft_factors(length):
    total = 2 * length
    first = max(2, total // 128)
    return (total, first, total // first)


def mix_last(field, table):
    return jnp.einsum("bckn,nm->bckm", field, table, precision=HIGHEST)


def forward_dft(field):
    batch, length, chans = field.shape
    total, first, second = dft_factors(length)
    half = first // 2
    blocks = field.reshape(batch, half, second, chans)
    cos_one, sin_one = phase_table(half, first, first)
    part_re = jnp.einsum("hk,bhnc->bckn", cos_one, blocks, precision=HIGHEST)
    part_im = -jnp.einsum("hk,bhnc->bckn", sin_one, blocks, precision=HIGHEST)
    cos_two, sin_two = phase_table(first, second, total)
    turn_re = part_re * cos_two + part_im * sin_two
    turn_im = part_im * cos_two - part_re * sin_two
    cos_three, sin_three = phase_table(second, second, second)
    spec_re = mix_last(turn_re, cos_three) + mix_last(turn_im, sin_three)
    spec_im = mix_last(turn_im, cos_three) - mix_last(turn_re, sin_three)
    return (spec_re, spec_im)


def inverse_dft(spec_re, spec_im):
    batch, chans, first, second = spec_re.shape
    total = first * second
    half = first // 2
    cos_three, sin_three = phase_table(second, second, second)
    back_re = mix_last(spec_re, cos_three) - mix_last(spec_im, sin_three)
    back_im = mix_last(spec_re, sin_three) + mix_last(spec_im, cos_three)
    cos_two, sin_two = phase_table(first, second, total)
    turn_re = back_re * cos_two - back_im * sin_two
    turn_im = back_re * sin_two + back_im * cos_two
    cos_one, sin_one = phase_table(half, first, first)
    blocks = jnp.einsum("hk,bckn->bhnc", cos_one, turn_re, precision=HIGHEST)
    blocks = blocks - jnp.einsum("hk,bckn->bhnc", sin_one, turn_im, precision=HIGHEST)
    return blocks.reshape(batch, half * second, chans) / total


def to_channels(field):
    return lax.all_to_all(field, "seq", split_axis=2, concat_axis=1, tiled=True)


def to_tokens(field):
    return lax.all_to_all(field, "seq", split_axis=1, concat_axis=2, tiled=True)


def general_body(tokens_in, w_in, w_out, w_up, w_down, norm_gains, kernel, taps, cotangent):
    w_in_rows, w_out_rows, w_up_rows, w_down_rows, gains = (
        lax.all_gather(w_in, "seq", axis=1, tiled=True),
        lax.all_gather(w_out, "seq", axis=1, tiled=True),
        lax.all_gather(w_up, "seq", axis=1, tiled=True),
        lax.all_gather(w_down, "seq", axis=1, tiled=True),
        lax.all_gather(norm_gains, "seq", axis=1, tiled=True),
    )
    full_in, full_out, full_up, full_down, kernel_cols = (
        lax.all_gather(w_in_rows, "dp", axis=0, tiled=True),
        lax.all_gather(w_out_rows, "dp", axis=0, tiled=True),
        lax.all_gather(w_up_rows, "dp", axis=0, tiled=True),
        lax.all_gather(w_down_rows, "dp", axis=0, tiled=True),
        lax.all_gather(kernel, "dp", axis=0, tiled=True),
    )
    num_seqs, local_len, width = tokens_in.shape
    total_rows = num_seqs * local_len
    inputs = tokens_in.reshape(total_rows, width).astype(jnp.float32)
    gains_wide = gains.astype(jnp.float32)
    normed, norm_back_one = jax.vjp(norm_rows, inputs, gains_wide[0])
    normed_low = normed.astype(jnp.bfloat16)
    proj = jnp.dot(normed_low, full_in, preferred_element_type=jnp.float32)
    values = proj[:, :width]
    gate_one = proj[:, width : 2 * width]
    gate_two = proj[:, 2 * width :]
    mixed_low = (gate_one * values).astype(jnp.bfloat16).reshape(num_seqs, local_len, width)
    by_channel = to_channels(mixed_low)
    filt, filter_back = jax.vjp(partial(shape_filter, taps=taps), kernel_cols.astype(jnp.float32))
    filt_re, filt_im = forward_dft(filt[None])
    sig_re, sig_im = forward_dft(by_channel.astype(jnp.float32))
    conv = inverse_dft(sig_re * filt_re - sig_im * filt_im, sig_re * filt_im + sig_im * filt_re)
    conv_tok = to_tokens(conv.astype(jnp.bfloat16)).reshape(total_rows, width).astype(jnp.float32)
    gated = (gate_two * conv_tok).astype(jnp.bfloat16)
    resid = inputs + jnp.dot(gated, full_out, preferred_element_type=jnp.float32)
    normed_two, norm_back_two = jax.vjp(norm_rows, resid, gains_wide[1])
    normed_two_low = normed_two.astype(jnp.bfloat16)
    hidden_pre = jnp.dot(normed_two_low, full_up, preferred_element_type=jnp.float32)
    active, gelu_back = jax.vjp(gelu_tanh, hidden_pre)
    active_low = active.astype(jnp.bfloat16)
    result = (resid + jnp.dot(active_low, full_down, preferred_element_type=jnp.float32)).astype(
        jnp.bfloat16
    )
    grad_rows = cotangent.reshape(total_rows, width)
    grad_down = contract_rows(active_low, grad_rows)
    grad_active = times_transposed(grad_rows, full_down)
    grad_pre = gelu_back(grad_active)[0].astype(jnp.bfloat16)
    grad_up = contract_rows(normed_two_low, grad_pre)
    grad_normed_two = times_transposed(grad_pre, full_up)
    grad_resid_part, grad_gain_two = norm_back_two(grad_normed_two)
    grad_resid = grad_rows.astype(jnp.float32) + grad_resid_part
    resid_low = grad_resid.astype(jnp.bfloat16)
    grad_outw = contract_rows(gated, resid_low)
    grad_gated = times_transposed(resid_low, full_out)
    grad_gate_two = grad_gated * conv_tok
    grad_conv = (grad_gated * gate_two).astype(jnp.bfloat16).reshape(num_seqs, local_len, width)
    grad_channel = to_channels(grad_conv).astype(jnp.float32)
    back_re, back_im = forward_dft(grad_channel)
    grad_signal = inverse_dft(
        back_re * filt_re + back_im * filt_im, back_im * filt_re - back_re * filt_im
    )
    cross_re = jnp.sum(back_re * sig_re + back_im * sig_im, axis=0, keepdims=True)
    cross_im = jnp.sum(back_im * sig_re - back_re * sig_im, axis=0, keepdims=True)
    grad_filt = inverse_dft(cross_re, cross_im)[0]
    grad_kern = filter_back(grad_filt)[0]
    grad_mixed = (
        to_tokens(grad_signal.astype(jnp.bfloat16)).reshape(total_rows, width).astype(jnp.float32)
    )
    grad_proj = jnp.concatenate([grad_mixed * gate_one, grad_mixed * values, grad_gate_two], axis=1)
    grad_proj = grad_proj.astype(jnp.bfloat16)
    grad_inw = contract_rows(normed_low, grad_proj)
    grad_normed = times_transposed(grad_proj, full_in)
    grad_input_part, grad_gain_one = norm_back_one(grad_normed)
    grad_inputs = (
        (grad_resid + grad_input_part).astype(jnp.bfloat16).reshape(num_seqs, local_len, width)
    )
    grad_gain_pair = jnp.stack([grad_gain_one, grad_gain_two])
    in_part, outw_part, up_part, down_part, kern_done = (
        lax.psum_scatter(
            grad_inw.astype(jnp.bfloat16), "dp", scatter_dimension=0, tiled=True
        ).astype(jnp.float32),
        lax.psum_scatter(
            grad_outw.astype(jnp.bfloat16), "dp", scatter_dimension=0, tiled=True
        ).astype(jnp.float32),
        lax.psum_scatter(
            grad_up.astype(jnp.bfloat16), "dp", scatter_dimension=0, tiled=True
        ).astype(jnp.float32),
        lax.psum_scatter(
            grad_down.astype(jnp.bfloat16), "dp", scatter_dimension=0, tiled=True
        ).astype(jnp.float32),
        lax.psum_scatter(
            grad_kern.astype(jnp.bfloat16), "dp", scatter_dimension=0, tiled=True
        ).astype(jnp.float32),
    )
    in_done, outw_done, up_done, down_done, gain_part = (
        lax.psum_scatter(
            in_part.astype(jnp.bfloat16), "seq", scatter_dimension=1, tiled=True
        ).astype(jnp.float32),
        lax.psum_scatter(
            outw_part.astype(jnp.bfloat16), "seq", scatter_dimension=1, tiled=True
        ).astype(jnp.float32),
        lax.psum_scatter(
            up_part.astype(jnp.bfloat16), "seq", scatter_dimension=1, tiled=True
        ).astype(jnp.float32),
        lax.psum_scatter(
            down_part.astype(jnp.bfloat16), "seq", scatter_dimension=1, tiled=True
        ).astype(jnp.float32),
        lax.psum_scatter(
            grad_gain_pair.astype(jnp.bfloat16), "seq", scatter_dimension=1, tiled=True
        ).astype(jnp.float32),
    )
    gain_done = lax.psum(gain_part, "dp")
    return (
        result.reshape(num_seqs, local_len, width),
        grad_inputs,
        in_done,
        outw_done,
        up_done,
        down_done,
        gain_done,
        kern_done,
    )


MESH = pl.DeviceIdType.MESH
BF = jnp.bfloat16
F32 = jnp.float32


class Remote:
    def __init__(self, wire, slot, src, dst, peer):
        self.wire, self.slot, self.src, self.dst, self.peer = wire, slot, src, dst, peer
        self.sent = False

    def named(self):
        return pltpu.make_async_remote_copy(
            src_ref=self.src(), dst_ref=self.dst(), send_sem=self.wire.send.at[self.slot],
            recv_sem=self.wire.recv.at[self.slot], device_id=self.peer, device_id_type=MESH,
        )

    def wait_recv(self):
        self.named().wait_recv()


class Wire:
    def __init__(self, send, recv, spots):
        self.send, self.recv, self.s, self.made = send, recv, spots, []

    def start(self, src, dst, peer, core=None, buffer=None):
        src, dst = (end if callable(end) else partial(lambda ref: ref, end) for end in (src, dst))
        copy = Remote(self, len(self.made), src, dst, peer)
        copy.buffer = buffer
        copy.named().start()
        self.made.append((core, copy))
        return copy

    def drain(self, src=None):
        made = [(core, copy) for core, copy in self.made if not copy.sent and src in (None, copy.buffer)]
        for which in (None, 0, 1):
            @self.s.on(which)
            def _():
                for core, copy in made:
                    if core == which:
                        copy.named().wait_send()
        for _, copy in made:
            copy.sent = True


class Local:
    def __init__(self, sems):
        self.sems, self.made, self.open = sems, 0, []

    def start(self, src, dst):
        copy = pltpu.make_async_copy(src, dst, self.sems.at[self.made])
        self.made += 1
        copy.start()
        self.open.append(copy)
        return copy

    def wait(self, copy):
        copy.wait()
        self.open = [other for other in self.open if other is not copy]

    def drain(self):
        for copy in list(self.open):
            self.wait(copy)


def arrived(copies):
    for copy in copies:
        copy.wait_recv()


class Spots:
    def __init__(self, num_z):
        dp, sq = lax.axis_index("dp"), lax.axis_index("seq")
        z, x, y, c = dp // 2, dp % 2, sq // 2, sq % 2
        self.num_z = num_z
        self.z, self.x, self.y, self.c = z, x, y, c
        self.own = dict(x=x, y=y, z=z)
        self.size = dict(x=2, y=2, z=num_z)
        self.core = self.at(z, x, y, 1 - c)
        self.others = dict(x=[1 - x], y=[1 - y], z=[(z + k) % num_z for k in range(1, num_z)])
        self.along = dict(
            x=[self.at(z, 1 - x, y, c)], y=[self.at(z, x, 1 - y, c)],
            z=[self.at(other, x, y, c) for other in self.others["z"]],
        )
        self.group = [((y + i) % 2, (c + j) % 2) for i, j in ((1, 0), (1, 1), (0, 1))]
        self.mates = [self.at(z, x, yy, cc) for yy, cc in self.group]

    def at(self, z, x, y, c):
        return (z * 2 + x, y * 2 + c)

    def on(self, core):
        return (lambda body: body()) if core is None else pl.when(self.c == core)

    def meet(self):
        barrier = pltpu.get_barrier_semaphore()
        peers = self.along["z"] + self.along["x"] + self.mates
        for peer in peers:
            pl.semaphore_signal(barrier, inc=1, device_id=peer, device_id_type=MESH)
        pl.semaphore_wait(barrier, len(peers))


def both_cores(orders):
    return [(None, orders[0])] if len(orders) == 1 else list(enumerate(orders))


def block_index(s, axes, wide, core, at=None):
    place = {**s.own, **(at or {})}
    index = tuple(slice(None) if axis in wide else place[axis] for axis in axes)
    return index if core is None else index + (core,)


class Gather:
    def __init__(self, wire, spots, full, axes, *orders, part=(), buffer=None):
        self.buffer = buffer
        self.wire, self.s, self.full, self.axes, self.part = wire, spots, full, axes, part
        self.orders, self.last = both_cores(orders), {}

    def view(self, have):
        return self.full.at[block_index(self.s, self.axes, have, self.s.c) + self.part]

    def settle(self):
        for core, copies in self.last.items():
            self.s.on(core)(partial(arrived, copies))
        self.last = {}

    def step(self, n):
        s = self.s
        if n == len(self.orders[0][1]):
            self.settle()
            view = partial(self.view, self.axes)
            self.last[None] = [self.wire.start(view, view, s.core, buffer=self.buffer)]
            return
        before, self.last = self.last, {}
        for core, order in self.orders:
            @s.on(core)
            def _():
                arrived(before.get(core, []))
                view = partial(self.view, order[:n])
                self.last[core] = [
                    self.wire.start(view, view, peer, core, self.buffer) for peer in s.along[order[n]]
                ]

    def done(self):
        self.settle()


class Rounds:
    LAG = 2

    def __init__(self, gathers):
        self.gathers, self.now = gathers, 0

    def run(self, count=1):
        for _ in range(count):
            for step in reversed(range(4)):
                k = self.now - step * self.LAG
                if 0 <= k < len(self.gathers) and step <= len(self.gathers[k].orders[0][1]):
                    self.gathers[k].step(step)
            self.now += 1


class Scatter:
    def __init__(self, wire, spots, total, axes, orders, from_core, got, result, part=()):
        self.wire, self.s, self.total, self.axes, self.part = wire, spots, total, axes, part
        self.orders = [(core, order[::-1]) for core, order in both_cores(orders)]
        self.from_core, self.got, self.result = from_core, got, result
        self.last = {}

    def mine(self, wide, at=None):
        return self.total.at[block_index(self.s, self.axes, wide, self.s.c, at) + self.part]

    def send_core(self):
        s = self.s
        whole = (slice(None),) * (len(self.axes) - 1)
        self.last = [
            self.wire.start(self.total.at[(i,) + whole + (1 - s.c,) + self.part],
                            self.from_core.at[(i,) + whole + self.part], s.core)
            for i in range(self.from_core.shape[0])
        ]

    def add_core(self):
        arrived(self.last)
        self.last = {}
        s = self.s
        count = math.prod(s.size[axis] for axis in self.axes)

        def one(i, _):
            at, left = {}, i
            for axis in reversed(self.axes):
                at[axis], left = left % s.size[axis], left // s.size[axis]
            into = self.mine("", at)
            term = self.from_core[tuple(at[axis] for axis in self.axes) + self.part]
            into[...] = (into[...].astype(F32) + term.astype(F32)).astype(BF)
            return 0
        lax.fori_loop(0, count, one, 0)

    def stages(self, order, n):
        s = self.s
        begin = 0
        for k in range(n + 1):
            wide = sorted(order[k + 1 :])
            count = math.prod(s.size[axis] for axis in wide)
            if k < n:
                begin += count * (s.size[order[k]] - 1)
        return order[n], wide, count, begin

    def slots(self, start, count):
        return self.got.at[(start if count is None else slice(start, start + count),) + self.part]

    def send(self, n):
        s = self.s
        for core, order in self.orders:
            axis, wide, count, begin = self.stages(order, n)

            @s.on(core)
            def _():
                self.last[core] = []
                for j, (other, peer) in enumerate(zip(s.others[axis], s.along[axis])):
                    outer = s.size[wide[0]] if len(wide) == 2 else 1
                    inner = count // outer
                    for i in range(outer):
                        at = {axis: other}
                        if len(wide) == 2:
                            at[wide[0]] = i
                        start = begin + j * count + i * inner
                        src = partial(self.mine, wide[-1:], at)
                        dst = partial(self.slots, start, inner if wide else None)
                        self.last[core].append(self.wire.start(src, dst, peer, core))

    def add(self, n):
        s = self.s
        for core, order in self.orders:
            axis, wide, count, begin = self.stages(order, n)
            peers = len(s.others[axis])

            @s.on(core)
            def _():
                arrived(self.last[core])
                if n == len(order) - 1:
                    total = self.mine("")[...].astype(F32)
                    for j in range(peers):
                        total = total + self.got[(begin + j,) + self.part].astype(F32)
                    self.result[self.part or ...] = total
                    return

                def one(i, _):
                    at, left = {}, i
                    for a in reversed(wide):
                        at[a], left = left % s.size[a], left // s.size[a]
                    into = self.mine("", at)
                    total = into[...].astype(F32)
                    for j in range(peers):
                        total = total + self.got[(begin + j * count + i,) + self.part].astype(F32)
                    into[...] = total.astype(BF)
                    return 0
                lax.fori_loop(0, count, one, 0)


    def go(self, n):
        if n == 0:
            self.add_core()
        else:
            self.add(n - 1)
        if n < len(self.orders[0][1]):
            self.send(n)


class Trade:
    def __init__(self, wire, spots, halves, ends):
        self.s, self.ends, self.pieces = spots, ends, len(halves[0])
        for core in range(2):
            for i, piece in enumerate(halves[core]):
                ends[core, i] = piece
        self.copy = wire.start(ends.at[1 - spots.c], ends.at[2], spots.core)

    def finish(self, out, turned=False):
        self.copy.wait_recv()
        c = self.s.c
        own, other = (
            jnp.concatenate([self.ends[k, i] for i in range(self.pieces)], axis=-1) for k in (c, 2)
        )
        both = jnp.concatenate([jnp.where(c == 0, own, other), jnp.where(c == 0, other, own)], axis=0)
        out[...] = both.T if turned else both


def column_halves(total):
    part = total.shape[-1] // 2
    return [[total[:, core * part : (core + 1) * part]] for core in range(2)]


def row_parts(rows):
    size = rows // PARTS
    return [(slice(i * size, (i + 1) * size),) for i in range(PARTS)]


def norm_parts(values):
    center = values - jnp.mean(values, axis=-1, keepdims=True)
    spread = jnp.mean(center * center, axis=-1, keepdims=True)
    scale = lax.rsqrt(spread + EPSILON)
    return center * scale, scale


def norm_back(normal, scale, grad, gain):
    p = grad * gain
    flat = jnp.mean(p, axis=-1, keepdims=True)
    along = jnp.mean(p * normal, axis=-1, keepdims=True)
    return (p - flat - normal * along) * scale, jnp.sum(grad * normal, axis=0, keepdims=True)


def dot(left, right):
    return jnp.dot(left, right, preferred_element_type=F32)


def dot_rows(left, right):
    return lax.dot_general(left, right, (((0,), (0,)), ((), ())), preferred_element_type=F32)


def dot_cols(left, right):
    return lax.dot_general(left, right, (((1,), (1,)), ((), ())), preferred_element_type=F32)


def live_taps(kern, taps):
    position = lax.broadcasted_iota(jnp.int32, kern.shape, 0)
    return position, position.astype(F32) < taps


def pool(values, position):
    length = values.shape[0]
    before = jnp.where(position == 0, 0.0, pltpu.roll(values, 1, 0))
    after = jnp.where(position == length - 1, 0.0, pltpu.roll(values, length - 1, 0))
    return (before + values + after) / 3.0


def make_filter(kern, taps):
    position, live = live_taps(kern, taps)
    masked = jnp.where(live, kern, 0.0)
    shrunk = masked - SHRINK_SCALE * jnp.tanh(masked / SHRINK_SCALE)
    return jnp.where(live, pool(shrunk, position), 0.0)


def kernel_back(kern, taps, grad):
    position, live = live_taps(kern, taps)
    slope = jnp.tanh(jnp.where(live, kern, 0.0) / SHRINK_SCALE)
    return jnp.where(live, pool(jnp.where(live, grad, 0.0), position) * slope * slope, 0.0)


GELU_K = math.sqrt(2.0 / math.pi)


def gelu_both(v):
    square = v * v
    t = jnp.tanh(GELU_K * v * (1.0 + 0.044715 * square))
    half = 0.5 * (1.0 + t)
    slope = half + 0.5 * v * (1.0 - t * t) * (GELU_K * (1.0 + 3 * 0.044715 * square))
    return v * half, slope


def spans(start, size, step=16):
    return pl.ds(pl.multiple_of(start, step), size)


def transform_table(length):
    k = 2 * np.arange(length)[:, None] + 1
    angle = np.pi / (4 * length) * ((k * k.T) % (8 * length))
    return np.concatenate([np.cos(angle), np.sin(angle)]).astype(np.float32).astype(ml_dtypes.bfloat16)


def twist_table(length):
    angle = np.pi / (4 * length) * (2 * np.arange(length) + 1)
    return np.stack([np.cos(angle), np.sin(angle)], axis=1).astype(np.float32)


ORDER_OUT = ("zxy", "zyx")
ORDER_UP = ("zxy", "zyx")
ORDER_DOWN = ("zxy", "yzx")
PARTS = 3
STEP = 256


def layer_kernel(
    num_z, length,
    tok, cot, w_in, w_out, w_up, w_down_t, kern_t, gains_in, taps_in, twist, table_hbm,
    out_o, grad_in_o, gin_o, gout_o, gup_o, gdn_o, gains_o, gkern_o,
    win_v, wout_v, wup_v, wdown_v, gdn_v, kern_v, small_v,
    pre_in, pre_out, pre_up, pre_down, pre_kern, w_down, kern,
    table_v, proj_v, normed_own, normed_v, sig_v, spec_v, filt_v, turned_v, conv_v, gated_ch,
    gated_v, resid_v, normed_two_v, act_v, slope_v,
    core_in, core_out, core_dn, core_kern,
    got_in, got_out, got_up, got_dn, got_kern,
    sum_in, sum_out, sum_up, sum_dn, sum_kern,
    ends_out, ends_up, ends_dn, ends_kern, swap_core, swap_y,
    gain_v, gain_got,
    send, recv, local,
):
    s = Spots(num_z)
    z, x, y, c = s.z, s.x, s.y, s.c
    wire, inner = Wire(send, recv, s), Local(local)
    load_table = inner.start(table_hbm, table_v)
    rows, width = tok.shape
    group, span = width // 2, rows // 2
    hidden = act_v.shape[1]
    block = width // (4 * num_z)
    me = 2 * y + c
    chunk, home = spans(me * span, span), spans(c * span, span)
    w_down[...] = w_down_t[...].T
    kern[...] = kern_t[...].T
    small_v[me, 0:2] = gains_in[...].astype(F32)
    small_v[me, 2:3] = taps_in[...].astype(F32)
    s.meet()

    half = w_in.shape[0] // 2
    trade_in = [
        wire.start(w_in.at[spans(cc * half, half)], pre_in.at[me], peer) for (yy, cc), peer in zip(s.group, s.mates)
    ]
    smalls = [wire.start(small_v.at[me], small_v.at[me], peer) for peer in s.mates]
    pairs = [(kern, pre_kern), (w_out, pre_out), (w_up, pre_up), (w_down, pre_down)]
    traded = []
    for src, pre in pairs:
        half = src.shape[0] // 2
        traded.append(wire.start(src.at[spans((1 - c) * half, half)], pre.at[c], s.core))
    half = w_in.shape[0] // 2
    pre_in[me] = w_in[spans(c * half, half)]
    for src, pre in pairs:
        half = src.shape[0] // 2
        pre[c] = src[spans(c * half, half)]

    g_in = [Gather(wire, s, win_v, "zx", "zx", part=(k,), buffer="in") for k in range(3)]
    g_kern = Gather(wire, s, kern_v, "zx", "zx", buffer="kern")
    g_out = Gather(wire, s, wout_v, "yzx", *ORDER_OUT)
    parts = row_parts(wup_v.shape[-2])
    g_up = [Gather(wire, s, wup_v, "yzx", *ORDER_UP, part=part, buffer="up") for part in parts]
    g_down = [Gather(wire, s, wdown_v, "yzx", *ORDER_DOWN, part=part, buffer="down") for part in parts]
    rounds = Rounds([*g_in, g_kern, g_out, *g_up, *g_down])

    def join(i):
        traded[i].wait_recv()
        pre = pairs[i][1]
        return jnp.concatenate([pre[0], pre[1]], axis=-1)

    arrived(trade_in)
    whole = jnp.concatenate([pre_in[k] for k in range(4)], axis=-1)
    for k in range(3):
        left, right = (whole[:, (2 * k + h) * group : (2 * k + h + 1) * group] for h in range(2))
        win_v[z, x, c, k] = jnp.where(y == 0, left, right)
        if k < 2:
            rounds.run()

    arrived(smalls)
    gains = jnp.concatenate([small_v[k] for k in range(4)], axis=-1)
    tile = 128

    def norm_one(i, _):
        at = spans(i * tile, tile)
        normed, _ = norm_parts(tok[at].astype(F32))
        normed_own[at] = (normed * gains[0:1]).astype(BF)
        return 0
    lax.fori_loop(0, rows // tile, norm_one, 0)
    to_group = [
        wire.start(normed_own.at[spans(cc * span, span)], normed_v.at[chunk], peer, buffer="normed")
        for (yy, cc), peer in zip(s.group, s.mates)
    ]
    normed_v[chunk] = normed_own[home]
    kern_v[z, x, c] = join(0)
    wout_v[y, z, x, c] = join(1)
    both = join(2)
    pieces = both.shape[-1] // group
    for q in range(pieces):
        wup_v[y, z, x, c, q * block : (q + 1) * block] = both[:, q * group : (q + 1) * group]
    wdown_v[y, z, x, c] = join(3)
    rounds.run(5)

    arrived(to_group)
    g_in[0].done()
    g_in[1].done()

    def project(k, at):
        return dot(normed_v[at], win_v[:, :, :, k].reshape(width, group))

    def mix(i, _):
        at = spans(i * STEP, STEP, STEP)
        value, gate = project(0, at), project(1, at)
        proj_v[0, at] = value.astype(BF)
        proj_v[1, at] = gate.astype(BF)
        sig_v[at] = (value * gate).astype(BF)
        return 0
    lax.fori_loop(0, length // STEP, mix, 0)
    rounds.run()
    g_in[2].done()

    def second_gate(i, _):
        at = spans(i * STEP, STEP, STEP)
        proj_v[2, at] = project(2, at).astype(BF)
        return 0
    lax.fori_loop(0, length // STEP, second_gate, 0)
    rounds.run()

    g_kern.done()
    taps_v = gain_v.at[2, 0:1]
    taps_v[:, 0:group] = jnp.concatenate([small_v[2 * y], small_v[2 * y + 1]], axis=-1)[2:3]

    def shape_taps(j, _):
        cols = spans(j * tile, tile, tile)
        filt = make_filter(kern_v[:, :, :, :, cols].reshape(length, tile).astype(F32), taps_v[:, cols])
        gated_ch[:, cols] = filt.astype(BF)
        return 0
    lax.fori_loop(0, group // tile, shape_taps, 0)
    inner.wait(load_table)

    def spectrum(i, _):
        real, imag = spans(i * STEP, STEP, STEP), spans(length + i * STEP, STEP, STEP)
        re, im = dot(table_v[real], gated_ch[...]), dot(table_v[imag], gated_ch[...])
        cosine, sine = twist[real, 0:1], twist[real, 1:2]
        filt_v[real] = (re * cosine + im * sine).astype(BF)
        filt_v[imag] = (im * cosine - re * sine).astype(BF)
        return 0
    lax.fori_loop(0, length // STEP, spectrum, 0)
    rounds.run()

    def convolve(i, _):
        real, imag = spans(i * STEP, STEP, STEP), spans(length + i * STEP, STEP, STEP)
        re_s, im_s = dot(table_v[real], sig_v[...]), dot(table_v[imag], sig_v[...])
        spec_v[real] = re_s.astype(BF)
        spec_v[imag] = im_s.astype(BF)
        re_f, im_f = filt_v[real].astype(F32), filt_v[imag].astype(F32)
        turned_v[real] = (re_s * re_f - im_s * im_f).astype(BF)
        turned_v[imag] = (re_s * im_f + im_s * re_f).astype(BF)
        return 0
    lax.fori_loop(0, length // STEP, convolve, 0)
    rounds.run()

    def back(i, _):
        at, imag = spans(i * STEP, STEP, STEP), spans(length + i * STEP, STEP, STEP)
        both = dot(table_v[at], turned_v[0:length]) + dot(table_v[imag], turned_v[length:])
        conv = (both * (1.0 / length)).astype(BF)
        conv_v[at] = conv
        gated_ch[at] = (proj_v[2, at].astype(F32) * conv.astype(F32)).astype(BF)
        return 0
    lax.fori_loop(0, length // STEP, back, 0)

    to_tokens = [
        wire.start(gated_ch.at[spans((2 * yy + cc) * span, span)], gated_v.at[y, home], peer, buffer="gated")
        for (yy, cc), peer in zip(s.group, s.mates)
    ]
    gated_v[y, home] = gated_ch[chunk]
    rounds.run()
    g_out.done()
    rounds.run()
    arrived(to_tokens)

    for k in range(2):
        cols = slice(k * group, (k + 1) * group)
        mixed = sum(
            dot(gated_v[h], wout_v[k, h * num_z // 2 : (h + 1) * num_z // 2].reshape(group, group)) for h in range(2)
        )
        resid_v[:, cols] = tok[:, cols].astype(F32) + mixed

    def norm_two(i, _):
        at = spans(i * tile, tile)
        normed, _ = norm_parts(resid_v[at])
        normed_two_v[at] = (normed * gains[1:2]).astype(BF)
        return 0
    lax.fori_loop(0, rows // tile, norm_two, 0)
    rounds.run(2)
    for g in g_up:
        g.done()

    def piece(ref, j):
        return ref.at[j // pieces, :, :, :, spans((j % pieces) * block, block)]

    def feed(j, _):
        weight, cols = piece(wup_v, j)[...].reshape(width, group), spans(j * group, group, 128)

        def rows_of(i, _):
            at = spans(i * span // 2, span // 2)
            act, slope = gelu_both(dot(normed_two_v[at], weight))
            act_v[at, cols] = act.astype(BF)
            slope_v[at, cols] = slope.astype(BF)
            return 0
        return lax.fori_loop(0, 4, rows_of, 0)
    lax.fori_loop(0, pieces, feed, 0)
    rounds.run()
    lax.fori_loop(pieces, 2 * pieces, feed, 0)
    rounds.run()

    down = [Scatter(wire, s, gdn_v, "yzx", ORDER_DOWN, core_dn, got_dn, sum_dn, part=part) for part in parts]
    deep = hidden // (2 * num_z)

    def down_grad(i, _):
        grad = dot_rows(act_v[:, spans(i * deep, deep, 128)], cot[...]).astype(BF)
        for h in range(2):
            gdn_v[h, i // 2, i % 2] = grad[:, h * group : (h + 1) * group].reshape(2, deep // 2, group)
        return 0
    lax.fori_loop(0, 2 * num_z, down_grad, 0)
    rounds.run()
    for g in down:
        g.send_core()
    for g in g_down:
        g.done()

    def pre_grad(i, _):
        at = spans(i * deep, deep, 128)
        grad = sum(
            dot_cols(cot[:, h * group : (h + 1) * group], wdown_v[h, i // 2, i % 2].reshape(deep, group))
            for h in range(2)
        )
        slope_v[:, at] = (slope_v[:, at].astype(F32) * grad).astype(BF)
        return 0
    lax.fori_loop(0, 2 * num_z, pre_grad, 0)
    gpre_v = slope_v
    down[0].go(0)
    down[1].go(0)
    wire.drain("normed")
    out_v = low_v = normed_own

    def down_out(i, _):
        at, cols = spans((i % 2) * span, span), spans(i // 2 * group, group, 128)
        grown = dot(act_v[at], wdown_v[i // 2].reshape(hidden, group))
        out_v[at, cols] = (resid_v[at, cols] + grown).astype(BF)
        return 0
    lax.fori_loop(0, 4, down_out, 0)
    store_out = inner.start(out_v, out_o)
    down[2].go(0)

    gnorm_got = [act_v.at[0:span, 0:width], act_v.at[span:, 0:width], act_v.at[0:span, width : 2 * width]]
    gout_v, gup_v, gin_v = wup_v.at[:, :, :, :, 0:block], wdown_v, win_v
    gch_v, gkern_v = sig_v, kern_v
    ggate_v = gated_ch
    up = [Scatter(wire, s, gup_v, "yzx", ORDER_UP, core_dn, got_up, sum_up, part=part) for part in parts]
    out = Scatter(wire, s, gout_v, "yzx", ORDER_OUT, core_out, got_out, sum_out)
    into = [Scatter(wire, s, gin_v, "zx", ("zx",), core_in, got_in, sum_in, part=(k,)) for k in range(3)]
    taps_grad = Scatter(wire, s, gkern_v, "zx", ("zx",), core_kern, got_kern, sum_kern)

    inner.wait(store_out)

    def norm_two_back(i, gain):
        at = spans(i * span, span)

        def up_back(j, total):
            weight = piece(wup_v, j)[...].reshape(width, group)
            return total + dot_cols(gpre_v[at, spans(j * group, group, 128)], weight)
        grad = lax.fori_loop(0, 2 * pieces, up_back, jnp.zeros((span, width), F32))
        normal, scale = norm_parts(resid_v[at])
        part, more = norm_back(normal, scale, grad, gains[1:2])
        part = cot[at].astype(F32) + part
        resid_v[at] = part
        low_v[at] = part.astype(BF)
        return gain + more
    gain_two = lax.fori_loop(0, 2, norm_two_back, jnp.zeros((1, width), F32))

    wire.drain("gated")
    for h in range(2):
        grad = sum(
            dot_cols(
                low_v[:, k * group : (k + 1) * group],
                wout_v[k, h * num_z // 2 : (h + 1) * num_z // 2].reshape(group, group),
            )
            for k in range(2)
        )
        ggate_v[h * rows : (h + 1) * rows] = grad.astype(BF)
    to_channels = [
        wire.start(ggate_v.at[spans(yy * rows + cc * span, span)], gch_v.at[chunk], peer)
        for (yy, cc), peer in zip(s.group, s.mates)
    ]
    gch_v[chunk] = ggate_v[spans(y * rows + c * span, span)]
    down[0].go(1)
    down[1].go(1)

    wire.drain("down")

    def up_grad(j, _):
        grad = dot_rows(normed_two_v[...], gpre_v[:, spans(j * group, group, 128)]).astype(BF)
        piece(gup_v, j)[...] = grad.reshape(num_z, 2, 2, block, group)
        return 0
    lax.fori_loop(0, 2 * pieces, up_grad, 0)
    arrived(to_channels[2:])
    for g in up:
        g.send_core()
    down[2].go(1)
    up[0].go(0)

    wire.drain("up")

    def out_grad(i, _):
        h, k = i // 2, i % 2
        grad = dot_rows(gated_v[h], low_v[:, spans(k * group, group, 128)]).astype(BF)
        gout_v[k, pl.ds(h * (num_z // 2), num_z // 2)] = grad.reshape(num_z // 2, 2, 2, block, group)
        return 0
    lax.fori_loop(0, 4, out_grad, 0)
    out.send_core()
    down[0].go(2)
    up[1].go(0)

    arrived(to_channels[:2])

    def gate(i, _):
        at = spans(i * STEP, STEP, STEP)
        grad = gch_v[at].astype(F32)
        gch_v[at] = (grad * proj_v[2, at].astype(F32)).astype(BF)
        proj_v[2, at] = (grad * conv_v[at].astype(F32)).astype(BF)
        return 0
    lax.fori_loop(0, length // STEP, gate, 0)

    def turn(i, _):
        real, imag = spans(i * STEP, STEP, STEP), spans(length + i * STEP, STEP, STEP)
        re, im = dot(table_v[real], gch_v[...]), dot(table_v[imag], gch_v[...])
        re_f, im_f = filt_v[real].astype(F32), filt_v[imag].astype(F32)
        filt_v[real] = (re_f * re + im_f * im).astype(BF)
        filt_v[imag] = (re_f * im - im_f * re).astype(BF)
        re_s, im_s = spec_v[real].astype(F32), spec_v[imag].astype(F32)
        re_k, im_k = re_s * re + im_s * im, re_s * im - im_s * re
        cosine, sine = twist[real, 0:1], twist[real, 1:2]
        spec_v[real] = (re_k * cosine - im_k * sine).astype(BF)
        spec_v[imag] = (im_k * cosine + re_k * sine).astype(BF)
        return 0
    lax.fori_loop(0, length // STEP, turn, 0)
    down[1].go(2)
    up[2].go(0)
    up[0].go(1)
    out.go(0)

    def signal_back(i, _):
        at, imag = spans(i * STEP, STEP, STEP), spans(length + i * STEP, STEP, STEP)
        both = dot(table_v[at], filt_v[0:length]) + dot(table_v[imag], filt_v[length:])
        grad = (both * (1.0 / length)).astype(BF).astype(F32)
        value, first = proj_v[0, at].astype(F32), proj_v[1, at].astype(F32)
        proj_v[0, at] = (grad * first).astype(BF)
        proj_v[1, at] = (grad * value).astype(BF)
        return 0
    lax.fori_loop(0, length // STEP, signal_back, 0)

    def normed_grad(j):
        grad = sum(
            dot_cols(proj_v[k, spans(j * span, span)], win_v[:, :, :, k].reshape(width, group)) for k in range(3)
        )
        return grad.astype(BF)

    def owner_part(i, _):
        yy, cc = (y + 1 - i // 2) % 2, (c + i // 2 + i) % 2
        gpre_v[0:span, spans(i * width, width, 128)] = normed_grad(2 * yy + cc)
        return 0
    lax.fori_loop(0, 4, owner_part, 0)
    to_owner = [
        wire.start(gpre_v.at[0:span, i * width : (i + 1) * width], gnorm_got[i], peer)
        for i, peer in enumerate(s.mates)
    ]
    mine = gpre_v.at[0:span, 3 * width : 4 * width]

    down[2].go(2)
    up[1].go(1)
    wire.drain("in")

    def in_grad(k, _):
        grad = dot_rows(normed_v[...], proj_v[k]).astype(BF)
        gin_v[:, :, :, k] = grad.reshape(num_z, 2, 2, block, group)
        return 0
    lax.fori_loop(0, 3, in_grad, 0)
    for k in range(3):
        into[k].send_core()
    up[0].go(2)
    for k in range(3):
        into[k].go(0)
    up[2].go(1)
    out.go(1)

    wire.drain("kern")

    def taps_back(j, _):
        cols = spans(j * tile, tile, tile)
        both = dot(table_v[0:length], spec_v[0:length, cols]) + dot(table_v[length:], spec_v[length:, cols])
        grad = kernel_back(kern_v[:, :, :, :, cols].reshape(length, tile).astype(F32), taps_v[:, cols],
                           both * (1.0 / length))
        gkern_v[:, :, :, :, cols] = grad.astype(BF).reshape(num_z, 2, 2, length // (4 * num_z), tile)
        return 0
    lax.fori_loop(0, group // tile, taps_back, 0)
    taps_grad.send_core()
    up[1].go(2)
    for k in range(3):
        into[k].go(1)
    taps_grad.go(0)
    up[2].go(2)
    out.go(2)
    for k in range(3):
        down[k].go(3)
    trade_dn = Trade(wire, s, column_halves(sum_dn), ends_dn)
    taps_grad.go(1)

    arrived(to_owner)

    def norm_one_back(i, gain):
        at, within = spans(i * tile, tile), spans(i % (span // tile) * tile, tile)
        across, diagonal, beside, here = (ref[within].astype(F32) for ref in (*gnorm_got, mine))
        grad = jnp.where(c == i // (span // tile), here + across, beside + diagonal)
        normal, scale = norm_parts(tok[at].astype(F32))
        part, more = norm_back(normal, scale, grad, gains[0:1])
        low_v[at] = (resid_v[at] + part).astype(BF)
        return gain + more
    gain_one = lax.fori_loop(0, rows // tile, norm_one_back, jnp.zeros((1, width), F32))
    inner.start(low_v, grad_in_o)

    gain_v[0] = jnp.concatenate([gain_one, gain_two, jnp.zeros((6, width), F32)], axis=0)
    got = [wire.start(gain_v.at[0], gain_got.at[k], peer) for k, peer in enumerate(s.mates)]
    arrived(got)
    gain_v[1] = gain_v[0] + gain_got[0] + gain_got[1] + gain_got[2]
    got = [wire.start(gain_v.at[1], gain_got.at[3], s.along["x"][0])]
    for k in range(3):
        up[k].go(3)
    rows_half = pieces // 2 * block
    column_pieces = [
        [sum_up[core * rows_half + q * block : core * rows_half + (q + 1) * block] for q in range(pieces // 2)]
        for core in range(2)
    ]
    trade_up = Trade(wire, s, column_pieces, ends_up)
    out.go(3)
    trade_out = Trade(wire, s, column_halves(sum_out), ends_out)
    arrived(got)
    gain_v[2] = gain_v[1] + gain_got[3]
    got = [wire.start(gain_v.at[2], gain_got.at[3 + k], peer) for k, peer in zip(range(1, num_z), s.along["z"])]

    for k in range(3):
        into[k].go(2)
    first, second, third = sum_in[y], sum_in[y + 1], sum_in[(y + 2) % 3]
    swap_core[0, 0], swap_core[0, 1] = first.astype(BF), second.astype(BF)
    swap_y[0] = third.astype(BF)
    swaps = [wire.start(swap_y.at[0], swap_y.at[1], s.mates[0]), wire.start(swap_y.at[0], swap_y.at[2], s.mates[1]),
             wire.start(swap_core.at[0], swap_core.at[1], s.core)]
    taps_grad.go(2)
    trade_kern = Trade(wire, s, column_halves(sum_kern), ends_kern)
    trade_dn.finish(gdn_o, turned=True)
    trade_up.finish(gup_o)
    trade_out.finish(gout_o)
    arrived(got)
    total = gain_v[2]
    for k in range(1, num_z):
        total = total + gain_got[3 + k]
    part = width // 4
    mine = total[:, 0:part]
    for k in range(1, 4):
        mine = jnp.where(me == k, total[:, k * part : (k + 1) * part], mine)
    gains_o[...] = mine[0:2]
    trade_kern.finish(gkern_o, turned=True)
    arrived(swaps)
    cut = group // 2
    for row, near, far in ((c, swap_core.at[0], swap_y.at[1]), (1 - c, swap_core.at[1], swap_y.at[2])):
        far = far[...].astype(F32)
        left = jnp.concatenate([near[0].astype(F32), far[:, 0:cut]], axis=-1)
        right = jnp.concatenate([far[:, cut:], near[1].astype(F32)], axis=-1)
        gin_o[spans(row * block, block)] = jnp.where(c == 0, left, right)
    wire.drain()
    inner.drain()


def vm(shape, dtype=BF):
    return pltpu.VMEM(tuple(shape), dtype)


VMEM_SPEC, HBM_SPEC = pl.BlockSpec(memory_space=pltpu.VMEM), pl.BlockSpec(memory_space=pl.ANY)


def layer(num_z, length, tokens, cot, w_in, w_out, w_up, w_down_t, kernel_t, gains, taps, twist, table):
    rows, width = tokens.shape
    group = width // 2
    part = w_down_t.shape[1]
    hidden = part * num_z * 2
    block = w_in.shape[0] // 2
    sds = jax.ShapeDtypeStruct
    axes = (2, num_z, 2, 2)
    units = dict(
        win=(3, block, group), wout=(block, group), wup=(hidden // width * block, group), wdown=(part // 2, group),
        kern=(kernel_t.shape[1] // 2, group),
    )
    lead = {name: axes[1:] if name in ("win", "kern") else axes for name in units}
    outs = [sds((rows, width), BF)] * 2
    outs += [sds((w.shape[0], w.shape[1]), F32) for w in (w_in, w_out, w_up, w_down_t)]
    outs += [sds((2, width // 4), F32), sds(kernel_t.shape, F32)]
    channel = vm((length, group))
    both = vm((2 * length, group))
    token = vm((rows, width))
    scratch = [vm(lead[name] + units[name]) for name in ("win", "wout", "wup", "wdown", "wdown", "kern")]
    scratch += [vm((4, 8, width // 4), F32)]
    scratch += [vm((4, block, w_in.shape[1])), vm((2, block, w_out.shape[1])), vm((2, block, w_up.shape[1])),
                vm((2, part // 2, w_down_t.shape[0])), vm((2, kernel_t.shape[1] // 2, kernel_t.shape[0])),
                vm(w_down_t.shape[::-1]), vm(kernel_t.shape[::-1])]
    scratch += [vm(table.shape), vm((3, length, group)), token, vm((length, width)), channel, both, both, both, channel,
                channel, vm((2, rows, group)), vm((rows, width), F32), token, vm((rows, hidden)), vm((rows, hidden))]
    names = ("win", "wout", "wup", "wdown", "kern")
    scratch += [vm(lead[name][:-1] + units[name]) for name in names if name != "wup"]
    blocks = {name: math.prod(lead[name]) // 2 - 1 for name in names}
    scratch += [vm((blocks[name],) + units[name]) for name in names] + [vm(units[name], F32) for name in names]
    scratch += [vm((3, 1, block, group // 2), F32), vm((3, hidden // width // 2, block, group), F32),
                vm((3, 1, part // 2, group // 2), F32), vm((3, 1, kernel_t.shape[1] // 2, group // 2), F32)]
    scratch += [vm((2, 2, block, group)), vm((3, block, group)), vm((3, 8, width), F32), vm((3 + num_z, 8, width), F32)]
    scratch += [pltpu.SemaphoreType.DMA((320,)), pltpu.SemaphoreType.DMA((320,)), pltpu.SemaphoreType.DMA((8,))]
    return pl.pallas_call(
        partial(layer_kernel, num_z, length),
        out_shape=outs,
        in_specs=[VMEM_SPEC] * 10 + [HBM_SPEC],
        out_specs=[HBM_SPEC] * 2 + [VMEM_SPEC] * 6,
        scratch_shapes=scratch,
        compiler_params=pltpu.CompilerParams(collective_id=0, has_side_effects=True, vmem_limit_bytes=63 * 2**20),
        cost_estimate=pl.CostEstimate(flops=34 * 10**9, bytes_accessed=20 * 10**6, transcendentals=2 * 10**6),
    )(tokens, cot, w_in, w_out, w_up, w_down_t, kernel_t, gains, taps, twist, table)


def publish(*arrays):
    def copy_all(*refs):
        for src, dst in zip(refs[: len(arrays)], refs[len(arrays) :]):
            dst[...] = src[...]

    return pl.pallas_call(
        copy_all,
        out_shape=[jax.ShapeDtypeStruct(a.shape, a.dtype) for a in arrays],
        in_specs=[VMEM_SPEC] * len(arrays),
        out_specs=[VMEM_SPEC] * len(arrays),
    )(*arrays)


def fits(num_dp, num_seq, tokens, w_in, w_out, w_up, w_down, kernel):
    if num_seq != 4 or num_dp % 4 or kernel.shape[0] * num_dp > 1024 or kernel.shape[0] * num_dp % 512:
        return False
    blocks = (w_in, w_out, w_up, w_down, kernel)
    return all(b.shape[0] % 32 == 0 and b.shape[1] * 2 % 128 == 0 for b in blocks) and tokens.shape[0] == 2


def body(num_dp, num_seq, tokens_in, w_in, w_out, w_up, w_down, norm_gains, kernel, taps, cotangent):
    if not fits(num_dp, num_seq, tokens_in, w_in, w_out, w_up, w_down, kernel):
        return general_body(tokens_in, w_in, w_out, w_up, w_down, norm_gains, kernel, taps, cotangent)
    width = tokens_in.shape[-1]
    length = kernel.shape[0] * num_dp
    table, twist = jnp.asarray(transform_table(length)), jnp.asarray(twist_table(length))
    tokens, cot = tokens_in.reshape(-1, width), cotangent.reshape(-1, width)
    results = layer(num_dp // 2, length, tokens, cot, w_in, w_out, w_up, w_down.T, kernel.T, norm_gains, taps[None],
                    twist, table)
    out, grad_in, gin, gout, gup, gdn, gains, gkern = publish(*results)
    return (out.reshape(tokens_in.shape), grad_in.reshape(tokens_in.shape), gin, gout, gup, gdn.T, gains, gkern.T)


def solution(mesh):
    return jax.shard_map(
        partial(body, mesh.shape["dp"], mesh.shape["seq"]),
        mesh=mesh,
        in_specs=(
            P("dp", "seq", None),
            P("dp", "seq"),
            P("dp", "seq"),
            P("dp", "seq"),
            P("dp", "seq"),
            P(None, "seq"),
            P("dp", "seq"),
            P("seq"),
            P("dp", "seq", None),
        ),
        out_specs=(
            P("dp", "seq", None),
            P("dp", "seq", None),
            P("dp", "seq"),
            P("dp", "seq"),
            P("dp", "seq"),
            P("dp", "seq"),
            P(None, "seq"),
            P("dp", "seq"),
        ),
        check_vma=False,
    )
```

```python
from functools import partial
import math

import jax
from jax.experimental import pallas as pl
from jax.experimental.pallas import tpu as pltpu
import ml_dtypes
import numpy as np
import jax.numpy as jnp
from jax import lax
from jax.sharding import PartitionSpec as P

EPSILON = 1e-05
SHRINK_SCALE = 0.003
HIGHEST = lax.Precision.HIGHEST


def norm_rows(values, gain):
    center = values - jnp.mean(values, axis=-1, keepdims=True)
    spread = jnp.mean(center * center, axis=-1, keepdims=True)
    return center * lax.rsqrt(spread + EPSILON) * gain


def shape_filter(kernel, taps):
    length = kernel.shape[0]
    position = jnp.arange(length, dtype=jnp.int32)[:, None]
    live_mask = (position < taps[None, :]).astype(kernel.dtype)
    masked = kernel * live_mask
    shrunk = masked - SHRINK_SCALE * jnp.tanh(masked / SHRINK_SCALE)
    padded = jnp.pad(shrunk, ((1, 1), (0, 0)))
    pooled = (padded[:-2] + padded[1:-1] + padded[2:]) / 3.0
    return pooled * live_mask


def gelu_tanh(values):
    return jax.nn.gelu(values, approximate=True)


def contract_rows(left, right):
    return lax.dot_general(
        left, right, (((0,), (0,)), ((), ())), preferred_element_type=jnp.float32
    )


def times_transposed(left, weight):
    return lax.dot_general(
        left, weight, (((1,), (1,)), ((), ())), preferred_element_type=jnp.float32
    )


def phase_table(count_rows, count_cols, period):
    row_index = lax.broadcasted_iota(jnp.int32, (count_rows, count_cols), 0)
    col_index = lax.broadcasted_iota(jnp.int32, (count_rows, count_cols), 1)
    angles = 2.0 * math.pi / period * (row_index * col_index % period).astype(jnp.float32)
    return (jnp.cos(angles), jnp.sin(angles))


def dft_factors(length):
    total = 2 * length
    first = max(2, total // 128)
    return (total, first, total // first)


def mix_last(field, table):
    return jnp.einsum("bckn,nm->bckm", field, table, precision=HIGHEST)


def forward_dft(field):
    batch, length, chans = field.shape
    total, first, second = dft_factors(length)
    half = first // 2
    blocks = field.reshape(batch, half, second, chans)
    cos_one, sin_one = phase_table(half, first, first)
    part_re = jnp.einsum("hk,bhnc->bckn", cos_one, blocks, precision=HIGHEST)
    part_im = -jnp.einsum("hk,bhnc->bckn", sin_one, blocks, precision=HIGHEST)
    cos_two, sin_two = phase_table(first, second, total)
    turn_re = part_re * cos_two + part_im * sin_two
    turn_im = part_im * cos_two - part_re * sin_two
    cos_three, sin_three = phase_table(second, second, second)
    spec_re = mix_last(turn_re, cos_three) + mix_last(turn_im, sin_three)
    spec_im = mix_last(turn_im, cos_three) - mix_last(turn_re, sin_three)
    return (spec_re, spec_im)


def inverse_dft(spec_re, spec_im):
    batch, chans, first, second = spec_re.shape
    total = first * second
    half = first // 2
    cos_three, sin_three = phase_table(second, second, second)
    back_re = mix_last(spec_re, cos_three) - mix_last(spec_im, sin_three)
    back_im = mix_last(spec_re, sin_three) + mix_last(spec_im, cos_three)
    cos_two, sin_two = phase_table(first, second, total)
    turn_re = back_re * cos_two - back_im * sin_two
    turn_im = back_re * sin_two + back_im * cos_two
    cos_one, sin_one = phase_table(half, first, first)
    blocks = jnp.einsum("hk,bckn->bhnc", cos_one, turn_re, precision=HIGHEST)
    blocks = blocks - jnp.einsum("hk,bckn->bhnc", sin_one, turn_im, precision=HIGHEST)
    return blocks.reshape(batch, half * second, chans) / total


def to_channels(field):
    return lax.all_to_all(field, "seq", split_axis=2, concat_axis=1, tiled=True)


def to_tokens(field):
    return lax.all_to_all(field, "seq", split_axis=1, concat_axis=2, tiled=True)


def general_body(tokens_in, w_in, w_out, w_up, w_down, norm_gains, kernel, taps, cotangent):
    w_in_rows, w_out_rows, w_up_rows, w_down_rows, gains = (
        lax.all_gather(w_in, "seq", axis=1, tiled=True),
        lax.all_gather(w_out, "seq", axis=1, tiled=True),
        lax.all_gather(w_up, "seq", axis=1, tiled=True),
        lax.all_gather(w_down, "seq", axis=1, tiled=True),
        lax.all_gather(norm_gains, "seq", axis=1, tiled=True),
    )
    full_in, full_out, full_up, full_down, kernel_cols = (
        lax.all_gather(w_in_rows, "dp", axis=0, tiled=True),
        lax.all_gather(w_out_rows, "dp", axis=0, tiled=True),
        lax.all_gather(w_up_rows, "dp", axis=0, tiled=True),
        lax.all_gather(w_down_rows, "dp", axis=0, tiled=True),
        lax.all_gather(kernel, "dp", axis=0, tiled=True),
    )
    num_seqs, local_len, width = tokens_in.shape
    total_rows = num_seqs * local_len
    inputs = tokens_in.reshape(total_rows, width).astype(jnp.float32)
    gains_wide = gains.astype(jnp.float32)
    normed, norm_back_one = jax.vjp(norm_rows, inputs, gains_wide[0])
    normed_low = normed.astype(jnp.bfloat16)
    proj = jnp.dot(normed_low, full_in, preferred_element_type=jnp.float32)
    values = proj[:, :width]
    gate_one = proj[:, width : 2 * width]
    gate_two = proj[:, 2 * width :]
    mixed_low = (gate_one * values).astype(jnp.bfloat16).reshape(num_seqs, local_len, width)
    by_channel = to_channels(mixed_low)
    filt, filter_back = jax.vjp(partial(shape_filter, taps=taps), kernel_cols.astype(jnp.float32))
    filt_re, filt_im = forward_dft(filt[None])
    sig_re, sig_im = forward_dft(by_channel.astype(jnp.float32))
    conv = inverse_dft(sig_re * filt_re - sig_im * filt_im, sig_re * filt_im + sig_im * filt_re)
    conv_tok = to_tokens(conv.astype(jnp.bfloat16)).reshape(total_rows, width).astype(jnp.float32)
    gated = (gate_two * conv_tok).astype(jnp.bfloat16)
    resid = inputs + jnp.dot(gated, full_out, preferred_element_type=jnp.float32)
    normed_two, norm_back_two = jax.vjp(norm_rows, resid, gains_wide[1])
    normed_two_low = normed_two.astype(jnp.bfloat16)
    hidden_pre = jnp.dot(normed_two_low, full_up, preferred_element_type=jnp.float32)
    active, gelu_back = jax.vjp(gelu_tanh, hidden_pre)
    active_low = active.astype(jnp.bfloat16)
    result = (resid + jnp.dot(active_low, full_down, preferred_element_type=jnp.float32)).astype(
        jnp.bfloat16
    )
    grad_rows = cotangent.reshape(total_rows, width)
    grad_down = contract_rows(active_low, grad_rows)
    grad_active = times_transposed(grad_rows, full_down)
    grad_pre = gelu_back(grad_active)[0].astype(jnp.bfloat16)
    grad_up = contract_rows(normed_two_low, grad_pre)
    grad_normed_two = times_transposed(grad_pre, full_up)
    grad_resid_part, grad_gain_two = norm_back_two(grad_normed_two)
    grad_resid = grad_rows.astype(jnp.float32) + grad_resid_part
    resid_low = grad_resid.astype(jnp.bfloat16)
    grad_outw = contract_rows(gated, resid_low)
    grad_gated = times_transposed(resid_low, full_out)
    grad_gate_two = grad_gated * conv_tok
    grad_conv = (grad_gated * gate_two).astype(jnp.bfloat16).reshape(num_seqs, local_len, width)
    grad_channel = to_channels(grad_conv).astype(jnp.float32)
    back_re, back_im = forward_dft(grad_channel)
    grad_signal = inverse_dft(
        back_re * filt_re + back_im * filt_im, back_im * filt_re - back_re * filt_im
    )
    cross_re = jnp.sum(back_re * sig_re + back_im * sig_im, axis=0, keepdims=True)
    cross_im = jnp.sum(back_im * sig_re - back_re * sig_im, axis=0, keepdims=True)
    grad_filt = inverse_dft(cross_re, cross_im)[0]
    grad_kern = filter_back(grad_filt)[0]
    grad_mixed = (
        to_tokens(grad_signal.astype(jnp.bfloat16)).reshape(total_rows, width).astype(jnp.float32)
    )
    grad_proj = jnp.concatenate([grad_mixed * gate_one, grad_mixed * values, grad_gate_two], axis=1)
    grad_proj = grad_proj.astype(jnp.bfloat16)
    grad_inw = contract_rows(normed_low, grad_proj)
    grad_normed = times_transposed(grad_proj, full_in)
    grad_input_part, grad_gain_one = norm_back_one(grad_normed)
    grad_inputs = (
        (grad_resid + grad_input_part).astype(jnp.bfloat16).reshape(num_seqs, local_len, width)
    )
    grad_gain_pair = jnp.stack([grad_gain_one, grad_gain_two])
    in_part, outw_part, up_part, down_part, kern_done = (
        lax.psum_scatter(
            grad_inw.astype(jnp.bfloat16), "dp", scatter_dimension=0, tiled=True
        ).astype(jnp.float32),
        lax.psum_scatter(
            grad_outw.astype(jnp.bfloat16), "dp", scatter_dimension=0, tiled=True
        ).astype(jnp.float32),
        lax.psum_scatter(
            grad_up.astype(jnp.bfloat16), "dp", scatter_dimension=0, tiled=True
        ).astype(jnp.float32),
        lax.psum_scatter(
            grad_down.astype(jnp.bfloat16), "dp", scatter_dimension=0, tiled=True
        ).astype(jnp.float32),
        lax.psum_scatter(
            grad_kern.astype(jnp.bfloat16), "dp", scatter_dimension=0, tiled=True
        ).astype(jnp.float32),
    )
    in_done, outw_done, up_done, down_done, gain_part = (
        lax.psum_scatter(
            in_part.astype(jnp.bfloat16), "seq", scatter_dimension=1, tiled=True
        ).astype(jnp.float32),
        lax.psum_scatter(
            outw_part.astype(jnp.bfloat16), "seq", scatter_dimension=1, tiled=True
        ).astype(jnp.float32),
        lax.psum_scatter(
            up_part.astype(jnp.bfloat16), "seq", scatter_dimension=1, tiled=True
        ).astype(jnp.float32),
        lax.psum_scatter(
            down_part.astype(jnp.bfloat16), "seq", scatter_dimension=1, tiled=True
        ).astype(jnp.float32),
        lax.psum_scatter(
            grad_gain_pair.astype(jnp.bfloat16), "seq", scatter_dimension=1, tiled=True
        ).astype(jnp.float32),
    )
    gain_done = lax.psum(gain_part, "dp")
    return (
        result.reshape(num_seqs, local_len, width),
        grad_inputs,
        in_done,
        outw_done,
        up_done,
        down_done,
        gain_done,
        kern_done,
    )


MESH = pl.DeviceIdType.MESH
BF = jnp.bfloat16
F32 = jnp.float32


class Remote:
    def __init__(self, wire, slot, src, dst, peer):
        self.wire, self.slot, self.src, self.dst, self.peer = wire, slot, src, dst, peer
        self.sent = False

    def named(self):
        return pltpu.make_async_remote_copy(
            src_ref=self.src(), dst_ref=self.dst(), send_sem=self.wire.send.at[self.slot],
            recv_sem=self.wire.recv.at[self.slot], device_id=self.peer, device_id_type=MESH,
        )

    def wait_recv(self):
        self.named().wait_recv()


class Wire:
    def __init__(self, send, recv, spots):
        self.send, self.recv, self.s, self.made = send, recv, spots, []

    def start(self, src, dst, peer, core=None, buffer=None):
        src, dst = (end if callable(end) else partial(lambda ref: ref, end) for end in (src, dst))
        copy = Remote(self, len(self.made), src, dst, peer)
        copy.buffer = buffer
        copy.named().start()
        self.made.append((core, copy))
        return copy

    def drain(self, src=None):
        made = [(core, copy) for core, copy in self.made if not copy.sent and src in (None, copy.buffer)]
        for which in (None, 0, 1):
            @self.s.on(which)
            def _():
                for core, copy in made:
                    if core == which:
                        copy.named().wait_send()
        for _, copy in made:
            copy.sent = True


class Local:
    def __init__(self, sems):
        self.sems, self.made, self.open = sems, 0, []

    def start(self, src, dst):
        copy = pltpu.make_async_copy(src, dst, self.sems.at[self.made])
        self.made += 1
        copy.start()
        self.open.append(copy)
        return copy

    def wait(self, copy):
        copy.wait()
        self.open = [other for other in self.open if other is not copy]

    def drain(self):
        for copy in list(self.open):
            self.wait(copy)


def arrived(copies):
    for copy in copies:
        copy.wait_recv()


class Spots:
    def __init__(self, num_z):
        dp, sq = lax.axis_index("dp"), lax.axis_index("seq")
        z, x, y, c = dp // 2, dp % 2, sq // 2, sq % 2
        self.num_z = num_z
        self.z, self.x, self.y, self.c = z, x, y, c
        self.own = dict(x=x, y=y, z=z)
        self.size = dict(x=2, y=2, z=num_z)
        self.core = self.at(z, x, y, 1 - c)
        self.others = dict(x=[1 - x], y=[1 - y], z=[(z + k) % num_z for k in range(1, num_z)])
        self.along = dict(
            x=[self.at(z, 1 - x, y, c)], y=[self.at(z, x, 1 - y, c)],
            z=[self.at(other, x, y, c) for other in self.others["z"]],
        )
        self.group = [((y + i) % 2, (c + j) % 2) for i, j in ((1, 0), (1, 1), (0, 1))]
        self.mates = [self.at(z, x, yy, cc) for yy, cc in self.group]

    def at(self, z, x, y, c):
        return (z * 2 + x, y * 2 + c)

    def on(self, core):
        return (lambda body: body()) if core is None else pl.when(self.c == core)

    def greet(self):
        for peer in self.along["z"] + self.along["x"] + self.mates:
            pl.semaphore_signal(pltpu.get_barrier_semaphore(), inc=1, device_id=peer, device_id_type=MESH)

    def meet(self):
        pl.semaphore_wait(pltpu.get_barrier_semaphore(), len(self.along["z"] + self.along["x"] + self.mates))


def both_cores(orders):
    return [(None, orders[0])] if len(orders) == 1 else list(enumerate(orders))


def block_index(s, axes, wide, core, at=None):
    place = {**s.own, **(at or {})}
    index = tuple(slice(None) if axis in wide else place[axis] for axis in axes)
    return index if core is None else index + (core,)


class Gather:
    def __init__(self, wire, spots, full, axes, *orders, part=(), buffer=None):
        self.buffer = buffer
        self.wire, self.s, self.full, self.axes, self.part = wire, spots, full, axes, part
        self.orders, self.last = both_cores(orders), {}

    def view(self, have):
        return self.full.at[block_index(self.s, self.axes, have, self.s.c) + self.part]

    def settle(self):
        for core, copies in self.last.items():
            self.s.on(core)(partial(arrived, copies))
        self.last = {}

    def step(self, n):
        s = self.s
        if n == len(self.orders[0][1]):
            self.settle()
            view = partial(self.view, self.axes)
            self.last[None] = [self.wire.start(view, view, s.core, buffer=self.buffer)]
            return
        before, self.last = self.last, {}
        for core, order in self.orders:
            @s.on(core)
            def _():
                arrived(before.get(core, []))
                view = partial(self.view, order[:n])
                self.last[core] = [
                    self.wire.start(view, view, peer, core, self.buffer) for peer in s.along[order[n]]
                ]

    def done(self):
        self.settle()


class Rounds:
    LAG = 2

    def __init__(self, gathers):
        self.gathers, self.now = gathers, 0

    def run(self, count=1):
        for _ in range(count):
            for step in reversed(range(4)):
                k = self.now - step * self.LAG
                if 0 <= k < len(self.gathers) and step <= len(self.gathers[k].orders[0][1]):
                    self.gathers[k].step(step)
            self.now += 1


class Scatter:
    def __init__(self, wire, spots, total, axes, orders, from_core, got, result, part=()):
        self.wire, self.s, self.total, self.axes, self.part = wire, spots, total, axes, part
        self.orders = [(core, order[::-1]) for core, order in both_cores(orders)]
        self.from_core, self.got, self.result = from_core, got, result
        self.last = {}

    def mine(self, wide, at=None):
        return self.total.at[block_index(self.s, self.axes, wide, self.s.c, at) + self.part]

    def send_core(self):
        s = self.s
        whole = (slice(None),) * (len(self.axes) - 1)
        self.last = [
            self.wire.start(self.total.at[(i,) + whole + (1 - s.c,) + self.part],
                            self.from_core.at[(i,) + whole + self.part], s.core)
            for i in range(self.from_core.shape[0])
        ]

    def add_core(self):
        arrived(self.last)
        self.last = {}
        s = self.s
        count = math.prod(s.size[axis] for axis in self.axes)

        def one(i, _):
            at, left = {}, i
            for axis in reversed(self.axes):
                at[axis], left = left % s.size[axis], left // s.size[axis]
            into = self.mine("", at)
            term = self.from_core[tuple(at[axis] for axis in self.axes) + self.part]
            into[...] = (into[...].astype(F32) + term.astype(F32)).astype(BF)
            return 0
        lax.fori_loop(0, count, one, 0)

    def stages(self, order, n):
        s = self.s
        begin = 0
        for k in range(n + 1):
            wide = sorted(order[k + 1 :])
            count = math.prod(s.size[axis] for axis in wide)
            if k < n:
                begin += count * (s.size[order[k]] - 1)
        return order[n], wide, count, begin

    def slots(self, start, count):
        return self.got.at[(start if count is None else slice(start, start + count),) + self.part]

    def send(self, n):
        s = self.s
        for core, order in self.orders:
            axis, wide, count, begin = self.stages(order, n)

            @s.on(core)
            def _():
                self.last[core] = []
                for j, (other, peer) in enumerate(zip(s.others[axis], s.along[axis])):
                    outer = s.size[wide[0]] if len(wide) == 2 else 1
                    inner = count // outer
                    for i in range(outer):
                        at = {axis: other}
                        if len(wide) == 2:
                            at[wide[0]] = i
                        start = begin + j * count + i * inner
                        src = partial(self.mine, wide[-1:], at)
                        dst = partial(self.slots, start, inner if wide else None)
                        self.last[core].append(self.wire.start(src, dst, peer, core))

    def add(self, n):
        s = self.s
        for core, order in self.orders:
            axis, wide, count, begin = self.stages(order, n)
            peers = len(s.others[axis])

            @s.on(core)
            def _():
                arrived(self.last[core])
                if n == len(order) - 1:
                    total = self.mine("")[...].astype(F32)
                    for j in range(peers):
                        total = total + self.got[(begin + j,) + self.part].astype(F32)
                    self.result[self.part or ...] = total
                    return

                def one(i, _):
                    at, left = {}, i
                    for a in reversed(wide):
                        at[a], left = left % s.size[a], left // s.size[a]
                    into = self.mine("", at)
                    total = into[...].astype(F32)
                    for j in range(peers):
                        total = total + self.got[(begin + j * count + i,) + self.part].astype(F32)
                    into[...] = total.astype(BF)
                    return 0
                lax.fori_loop(0, count, one, 0)


    def go(self, n):
        if n == 0:
            self.add_core()
        else:
            self.add(n - 1)
        if n < len(self.orders[0][1]):
            self.send(n)


class Trade:
    def __init__(self, wire, spots, halves, ends):
        self.s, self.ends, self.pieces = spots, ends, len(halves[0])
        for core in range(2):
            for i, piece in enumerate(halves[core]):
                ends[core, i] = piece
        self.copy = wire.start(ends.at[1 - spots.c], ends.at[2], spots.core)

    def finish(self, out, turned=False):
        self.copy.wait_recv()
        c = self.s.c
        own, other = (
            jnp.concatenate([self.ends[k, i] for i in range(self.pieces)], axis=-1) for k in (c, 2)
        )
        both = jnp.concatenate([jnp.where(c == 0, own, other), jnp.where(c == 0, other, own)], axis=0)
        out[...] = both.T if turned else both


def column_halves(total):
    part = total.shape[-1] // 2
    return [[total[:, core * part : (core + 1) * part]] for core in range(2)]


def row_parts(rows):
    size = rows // PARTS
    return [(slice(i * size, (i + 1) * size),) for i in range(PARTS)]


def norm_parts(values):
    center = values - jnp.mean(values, axis=-1, keepdims=True)
    spread = jnp.mean(center * center, axis=-1, keepdims=True)
    scale = lax.rsqrt(spread + EPSILON)
    return center * scale, scale


def norm_back(normal, scale, grad, gain):
    p = grad * gain
    flat = jnp.mean(p, axis=-1, keepdims=True)
    along = jnp.mean(p * normal, axis=-1, keepdims=True)
    return (p - flat - normal * along) * scale, jnp.sum(grad * normal, axis=0, keepdims=True)


def dot(left, right):
    return jnp.dot(left, right, preferred_element_type=F32)


def dot_rows(left, right):
    return lax.dot_general(left, right, (((0,), (0,)), ((), ())), preferred_element_type=F32)


def dot_cols(left, right):
    return lax.dot_general(left, right, (((1,), (1,)), ((), ())), preferred_element_type=F32)


def live_taps(kern, taps):
    position = lax.broadcasted_iota(jnp.int32, kern.shape, 0)
    return position, position.astype(F32) < taps


def pool(values, position):
    length = values.shape[0]
    before = jnp.where(position == 0, 0.0, pltpu.roll(values, 1, 0))
    after = jnp.where(position == length - 1, 0.0, pltpu.roll(values, length - 1, 0))
    return (before + values + after) / 3.0


def make_filter(kern, taps):
    position, live = live_taps(kern, taps)
    masked = jnp.where(live, kern, 0.0)
    shrunk = masked - SHRINK_SCALE * jnp.tanh(masked / SHRINK_SCALE)
    return jnp.where(live, pool(shrunk, position), 0.0)


def kernel_back(kern, taps, grad):
    position, live = live_taps(kern, taps)
    slope = jnp.tanh(jnp.where(live, kern, 0.0) / SHRINK_SCALE)
    return jnp.where(live, pool(jnp.where(live, grad, 0.0), position) * slope * slope, 0.0)


GELU_K = math.sqrt(2.0 / math.pi)


def gelu_both(v):
    square = v * v
    t = jnp.tanh(GELU_K * v * (1.0 + 0.044715 * square))
    half = 0.5 * (1.0 + t)
    slope = half + 0.5 * v * (1.0 - t * t) * (GELU_K * (1.0 + 3 * 0.044715 * square))
    return v * half, slope


def spans(start, size, step=16):
    return pl.ds(pl.multiple_of(start, step), size)


def transform_table(length):
    k = 2 * np.arange(length)[:, None] + 1
    angle = np.pi / (4 * length) * ((k * k.T) % (8 * length))
    return np.concatenate([np.cos(angle), np.sin(angle)]).astype(np.float32).astype(ml_dtypes.bfloat16)


def twist_table(length):
    angle = np.pi / (4 * length) * (2 * np.arange(length) + 1)
    return np.stack([np.cos(angle), np.sin(angle)], axis=1).astype(np.float32)


ORDER_OUT = ("zxy", "zyx")
ORDER_UP = ("zxy", "yzx")
ORDER_DOWN = ("zxy", "yzx")
BACK_OUT = ("zxy", "zyx")
BACK_UP = ("zxy", "yzx")
BACK_DOWN = ("zxy", "yzx")
PARTS = 4
STEP = 256


def layer_kernel(
    num_z, length,
    tok, cot, w_in, w_out, w_up, w_down_t, kern_t, gains_in, taps_in, twist, table_hbm,
    out_o, grad_in_o, gin_o, gout_o, gup_o, gdn_o, gains_o, gkern_o,
    win_v, wout_v, wup_v, wdown_v, gdn_v, kern_v, small_v,
    pre_in, pre_out, pre_up, pre_down, pre_kern, w_down, kern,
    table_v, proj_v, normed_own, normed_v, sig_v, spec_v, filt_v, turned_v, conv_v, gated_ch,
    gated_v, resid_v, normed_two_v, act_v, slope_v,
    core_in, core_out, core_dn, core_kern,
    got_in, got_out, got_up, got_dn, got_kern,
    sum_in, sum_out, sum_up, sum_dn, sum_kern,
    ends_out, ends_up, ends_dn, ends_kern, swap_core, swap_y,
    gain_v, gain_got,
    send, recv, local,
):
    s = Spots(num_z)
    z, x, y, c = s.z, s.x, s.y, s.c
    wire, inner = Wire(send, recv, s), Local(local)
    load_table = inner.start(table_hbm, table_v)
    rows, width = tok.shape
    group, span = width // 2, rows // 2
    hidden = act_v.shape[1]
    block = width // (4 * num_z)
    me = 2 * y + c
    chunk, home = spans(me * span, span), spans(c * span, span)
    w_down[...] = w_down_t[...].T
    kern[...] = kern_t[...].T
    small_v[me, 0:2] = gains_in[...].astype(F32)
    small_v[me, 2:3] = taps_in[...].astype(F32)
    tile = 128

    def norm_one(i, _):
        at = spans(i * tile, tile)
        resid_v[at], _ = norm_parts(tok[at].astype(F32))
        return 0
    s.greet()
    lax.fori_loop(0, rows // tile, norm_one, 0)
    s.meet()

    smalls = [wire.start(small_v.at[me], small_v.at[me], peer) for peer in s.mates]
    half = w_in.shape[0] // 2
    trade_in = [
        wire.start(w_in.at[spans(cc * half, half)], pre_in.at[me], peer) for (yy, cc), peer in zip(s.group, s.mates)
    ]
    pairs = [(kern, pre_kern), (w_out, pre_out), (w_up, pre_up), (w_down, pre_down)]
    traded = []
    for src, pre in pairs:
        half = src.shape[0] // 2
        traded.append(wire.start(src.at[spans((1 - c) * half, half)], pre.at[c], s.core))
    half = w_in.shape[0] // 2
    pre_in[me] = w_in[spans(c * half, half)]
    for src, pre in pairs:
        half = src.shape[0] // 2
        pre[c] = src[spans(c * half, half)]

    g_in = [Gather(wire, s, win_v, "zx", "zx", part=(k,), buffer="in") for k in range(3)]
    g_kern = Gather(wire, s, kern_v, "zx", "zx", buffer="kern")
    g_out = Gather(wire, s, wout_v, "yzx", *ORDER_OUT)
    parts = row_parts(wup_v.shape[-2])
    g_up = [Gather(wire, s, wup_v, "yzx", *ORDER_UP, part=part, buffer="up") for part in parts]
    g_down = [Gather(wire, s, wdown_v, "yzx", *ORDER_DOWN, part=part, buffer="down") for part in parts]
    rounds = Rounds([*g_in, g_kern, g_out, *g_up, *g_down])

    def join(i):
        traded[i].wait_recv()
        pre = pairs[i][1]
        return jnp.concatenate([pre[0], pre[1]], axis=-1)

    arrived(smalls)
    gains = jnp.concatenate([small_v[k] for k in range(4)], axis=-1)

    def normed_rows(i, _):
        at = spans(i * tile, tile)
        normed_own[at] = (resid_v[at] * gains[0:1]).astype(BF)
        return 0
    lax.fori_loop(0, rows // tile, normed_rows, 0)
    to_group = [
        wire.start(normed_own.at[spans(cc * span, span)], normed_v.at[chunk], peer, buffer="normed")
        for (yy, cc), peer in zip(s.group, s.mates)
    ]
    normed_v[chunk] = normed_own[home]
    arrived(trade_in)
    whole = jnp.concatenate([pre_in[k] for k in range(4)], axis=-1)
    for k in range(3):
        left, right = (whole[:, (2 * k + h) * group : (2 * k + h + 1) * group] for h in range(2))
        win_v[z, x, c, k] = jnp.where(y == 0, left, right)
        if k < 2:
            rounds.run()

    kern_v[z, x, c] = join(0)
    wout_v[y, z, x, c] = join(1)
    both = join(2)
    pieces = both.shape[-1] // group
    for q in range(pieces):
        wup_v[y, z, x, c, q * block : (q + 1) * block] = both[:, q * group : (q + 1) * group]
    wdown_v[y, z, x, c] = join(3)
    rounds.run(5)

    arrived(to_group)
    g_in[0].done()
    g_in[1].done()

    def project(k, at):
        return dot(normed_v[at], win_v[:, :, :, k].reshape(width, group))

    def mix(i, _):
        at = spans(i * STEP, STEP, STEP)
        value, gate = project(0, at), project(1, at)
        proj_v[0, at] = value.astype(BF)
        proj_v[1, at] = gate.astype(BF)
        sig_v[at] = (value * gate).astype(BF)
        return 0
    lax.fori_loop(0, length // STEP, mix, 0)
    rounds.run()
    g_in[2].done()

    def second_gate(i, _):
        at = spans(i * STEP, STEP, STEP)
        proj_v[2, at] = project(2, at).astype(BF)
        return 0
    lax.fori_loop(0, length // STEP, second_gate, 0)
    rounds.run()

    g_kern.done()
    taps_v = gain_v.at[2, 0:1]
    taps_v[:, 0:group] = jnp.concatenate([small_v[2 * y], small_v[2 * y + 1]], axis=-1)[2:3]

    def shape_taps(j, _):
        cols = spans(j * tile, tile, tile)
        filt = make_filter(kern_v[:, :, :, :, cols].reshape(length, tile).astype(F32), taps_v[:, cols])
        gated_ch[:, cols] = filt.astype(BF)
        return 0
    lax.fori_loop(0, group // tile, shape_taps, 0)
    inner.wait(load_table)

    def spectrum(i, _):
        real, imag = spans(i * STEP, STEP, STEP), spans(length + i * STEP, STEP, STEP)
        re, im = dot(table_v[real], gated_ch[...]), dot(table_v[imag], gated_ch[...])
        cosine, sine = twist[real, 0:1], twist[real, 1:2]
        filt_v[real] = (re * cosine + im * sine).astype(BF)
        filt_v[imag] = (im * cosine - re * sine).astype(BF)
        return 0
    lax.fori_loop(0, length // STEP, spectrum, 0)
    rounds.run()

    def convolve(i, _):
        real, imag = spans(i * STEP, STEP, STEP), spans(length + i * STEP, STEP, STEP)
        re_s, im_s = dot(table_v[real], sig_v[...]), dot(table_v[imag], sig_v[...])
        spec_v[real] = re_s.astype(BF)
        spec_v[imag] = im_s.astype(BF)
        re_f, im_f = filt_v[real].astype(F32), filt_v[imag].astype(F32)
        turned_v[real] = (re_s * re_f - im_s * im_f).astype(BF)
        turned_v[imag] = (re_s * im_f + im_s * re_f).astype(BF)
        return 0
    lax.fori_loop(0, length // STEP, convolve, 0)
    rounds.run()

    def back(i, _):
        at, imag = spans(i * STEP, STEP, STEP), spans(length + i * STEP, STEP, STEP)
        both = dot(table_v[at], turned_v[0:length]) + dot(table_v[imag], turned_v[length:])
        conv = (both * (1.0 / length)).astype(BF)
        conv_v[at] = conv
        gated_ch[at] = (proj_v[2, at].astype(F32) * conv.astype(F32)).astype(BF)
        return 0
    lax.fori_loop(0, length // STEP, back, 0)

    to_tokens = [
        wire.start(gated_ch.at[spans((2 * yy + cc) * span, span)], gated_v.at[y, home], peer, buffer="gated")
        for (yy, cc), peer in zip(s.group, s.mates)
    ]
    gated_v[y, home] = gated_ch[chunk]
    rounds.run()
    g_out.done()
    rounds.run()
    arrived(to_tokens)

    for k in range(2):
        cols = slice(k * group, (k + 1) * group)
        mixed = sum(
            dot(gated_v[h], wout_v[k, h * num_z // 2 : (h + 1) * num_z // 2].reshape(group, group)) for h in range(2)
        )
        resid_v[:, cols] = tok[:, cols].astype(F32) + mixed

    def norm_two(i, _):
        at = spans(i * tile, tile)
        normed, _ = norm_parts(resid_v[at])
        normed_two_v[at] = (normed * gains[1:2]).astype(BF)
        return 0
    lax.fori_loop(0, rows // tile, norm_two, 0)

    def piece(ref, j):
        return ref.at[j // pieces, :, :, :, spans((j % pieces) * block, block)]

    for q in range(pieces):
        g_up[q].done()

        def feed(i, _):
            j = i // 2 * pieces + q
            at, cols = spans(i % 2 * span, span), spans(j * group, group, 128)
            act, slope = gelu_both(dot(normed_two_v[at], piece(wup_v, j)[...].reshape(width, group)))
            act_v[at, cols] = act.astype(BF)
            slope_v[at, cols] = slope.astype(BF)
            return 0
        lax.fori_loop(0, 4, feed, 0)
        rounds.run()

    down = [Scatter(wire, s, gdn_v, "yzx", BACK_DOWN, core_dn, got_dn, sum_dn, part=part) for part in parts]
    deep = hidden // (2 * num_z)

    def down_grad(i, _):
        grad = dot_rows(act_v[:, spans(i * deep, deep, 128)], cot[...]).astype(BF)
        for h in range(2):
            gdn_v[h, i // 2, i % 2] = grad[:, h * group : (h + 1) * group].reshape(2, deep // 2, group)
        return 0
    lax.fori_loop(0, 2 * num_z, down_grad, 0)
    rounds.run()
    for g in down:
        g.send_core()
    rounds.run()
    for g in g_down:
        g.done()
    down[0].go(0)
    down[1].go(0)

    def pre_grad(i, _):
        at, cols = spans(i // num_z * span, span), spans(i % num_z * 2 * deep, 2 * deep, 128)
        grad = sum(
            dot_cols(cot[at, h * group : (h + 1) * group], wdown_v[h, i % num_z].reshape(2 * deep, group))
            for h in range(2)
        )
        slope_v[at, cols] = (slope_v[at, cols].astype(F32) * grad).astype(BF)
        return 0
    lax.fori_loop(0, 2 * num_z, pre_grad, 0)
    gpre_v = slope_v
    down[2].go(0)
    down[3].go(0)

    wire.drain("normed")
    low_v = normed_own
    gnorm_got = [[turned_v.at[(2 * i + h) * span : (2 * i + h + 1) * span] for h in range(2)] for i in range(3)]
    gout_v, gup_v, gin_v = wdown_v.at[:, :, :, :, 0:block], wup_v, win_v
    gch_v, gkern_v = sig_v, kern_v
    ggate_v = gated_ch
    up = [Scatter(wire, s, gup_v, "yzx", BACK_UP, core_dn, got_up, sum_up, part=part) for part in parts]
    out = Scatter(wire, s, gout_v, "yzx", BACK_OUT, core_out, got_out, sum_out)
    into = [Scatter(wire, s, gin_v, "zx", ("zx",), core_in, got_in, sum_in, part=(k,)) for k in range(3)]
    taps_grad = Scatter(wire, s, gkern_v, "zx", ("zx",), core_kern, got_kern, sum_kern)


    def norm_two_back(i, gain):
        at = spans(i * span, span)

        grad = sum(
            dot_cols(gpre_v[at, j * group : (j + 1) * group], piece(wup_v, j)[...].reshape(width, group))
            for j in range(2 * pieces)
        )
        normal, scale = norm_parts(resid_v[at])
        part, more = norm_back(normal, scale, grad, gains[1:2])
        low_v[at] = (cot[at].astype(F32) + part).astype(BF)
        return gain + more
    gain_two = lax.fori_loop(0, 2, norm_two_back, jnp.zeros((1, width), F32))

    wire.drain("gated")
    for h in range(2):
        grad = sum(
            dot_cols(
                low_v[:, k * group : (k + 1) * group],
                wout_v[k, h * num_z // 2 : (h + 1) * num_z // 2].reshape(group, group),
            )
            for k in range(2)
        )
        ggate_v[h * rows : (h + 1) * rows] = grad.astype(BF)
    to_channels = [
        wire.start(ggate_v.at[spans(yy * rows + cc * span, span)], gch_v.at[chunk], peer)
        for (yy, cc), peer in zip(s.group, s.mates)
    ]
    gch_v[chunk] = ggate_v[spans(y * rows + c * span, span)]
    wire.drain("up")

    def up_grad(q, yy, _):
        j = yy * pieces + q
        grad = dot_rows(normed_two_v[...], gpre_v[:, spans(j * group, group, 128)]).astype(BF)
        piece(gup_v, j)[...] = grad.reshape(num_z, 2, 2, block, group)
        return 0

    for q in range(pieces):
        lax.fori_loop(0, 2, partial(up_grad, q), 0)
        if q == 0:
            arrived(to_channels[2:])
        up[q].send_core()
        if q % 2:
            down[q - 1].go(1)
            down[q].go(1)
            up[q - 1].go(0)

    def down_out(i, _):
        at = spans(i * span, span)
        grown = jnp.concatenate([dot(act_v[at], wdown_v[h].reshape(hidden, group)) for h in range(2)], axis=-1)
        act_v[at, 0:width] = (resid_v[at] + grown).astype(BF)
        return 0
    lax.fori_loop(0, 2, down_out, 0)
    inner.start(act_v.at[:, 0:width], out_o)
    up[1].go(0)
    up[3].go(0)
    wire.drain("down")

    def out_grad(i, _):
        h, k = i // 2, i % 2
        grad = dot_rows(gated_v[h], low_v[:, spans(k * group, group, 128)]).astype(BF)
        gout_v[k, pl.ds(h * (num_z // 2), num_z // 2)] = grad.reshape(num_z // 2, 2, 2, block, group)
        return 0
    lax.fori_loop(0, 4, out_grad, 0)
    out.send_core()
    down[0].go(2)
    down[1].go(2)

    arrived(to_channels[:2])

    def gate(i, _):
        at = spans(i * STEP, STEP, STEP)
        grad = gch_v[at].astype(F32)
        gch_v[at] = (grad * proj_v[2, at].astype(F32)).astype(BF)
        proj_v[2, at] = (grad * conv_v[at].astype(F32)).astype(BF)
        return 0
    lax.fori_loop(0, length // STEP, gate, 0)

    wire.drain("in")

    def in_grad(k):
        grad = dot_rows(normed_v[...], proj_v[k]).astype(BF)
        gin_v[:, :, :, k] = grad.reshape(num_z, 2, 2, block, group)
        into[k].send_core()

    def turn(i, _):
        real, imag = spans(i * STEP, STEP, STEP), spans(length + i * STEP, STEP, STEP)
        re, im = dot(table_v[real], gch_v[...]), dot(table_v[imag], gch_v[...])
        re_f, im_f = filt_v[real].astype(F32), filt_v[imag].astype(F32)
        filt_v[real] = (re_f * re + im_f * im).astype(BF)
        filt_v[imag] = (re_f * im - im_f * re).astype(BF)
        re_s, im_s = spec_v[real].astype(F32), spec_v[imag].astype(F32)
        re_k, im_k = re_s * re + im_s * im, re_s * im - im_s * re
        cosine, sine = twist[real, 0:1], twist[real, 1:2]
        spec_v[real] = (re_k * cosine - im_k * sine).astype(BF)
        spec_v[imag] = (im_k * cosine + re_k * sine).astype(BF)
        return 0
    lax.fori_loop(0, length // STEP, turn, 0)
    down[2].go(2)
    down[3].go(2)
    up[0].go(1)
    up[1].go(1)
    out.go(0)

    def signal_back(i, _):
        at, imag = spans(i * STEP, STEP, STEP), spans(length + i * STEP, STEP, STEP)
        both = dot(table_v[at], filt_v[0:length]) + dot(table_v[imag], filt_v[length:])
        grad = (both * (1.0 / length)).astype(BF).astype(F32)
        value, first = proj_v[0, at].astype(F32), proj_v[1, at].astype(F32)
        proj_v[0, at] = (grad * first).astype(BF)
        proj_v[1, at] = (grad * value).astype(BF)
        return 0
    lax.fori_loop(0, length // STEP, signal_back, 0)

    def part_at(j, h):
        return gpre_v.at[spans(j % 2 * span, span), spans(j // 2 * width + h * group, group, 128)]

    to_owner = []
    for h in range(2):
        grad = sum(
            dot_cols(proj_v[k], win_v[h * num_z // 2 : (h + 1) * num_z // 2, :, :, k].reshape(group, group))
            for k in range(3)
        ).astype(BF)
        for j in range(4):
            part_at(j, h)[...] = grad[j * span : (j + 1) * span]
        to_owner += [
            wire.start(partial(part_at, 2 * yy + cc, h), gnorm_got[i][h], peer)
            for i, ((yy, cc), peer) in enumerate(zip(s.group, s.mates))
        ]

    up[2].go(1)
    up[3].go(1)
    for k in range(3):
        in_grad(k)
    up[0].go(2)
    for k in range(3):
        into[k].go(0)
    up[1].go(2)
    out.go(1)

    wire.drain("kern")

    def taps_back(j, _):
        cols = spans(j * tile, tile, tile)
        both = dot(table_v[0:length], spec_v[0:length, cols]) + dot(table_v[length:], spec_v[length:, cols])
        grad = kernel_back(kern_v[:, :, :, :, cols].reshape(length, tile).astype(F32), taps_v[:, cols],
                           both * (1.0 / length))
        gkern_v[:, :, :, :, cols] = grad.astype(BF).reshape(num_z, 2, 2, length // (4 * num_z), tile)
        return 0
    lax.fori_loop(0, group // tile, taps_back, 0)
    taps_grad.send_core()
    for k in range(3):
        into[k].go(1)
    taps_grad.go(0)
    up[2].go(2)
    up[3].go(2)
    for k in range(4):
        down[k].go(3)
    trade_dn = Trade(wire, s, column_halves(sum_dn), ends_dn)
    taps_grad.go(1)
    out.go(2)

    arrived(to_owner)

    def norm_one_back(i, gain):
        at, within = spans(i * tile, tile), spans(i % (span // tile) * tile, tile)
        across, diagonal, beside = (
            jnp.concatenate([ref[within].astype(F32) for ref in pair], axis=-1) for pair in gnorm_got
        )
        here = jnp.concatenate([part_at(me, h)[within].astype(F32) for h in range(2)], axis=-1)
        grad = jnp.where(c == i // (span // tile), here + across, beside + diagonal)
        normal, scale = norm_parts(tok[at].astype(F32))
        part, more = norm_back(normal, scale, grad, gains[0:1])
        low_v[at] = (low_v[at].astype(F32) + part).astype(BF)
        return gain + more
    gain_one = lax.fori_loop(0, rows // tile, norm_one_back, jnp.zeros((1, width), F32))
    inner.start(low_v, grad_in_o)

    gain_v[0] = jnp.concatenate([gain_one, gain_two, jnp.zeros((6, width), F32)], axis=0)
    got = [wire.start(gain_v.at[0], gain_got.at[k], peer) for k, peer in enumerate(s.mates)]
    arrived(got)
    gain_v[1] = gain_v[0] + gain_got[0] + gain_got[1] + gain_got[2]
    got = [wire.start(gain_v.at[1], gain_got.at[3], s.along["x"][0])]
    for k in range(4):
        up[k].go(3)
    rows_half = pieces // 2 * block
    column_pieces = [
        [sum_up[core * rows_half + q * block : core * rows_half + (q + 1) * block] for q in range(pieces // 2)]
        for core in range(2)
    ]
    trade_up = Trade(wire, s, column_pieces, ends_up)
    out.go(3)
    trade_out = Trade(wire, s, column_halves(sum_out), ends_out)
    arrived(got)
    gain_v[2] = gain_v[1] + gain_got[3]
    got = [wire.start(gain_v.at[2], gain_got.at[3 + k], peer) for k, peer in zip(range(1, num_z), s.along["z"])]

    for k in range(3):
        into[k].go(2)
    first, second, third = sum_in[y], sum_in[y + 1], sum_in[(y + 2) % 3]
    swap_core[0, 0], swap_core[0, 1] = first.astype(BF), second.astype(BF)
    swap_y[0] = third.astype(BF)
    swaps = [wire.start(swap_y.at[0], swap_y.at[1], s.mates[0]), wire.start(swap_y.at[0], swap_y.at[2], s.mates[1]),
             wire.start(swap_core.at[0], swap_core.at[1], s.core)]
    taps_grad.go(2)
    trade_kern = Trade(wire, s, column_halves(sum_kern), ends_kern)
    trade_dn.finish(gdn_o, turned=True)
    trade_up.finish(gup_o)
    trade_out.finish(gout_o)
    arrived(got)
    total = gain_v[2]
    for k in range(1, num_z):
        total = total + gain_got[3 + k]
    part = width // 4
    mine = total[:, 0:part]
    for k in range(1, 4):
        mine = jnp.where(me == k, total[:, k * part : (k + 1) * part], mine)
    gains_o[...] = mine[0:2]
    trade_kern.finish(gkern_o, turned=True)
    arrived(swaps)
    cut = group // 2
    for row, near, far in ((c, swap_core.at[0], swap_y.at[1]), (1 - c, swap_core.at[1], swap_y.at[2])):
        far = far[...].astype(F32)
        left = jnp.concatenate([near[0].astype(F32), far[:, 0:cut]], axis=-1)
        right = jnp.concatenate([far[:, cut:], near[1].astype(F32)], axis=-1)
        gin_o[spans(row * block, block)] = jnp.where(c == 0, left, right)
    wire.drain()
    inner.drain()


def vm(shape, dtype=BF):
    return pltpu.VMEM(tuple(shape), dtype)


VMEM_SPEC, HBM_SPEC = pl.BlockSpec(memory_space=pltpu.VMEM), pl.BlockSpec(memory_space=pl.ANY)


def layer(num_z, length, tokens, cot, w_in, w_out, w_up, w_down_t, kernel_t, gains, taps, twist, table):
    rows, width = tokens.shape
    group = width // 2
    part = w_down_t.shape[1]
    hidden = part * num_z * 2
    block = w_in.shape[0] // 2
    sds = jax.ShapeDtypeStruct
    axes = (2, num_z, 2, 2)
    units = dict(
        win=(3, block, group), wout=(block, group), wup=(hidden // width * block, group), wdown=(part // 2, group),
        kern=(kernel_t.shape[1] // 2, group),
    )
    lead = {name: axes[1:] if name in ("win", "kern") else axes for name in units}
    outs = [sds((rows, width), BF)] * 2
    outs += [sds((w.shape[0], w.shape[1]), F32) for w in (w_in, w_out, w_up, w_down_t)]
    outs += [sds((2, width // 4), F32), sds(kernel_t.shape, F32)]
    channel = vm((length, group))
    both = vm((2 * length, group))
    token = vm((rows, width))
    scratch = [vm(lead[name] + units[name]) for name in ("win", "wout", "wup", "wdown", "wdown", "kern")]
    scratch += [vm((4, 8, width // 4), F32)]
    scratch += [vm((4, block, w_in.shape[1])), vm((2, block, w_out.shape[1])), vm((2, block, w_up.shape[1])),
                vm((2, part // 2, w_down_t.shape[0])), vm((2, kernel_t.shape[1] // 2, kernel_t.shape[0])),
                vm(w_down_t.shape[::-1]), vm(kernel_t.shape[::-1])]
    scratch += [vm(table.shape), vm((3, length, group)), token, vm((length, width)), channel, both, both, both, channel,
                channel, vm((2, rows, group)), vm((rows, width), F32), token, vm((rows, hidden)), vm((rows, hidden))]
    names = ("win", "wout", "wup", "wdown", "kern")
    scratch += [vm(lead[name][:-1] + units[name]) for name in names if name != "wup"]
    blocks = {name: math.prod(lead[name]) // 2 - 1 for name in names}
    scratch += [vm((blocks[name],) + units[name]) for name in names] + [vm(units[name], F32) for name in names]
    scratch += [vm((3, 1, block, group // 2), F32), vm((3, hidden // width // 2, block, group), F32),
                vm((3, 1, part // 2, group // 2), F32), vm((3, 1, kernel_t.shape[1] // 2, group // 2), F32)]
    scratch += [vm((2, 2, block, group)), vm((3, block, group)), vm((3, 8, width), F32), vm((3 + num_z, 8, width), F32)]
    scratch += [pltpu.SemaphoreType.DMA((320,)), pltpu.SemaphoreType.DMA((320,)), pltpu.SemaphoreType.DMA((8,))]
    return pl.pallas_call(
        partial(layer_kernel, num_z, length),
        out_shape=outs,
        in_specs=[VMEM_SPEC] * 10 + [HBM_SPEC],
        out_specs=[HBM_SPEC] * 2 + [VMEM_SPEC] * 6,
        scratch_shapes=scratch,
        compiler_params=pltpu.CompilerParams(collective_id=0, has_side_effects=True, vmem_limit_bytes=67 * 10**6),
        cost_estimate=pl.CostEstimate(flops=34 * 10**9, bytes_accessed=20 * 10**6, transcendentals=2 * 10**6),
    )(tokens, cot, w_in, w_out, w_up, w_down_t, kernel_t, gains, taps, twist, table)


def publish(*arrays):
    def copy_all(*refs):
        for src, dst in zip(refs[: len(arrays)], refs[len(arrays) :]):
            dst[...] = src[...]

    return pl.pallas_call(
        copy_all,
        out_shape=[jax.ShapeDtypeStruct(a.shape, a.dtype) for a in arrays],
        in_specs=[VMEM_SPEC] * len(arrays),
        out_specs=[VMEM_SPEC] * len(arrays),
    )(*arrays)


def fits(num_dp, num_seq, tokens, w_in, w_out, w_up, w_down, kernel):
    if num_seq != 4 or num_dp % 4 or kernel.shape[0] * num_dp > 1024 or kernel.shape[0] * num_dp % 512:
        return False
    blocks = (w_in, w_out, w_up, w_down, kernel)
    return all(b.shape[0] % 32 == 0 and b.shape[1] * 2 % 128 == 0 for b in blocks) and tokens.shape[0] == 2


def body(num_dp, num_seq, tokens_in, w_in, w_out, w_up, w_down, norm_gains, kernel, taps, cotangent):
    if not fits(num_dp, num_seq, tokens_in, w_in, w_out, w_up, w_down, kernel):
        return general_body(tokens_in, w_in, w_out, w_up, w_down, norm_gains, kernel, taps, cotangent)
    width = tokens_in.shape[-1]
    length = kernel.shape[0] * num_dp
    table, twist = jnp.asarray(transform_table(length)), jnp.asarray(twist_table(length))
    tokens, cot = tokens_in.reshape(-1, width), cotangent.reshape(-1, width)
    results = layer(num_dp // 2, length, tokens, cot, w_in, w_out, w_up, w_down.T, kernel.T, norm_gains, taps[None],
                    twist, table)
    out, grad_in, gin, gout, gup, gdn, gains, gkern = publish(*results)
    return (out.reshape(tokens_in.shape), grad_in.reshape(tokens_in.shape), gin, gout, gup, gdn.T, gains, gkern.T)


def solution(mesh):
    return jax.shard_map(
        partial(body, mesh.shape["dp"], mesh.shape["seq"]),
        mesh=mesh,
        in_specs=(
            P("dp", "seq", None),
            P("dp", "seq"),
            P("dp", "seq"),
            P("dp", "seq"),
            P("dp", "seq"),
            P(None, "seq"),
            P("dp", "seq"),
            P("seq"),
            P("dp", "seq", None),
        ),
        out_specs=(
            P("dp", "seq", None),
            P("dp", "seq", None),
            P("dp", "seq"),
            P("dp", "seq"),
            P("dp", "seq"),
            P("dp", "seq"),
            P(None, "seq"),
            P("dp", "seq"),
        ),
        check_vma=False,
    )
```

```python
from functools import partial
import math

import jax
from jax.experimental import pallas as pl
from jax.experimental.pallas import tpu as pltpu
import ml_dtypes
import numpy as np
import jax.numpy as jnp
from jax import lax
from jax.sharding import PartitionSpec as P

EPSILON = 1e-05
SHRINK_SCALE = 0.003
HIGHEST = lax.Precision.HIGHEST


def norm_rows(values, gain):
    center = values - jnp.mean(values, axis=-1, keepdims=True)
    spread = jnp.mean(center * center, axis=-1, keepdims=True)
    return center * lax.rsqrt(spread + EPSILON) * gain


def shape_filter(kernel, taps):
    length = kernel.shape[0]
    position = jnp.arange(length, dtype=jnp.int32)[:, None]
    live_mask = (position < taps[None, :]).astype(kernel.dtype)
    masked = kernel * live_mask
    shrunk = masked - SHRINK_SCALE * jnp.tanh(masked / SHRINK_SCALE)
    padded = jnp.pad(shrunk, ((1, 1), (0, 0)))
    pooled = (padded[:-2] + padded[1:-1] + padded[2:]) / 3.0
    return pooled * live_mask


def gelu_tanh(values):
    return jax.nn.gelu(values, approximate=True)


def contract_rows(left, right):
    return lax.dot_general(
        left, right, (((0,), (0,)), ((), ())), preferred_element_type=jnp.float32
    )


def times_transposed(left, weight):
    return lax.dot_general(
        left, weight, (((1,), (1,)), ((), ())), preferred_element_type=jnp.float32
    )


def phase_table(count_rows, count_cols, period):
    row_index = lax.broadcasted_iota(jnp.int32, (count_rows, count_cols), 0)
    col_index = lax.broadcasted_iota(jnp.int32, (count_rows, count_cols), 1)
    angles = 2.0 * math.pi / period * (row_index * col_index % period).astype(jnp.float32)
    return (jnp.cos(angles), jnp.sin(angles))


def dft_factors(length):
    total = 2 * length
    first = max(2, total // 128)
    return (total, first, total // first)


def mix_last(field, table):
    return jnp.einsum("bckn,nm->bckm", field, table, precision=HIGHEST)


def forward_dft(field):
    batch, length, chans = field.shape
    total, first, second = dft_factors(length)
    half = first // 2
    blocks = field.reshape(batch, half, second, chans)
    cos_one, sin_one = phase_table(half, first, first)
    part_re = jnp.einsum("hk,bhnc->bckn", cos_one, blocks, precision=HIGHEST)
    part_im = -jnp.einsum("hk,bhnc->bckn", sin_one, blocks, precision=HIGHEST)
    cos_two, sin_two = phase_table(first, second, total)
    turn_re = part_re * cos_two + part_im * sin_two
    turn_im = part_im * cos_two - part_re * sin_two
    cos_three, sin_three = phase_table(second, second, second)
    spec_re = mix_last(turn_re, cos_three) + mix_last(turn_im, sin_three)
    spec_im = mix_last(turn_im, cos_three) - mix_last(turn_re, sin_three)
    return (spec_re, spec_im)


def inverse_dft(spec_re, spec_im):
    batch, chans, first, second = spec_re.shape
    total = first * second
    half = first // 2
    cos_three, sin_three = phase_table(second, second, second)
    back_re = mix_last(spec_re, cos_three) - mix_last(spec_im, sin_three)
    back_im = mix_last(spec_re, sin_three) + mix_last(spec_im, cos_three)
    cos_two, sin_two = phase_table(first, second, total)
    turn_re = back_re * cos_two - back_im * sin_two
    turn_im = back_re * sin_two + back_im * cos_two
    cos_one, sin_one = phase_table(half, first, first)
    blocks = jnp.einsum("hk,bckn->bhnc", cos_one, turn_re, precision=HIGHEST)
    blocks = blocks - jnp.einsum("hk,bckn->bhnc", sin_one, turn_im, precision=HIGHEST)
    return blocks.reshape(batch, half * second, chans) / total


def to_channels(field):
    return lax.all_to_all(field, "seq", split_axis=2, concat_axis=1, tiled=True)


def to_tokens(field):
    return lax.all_to_all(field, "seq", split_axis=1, concat_axis=2, tiled=True)


def general_body(tokens_in, w_in, w_out, w_up, w_down, norm_gains, kernel, taps, cotangent):
    w_in_rows, w_out_rows, w_up_rows, w_down_rows, gains = (
        lax.all_gather(w_in, "seq", axis=1, tiled=True),
        lax.all_gather(w_out, "seq", axis=1, tiled=True),
        lax.all_gather(w_up, "seq", axis=1, tiled=True),
        lax.all_gather(w_down, "seq", axis=1, tiled=True),
        lax.all_gather(norm_gains, "seq", axis=1, tiled=True),
    )
    full_in, full_out, full_up, full_down, kernel_cols = (
        lax.all_gather(w_in_rows, "dp", axis=0, tiled=True),
        lax.all_gather(w_out_rows, "dp", axis=0, tiled=True),
        lax.all_gather(w_up_rows, "dp", axis=0, tiled=True),
        lax.all_gather(w_down_rows, "dp", axis=0, tiled=True),
        lax.all_gather(kernel, "dp", axis=0, tiled=True),
    )
    num_seqs, local_len, width = tokens_in.shape
    total_rows = num_seqs * local_len
    inputs = tokens_in.reshape(total_rows, width).astype(jnp.float32)
    gains_wide = gains.astype(jnp.float32)
    normed, norm_back_one = jax.vjp(norm_rows, inputs, gains_wide[0])
    normed_low = normed.astype(jnp.bfloat16)
    proj = jnp.dot(normed_low, full_in, preferred_element_type=jnp.float32)
    values = proj[:, :width]
    gate_one = proj[:, width : 2 * width]
    gate_two = proj[:, 2 * width :]
    mixed_low = (gate_one * values).astype(jnp.bfloat16).reshape(num_seqs, local_len, width)
    by_channel = to_channels(mixed_low)
    filt, filter_back = jax.vjp(partial(shape_filter, taps=taps), kernel_cols.astype(jnp.float32))
    filt_re, filt_im = forward_dft(filt[None])
    sig_re, sig_im = forward_dft(by_channel.astype(jnp.float32))
    conv = inverse_dft(sig_re * filt_re - sig_im * filt_im, sig_re * filt_im + sig_im * filt_re)
    conv_tok = to_tokens(conv.astype(jnp.bfloat16)).reshape(total_rows, width).astype(jnp.float32)
    gated = (gate_two * conv_tok).astype(jnp.bfloat16)
    resid = inputs + jnp.dot(gated, full_out, preferred_element_type=jnp.float32)
    normed_two, norm_back_two = jax.vjp(norm_rows, resid, gains_wide[1])
    normed_two_low = normed_two.astype(jnp.bfloat16)
    hidden_pre = jnp.dot(normed_two_low, full_up, preferred_element_type=jnp.float32)
    active, gelu_back = jax.vjp(gelu_tanh, hidden_pre)
    active_low = active.astype(jnp.bfloat16)
    result = (resid + jnp.dot(active_low, full_down, preferred_element_type=jnp.float32)).astype(
        jnp.bfloat16
    )
    grad_rows = cotangent.reshape(total_rows, width)
    grad_down = contract_rows(active_low, grad_rows)
    grad_active = times_transposed(grad_rows, full_down)
    grad_pre = gelu_back(grad_active)[0].astype(jnp.bfloat16)
    grad_up = contract_rows(normed_two_low, grad_pre)
    grad_normed_two = times_transposed(grad_pre, full_up)
    grad_resid_part, grad_gain_two = norm_back_two(grad_normed_two)
    grad_resid = grad_rows.astype(jnp.float32) + grad_resid_part
    resid_low = grad_resid.astype(jnp.bfloat16)
    grad_outw = contract_rows(gated, resid_low)
    grad_gated = times_transposed(resid_low, full_out)
    grad_gate_two = grad_gated * conv_tok
    grad_conv = (grad_gated * gate_two).astype(jnp.bfloat16).reshape(num_seqs, local_len, width)
    grad_channel = to_channels(grad_conv).astype(jnp.float32)
    back_re, back_im = forward_dft(grad_channel)
    grad_signal = inverse_dft(
        back_re * filt_re + back_im * filt_im, back_im * filt_re - back_re * filt_im
    )
    cross_re = jnp.sum(back_re * sig_re + back_im * sig_im, axis=0, keepdims=True)
    cross_im = jnp.sum(back_im * sig_re - back_re * sig_im, axis=0, keepdims=True)
    grad_filt = inverse_dft(cross_re, cross_im)[0]
    grad_kern = filter_back(grad_filt)[0]
    grad_mixed = (
        to_tokens(grad_signal.astype(jnp.bfloat16)).reshape(total_rows, width).astype(jnp.float32)
    )
    grad_proj = jnp.concatenate([grad_mixed * gate_one, grad_mixed * values, grad_gate_two], axis=1)
    grad_proj = grad_proj.astype(jnp.bfloat16)
    grad_inw = contract_rows(normed_low, grad_proj)
    grad_normed = times_transposed(grad_proj, full_in)
    grad_input_part, grad_gain_one = norm_back_one(grad_normed)
    grad_inputs = (
        (grad_resid + grad_input_part).astype(jnp.bfloat16).reshape(num_seqs, local_len, width)
    )
    grad_gain_pair = jnp.stack([grad_gain_one, grad_gain_two])
    in_part, outw_part, up_part, down_part, kern_done = (
        lax.psum_scatter(
            grad_inw.astype(jnp.bfloat16), "dp", scatter_dimension=0, tiled=True
        ).astype(jnp.float32),
        lax.psum_scatter(
            grad_outw.astype(jnp.bfloat16), "dp", scatter_dimension=0, tiled=True
        ).astype(jnp.float32),
        lax.psum_scatter(
            grad_up.astype(jnp.bfloat16), "dp", scatter_dimension=0, tiled=True
        ).astype(jnp.float32),
        lax.psum_scatter(
            grad_down.astype(jnp.bfloat16), "dp", scatter_dimension=0, tiled=True
        ).astype(jnp.float32),
        lax.psum_scatter(
            grad_kern.astype(jnp.bfloat16), "dp", scatter_dimension=0, tiled=True
        ).astype(jnp.float32),
    )
    in_done, outw_done, up_done, down_done, gain_part = (
        lax.psum_scatter(
            in_part.astype(jnp.bfloat16), "seq", scatter_dimension=1, tiled=True
        ).astype(jnp.float32),
        lax.psum_scatter(
            outw_part.astype(jnp.bfloat16), "seq", scatter_dimension=1, tiled=True
        ).astype(jnp.float32),
        lax.psum_scatter(
            up_part.astype(jnp.bfloat16), "seq", scatter_dimension=1, tiled=True
        ).astype(jnp.float32),
        lax.psum_scatter(
            down_part.astype(jnp.bfloat16), "seq", scatter_dimension=1, tiled=True
        ).astype(jnp.float32),
        lax.psum_scatter(
            grad_gain_pair.astype(jnp.bfloat16), "seq", scatter_dimension=1, tiled=True
        ).astype(jnp.float32),
    )
    gain_done = lax.psum(gain_part, "dp")
    return (
        result.reshape(num_seqs, local_len, width),
        grad_inputs,
        in_done,
        outw_done,
        up_done,
        down_done,
        gain_done,
        kern_done,
    )


MESH = pl.DeviceIdType.MESH
BF = jnp.bfloat16
F32 = jnp.float32


class Remote:
    def __init__(self, wire, slot, src, dst, peer):
        self.wire, self.slot, self.src, self.dst, self.peer = wire, slot, src, dst, peer
        self.sent = False

    def named(self):
        return pltpu.make_async_remote_copy(
            src_ref=self.src(), dst_ref=self.dst(), send_sem=self.wire.send.at[self.slot],
            recv_sem=self.wire.recv.at[self.slot], device_id=self.peer, device_id_type=MESH,
        )

    def wait_recv(self):
        self.named().wait_recv()


class Wire:
    def __init__(self, send, recv, spots):
        self.send, self.recv, self.s, self.made = send, recv, spots, []

    def start(self, src, dst, peer, core=None, buffer=None):
        src, dst = (end if callable(end) else partial(lambda ref: ref, end) for end in (src, dst))
        copy = Remote(self, len(self.made), src, dst, peer)
        copy.buffer = buffer
        copy.named().start()
        self.made.append((core, copy))
        return copy

    def drain(self, src=None):
        made = [(core, copy) for core, copy in self.made if not copy.sent and src in (None, copy.buffer)]
        for which in (None, 0, 1):
            @self.s.on(which)
            def _():
                for core, copy in made:
                    if core == which:
                        copy.named().wait_send()
        for _, copy in made:
            copy.sent = True


class Local:
    def __init__(self, sems):
        self.sems, self.made, self.open = sems, 0, []

    def start(self, src, dst):
        copy = pltpu.make_async_copy(src, dst, self.sems.at[self.made])
        self.made += 1
        copy.start()
        self.open.append(copy)
        return copy

    def wait(self, copy):
        copy.wait()
        self.open = [other for other in self.open if other is not copy]

    def drain(self):
        for copy in list(self.open):
            self.wait(copy)


def arrived(copies):
    for copy in copies:
        copy.wait_recv()


class Spots:
    def __init__(self, num_z):
        dp, sq = lax.axis_index("dp"), lax.axis_index("seq")
        z, x, y, c = dp // 2, dp % 2, sq // 2, sq % 2
        self.num_z = num_z
        self.z, self.x, self.y, self.c = z, x, y, c
        self.own = dict(x=x, y=y, z=z)
        self.size = dict(x=2, y=2, z=num_z)
        self.core = self.at(z, x, y, 1 - c)
        self.others = dict(x=[1 - x], y=[1 - y], z=[(z + k) % num_z for k in range(1, num_z)])
        self.along = dict(
            x=[self.at(z, 1 - x, y, c)], y=[self.at(z, x, 1 - y, c)],
            z=[self.at(other, x, y, c) for other in self.others["z"]],
        )
        self.group = [((y + i) % 2, (c + j) % 2) for i, j in ((1, 0), (1, 1), (0, 1))]
        self.mates = [self.at(z, x, yy, cc) for yy, cc in self.group]

    def at(self, z, x, y, c):
        return (z * 2 + x, y * 2 + c)

    def on(self, core):
        return (lambda body: body()) if core is None else pl.when(self.c == core)

    def greet(self):
        for peer in self.along["z"] + self.along["x"] + self.mates:
            pl.semaphore_signal(pltpu.get_barrier_semaphore(), inc=1, device_id=peer, device_id_type=MESH)

    def meet(self):
        pl.semaphore_wait(pltpu.get_barrier_semaphore(), len(self.along["z"] + self.along["x"] + self.mates))


def both_cores(orders):
    return [(None, orders[0])] if len(orders) == 1 else list(enumerate(orders))


def block_index(s, axes, wide, core, at=None):
    place = {**s.own, **(at or {})}
    index = tuple(slice(None) if axis in wide else place[axis] for axis in axes)
    return index if core is None else index + (core,)


class Gather:
    def __init__(self, wire, spots, full, axes, *orders, part=(), buffer=None):
        self.buffer = buffer
        self.wire, self.s, self.full, self.axes, self.part = wire, spots, full, axes, part
        self.orders, self.last = both_cores(orders), {}

    def view(self, have):
        return self.full.at[block_index(self.s, self.axes, have, self.s.c) + self.part]

    def settle(self):
        for core, copies in self.last.items():
            self.s.on(core)(partial(arrived, copies))
        self.last = {}

    def step(self, n):
        s = self.s
        if n == len(self.orders[0][1]):
            self.settle()
            view = partial(self.view, self.axes)
            self.last[None] = [self.wire.start(view, view, s.core, buffer=self.buffer)]
            return
        before, self.last = self.last, {}
        for core, order in self.orders:
            @s.on(core)
            def _():
                arrived(before.get(core, []))
                view = partial(self.view, order[:n])
                self.last[core] = [
                    self.wire.start(view, view, peer, core, self.buffer) for peer in s.along[order[n]]
                ]

    def done(self):
        self.settle()


class Rounds:
    LAG = 2

    def __init__(self, gathers):
        self.gathers, self.now = gathers, 0

    def run(self, count=1):
        for _ in range(count):
            for step in reversed(range(4)):
                k = self.now - step * self.LAG
                if 0 <= k < len(self.gathers) and step <= len(self.gathers[k].orders[0][1]):
                    self.gathers[k].step(step)
            self.now += 1


class Scatter:
    def __init__(self, wire, spots, total, axes, orders, from_core, got, result, part=()):
        self.wire, self.s, self.total, self.axes, self.part = wire, spots, total, axes, part
        self.orders = [(core, order[::-1]) for core, order in both_cores(orders)]
        self.from_core, self.got, self.result = from_core, got, result
        self.last = {}

    def mine(self, wide, at=None):
        return self.total.at[block_index(self.s, self.axes, wide, self.s.c, at) + self.part]

    def send_core(self):
        s = self.s
        whole = (slice(None),) * (len(self.axes) - 1)
        self.last = [
            self.wire.start(self.total.at[(i,) + whole + (1 - s.c,) + self.part],
                            self.from_core.at[(i,) + whole + self.part], s.core)
            for i in range(self.from_core.shape[0])
        ]

    def add_core(self):
        arrived(self.last)
        self.last = {}
        s = self.s
        count = math.prod(s.size[axis] for axis in self.axes)

        def one(i, _):
            at, left = {}, i
            for axis in reversed(self.axes):
                at[axis], left = left % s.size[axis], left // s.size[axis]
            into = self.mine("", at)
            term = self.from_core[tuple(at[axis] for axis in self.axes) + self.part]
            into[...] = (into[...].astype(F32) + term.astype(F32)).astype(BF)
            return 0
        lax.fori_loop(0, count, one, 0)

    def stages(self, order, n):
        s = self.s
        begin = 0
        for k in range(n + 1):
            wide = sorted(order[k + 1 :])
            count = math.prod(s.size[axis] for axis in wide)
            if k < n:
                begin += count * (s.size[order[k]] - 1)
        return order[n], wide, count, begin

    def slots(self, start, count):
        return self.got.at[(start if count is None else slice(start, start + count),) + self.part]

    def send(self, n):
        s = self.s
        for core, order in self.orders:
            axis, wide, count, begin = self.stages(order, n)

            @s.on(core)
            def _():
                self.last[core] = []
                for j, (other, peer) in enumerate(zip(s.others[axis], s.along[axis])):
                    outer = s.size[wide[0]] if len(wide) == 2 else 1
                    inner = count // outer
                    for i in range(outer):
                        at = {axis: other}
                        if len(wide) == 2:
                            at[wide[0]] = i
                        start = begin + j * count + i * inner
                        src = partial(self.mine, wide[-1:], at)
                        dst = partial(self.slots, start, inner if wide else None)
                        self.last[core].append(self.wire.start(src, dst, peer, core))

    def add(self, n):
        s = self.s
        for core, order in self.orders:
            axis, wide, count, begin = self.stages(order, n)
            peers = len(s.others[axis])

            @s.on(core)
            def _():
                arrived(self.last[core])
                if n == len(order) - 1:
                    total = self.mine("")[...].astype(F32)
                    for j in range(peers):
                        total = total + self.got[(begin + j,) + self.part].astype(F32)
                    self.result[self.part or ...] = total
                    return

                def one(i, _):
                    at, left = {}, i
                    for a in reversed(wide):
                        at[a], left = left % s.size[a], left // s.size[a]
                    into = self.mine("", at)
                    total = into[...].astype(F32)
                    for j in range(peers):
                        total = total + self.got[(begin + j * count + i,) + self.part].astype(F32)
                    into[...] = total.astype(BF)
                    return 0
                lax.fori_loop(0, count, one, 0)


    def go(self, n):
        if n == 0:
            self.add_core()
        else:
            self.add(n - 1)
        if n < len(self.orders[0][1]):
            self.send(n)


class Trade:
    def __init__(self, wire, spots, halves, ends):
        self.s, self.ends, self.pieces = spots, ends, len(halves[0])
        for core in range(2):
            for i, piece in enumerate(halves[core]):
                ends[core, i] = piece
        self.copy = wire.start(ends.at[1 - spots.c], ends.at[2], spots.core)

    def finish(self, out, turned=False):
        self.copy.wait_recv()
        c = self.s.c
        own, other = (
            jnp.concatenate([self.ends[k, i] for i in range(self.pieces)], axis=-1) for k in (c, 2)
        )
        both = jnp.concatenate([jnp.where(c == 0, own, other), jnp.where(c == 0, other, own)], axis=0)
        out[...] = both.T if turned else both


def column_halves(total):
    part = total.shape[-1] // 2
    return [[total[:, core * part : (core + 1) * part]] for core in range(2)]


def row_parts(rows):
    size = rows // PARTS
    return [(slice(i * size, (i + 1) * size),) for i in range(PARTS)]


def norm_parts(values):
    center = values - jnp.mean(values, axis=-1, keepdims=True)
    spread = jnp.mean(center * center, axis=-1, keepdims=True)
    scale = lax.rsqrt(spread + EPSILON)
    return center * scale, scale


def norm_back(normal, scale, grad, gain):
    p = grad * gain
    flat = jnp.mean(p, axis=-1, keepdims=True)
    along = jnp.mean(p * normal, axis=-1, keepdims=True)
    return (p - flat - normal * along) * scale, jnp.sum(grad * normal, axis=0, keepdims=True)


def dot(left, right):
    return jnp.dot(left, right, preferred_element_type=F32)


def dot_rows(left, right):
    return lax.dot_general(left, right, (((0,), (0,)), ((), ())), preferred_element_type=F32)


def dot_cols(left, right):
    return lax.dot_general(left, right, (((1,), (1,)), ((), ())), preferred_element_type=F32)


def live_taps(kern, taps):
    position = lax.broadcasted_iota(jnp.int32, kern.shape, 0)
    return position, position.astype(F32) < taps


def pool(values, position):
    length = values.shape[0]
    before = jnp.where(position == 0, 0.0, pltpu.roll(values, 1, 0))
    after = jnp.where(position == length - 1, 0.0, pltpu.roll(values, length - 1, 0))
    return (before + values + after) / 3.0


def make_filter(kern, taps):
    position, live = live_taps(kern, taps)
    masked = jnp.where(live, kern, 0.0)
    shrunk = masked - SHRINK_SCALE * jnp.tanh(masked / SHRINK_SCALE)
    return jnp.where(live, pool(shrunk, position), 0.0)


def kernel_back(kern, taps, grad):
    position, live = live_taps(kern, taps)
    slope = jnp.tanh(jnp.where(live, kern, 0.0) / SHRINK_SCALE)
    return jnp.where(live, pool(jnp.where(live, grad, 0.0), position) * slope * slope, 0.0)


GELU_K = math.sqrt(2.0 / math.pi)


def gelu_both(v):
    square = v * v
    t = jnp.tanh(GELU_K * v * (1.0 + 0.044715 * square))
    half = 0.5 * (1.0 + t)
    slope = half + 0.5 * v * (1.0 - t * t) * (GELU_K * (1.0 + 3 * 0.044715 * square))
    return v * half, slope


def spans(start, size, step=16):
    return pl.ds(pl.multiple_of(start, step), size)


def transform_table(length):
    k = 2 * np.arange(length)[:, None] + 1
    angle = np.pi / (4 * length) * ((k * k.T) % (8 * length))
    return np.concatenate([np.cos(angle), np.sin(angle)]).astype(np.float32).astype(ml_dtypes.bfloat16)


def twist_table(length):
    angle = np.pi / (4 * length) * (2 * np.arange(length) + 1)
    return np.stack([np.cos(angle), np.sin(angle)], axis=1).astype(np.float32)


ORDER_OUT = ("zxy", "zyx")
ORDER_UP = ("zxy", "yzx")
ORDER_DOWN = ("zxy", "yzx")
BACK_OUT = ("zxy", "zyx")
BACK_UP = ("zxy", "yzx")
BACK_DOWN = ("zxy", "yzx")
PARTS = 4
STEP = 256


def layer_kernel(
    num_z, length,
    tok, cot, w_in, w_out, w_up, w_down_t, kern_t, gains_in, taps_in, twist, table_hbm,
    out_o, grad_in_o, gin_o, gout_o, gup_o, gdn_o, gains_o, gkern_o,
    win_v, wout_v, wup_v, wdown_v, gdn_v, kern_v, small_v,
    pre_in, pre_out, pre_up, pre_down, pre_kern, w_down, kern,
    table_v, proj_v, normed_own, normed_v, sig_v, spec_v, filt_v, turned_v, conv_v, gated_ch,
    gated_v, resid_v, normed_two_v, act_v, slope_v,
    core_in, core_out, core_dn, core_kern,
    got_in, got_out, got_up, got_dn, got_kern,
    sum_in, sum_out, sum_up, sum_dn, sum_kern,
    ends_out, ends_up, ends_dn, ends_kern, swap_core, swap_y,
    gain_v, gain_got,
    send, recv, local,
):
    s = Spots(num_z)
    z, x, y, c = s.z, s.x, s.y, s.c
    wire, inner = Wire(send, recv, s), Local(local)
    load_table = inner.start(table_hbm, table_v)
    rows, width = tok.shape
    group, span = width // 2, rows // 2
    hidden = act_v.shape[1]
    block = width // (4 * num_z)
    me = 2 * y + c
    chunk, home = spans(me * span, span), spans(c * span, span)
    w_down[...] = w_down_t[...].T
    kern[...] = kern_t[...].T
    small_v[me, 0:2] = gains_in[...].astype(F32)
    small_v[me, 2:3] = taps_in[...].astype(F32)
    tile = 128

    def norm_one(i, _):
        at = spans(i * tile, tile)
        resid_v[at], _ = norm_parts(tok[at].astype(F32))
        return 0
    s.greet()
    lax.fori_loop(0, rows // tile, norm_one, 0)
    s.meet()

    smalls = [wire.start(small_v.at[me], small_v.at[me], peer) for peer in s.mates]
    half = w_in.shape[0] // 2
    trade_in = [
        wire.start(w_in.at[spans(cc * half, half)], pre_in.at[me], peer) for (yy, cc), peer in zip(s.group, s.mates)
    ]
    pairs = [(kern, pre_kern), (w_out, pre_out), (w_up, pre_up), (w_down, pre_down)]
    traded = []
    for src, pre in pairs:
        half = src.shape[0] // 2
        traded.append(wire.start(src.at[spans((1 - c) * half, half)], pre.at[c], s.core))
    half = w_in.shape[0] // 2
    pre_in[me] = w_in[spans(c * half, half)]
    for src, pre in pairs:
        half = src.shape[0] // 2
        pre[c] = src[spans(c * half, half)]

    g_in = [Gather(wire, s, win_v, "zx", "zx", part=(k,), buffer="in") for k in range(3)]
    g_kern = Gather(wire, s, kern_v, "zx", "zx", buffer="kern")
    g_out = Gather(wire, s, wout_v, "yzx", *ORDER_OUT)
    parts = row_parts(wup_v.shape[-2])
    g_up = [Gather(wire, s, wup_v, "yzx", *ORDER_UP, part=part, buffer="up") for part in parts]
    g_down = [Gather(wire, s, wdown_v, "yzx", *ORDER_DOWN, part=part, buffer="down") for part in parts]
    rounds = Rounds([*g_in, g_kern, g_out, *g_up, *g_down])

    def join(i):
        traded[i].wait_recv()
        pre = pairs[i][1]
        return jnp.concatenate([pre[0], pre[1]], axis=-1)

    arrived(smalls)
    gains = jnp.concatenate([small_v[k] for k in range(4)], axis=-1)

    def normed_rows(i, _):
        at = spans(i * tile, tile)
        normed_own[at] = (resid_v[at] * gains[0:1]).astype(BF)
        return 0
    lax.fori_loop(0, rows // tile, normed_rows, 0)
    to_group = [
        wire.start(normed_own.at[spans(cc * span, span)], normed_v.at[chunk], peer, buffer="normed")
        for (yy, cc), peer in zip(s.group, s.mates)
    ]
    normed_v[chunk] = normed_own[home]
    arrived(trade_in)
    whole = jnp.concatenate([pre_in[k] for k in range(4)], axis=-1)
    for k in range(3):
        left, right = (whole[:, (2 * k + h) * group : (2 * k + h + 1) * group] for h in range(2))
        win_v[z, x, c, k] = jnp.where(y == 0, left, right)
        if k < 2:
            rounds.run()

    kern_v[z, x, c] = join(0)
    wout_v[y, z, x, c] = join(1)
    both = join(2)
    pieces = both.shape[-1] // group
    for q in range(pieces):
        wup_v[y, z, x, c, q * block : (q + 1) * block] = both[:, q * group : (q + 1) * group]
    wdown_v[y, z, x, c] = join(3)
    rounds.run(5)

    arrived(to_group)
    g_in[0].done()
    g_in[1].done()

    def project(k, at):
        return dot(normed_v[at], win_v[:, :, :, k].reshape(width, group))

    def mix(i, _):
        at = spans(i * STEP, STEP, STEP)
        value, gate = project(0, at), project(1, at)
        proj_v[0, at] = value.astype(BF)
        proj_v[1, at] = gate.astype(BF)
        sig_v[at] = (value * gate).astype(BF)
        return 0
    lax.fori_loop(0, length // STEP, mix, 0)
    rounds.run()
    g_in[2].done()

    def second_gate(i, _):
        at = spans(i * STEP, STEP, STEP)
        proj_v[2, at] = project(2, at).astype(BF)
        return 0
    lax.fori_loop(0, length // STEP, second_gate, 0)
    rounds.run()

    g_kern.done()
    taps_v = gain_v.at[2, 0:1]
    taps_v[:, 0:group] = jnp.concatenate([small_v[2 * y], small_v[2 * y + 1]], axis=-1)[2:3]

    def shape_taps(j, _):
        cols = spans(j * tile, tile, tile)
        filt = make_filter(kern_v[:, :, :, :, cols].reshape(length, tile).astype(F32), taps_v[:, cols])
        gated_ch[:, cols] = filt.astype(BF)
        return 0
    lax.fori_loop(0, group // tile, shape_taps, 0)
    inner.wait(load_table)

    def spectrum(i, _):
        real, imag = spans(i * STEP, STEP, STEP), spans(length + i * STEP, STEP, STEP)
        re, im = dot(table_v[real], gated_ch[...]), dot(table_v[imag], gated_ch[...])
        cosine, sine = twist[real, 0:1], twist[real, 1:2]
        filt_v[real] = (re * cosine + im * sine).astype(BF)
        filt_v[imag] = (im * cosine - re * sine).astype(BF)
        return 0
    lax.fori_loop(0, length // STEP, spectrum, 0)
    rounds.run()

    def convolve(i, _):
        real, imag = spans(i * STEP, STEP, STEP), spans(length + i * STEP, STEP, STEP)
        re_s, im_s = dot(table_v[real], sig_v[...]), dot(table_v[imag], sig_v[...])
        spec_v[real] = re_s.astype(BF)
        spec_v[imag] = im_s.astype(BF)
        re_f, im_f = filt_v[real].astype(F32), filt_v[imag].astype(F32)
        turned_v[real] = (re_s * re_f - im_s * im_f).astype(BF)
        turned_v[imag] = (re_s * im_f + im_s * re_f).astype(BF)
        return 0
    lax.fori_loop(0, length // STEP, convolve, 0)
    rounds.run()

    def back(i, _):
        at, imag = spans(i * STEP, STEP, STEP), spans(length + i * STEP, STEP, STEP)
        both = dot(table_v[at], turned_v[0:length]) + dot(table_v[imag], turned_v[length:])
        conv = (both * (1.0 / length)).astype(BF)
        conv_v[at] = conv
        gated_ch[at] = (proj_v[2, at].astype(F32) * conv.astype(F32)).astype(BF)
        return 0
    lax.fori_loop(0, length // STEP, back, 0)

    to_tokens = [
        wire.start(gated_ch.at[spans((2 * yy + cc) * span, span)], gated_v.at[y, home], peer, buffer="gated")
        for (yy, cc), peer in zip(s.group, s.mates)
    ]
    gated_v[y, home] = gated_ch[chunk]
    rounds.run()
    g_out.done()
    rounds.run()
    arrived(to_tokens)

    for k in range(2):
        cols = slice(k * group, (k + 1) * group)
        mixed = sum(
            dot(gated_v[h], wout_v[k, h * num_z // 2 : (h + 1) * num_z // 2].reshape(group, group)) for h in range(2)
        )
        resid_v[:, cols] = tok[:, cols].astype(F32) + mixed

    def norm_two(i, _):
        at = spans(i * tile, tile)
        normed, _ = norm_parts(resid_v[at])
        normed_two_v[at] = (normed * gains[1:2]).astype(BF)
        return 0
    lax.fori_loop(0, rows // tile, norm_two, 0)

    def piece(ref, j):
        return ref.at[j // pieces, :, :, :, spans((j % pieces) * block, block)]

    for q in range(pieces):
        g_up[q].done()

        def feed(i, _):
            j = i // 2 * pieces + q
            at, cols = spans(i % 2 * span, span), spans(j * group, group, 128)
            act, slope = gelu_both(dot(normed_two_v[at], piece(wup_v, j)[...].reshape(width, group)))
            act_v[at, cols] = act.astype(BF)
            slope_v[at, cols] = slope.astype(BF)
            return 0
        lax.fori_loop(0, 4, feed, 0)
        rounds.run()

    down = [Scatter(wire, s, gdn_v, "yzx", BACK_DOWN, core_dn, got_dn, sum_dn, part=part) for part in parts]
    deep = hidden // (2 * num_z)

    def down_grad(i, _):
        grad = dot_rows(act_v[:, spans(i * deep, deep, 128)], cot[...]).astype(BF)
        for h in range(2):
            gdn_v[h, i // 2, i % 2] = grad[:, h * group : (h + 1) * group].reshape(2, deep // 2, group)
        return 0
    lax.fori_loop(0, 2 * num_z, down_grad, 0)
    rounds.run()
    for g in down:
        g.send_core()
    rounds.run()
    for g in g_down:
        g.done()
    down[0].go(0)
    down[1].go(0)

    def pre_grad(i, _):
        at, cols = spans(i // num_z * span, span), spans(i % num_z * 2 * deep, 2 * deep, 128)
        grad = sum(
            dot_cols(cot[at, h * group : (h + 1) * group], wdown_v[h, i % num_z].reshape(2 * deep, group))
            for h in range(2)
        )
        slope_v[at, cols] = (slope_v[at, cols].astype(F32) * grad).astype(BF)
        return 0
    lax.fori_loop(0, 2 * num_z, pre_grad, 0)
    gpre_v = slope_v
    down[2].go(0)
    down[3].go(0)

    wire.drain("normed")
    low_v = normed_own
    gnorm_got = [[turned_v.at[(2 * i + h) * span : (2 * i + h + 1) * span] for h in range(2)] for i in range(3)]
    gout_v, gup_v, gin_v = wdown_v.at[:, :, :, :, 0:block], wup_v, win_v
    gch_v, gkern_v = sig_v, kern_v
    ggate_v = gated_ch
    up = [Scatter(wire, s, gup_v, "yzx", BACK_UP, core_dn, got_up, sum_up, part=part) for part in parts]
    out = Scatter(wire, s, gout_v, "yzx", BACK_OUT, core_out, got_out, sum_out)
    into = [Scatter(wire, s, gin_v, "zx", ("zx",), core_in, got_in, sum_in, part=(k,)) for k in range(3)]
    taps_grad = Scatter(wire, s, gkern_v, "zx", ("zx",), core_kern, got_kern, sum_kern)


    def norm_two_back(i, gain):
        at = spans(i * span, span)

        grad = sum(
            dot_cols(gpre_v[at, j * group : (j + 1) * group], piece(wup_v, j)[...].reshape(width, group))
            for j in range(2 * pieces)
        )
        normal, scale = norm_parts(resid_v[at])
        part, more = norm_back(normal, scale, grad, gains[1:2])
        low_v[at] = (cot[at].astype(F32) + part).astype(BF)
        return gain + more
    gain_two = lax.fori_loop(0, 2, norm_two_back, jnp.zeros((1, width), F32))

    wire.drain("gated")
    for h in range(2):
        grad = sum(
            dot_cols(
                low_v[:, k * group : (k + 1) * group],
                wout_v[k, h * num_z // 2 : (h + 1) * num_z // 2].reshape(group, group),
            )
            for k in range(2)
        )
        ggate_v[h * rows : (h + 1) * rows] = grad.astype(BF)
    to_channels = [
        wire.start(ggate_v.at[spans(yy * rows + cc * span, span)], gch_v.at[chunk], peer)
        for (yy, cc), peer in zip(s.group, s.mates)
    ]
    gch_v[chunk] = ggate_v[spans(y * rows + c * span, span)]
    wire.drain("up")

    def up_grad(q, yy, _):
        j = yy * pieces + q
        grad = dot_rows(normed_two_v[...], gpre_v[:, spans(j * group, group, 128)]).astype(BF)
        piece(gup_v, j)[...] = grad.reshape(num_z, 2, 2, block, group)
        return 0

    for q in range(pieces):
        lax.fori_loop(0, 2, partial(up_grad, q), 0)
        if q == 0:
            arrived(to_channels[2:])
        up[q].send_core()
        if q % 2:
            down[q - 1].go(1)
            down[q].go(1)
            up[q - 1].go(0)

    def down_out(i, _):
        at = spans(i * span, span)
        grown = jnp.concatenate([dot(act_v[at], wdown_v[h].reshape(hidden, group)) for h in range(2)], axis=-1)
        act_v[at, 0:width] = (resid_v[at] + grown).astype(BF)
        return 0
    lax.fori_loop(0, 2, down_out, 0)
    inner.start(act_v.at[:, 0:width], out_o)
    up[1].go(0)
    up[3].go(0)
    wire.drain("down")

    def out_grad(i, _):
        h, k = i // 2, i % 2
        grad = dot_rows(gated_v[h], low_v[:, spans(k * group, group, 128)]).astype(BF)
        gout_v[k, pl.ds(h * (num_z // 2), num_z // 2)] = grad.reshape(num_z // 2, 2, 2, block, group)
        return 0
    lax.fori_loop(0, 4, out_grad, 0)
    out.send_core()
    down[0].go(2)
    down[1].go(2)
    out.go(0)

    arrived(to_channels[:2])

    def gate(i, _):
        at = spans(i * STEP, STEP, STEP)
        grad = gch_v[at].astype(F32)
        gch_v[at] = (grad * proj_v[2, at].astype(F32)).astype(BF)
        proj_v[2, at] = (grad * conv_v[at].astype(F32)).astype(BF)
        return 0
    lax.fori_loop(0, length // STEP, gate, 0)

    wire.drain("in")

    def in_grad(k):
        grad = dot_rows(normed_v[...], proj_v[k]).astype(BF)
        gin_v[:, :, :, k] = grad.reshape(num_z, 2, 2, block, group)
        into[k].send_core()

    def turn(i, _):
        real, imag = spans(i * STEP, STEP, STEP), spans(length + i * STEP, STEP, STEP)
        re, im = dot(table_v[real], gch_v[...]), dot(table_v[imag], gch_v[...])
        re_f, im_f = filt_v[real].astype(F32), filt_v[imag].astype(F32)
        filt_v[real] = (re_f * re + im_f * im).astype(BF)
        filt_v[imag] = (re_f * im - im_f * re).astype(BF)
        re_s, im_s = spec_v[real].astype(F32), spec_v[imag].astype(F32)
        re_k, im_k = re_s * re + im_s * im, re_s * im - im_s * re
        cosine, sine = twist[real, 0:1], twist[real, 1:2]
        spec_v[real] = (re_k * cosine - im_k * sine).astype(BF)
        spec_v[imag] = (im_k * cosine + re_k * sine).astype(BF)
        return 0
    lax.fori_loop(0, length // STEP, turn, 0)
    down[2].go(2)
    down[3].go(2)
    up[0].go(1)
    up[1].go(1)

    def signal_back(i, _):
        at, imag = spans(i * STEP, STEP, STEP), spans(length + i * STEP, STEP, STEP)
        both = dot(table_v[at], filt_v[0:length]) + dot(table_v[imag], filt_v[length:])
        grad = (both * (1.0 / length)).astype(BF).astype(F32)
        value, first = proj_v[0, at].astype(F32), proj_v[1, at].astype(F32)
        proj_v[0, at] = (grad * first).astype(BF)
        proj_v[1, at] = (grad * value).astype(BF)
        return 0
    lax.fori_loop(0, length // STEP, signal_back, 0)

    def part_at(j, h):
        return gpre_v.at[spans(j % 2 * span, span), spans(j // 2 * width + h * group, group, 128)]

    to_owner = []
    for h in range(2):
        grad = sum(
            dot_cols(proj_v[k], win_v[h * num_z // 2 : (h + 1) * num_z // 2, :, :, k].reshape(group, group))
            for k in range(3)
        ).astype(BF)
        for j in range(4):
            part_at(j, h)[...] = grad[j * span : (j + 1) * span]
        to_owner += [
            wire.start(partial(part_at, 2 * yy + cc, h), gnorm_got[i][h], peer)
            for i, ((yy, cc), peer) in enumerate(zip(s.group, s.mates))
        ]

    up[2].go(1)
    up[3].go(1)
    for k in range(3):
        in_grad(k)
    up[0].go(2)
    for k in range(3):
        into[k].go(0)

    def gain_part(j, total):
        grad = jnp.concatenate([part_at(j, h)[...].astype(F32) for h in range(2)], axis=-1)
        return total + jnp.sum(grad * normed_v[spans(j * span, span)].astype(F32), axis=0, keepdims=True)
    gain_one = lax.fori_loop(0, 4, gain_part, jnp.zeros((1, width), F32)) / gains[0:1]
    gain_v[0] = jnp.concatenate([gain_one, gain_two, jnp.zeros((6, width), F32)], axis=0)
    gain_got_one = [wire.start(gain_v.at[0], gain_got.at[k], peer) for k, peer in enumerate(s.mates)]
    up[1].go(2)
    out.go(1)

    wire.drain("kern")

    def taps_signal(i, _):
        at, imag = spans(i * STEP, STEP, STEP), spans(length + i * STEP, STEP, STEP)
        both = dot(table_v[at], spec_v[0:length]) + dot(table_v[imag], spec_v[length:])
        resid_v[spans(i % tall * STEP, STEP, STEP), spans(i // tall * group, group, 128)] = both
        return 0
    tall = rows // STEP
    lax.fori_loop(0, length // STEP, taps_signal, 0)

    def taps_back(j, _):
        cols = spans(j * tile, tile, tile)
        both = jnp.concatenate([resid_v[:, cols], resid_v[:, spans(group + j * tile, tile, tile)]], axis=0)
        grad = kernel_back(kern_v[:, :, :, :, cols].reshape(length, tile).astype(F32), taps_v[:, cols],
                           both * (1.0 / length))
        gkern_v[:, :, :, :, cols] = grad.astype(BF).reshape(num_z, 2, 2, length // (4 * num_z), tile)
        return 0
    lax.fori_loop(0, group // tile, taps_back, 0)
    taps_grad.send_core()
    for k in range(3):
        into[k].go(1)
    taps_grad.go(0)
    up[2].go(2)
    up[3].go(2)
    arrived(to_owner)
    arrived(gain_got_one)
    gain_v[1] = gain_v[0] + gain_got[0] + gain_got[1] + gain_got[2]
    got = [wire.start(gain_v.at[1], gain_got.at[3], s.along["x"][0])]

    def norm_one_back(i, _):
        at, within = spans(i * tile, tile), spans(i % (span // tile) * tile, tile)
        across, diagonal, beside = (
            jnp.concatenate([ref[within].astype(F32) for ref in pair], axis=-1) for pair in gnorm_got
        )
        here = jnp.concatenate([part_at(me, h)[within].astype(F32) for h in range(2)], axis=-1)
        grad = jnp.where(c == i // (span // tile), here + across, beside + diagonal)
        normal, scale = norm_parts(tok[at].astype(F32))
        part, _ = norm_back(normal, scale, grad, gains[0:1])
        low_v[at] = (low_v[at].astype(F32) + part).astype(BF)
        return 0
    lax.fori_loop(0, rows // tile, norm_one_back, 0)
    inner.start(low_v, grad_in_o)

    for k in range(4):
        down[k].go(3)
    trade_dn = Trade(wire, s, column_halves(sum_dn), ends_dn)
    taps_grad.go(1)
    out.go(2)

    for k in range(4):
        up[k].go(3)
    rows_half = pieces // 2 * block
    column_pieces = [
        [sum_up[core * rows_half + q * block : core * rows_half + (q + 1) * block] for q in range(pieces // 2)]
        for core in range(2)
    ]
    arrived(got)
    gain_v[2] = gain_v[1] + gain_got[3]
    got = [wire.start(gain_v.at[2], gain_got.at[3 + k], peer) for k, peer in zip(range(1, num_z), s.along["z"])]
    trade_up = Trade(wire, s, column_pieces, ends_up)
    out.go(3)
    trade_out = Trade(wire, s, column_halves(sum_out), ends_out)

    for k in range(3):
        into[k].go(2)
    first, second, third = sum_in[y], sum_in[y + 1], sum_in[(y + 2) % 3]
    swap_core[0, 0], swap_core[0, 1] = first.astype(BF), second.astype(BF)
    swap_y[0] = third.astype(BF)
    swaps = [wire.start(swap_y.at[0], swap_y.at[1], s.mates[0]), wire.start(swap_y.at[0], swap_y.at[2], s.mates[1]),
             wire.start(swap_core.at[0], swap_core.at[1], s.core)]
    taps_grad.go(2)
    trade_kern = Trade(wire, s, column_halves(sum_kern), ends_kern)
    trade_dn.finish(gdn_o, turned=True)
    trade_up.finish(gup_o)
    trade_out.finish(gout_o)
    arrived(got)
    total = gain_v[2]
    for k in range(1, num_z):
        total = total + gain_got[3 + k]
    part = width // 4
    mine = total[:, 0:part]
    for k in range(1, 4):
        mine = jnp.where(me == k, total[:, k * part : (k + 1) * part], mine)
    gains_o[...] = mine[0:2]
    trade_kern.finish(gkern_o, turned=True)
    arrived(swaps)
    cut = group // 2
    for row, near, far in ((c, swap_core.at[0], swap_y.at[1]), (1 - c, swap_core.at[1], swap_y.at[2])):
        far = far[...].astype(F32)
        left = jnp.concatenate([near[0].astype(F32), far[:, 0:cut]], axis=-1)
        right = jnp.concatenate([far[:, cut:], near[1].astype(F32)], axis=-1)
        gin_o[spans(row * block, block)] = jnp.where(c == 0, left, right)
    wire.drain()
    inner.drain()


def vm(shape, dtype=BF):
    return pltpu.VMEM(tuple(shape), dtype)


VMEM_SPEC, HBM_SPEC = pl.BlockSpec(memory_space=pltpu.VMEM), pl.BlockSpec(memory_space=pl.ANY)


def layer(num_z, length, tokens, cot, w_in, w_out, w_up, w_down_t, kernel_t, gains, taps, twist, table):
    rows, width = tokens.shape
    group = width // 2
    part = w_down_t.shape[1]
    hidden = part * num_z * 2
    block = w_in.shape[0] // 2
    sds = jax.ShapeDtypeStruct
    axes = (2, num_z, 2, 2)
    units = dict(
        win=(3, block, group), wout=(block, group), wup=(hidden // width * block, group), wdown=(part // 2, group),
        kern=(kernel_t.shape[1] // 2, group),
    )
    lead = {name: axes[1:] if name in ("win", "kern") else axes for name in units}
    outs = [sds((rows, width), BF)] * 2
    outs += [sds((w.shape[0], w.shape[1]), F32) for w in (w_in, w_out, w_up, w_down_t)]
    outs += [sds((2, width // 4), F32), sds(kernel_t.shape, F32)]
    channel = vm((length, group))
    both = vm((2 * length, group))
    token = vm((rows, width))
    scratch = [vm(lead[name] + units[name]) for name in ("win", "wout", "wup", "wdown", "wdown", "kern")]
    scratch += [vm((4, 8, width // 4), F32)]
    scratch += [vm((4, block, w_in.shape[1])), vm((2, block, w_out.shape[1])), vm((2, block, w_up.shape[1])),
                vm((2, part // 2, w_down_t.shape[0])), vm((2, kernel_t.shape[1] // 2, kernel_t.shape[0])),
                vm(w_down_t.shape[::-1]), vm(kernel_t.shape[::-1])]
    scratch += [vm(table.shape), vm((3, length, group)), token, vm((length, width)), channel, both, both, both, channel,
                channel, vm((2, rows, group)), vm((rows, width), F32), token, vm((rows, hidden)), vm((rows, hidden))]
    names = ("win", "wout", "wup", "wdown", "kern")
    scratch += [vm(lead[name][:-1] + units[name]) for name in names if name != "wup"]
    blocks = {name: math.prod(lead[name]) // 2 - 1 for name in names}
    scratch += [vm((blocks[name],) + units[name]) for name in names] + [vm(units[name], F32) for name in names]
    scratch += [vm((3, 1, block, group // 2), F32), vm((3, hidden // width // 2, block, group), F32),
                vm((3, 1, part // 2, group // 2), F32), vm((3, 1, kernel_t.shape[1] // 2, group // 2), F32)]
    scratch += [vm((2, 2, block, group)), vm((3, block, group)), vm((3, 8, width), F32), vm((3 + num_z, 8, width), F32)]
    scratch += [pltpu.SemaphoreType.DMA((320,)), pltpu.SemaphoreType.DMA((320,)), pltpu.SemaphoreType.DMA((8,))]
    return pl.pallas_call(
        partial(layer_kernel, num_z, length),
        out_shape=outs,
        in_specs=[VMEM_SPEC] * 10 + [HBM_SPEC],
        out_specs=[HBM_SPEC] * 2 + [VMEM_SPEC] * 6,
        scratch_shapes=scratch,
        compiler_params=pltpu.CompilerParams(collective_id=0, has_side_effects=True, vmem_limit_bytes=67 * 10**6),
        cost_estimate=pl.CostEstimate(flops=34 * 10**9, bytes_accessed=20 * 10**6, transcendentals=2 * 10**6),
    )(tokens, cot, w_in, w_out, w_up, w_down_t, kernel_t, gains, taps, twist, table)


def publish(*arrays):
    def copy_all(*refs):
        for src, dst in zip(refs[: len(arrays)], refs[len(arrays) :]):
            dst[...] = src[...]

    return pl.pallas_call(
        copy_all,
        out_shape=[jax.ShapeDtypeStruct(a.shape, a.dtype) for a in arrays],
        in_specs=[VMEM_SPEC] * len(arrays),
        out_specs=[VMEM_SPEC] * len(arrays),
    )(*arrays)


def fits(num_dp, num_seq, tokens, w_in, w_out, w_up, w_down, kernel):
    if num_seq != 4 or num_dp % 4 or kernel.shape[0] * num_dp > 1024 or kernel.shape[0] * num_dp % 512:
        return False
    blocks = (w_in, w_out, w_up, w_down, kernel)
    return all(b.shape[0] % 32 == 0 and b.shape[1] * 2 % 128 == 0 for b in blocks) and tokens.shape[0] == 2


def body(num_dp, num_seq, tokens_in, w_in, w_out, w_up, w_down, norm_gains, kernel, taps, cotangent):
    if not fits(num_dp, num_seq, tokens_in, w_in, w_out, w_up, w_down, kernel):
        return general_body(tokens_in, w_in, w_out, w_up, w_down, norm_gains, kernel, taps, cotangent)
    width = tokens_in.shape[-1]
    length = kernel.shape[0] * num_dp
    table, twist = jnp.asarray(transform_table(length)), jnp.asarray(twist_table(length))
    tokens, cot = tokens_in.reshape(-1, width), cotangent.reshape(-1, width)
    results = layer(num_dp // 2, length, tokens, cot, w_in, w_out, w_up, w_down.T, kernel.T, norm_gains, taps[None],
                    twist, table)
    out, grad_in, gin, gout, gup, gdn, gains, gkern = publish(*results)
    return (out.reshape(tokens_in.shape), grad_in.reshape(tokens_in.shape), gin, gout, gup, gdn.T, gains, gkern.T)


def solution(mesh):
    return jax.shard_map(
        partial(body, mesh.shape["dp"], mesh.shape["seq"]),
        mesh=mesh,
        in_specs=(
            P("dp", "seq", None),
            P("dp", "seq"),
            P("dp", "seq"),
            P("dp", "seq"),
            P("dp", "seq"),
            P(None, "seq"),
            P("dp", "seq"),
            P("seq"),
            P("dp", "seq", None),
        ),
        out_specs=(
            P("dp", "seq", None),
            P("dp", "seq", None),
            P("dp", "seq"),
            P("dp", "seq"),
            P("dp", "seq"),
            P("dp", "seq"),
            P(None, "seq"),
            P("dp", "seq"),
        ),
        check_vma=False,
    )
```

```python
from functools import partial
import math

import jax
from jax.experimental import pallas as pl
from jax.experimental.pallas import tpu as pltpu
import ml_dtypes
import numpy as np
import jax.numpy as jnp
from jax import lax
from jax.sharding import PartitionSpec as P

EPSILON = 1e-05
SHRINK_SCALE = 0.003
HIGHEST = lax.Precision.HIGHEST


def norm_rows(values, gain):
    center = values - jnp.mean(values, axis=-1, keepdims=True)
    spread = jnp.mean(center * center, axis=-1, keepdims=True)
    return center * lax.rsqrt(spread + EPSILON) * gain


def shape_filter(kernel, taps):
    length = kernel.shape[0]
    position = jnp.arange(length, dtype=jnp.int32)[:, None]
    live_mask = (position < taps[None, :]).astype(kernel.dtype)
    masked = kernel * live_mask
    shrunk = masked - SHRINK_SCALE * jnp.tanh(masked / SHRINK_SCALE)
    padded = jnp.pad(shrunk, ((1, 1), (0, 0)))
    pooled = (padded[:-2] + padded[1:-1] + padded[2:]) / 3.0
    return pooled * live_mask


def gelu_tanh(values):
    return jax.nn.gelu(values, approximate=True)


def contract_rows(left, right):
    return lax.dot_general(
        left, right, (((0,), (0,)), ((), ())), preferred_element_type=jnp.float32
    )


def times_transposed(left, weight):
    return lax.dot_general(
        left, weight, (((1,), (1,)), ((), ())), preferred_element_type=jnp.float32
    )


def phase_table(count_rows, count_cols, period):
    row_index = lax.broadcasted_iota(jnp.int32, (count_rows, count_cols), 0)
    col_index = lax.broadcasted_iota(jnp.int32, (count_rows, count_cols), 1)
    angles = 2.0 * math.pi / period * (row_index * col_index % period).astype(jnp.float32)
    return (jnp.cos(angles), jnp.sin(angles))


def dft_factors(length):
    total = 2 * length
    first = max(2, total // 128)
    return (total, first, total // first)


def mix_last(field, table):
    return jnp.einsum("bckn,nm->bckm", field, table, precision=HIGHEST)


def forward_dft(field):
    batch, length, chans = field.shape
    total, first, second = dft_factors(length)
    half = first // 2
    blocks = field.reshape(batch, half, second, chans)
    cos_one, sin_one = phase_table(half, first, first)
    part_re = jnp.einsum("hk,bhnc->bckn", cos_one, blocks, precision=HIGHEST)
    part_im = -jnp.einsum("hk,bhnc->bckn", sin_one, blocks, precision=HIGHEST)
    cos_two, sin_two = phase_table(first, second, total)
    turn_re = part_re * cos_two + part_im * sin_two
    turn_im = part_im * cos_two - part_re * sin_two
    cos_three, sin_three = phase_table(second, second, second)
    spec_re = mix_last(turn_re, cos_three) + mix_last(turn_im, sin_three)
    spec_im = mix_last(turn_im, cos_three) - mix_last(turn_re, sin_three)
    return (spec_re, spec_im)


def inverse_dft(spec_re, spec_im):
    batch, chans, first, second = spec_re.shape
    total = first * second
    half = first // 2
    cos_three, sin_three = phase_table(second, second, second)
    back_re = mix_last(spec_re, cos_three) - mix_last(spec_im, sin_three)
    back_im = mix_last(spec_re, sin_three) + mix_last(spec_im, cos_three)
    cos_two, sin_two = phase_table(first, second, total)
    turn_re = back_re * cos_two - back_im * sin_two
    turn_im = back_re * sin_two + back_im * cos_two
    cos_one, sin_one = phase_table(half, first, first)
    blocks = jnp.einsum("hk,bckn->bhnc", cos_one, turn_re, precision=HIGHEST)
    blocks = blocks - jnp.einsum("hk,bckn->bhnc", sin_one, turn_im, precision=HIGHEST)
    return blocks.reshape(batch, half * second, chans) / total


def to_channels(field):
    return lax.all_to_all(field, "seq", split_axis=2, concat_axis=1, tiled=True)


def to_tokens(field):
    return lax.all_to_all(field, "seq", split_axis=1, concat_axis=2, tiled=True)


def general_body(tokens_in, w_in, w_out, w_up, w_down, norm_gains, kernel, taps, cotangent):
    w_in_rows, w_out_rows, w_up_rows, w_down_rows, gains = (
        lax.all_gather(w_in, "seq", axis=1, tiled=True),
        lax.all_gather(w_out, "seq", axis=1, tiled=True),
        lax.all_gather(w_up, "seq", axis=1, tiled=True),
        lax.all_gather(w_down, "seq", axis=1, tiled=True),
        lax.all_gather(norm_gains, "seq", axis=1, tiled=True),
    )
    full_in, full_out, full_up, full_down, kernel_cols = (
        lax.all_gather(w_in_rows, "dp", axis=0, tiled=True),
        lax.all_gather(w_out_rows, "dp", axis=0, tiled=True),
        lax.all_gather(w_up_rows, "dp", axis=0, tiled=True),
        lax.all_gather(w_down_rows, "dp", axis=0, tiled=True),
        lax.all_gather(kernel, "dp", axis=0, tiled=True),
    )
    num_seqs, local_len, width = tokens_in.shape
    total_rows = num_seqs * local_len
    inputs = tokens_in.reshape(total_rows, width).astype(jnp.float32)
    gains_wide = gains.astype(jnp.float32)
    normed, norm_back_one = jax.vjp(norm_rows, inputs, gains_wide[0])
    normed_low = normed.astype(jnp.bfloat16)
    proj = jnp.dot(normed_low, full_in, preferred_element_type=jnp.float32)
    values = proj[:, :width]
    gate_one = proj[:, width : 2 * width]
    gate_two = proj[:, 2 * width :]
    mixed_low = (gate_one * values).astype(jnp.bfloat16).reshape(num_seqs, local_len, width)
    by_channel = to_channels(mixed_low)
    filt, filter_back = jax.vjp(partial(shape_filter, taps=taps), kernel_cols.astype(jnp.float32))
    filt_re, filt_im = forward_dft(filt[None])
    sig_re, sig_im = forward_dft(by_channel.astype(jnp.float32))
    conv = inverse_dft(sig_re * filt_re - sig_im * filt_im, sig_re * filt_im + sig_im * filt_re)
    conv_tok = to_tokens(conv.astype(jnp.bfloat16)).reshape(total_rows, width).astype(jnp.float32)
    gated = (gate_two * conv_tok).astype(jnp.bfloat16)
    resid = inputs + jnp.dot(gated, full_out, preferred_element_type=jnp.float32)
    normed_two, norm_back_two = jax.vjp(norm_rows, resid, gains_wide[1])
    normed_two_low = normed_two.astype(jnp.bfloat16)
    hidden_pre = jnp.dot(normed_two_low, full_up, preferred_element_type=jnp.float32)
    active, gelu_back = jax.vjp(gelu_tanh, hidden_pre)
    active_low = active.astype(jnp.bfloat16)
    result = (resid + jnp.dot(active_low, full_down, preferred_element_type=jnp.float32)).astype(
        jnp.bfloat16
    )
    grad_rows = cotangent.reshape(total_rows, width)
    grad_down = contract_rows(active_low, grad_rows)
    grad_active = times_transposed(grad_rows, full_down)
    grad_pre = gelu_back(grad_active)[0].astype(jnp.bfloat16)
    grad_up = contract_rows(normed_two_low, grad_pre)
    grad_normed_two = times_transposed(grad_pre, full_up)
    grad_resid_part, grad_gain_two = norm_back_two(grad_normed_two)
    grad_resid = grad_rows.astype(jnp.float32) + grad_resid_part
    resid_low = grad_resid.astype(jnp.bfloat16)
    grad_outw = contract_rows(gated, resid_low)
    grad_gated = times_transposed(resid_low, full_out)
    grad_gate_two = grad_gated * conv_tok
    grad_conv = (grad_gated * gate_two).astype(jnp.bfloat16).reshape(num_seqs, local_len, width)
    grad_channel = to_channels(grad_conv).astype(jnp.float32)
    back_re, back_im = forward_dft(grad_channel)
    grad_signal = inverse_dft(
        back_re * filt_re + back_im * filt_im, back_im * filt_re - back_re * filt_im
    )
    cross_re = jnp.sum(back_re * sig_re + back_im * sig_im, axis=0, keepdims=True)
    cross_im = jnp.sum(back_im * sig_re - back_re * sig_im, axis=0, keepdims=True)
    grad_filt = inverse_dft(cross_re, cross_im)[0]
    grad_kern = filter_back(grad_filt)[0]
    grad_mixed = (
        to_tokens(grad_signal.astype(jnp.bfloat16)).reshape(total_rows, width).astype(jnp.float32)
    )
    grad_proj = jnp.concatenate([grad_mixed * gate_one, grad_mixed * values, grad_gate_two], axis=1)
    grad_proj = grad_proj.astype(jnp.bfloat16)
    grad_inw = contract_rows(normed_low, grad_proj)
    grad_normed = times_transposed(grad_proj, full_in)
    grad_input_part, grad_gain_one = norm_back_one(grad_normed)
    grad_inputs = (
        (grad_resid + grad_input_part).astype(jnp.bfloat16).reshape(num_seqs, local_len, width)
    )
    grad_gain_pair = jnp.stack([grad_gain_one, grad_gain_two])
    in_part, outw_part, up_part, down_part, kern_done = (
        lax.psum_scatter(
            grad_inw.astype(jnp.bfloat16), "dp", scatter_dimension=0, tiled=True
        ).astype(jnp.float32),
        lax.psum_scatter(
            grad_outw.astype(jnp.bfloat16), "dp", scatter_dimension=0, tiled=True
        ).astype(jnp.float32),
        lax.psum_scatter(
            grad_up.astype(jnp.bfloat16), "dp", scatter_dimension=0, tiled=True
        ).astype(jnp.float32),
        lax.psum_scatter(
            grad_down.astype(jnp.bfloat16), "dp", scatter_dimension=0, tiled=True
        ).astype(jnp.float32),
        lax.psum_scatter(
            grad_kern.astype(jnp.bfloat16), "dp", scatter_dimension=0, tiled=True
        ).astype(jnp.float32),
    )
    in_done, outw_done, up_done, down_done, gain_part = (
        lax.psum_scatter(
            in_part.astype(jnp.bfloat16), "seq", scatter_dimension=1, tiled=True
        ).astype(jnp.float32),
        lax.psum_scatter(
            outw_part.astype(jnp.bfloat16), "seq", scatter_dimension=1, tiled=True
        ).astype(jnp.float32),
        lax.psum_scatter(
            up_part.astype(jnp.bfloat16), "seq", scatter_dimension=1, tiled=True
        ).astype(jnp.float32),
        lax.psum_scatter(
            down_part.astype(jnp.bfloat16), "seq", scatter_dimension=1, tiled=True
        ).astype(jnp.float32),
        lax.psum_scatter(
            grad_gain_pair.astype(jnp.bfloat16), "seq", scatter_dimension=1, tiled=True
        ).astype(jnp.float32),
    )
    gain_done = lax.psum(gain_part, "dp")
    return (
        result.reshape(num_seqs, local_len, width),
        grad_inputs,
        in_done,
        outw_done,
        up_done,
        down_done,
        gain_done,
        kern_done,
    )


MESH = pl.DeviceIdType.MESH
BF = jnp.bfloat16
F32 = jnp.float32


class Remote:
    def __init__(self, wire, slot, src, dst, peer):
        self.wire, self.slot, self.src, self.dst, self.peer = wire, slot, src, dst, peer
        self.sent = False

    def named(self):
        return pltpu.make_async_remote_copy(
            src_ref=self.src(), dst_ref=self.dst(), send_sem=self.wire.send.at[self.slot],
            recv_sem=self.wire.recv.at[self.slot], device_id=self.peer, device_id_type=MESH,
        )

    def wait_recv(self):
        self.named().wait_recv()


class Wire:
    def __init__(self, send, recv, spots):
        self.send, self.recv, self.s, self.made = send, recv, spots, []

    def start(self, src, dst, peer, core=None, buffer=None):
        src, dst = (end if callable(end) else partial(lambda ref: ref, end) for end in (src, dst))
        copy = Remote(self, len(self.made), src, dst, peer)
        copy.buffer = buffer
        copy.named().start()
        self.made.append((core, copy))
        return copy

    def drain(self, src=None):
        made = [(core, copy) for core, copy in self.made if not copy.sent and src in (None, copy.buffer)]
        for which in (None, 0, 1):
            @self.s.on(which)
            def _():
                for core, copy in made:
                    if core == which:
                        copy.named().wait_send()
        for _, copy in made:
            copy.sent = True


class Local:
    def __init__(self, sems):
        self.sems, self.made, self.open = sems, 0, []

    def start(self, src, dst):
        copy = pltpu.make_async_copy(src, dst, self.sems.at[self.made])
        self.made += 1
        copy.start()
        self.open.append(copy)
        return copy

    def wait(self, copy):
        copy.wait()
        self.open = [other for other in self.open if other is not copy]

    def drain(self):
        for copy in list(self.open):
            self.wait(copy)


def arrived(copies):
    for copy in copies:
        copy.wait_recv()


class Spots:
    def __init__(self, num_z):
        dp, sq = lax.axis_index("dp"), lax.axis_index("seq")
        z, x, y, c = dp // 2, dp % 2, sq // 2, sq % 2
        self.num_z = num_z
        self.z, self.x, self.y, self.c = z, x, y, c
        self.own = dict(x=x, y=y, z=z)
        self.size = dict(x=2, y=2, z=num_z)
        self.core = self.at(z, x, y, 1 - c)
        self.others = dict(x=[1 - x], y=[1 - y], z=[(z + k) % num_z for k in range(1, num_z)])
        self.along = dict(
            x=[self.at(z, 1 - x, y, c)], y=[self.at(z, x, 1 - y, c)],
            z=[self.at(other, x, y, c) for other in self.others["z"]],
        )
        self.group = [((y + i) % 2, (c + j) % 2) for i, j in ((1, 0), (1, 1), (0, 1))]
        self.mates = [self.at(z, x, yy, cc) for yy, cc in self.group]

    def at(self, z, x, y, c):
        return (z * 2 + x, y * 2 + c)

    def on(self, core):
        return (lambda body: body()) if core is None else pl.when(self.c == core)

    def greet(self):
        for peer in self.along["z"] + self.along["x"] + self.mates:
            pl.semaphore_signal(pltpu.get_barrier_semaphore(), inc=1, device_id=peer, device_id_type=MESH)

    def meet(self):
        pl.semaphore_wait(pltpu.get_barrier_semaphore(), len(self.along["z"] + self.along["x"] + self.mates))


def both_cores(orders):
    return [(None, orders[0])] if len(orders) == 1 else list(enumerate(orders))


def block_index(s, axes, wide, core, at=None):
    place = {**s.own, **(at or {})}
    index = tuple(slice(None) if axis in wide else place[axis] for axis in axes)
    return index if core is None else index + (core,)


class Gather:
    def __init__(self, wire, spots, full, axes, *orders, part=(), buffer=None):
        self.buffer = buffer
        self.wire, self.s, self.full, self.axes, self.part = wire, spots, full, axes, part
        self.orders, self.last = both_cores(orders), {}

    def view(self, have):
        return self.full.at[block_index(self.s, self.axes, have, self.s.c) + self.part]

    def settle(self):
        for core, copies in self.last.items():
            self.s.on(core)(partial(arrived, copies))
        self.last = {}

    def step(self, n):
        s = self.s
        if n == len(self.orders[0][1]):
            self.settle()
            view = partial(self.view, self.axes)
            self.last[None] = [self.wire.start(view, view, s.core, buffer=self.buffer)]
            return
        before, self.last = self.last, {}
        for core, order in self.orders:
            @s.on(core)
            def _():
                arrived(before.get(core, []))
                view = partial(self.view, order[:n])
                self.last[core] = [
                    self.wire.start(view, view, peer, core, self.buffer) for peer in s.along[order[n]]
                ]

    def done(self):
        self.settle()


class Rounds:
    LAG = 2

    def __init__(self, gathers):
        self.gathers, self.now = gathers, 0

    def run(self, count=1):
        for _ in range(count):
            for step in reversed(range(4)):
                k = self.now - step * self.LAG
                if 0 <= k < len(self.gathers) and step <= len(self.gathers[k].orders[0][1]):
                    self.gathers[k].step(step)
            self.now += 1


class Scatter:
    def __init__(self, wire, spots, total, axes, orders, from_core, got, result, part=()):
        self.wire, self.s, self.total, self.axes, self.part = wire, spots, total, axes, part
        self.orders = [(core, order[::-1]) for core, order in both_cores(orders)]
        self.from_core, self.got, self.result = from_core, got, result
        self.last = {}

    def mine(self, wide, at=None):
        return self.total.at[block_index(self.s, self.axes, wide, self.s.c, at) + self.part]

    def send_core(self):
        s = self.s
        whole = (slice(None),) * (len(self.axes) - 1)
        self.last = [
            self.wire.start(self.total.at[(i,) + whole + (1 - s.c,) + self.part],
                            self.from_core.at[(i,) + whole + self.part], s.core)
            for i in range(self.from_core.shape[0])
        ]

    def add_core(self):
        arrived(self.last)
        self.last = {}
        s = self.s
        count = math.prod(s.size[axis] for axis in self.axes)

        def one(i, _):
            at, left = {}, i
            for axis in reversed(self.axes):
                at[axis], left = left % s.size[axis], left // s.size[axis]
            into = self.mine("", at)
            term = self.from_core[tuple(at[axis] for axis in self.axes) + self.part]
            into[...] = (into[...].astype(F32) + term.astype(F32)).astype(BF)
            return 0
        lax.fori_loop(0, count, one, 0)

    def stages(self, order, n):
        s = self.s
        begin = 0
        for k in range(n + 1):
            wide = sorted(order[k + 1 :])
            count = math.prod(s.size[axis] for axis in wide)
            if k < n:
                begin += count * (s.size[order[k]] - 1)
        return order[n], wide, count, begin

    def slots(self, start, count):
        return self.got.at[(start if count is None else slice(start, start + count),) + self.part]

    def send(self, n):
        s = self.s
        for core, order in self.orders:
            axis, wide, count, begin = self.stages(order, n)

            @s.on(core)
            def _():
                self.last[core] = []
                for j, (other, peer) in enumerate(zip(s.others[axis], s.along[axis])):
                    outer = s.size[wide[0]] if len(wide) == 2 else 1
                    inner = count // outer
                    for i in range(outer):
                        at = {axis: other}
                        if len(wide) == 2:
                            at[wide[0]] = i
                        start = begin + j * count + i * inner
                        src = partial(self.mine, wide[-1:], at)
                        dst = partial(self.slots, start, inner if wide else None)
                        self.last[core].append(self.wire.start(src, dst, peer, core))

    def add(self, n):
        s = self.s
        for core, order in self.orders:
            axis, wide, count, begin = self.stages(order, n)
            peers = len(s.others[axis])

            @s.on(core)
            def _():
                arrived(self.last[core])
                if n == len(order) - 1:
                    total = self.mine("")[...].astype(F32)
                    for j in range(peers):
                        total = total + self.got[(begin + j,) + self.part].astype(F32)
                    self.result[self.part or ...] = total
                    return

                def one(i, _):
                    at, left = {}, i
                    for a in reversed(wide):
                        at[a], left = left % s.size[a], left // s.size[a]
                    into = self.mine("", at)
                    total = into[...].astype(F32)
                    for j in range(peers):
                        total = total + self.got[(begin + j * count + i,) + self.part].astype(F32)
                    into[...] = total.astype(BF)
                    return 0
                lax.fori_loop(0, count, one, 0)


    def go(self, n):
        if n == 0:
            self.add_core()
        else:
            self.add(n - 1)
        if n < len(self.orders[0][1]):
            self.send(n)


class Trade:
    def __init__(self, wire, spots, halves, ends):
        self.s, self.ends, self.pieces = spots, ends, len(halves[0])
        for core in range(2):
            for i, piece in enumerate(halves[core]):
                ends[core, i] = piece
        self.copy = wire.start(ends.at[1 - spots.c], ends.at[2], spots.core)

    def finish(self, out, turned=False):
        self.copy.wait_recv()
        c = self.s.c
        own, other = (
            jnp.concatenate([self.ends[k, i] for i in range(self.pieces)], axis=-1) for k in (c, 2)
        )
        both = jnp.concatenate([jnp.where(c == 0, own, other), jnp.where(c == 0, other, own)], axis=0)
        out[...] = both.T if turned else both


def column_halves(total):
    part = total.shape[-1] // 2
    return [[total[:, core * part : (core + 1) * part]] for core in range(2)]


def row_parts(rows):
    size = rows // PARTS
    return [(slice(i * size, (i + 1) * size),) for i in range(PARTS)]


def norm_parts(values):
    center = values - jnp.mean(values, axis=-1, keepdims=True)
    spread = jnp.mean(center * center, axis=-1, keepdims=True)
    scale = lax.rsqrt(spread + EPSILON)
    return center * scale, scale


def norm_back(normal, scale, grad, gain):
    p = grad * gain
    flat = jnp.mean(p, axis=-1, keepdims=True)
    along = jnp.mean(p * normal, axis=-1, keepdims=True)
    return (p - flat - normal * along) * scale, jnp.sum(grad * normal, axis=0, keepdims=True)


def dot(left, right):
    return jnp.dot(left, right, preferred_element_type=F32)


def dot_rows(left, right):
    return lax.dot_general(left, right, (((0,), (0,)), ((), ())), preferred_element_type=F32)


def dot_cols(left, right):
    return lax.dot_general(left, right, (((1,), (1,)), ((), ())), preferred_element_type=F32)


def live_taps(kern, taps):
    position = lax.broadcasted_iota(jnp.int32, kern.shape, 0)
    return position, position.astype(F32) < taps


def pool(values, position):
    length = values.shape[0]
    before = jnp.where(position == 0, 0.0, pltpu.roll(values, 1, 0))
    after = jnp.where(position == length - 1, 0.0, pltpu.roll(values, length - 1, 0))
    return (before + values + after) / 3.0


def make_filter(kern, taps):
    position, live = live_taps(kern, taps)
    masked = jnp.where(live, kern, 0.0)
    shrunk = masked - SHRINK_SCALE * jnp.tanh(masked / SHRINK_SCALE)
    return jnp.where(live, pool(shrunk, position), 0.0)


def kernel_back(kern, taps, grad):
    position, live = live_taps(kern, taps)
    slope = jnp.tanh(jnp.where(live, kern, 0.0) / SHRINK_SCALE)
    return jnp.where(live, pool(jnp.where(live, grad, 0.0), position) * slope * slope, 0.0)


GELU_K = math.sqrt(2.0 / math.pi)


def gelu_both(v):
    square = v * v
    t = jnp.tanh(GELU_K * v * (1.0 + 0.044715 * square))
    half = 0.5 * (1.0 + t)
    slope = half + 0.5 * v * (1.0 - t * t) * (GELU_K * (1.0 + 3 * 0.044715 * square))
    return v * half, slope


def spans(start, size, step=16):
    return pl.ds(pl.multiple_of(start, step), size)


def transform_table(length):
    k = 2 * np.arange(length)[:, None] + 1
    angle = np.pi / (4 * length) * ((k * k.T) % (8 * length))
    return np.concatenate([np.cos(angle), np.sin(angle)]).astype(np.float32).astype(ml_dtypes.bfloat16)


def twist_table(length):
    angle = np.pi / (4 * length) * (2 * np.arange(length) + 1)
    return np.stack([np.cos(angle), np.sin(angle)], axis=1).astype(np.float32)


ORDER_OUT = ("zxy", "zyx")
ORDER_UP = ("zxy", "yzx")
ORDER_DOWN = ("zxy", "yzx")
BACK_OUT = ("zxy", "zyx")
BACK_UP = ("zxy", "yzx")
BACK_DOWN = ("zxy", "yzx")
PARTS = 4
STEP = 256


def layer_kernel(
    num_z, length,
    tok, cot, w_in, w_out, w_up, w_down_t, kern_t, gains_in, taps_in, twist, table_hbm,
    out_o, grad_in_o, gin_o, gout_o, gup_o, gdn_o, gains_o, gkern_o,
    win_v, wout_v, wup_v, wdown_v, gdn_v, kern_v, small_v,
    pre_in, pre_out, pre_up, pre_down, pre_kern, w_down, kern,
    table_v, proj_v, normed_own, normed_v, sig_v, spec_v, filt_v, turned_v, conv_v, gated_ch,
    gated_v, resid_v, normed_two_v, act_v, slope_v,
    core_in, core_out, core_dn, core_kern,
    got_in, got_out, got_up, got_dn, got_kern,
    sum_in, sum_out, sum_up, sum_dn, sum_kern,
    ends_out, ends_up, ends_dn, ends_kern, swap_core, swap_y,
    gain_v, gain_got,
    send, recv, local,
):
    s = Spots(num_z)
    z, x, y, c = s.z, s.x, s.y, s.c
    wire, inner = Wire(send, recv, s), Local(local)
    load_table = inner.start(table_hbm, table_v)
    rows, width = tok.shape
    group, span = width // 2, rows // 2
    hidden = act_v.shape[1]
    block = width // (4 * num_z)
    me = 2 * y + c
    chunk, home = spans(me * span, span), spans(c * span, span)
    w_down[...] = w_down_t[...].T
    kern[...] = kern_t[...].T
    small_v[me, 0:2] = gains_in[...].astype(F32)
    small_v[me, 2:3] = taps_in[...].astype(F32)
    tile = 128

    def norm_one(i, _):
        at = spans(i * tile, tile)
        resid_v[at], _ = norm_parts(tok[at].astype(F32))
        return 0
    s.greet()
    lax.fori_loop(0, rows // tile, norm_one, 0)
    s.meet()

    smalls = [wire.start(small_v.at[me], small_v.at[me], peer) for peer in s.mates]
    half = w_in.shape[0] // 2
    trade_in = [
        wire.start(w_in.at[spans(cc * half, half)], pre_in.at[me], peer) for (yy, cc), peer in zip(s.group, s.mates)
    ]
    pairs = [(kern, pre_kern), (w_out, pre_out), (w_up, pre_up), (w_down, pre_down)]
    traded = []
    for src, pre in pairs:
        half = src.shape[0] // 2
        traded.append(wire.start(src.at[spans((1 - c) * half, half)], pre.at[c], s.core))
    half = w_in.shape[0] // 2
    pre_in[me] = w_in[spans(c * half, half)]
    for src, pre in pairs:
        half = src.shape[0] // 2
        pre[c] = src[spans(c * half, half)]

    g_in = [Gather(wire, s, win_v, "zx", "zx", part=(k,), buffer="in") for k in range(3)]
    g_kern = Gather(wire, s, kern_v, "zx", "zx", buffer="kern")
    g_out = Gather(wire, s, wout_v, "yzx", *ORDER_OUT)
    parts = row_parts(wup_v.shape[-2])
    g_up = [Gather(wire, s, wup_v, "yzx", *ORDER_UP, part=part, buffer="up") for part in parts]
    g_down = [Gather(wire, s, wdown_v, "yzx", *ORDER_DOWN, part=part, buffer="down") for part in parts]
    rounds = Rounds([*g_in, g_kern, g_out, *g_up, *g_down])

    def join(i):
        traded[i].wait_recv()
        pre = pairs[i][1]
        return jnp.concatenate([pre[0], pre[1]], axis=-1)

    arrived(smalls)
    gains = jnp.concatenate([small_v[k] for k in range(4)], axis=-1)

    def normed_rows(i, _):
        at = spans(i * tile, tile)
        normed_own[at] = (resid_v[at] * gains[0:1]).astype(BF)
        return 0
    lax.fori_loop(0, rows // tile, normed_rows, 0)
    to_group = [
        wire.start(normed_own.at[spans(cc * span, span)], normed_v.at[chunk], peer, buffer="normed")
        for (yy, cc), peer in zip(s.group, s.mates)
    ]
    normed_v[chunk] = normed_own[home]
    arrived(trade_in)
    whole = jnp.concatenate([pre_in[k] for k in range(4)], axis=-1)
    for k in range(3):
        left, right = (whole[:, (2 * k + h) * group : (2 * k + h + 1) * group] for h in range(2))
        win_v[z, x, c, k] = jnp.where(y == 0, left, right)
        if k < 2:
            rounds.run()

    kern_v[z, x, c] = join(0)
    wout_v[y, z, x, c] = join(1)
    both = join(2)
    pieces = both.shape[-1] // group
    for q in range(pieces):
        wup_v[y, z, x, c, q * block : (q + 1) * block] = both[:, q * group : (q + 1) * group]
    wdown_v[y, z, x, c] = join(3)
    rounds.run(5)

    arrived(to_group)
    g_in[0].done()
    g_in[1].done()

    def project(k, at):
        return dot(normed_v[at], win_v[:, :, :, k].reshape(width, group))

    def mix(i, _):
        at = spans(i * STEP, STEP, STEP)
        value, gate = project(0, at), project(1, at)
        proj_v[0, at] = value.astype(BF)
        proj_v[1, at] = gate.astype(BF)
        sig_v[at] = (value * gate).astype(BF)
        return 0
    lax.fori_loop(0, length // STEP, mix, 0)
    rounds.run()
    g_in[2].done()

    def second_gate(i, _):
        at = spans(i * STEP, STEP, STEP)
        proj_v[2, at] = project(2, at).astype(BF)
        return 0
    lax.fori_loop(0, length // STEP, second_gate, 0)
    rounds.run()

    g_kern.done()
    taps_v = gain_v.at[2, 0:1]
    taps_v[:, 0:group] = jnp.concatenate([small_v[2 * y], small_v[2 * y + 1]], axis=-1)[2:3]

    def shape_taps(j, _):
        cols = spans(j * tile, tile, tile)
        filt = make_filter(kern_v[:, :, :, :, cols].reshape(length, tile).astype(F32), taps_v[:, cols])
        gated_ch[:, cols] = filt.astype(BF)
        return 0
    lax.fori_loop(0, group // tile, shape_taps, 0)
    inner.wait(load_table)

    def spectrum(i, _):
        real, imag = spans(i * STEP, STEP, STEP), spans(length + i * STEP, STEP, STEP)
        re, im = dot(table_v[real], gated_ch[...]), dot(table_v[imag], gated_ch[...])
        cosine, sine = twist[real, 0:1], twist[real, 1:2]
        filt_v[real] = (re * cosine + im * sine).astype(BF)
        filt_v[imag] = (im * cosine - re * sine).astype(BF)
        return 0
    lax.fori_loop(0, length // STEP, spectrum, 0)
    rounds.run()

    def convolve(i, _):
        real, imag = spans(i * STEP, STEP, STEP), spans(length + i * STEP, STEP, STEP)
        re_s, im_s = dot(table_v[real], sig_v[...]), dot(table_v[imag], sig_v[...])
        spec_v[real] = re_s.astype(BF)
        spec_v[imag] = im_s.astype(BF)
        re_f, im_f = filt_v[real].astype(F32), filt_v[imag].astype(F32)
        turned_v[real] = (re_s * re_f - im_s * im_f).astype(BF)
        turned_v[imag] = (re_s * im_f + im_s * re_f).astype(BF)
        return 0
    lax.fori_loop(0, length // STEP, convolve, 0)
    rounds.run()

    def back(i, _):
        at, imag = spans(i * STEP, STEP, STEP), spans(length + i * STEP, STEP, STEP)
        both = dot(table_v[at], turned_v[0:length]) + dot(table_v[imag], turned_v[length:])
        conv = (both * (1.0 / length)).astype(BF)
        conv_v[at] = conv
        gated_ch[at] = (proj_v[2, at].astype(F32) * conv.astype(F32)).astype(BF)
        return 0
    lax.fori_loop(0, length // STEP, back, 0)

    to_tokens = [
        wire.start(gated_ch.at[spans((2 * yy + cc) * span, span)], gated_v.at[y, home], peer, buffer="gated")
        for (yy, cc), peer in zip(s.group, s.mates)
    ]
    gated_v[y, home] = gated_ch[chunk]
    rounds.run()
    g_out.done()
    rounds.run()
    arrived(to_tokens)

    for k in range(2):
        cols = slice(k * group, (k + 1) * group)
        mixed = sum(
            dot(gated_v[h], wout_v[k, h * num_z // 2 : (h + 1) * num_z // 2].reshape(group, group)) for h in range(2)
        )
        resid_v[:, cols] = tok[:, cols].astype(F32) + mixed

    def norm_two(i, _):
        at = spans(i * tile, tile)
        normed, _ = norm_parts(resid_v[at])
        normed_two_v[at] = (normed * gains[1:2]).astype(BF)
        return 0
    lax.fori_loop(0, rows // tile, norm_two, 0)

    def piece(ref, j):
        return ref.at[j // pieces, :, :, :, spans((j % pieces) * block, block)]

    for q in range(pieces):
        g_up[q].done()

        def feed(i, _):
            j = i // 2 * pieces + q
            at, cols = spans(i % 2 * span, span), spans(j * group, group, 128)
            act, slope = gelu_both(dot(normed_two_v[at], piece(wup_v, j)[...].reshape(width, group)))
            act_v[at, cols] = act.astype(BF)
            slope_v[at, cols] = slope.astype(BF)
            return 0
        lax.fori_loop(0, 4, feed, 0)
        rounds.run()

    down = [Scatter(wire, s, gdn_v, "yzx", BACK_DOWN, core_dn, got_dn, sum_dn, part=part) for part in parts]
    deep = hidden // (2 * num_z)

    def down_grad(i, _):
        grad = dot_rows(act_v[:, spans(i * deep, deep, 128)], cot[...]).astype(BF)
        for h in range(2):
            gdn_v[h, i // 2, i % 2] = grad[:, h * group : (h + 1) * group].reshape(2, deep // 2, group)
        return 0
    lax.fori_loop(0, 2 * num_z, down_grad, 0)
    rounds.run()
    for g in down:
        g.send_core()
    rounds.run()
    for g in g_down:
        g.done()
    for g in down:
        g.go(0)

    def pre_grad(i, _):
        at, cols = spans(i // num_z * span, span), spans(i % num_z * 2 * deep, 2 * deep, 128)
        grad = sum(
            dot_cols(cot[at, h * group : (h + 1) * group], wdown_v[h, i % num_z].reshape(2 * deep, group))
            for h in range(2)
        )
        slope_v[at, cols] = (slope_v[at, cols].astype(F32) * grad).astype(BF)
        return 0
    lax.fori_loop(0, 2 * num_z, pre_grad, 0)
    gpre_v = slope_v

    wire.drain("normed")
    low_v = normed_own
    gnorm_got = [[turned_v.at[(2 * i + h) * span : (2 * i + h + 1) * span] for h in range(2)] for i in range(3)]
    gout_v, gup_v, gin_v = wdown_v.at[:, :, :, :, 0:block], wup_v, win_v
    gch_v, gkern_v = sig_v, kern_v
    ggate_v = gated_ch
    up = [Scatter(wire, s, gup_v, "yzx", BACK_UP, core_dn, got_up, sum_up, part=part) for part in parts]
    out = Scatter(wire, s, gout_v, "yzx", BACK_OUT, core_out, got_out, sum_out)
    into = [Scatter(wire, s, gin_v, "zx", ("zx",), core_in, got_in, sum_in, part=(k,)) for k in range(3)]
    taps_grad = Scatter(wire, s, gkern_v, "zx", ("zx",), core_kern, got_kern, sum_kern)


    def norm_two_back(i, gain):
        at = spans(i * span, span)

        grad = sum(
            dot_cols(gpre_v[at, j * group : (j + 1) * group], piece(wup_v, j)[...].reshape(width, group))
            for j in range(2 * pieces)
        )
        normal, scale = norm_parts(resid_v[at])
        part, more = norm_back(normal, scale, grad, gains[1:2])
        low_v[at] = (cot[at].astype(F32) + part).astype(BF)
        return gain + more
    gain_two = lax.fori_loop(0, 2, norm_two_back, jnp.zeros((1, width), F32))

    wire.drain("gated")
    for h in range(2):
        grad = sum(
            dot_cols(
                low_v[:, k * group : (k + 1) * group],
                wout_v[k, h * num_z // 2 : (h + 1) * num_z // 2].reshape(group, group),
            )
            for k in range(2)
        )
        ggate_v[h * rows : (h + 1) * rows] = grad.astype(BF)
    to_channels = [
        wire.start(ggate_v.at[spans(yy * rows + cc * span, span)], gch_v.at[chunk], peer)
        for (yy, cc), peer in zip(s.group, s.mates)
    ]
    gch_v[chunk] = ggate_v[spans(y * rows + c * span, span)]
    wire.drain("up")

    def up_grad(q, yy, _):
        j = yy * pieces + q
        grad = dot_rows(normed_two_v[...], gpre_v[:, spans(j * group, group, 128)]).astype(BF)
        piece(gup_v, j)[...] = grad.reshape(num_z, 2, 2, block, group)
        return 0

    for q in range(pieces):
        lax.fori_loop(0, 2, partial(up_grad, q), 0)
        if q == 0:
            arrived(to_channels[2:])
        up[q].send_core()
        if q % 2:
            down[q - 1].go(1)
            down[q].go(1)
            up[q - 1].go(0)

    def down_out(i, _):
        at = spans(i * span, span)
        grown = jnp.concatenate([dot(act_v[at], wdown_v[h].reshape(hidden, group)) for h in range(2)], axis=-1)
        act_v[at, 0:width] = (resid_v[at] + grown).astype(BF)
        return 0
    lax.fori_loop(0, 2, down_out, 0)
    inner.start(act_v.at[:, 0:width], out_o)
    up[1].go(0)
    up[3].go(0)
    wire.drain("down")

    def out_grad(i, _):
        h, k = i // 2, i % 2
        grad = dot_rows(gated_v[h], low_v[:, spans(k * group, group, 128)]).astype(BF)
        gout_v[k, pl.ds(h * (num_z // 2), num_z // 2)] = grad.reshape(num_z // 2, 2, 2, block, group)
        return 0
    lax.fori_loop(0, 4, out_grad, 0)
    out.send_core()
    down[0].go(2)
    down[1].go(2)
    out.go(0)

    arrived(to_channels[:2])

    def gate(i, _):
        at = spans(i * STEP, STEP, STEP)
        grad = gch_v[at].astype(F32)
        gch_v[at] = (grad * proj_v[2, at].astype(F32)).astype(BF)
        proj_v[2, at] = (grad * conv_v[at].astype(F32)).astype(BF)
        return 0
    lax.fori_loop(0, length // STEP, gate, 0)

    wire.drain("in")

    def in_grad(k):
        grad = dot_rows(normed_v[...], proj_v[k]).astype(BF)
        gin_v[:, :, :, k] = grad.reshape(num_z, 2, 2, block, group)
        into[k].send_core()

    def turn(i, _):
        real, imag = spans(i * STEP, STEP, STEP), spans(length + i * STEP, STEP, STEP)
        re, im = dot(table_v[real], gch_v[...]), dot(table_v[imag], gch_v[...])
        re_f, im_f = filt_v[real].astype(F32), filt_v[imag].astype(F32)
        filt_v[real] = (re_f * re + im_f * im).astype(BF)
        filt_v[imag] = (re_f * im - im_f * re).astype(BF)
        re_s, im_s = spec_v[real].astype(F32), spec_v[imag].astype(F32)
        re_k, im_k = re_s * re + im_s * im, re_s * im - im_s * re
        cosine, sine = twist[real, 0:1], twist[real, 1:2]
        spec_v[real] = (re_k * cosine - im_k * sine).astype(BF)
        spec_v[imag] = (im_k * cosine + re_k * sine).astype(BF)
        return 0
    lax.fori_loop(0, length // STEP, turn, 0)
    down[2].go(2)
    down[3].go(2)
    up[0].go(1)
    up[1].go(1)

    def signal_back(i, _):
        at, imag = spans(i * STEP, STEP, STEP), spans(length + i * STEP, STEP, STEP)
        both = dot(table_v[at], filt_v[0:length]) + dot(table_v[imag], filt_v[length:])
        grad = (both * (1.0 / length)).astype(BF).astype(F32)
        value, first = proj_v[0, at].astype(F32), proj_v[1, at].astype(F32)
        proj_v[0, at] = (grad * first).astype(BF)
        proj_v[1, at] = (grad * value).astype(BF)
        return 0
    lax.fori_loop(0, length // STEP, signal_back, 0)

    def part_at(j, h):
        return gpre_v.at[spans(j % 2 * span, span), spans(j // 2 * width + h * group, group, 128)]

    to_owner = []
    for h in range(2):
        grad = sum(
            dot_cols(proj_v[k], win_v[h * num_z // 2 : (h + 1) * num_z // 2, :, :, k].reshape(group, group))
            for k in range(3)
        ).astype(BF)
        for j in range(4):
            part_at(j, h)[...] = grad[j * span : (j + 1) * span]
        to_owner += [
            wire.start(partial(part_at, 2 * yy + cc, h), gnorm_got[i][h], peer)
            for i, ((yy, cc), peer) in enumerate(zip(s.group, s.mates))
        ]

    up[2].go(1)
    up[3].go(1)
    for k in range(3):
        in_grad(k)
    up[0].go(2)
    for k in range(3):
        into[k].go(0)

    def gain_part(j, total):
        grad = jnp.concatenate([part_at(j, h)[...].astype(F32) for h in range(2)], axis=-1)
        return total + jnp.sum(grad * normed_v[spans(j * span, span)].astype(F32), axis=0, keepdims=True)
    gain_one = lax.fori_loop(0, 4, gain_part, jnp.zeros((1, width), F32)) / gains[0:1]
    gain_v[0] = jnp.concatenate([gain_one, gain_two, jnp.zeros((6, width), F32)], axis=0)
    gain_got_one = [wire.start(gain_v.at[0], gain_got.at[k], peer) for k, peer in enumerate(s.mates)]
    up[1].go(2)
    out.go(1)

    wire.drain("kern")

    def taps_signal(i, _):
        at, imag = spans(i * STEP, STEP, STEP), spans(length + i * STEP, STEP, STEP)
        both = dot(table_v[at], spec_v[0:length]) + dot(table_v[imag], spec_v[length:])
        resid_v[spans(i % tall * STEP, STEP, STEP), spans(i // tall * group, group, 128)] = both
        return 0
    tall = rows // STEP
    lax.fori_loop(0, length // STEP, taps_signal, 0)

    def taps_back(j, _):
        cols = spans(j * tile, tile, tile)
        both = jnp.concatenate([resid_v[:, cols], resid_v[:, spans(group + j * tile, tile, tile)]], axis=0)
        grad = kernel_back(kern_v[:, :, :, :, cols].reshape(length, tile).astype(F32), taps_v[:, cols],
                           both * (1.0 / length))
        gkern_v[:, :, :, :, cols] = grad.astype(BF).reshape(num_z, 2, 2, length // (4 * num_z), tile)
        return 0
    lax.fori_loop(0, group // tile, taps_back, 0)
    taps_grad.send_core()
    for k in range(3):
        into[k].go(1)
    taps_grad.go(0)
    up[2].go(2)
    up[3].go(2)
    arrived(to_owner)
    arrived(gain_got_one)
    gain_v[1] = gain_v[0] + gain_got[0] + gain_got[1] + gain_got[2]
    got = [wire.start(gain_v.at[1], gain_got.at[3], s.along["x"][0])]

    def norm_one_back(i, _):
        at, within = spans(i * tile, tile), spans(i % (span // tile) * tile, tile)
        across, diagonal, beside = (
            jnp.concatenate([ref[within].astype(F32) for ref in pair], axis=-1) for pair in gnorm_got
        )
        here = jnp.concatenate([part_at(me, h)[within].astype(F32) for h in range(2)], axis=-1)
        grad = jnp.where(c == i // (span // tile), here + across, beside + diagonal)
        normal, scale = norm_parts(tok[at].astype(F32))
        part, _ = norm_back(normal, scale, grad, gains[0:1])
        low_v[at] = (low_v[at].astype(F32) + part).astype(BF)
        return 0
    lax.fori_loop(0, rows // tile, norm_one_back, 0)
    inner.start(low_v, grad_in_o)

    for k in range(4):
        down[k].go(3)
    trade_dn = Trade(wire, s, column_halves(sum_dn), ends_dn)
    taps_grad.go(1)
    out.go(2)

    for k in range(4):
        up[k].go(3)
    rows_half = pieces // 2 * block
    column_pieces = [
        [sum_up[core * rows_half + q * block : core * rows_half + (q + 1) * block] for q in range(pieces // 2)]
        for core in range(2)
    ]
    arrived(got)
    gain_v[2] = gain_v[1] + gain_got[3]
    got = [wire.start(gain_v.at[2], gain_got.at[3 + k], peer) for k, peer in zip(range(1, num_z), s.along["z"])]
    trade_up = Trade(wire, s, column_pieces, ends_up)
    out.go(3)
    trade_out = Trade(wire, s, column_halves(sum_out), ends_out)

    for k in range(3):
        into[k].go(2)
    first, second, third = sum_in[y], sum_in[y + 1], sum_in[(y + 2) % 3]
    swap_core[0, 0], swap_core[0, 1] = first.astype(BF), second.astype(BF)
    swap_y[0] = third.astype(BF)
    swaps = [wire.start(swap_y.at[0], swap_y.at[1], s.mates[0]), wire.start(swap_y.at[0], swap_y.at[2], s.mates[1]),
             wire.start(swap_core.at[0], swap_core.at[1], s.core)]
    taps_grad.go(2)
    trade_kern = Trade(wire, s, column_halves(sum_kern), ends_kern)
    trade_dn.finish(gdn_o, turned=True)
    trade_up.finish(gup_o)
    trade_out.finish(gout_o)
    arrived(got)
    total = gain_v[2]
    for k in range(1, num_z):
        total = total + gain_got[3 + k]
    part = width // 4
    mine = total[:, 0:part]
    for k in range(1, 4):
        mine = jnp.where(me == k, total[:, k * part : (k + 1) * part], mine)
    gains_o[...] = mine[0:2]
    trade_kern.finish(gkern_o, turned=True)
    arrived(swaps)
    cut = group // 2
    for row, near, far in ((c, swap_core.at[0], swap_y.at[1]), (1 - c, swap_core.at[1], swap_y.at[2])):
        far = far[...].astype(F32)
        left = jnp.concatenate([near[0].astype(F32), far[:, 0:cut]], axis=-1)
        right = jnp.concatenate([far[:, cut:], near[1].astype(F32)], axis=-1)
        gin_o[spans(row * block, block)] = jnp.where(c == 0, left, right)
    wire.drain()
    inner.drain()


def vm(shape, dtype=BF):
    return pltpu.VMEM(tuple(shape), dtype)


VMEM_SPEC, HBM_SPEC = pl.BlockSpec(memory_space=pltpu.VMEM), pl.BlockSpec(memory_space=pl.ANY)


def layer(num_z, length, tokens, cot, w_in, w_out, w_up, w_down_t, kernel_t, gains, taps, twist, table):
    rows, width = tokens.shape
    group = width // 2
    part = w_down_t.shape[1]
    hidden = part * num_z * 2
    block = w_in.shape[0] // 2
    sds = jax.ShapeDtypeStruct
    axes = (2, num_z, 2, 2)
    units = dict(
        win=(3, block, group), wout=(block, group), wup=(hidden // width * block, group), wdown=(part // 2, group),
        kern=(kernel_t.shape[1] // 2, group),
    )
    lead = {name: axes[1:] if name in ("win", "kern") else axes for name in units}
    outs = [sds((rows, width), BF)] * 2
    outs += [sds((w.shape[0], w.shape[1]), F32) for w in (w_in, w_out, w_up, w_down_t)]
    outs += [sds((2, width // 4), F32), sds(kernel_t.shape, F32)]
    channel = vm((length, group))
    both = vm((2 * length, group))
    token = vm((rows, width))
    scratch = [vm(lead[name] + units[name]) for name in ("win", "wout", "wup", "wdown", "wdown", "kern")]
    scratch += [vm((4, 8, width // 4), F32)]
    scratch += [vm((4, block, w_in.shape[1])), vm((2, block, w_out.shape[1])), vm((2, block, w_up.shape[1])),
                vm((2, part // 2, w_down_t.shape[0])), vm((2, kernel_t.shape[1] // 2, kernel_t.shape[0])),
                vm(w_down_t.shape[::-1]), vm(kernel_t.shape[::-1])]
    scratch += [vm(table.shape), vm((3, length, group)), token, vm((length, width)), channel, both, both, both, channel,
                channel, vm((2, rows, group)), vm((rows, width), F32), token, vm((rows, hidden)), vm((rows, hidden))]
    names = ("win", "wout", "wup", "wdown", "kern")
    scratch += [vm(lead[name][:-1] + units[name]) for name in names if name != "wup"]
    blocks = {name: math.prod(lead[name]) // 2 - 1 for name in names}
    scratch += [vm((blocks[name],) + units[name]) for name in names] + [vm(units[name], F32) for name in names]
    scratch += [vm((3, 1, block, group // 2), F32), vm((3, hidden // width // 2, block, group), F32),
                vm((3, 1, part // 2, group // 2), F32), vm((3, 1, kernel_t.shape[1] // 2, group // 2), F32)]
    scratch += [vm((2, 2, block, group)), vm((3, block, group)), vm((3, 8, width), F32), vm((3 + num_z, 8, width), F32)]
    scratch += [pltpu.SemaphoreType.DMA((320,)), pltpu.SemaphoreType.DMA((320,)), pltpu.SemaphoreType.DMA((8,))]
    return pl.pallas_call(
        partial(layer_kernel, num_z, length),
        out_shape=outs,
        in_specs=[VMEM_SPEC] * 10 + [HBM_SPEC],
        out_specs=[HBM_SPEC] * 2 + [VMEM_SPEC] * 6,
        scratch_shapes=scratch,
        compiler_params=pltpu.CompilerParams(collective_id=0, has_side_effects=True, vmem_limit_bytes=67 * 10**6),
        cost_estimate=pl.CostEstimate(flops=34 * 10**9, bytes_accessed=20 * 10**6, transcendentals=2 * 10**6),
    )(tokens, cot, w_in, w_out, w_up, w_down_t, kernel_t, gains, taps, twist, table)


def publish(*arrays):
    count = len(arrays)

    def copy_all(*refs):
        held, sems = refs[2 * count : 3 * count], refs[3 * count]
        loads = [pltpu.make_async_copy(refs[i], held[i], sems.at[0, i]) for i in range(count)]
        stores = [pltpu.make_async_copy(held[i], refs[count + i], sems.at[1, i]) for i in range(count)]
        for load in loads:
            load.start()
        for load, store in zip(loads, stores):
            load.wait()
            store.start()
        for store in stores:
            store.wait()

    return pl.pallas_call(
        copy_all,
        out_shape=[jax.ShapeDtypeStruct(a.shape, a.dtype) for a in arrays],
        in_specs=[HBM_SPEC] * count,
        out_specs=[HBM_SPEC] * count,
        scratch_shapes=[vm(a.shape, a.dtype) for a in arrays] + [pltpu.SemaphoreType.DMA((2, count))],
    )(*arrays)


def fits(num_dp, num_seq, tokens, w_in, w_out, w_up, w_down, kernel):
    if num_seq != 4 or num_dp % 4 or kernel.shape[0] * num_dp > 1024 or kernel.shape[0] * num_dp % 512:
        return False
    blocks = (w_in, w_out, w_up, w_down, kernel)
    return all(b.shape[0] % 32 == 0 and b.shape[1] * 2 % 128 == 0 for b in blocks) and tokens.shape[0] == 2


def body(num_dp, num_seq, tokens_in, w_in, w_out, w_up, w_down, norm_gains, kernel, taps, cotangent):
    if not fits(num_dp, num_seq, tokens_in, w_in, w_out, w_up, w_down, kernel):
        return general_body(tokens_in, w_in, w_out, w_up, w_down, norm_gains, kernel, taps, cotangent)
    width = tokens_in.shape[-1]
    length = kernel.shape[0] * num_dp
    table, twist = jnp.asarray(transform_table(length)), jnp.asarray(twist_table(length))
    tokens, cot = tokens_in.reshape(-1, width), cotangent.reshape(-1, width)
    results = layer(num_dp // 2, length, tokens, cot, w_in, w_out, w_up, w_down.T, kernel.T, norm_gains, taps[None],
                    twist, table)
    out, grad_in, gin, gout, gup, gdn, gains, gkern = publish(*results)
    return (out.reshape(tokens_in.shape), grad_in.reshape(tokens_in.shape), gin, gout, gup, gdn.T, gains, gkern.T)


def solution(mesh):
    return jax.shard_map(
        partial(body, mesh.shape["dp"], mesh.shape["seq"]),
        mesh=mesh,
        in_specs=(
            P("dp", "seq", None),
            P("dp", "seq"),
            P("dp", "seq"),
            P("dp", "seq"),
            P("dp", "seq"),
            P(None, "seq"),
            P("dp", "seq"),
            P("seq"),
            P("dp", "seq", None),
        ),
        out_specs=(
            P("dp", "seq", None),
            P("dp", "seq", None),
            P("dp", "seq"),
            P("dp", "seq"),
            P("dp", "seq"),
            P("dp", "seq"),
            P(None, "seq"),
            P("dp", "seq"),
        ),
        check_vma=False,
    )
```
